32 devices in a mesh: dp: 8 (over y, x, core), head: 4 (over z).
Axes of the slice: x: 2, y: 2, z: 4, core: 2. Of those that a mesh axis runs over, the one named last changes fastest.
Arguments:
- tokens: bfloat16 [16384, 768], P(('dp', 'head')), may hold values from -6 to 6
- cotangent: float32 [16384, 768], P(('dp', 'head')), may hold values from -6 to 6
- lengths: int32 [16], P('dp'), may hold values from 128 to 1920, as said below
- qkv_master: float32 [768, 2304], P('dp'), may hold values from -0.21875 to 0.21875
- out_master: float32 [768, 768], P('dp'), may hold values from -6 to 6
- up_master: float32 [768, 3072], P('dp'), may hold values from -0.21875 to 0.21875
- down_master: float32 [3072, 768], P('dp'), may hold values from -0.109375 to 0.109375
- vector_master: float32 [13, 768], replicated, may hold values from -0.9 to 1.6
- qkv_first: float32 [768, 2304], P('dp'), may hold values from -24 to 24
- qkv_second: float32 [768, 2304], P('dp'), may hold values from 1.47456 to 5.89824
- out_first: float32 [768, 768], P('dp'), may hold values from -4 to 4
- out_second: float32 [768, 768], P('dp'), may hold values from 0.01024 to 0.04096
- up_first: float32 [768, 3072], P('dp'), may hold values from -16 to 16
- up_second: float32 [768, 3072], P('dp'), may hold values from 0.65536 to 2.62144
- down_first: float32 [3072, 768], P('dp'), may hold values from -32 to 32
- down_second: float32 [3072, 768], P('dp'), may hold values from 2.62144 to 10.48576
- vector_first: float32 [13, 768], replicated, may hold values from -40 to 40
- vector_second: float32 [13, 768], replicated, may hold values from 4.096 to 16.384
Outputs:
- output: bfloat16 [16384, 768], P(('dp', 'head'))
- input_grad: float32 [16384, 768], P(('dp', 'head'))
- qkv_first_new: float32 [768, 2304], P('dp')
- qkv_second_new: float32 [768, 2304], P('dp')
- qkv_master_new: float32 [768, 2304], P('dp')
- out_first_new: float32 [768, 768], P('dp')
- out_second_new: float32 [768, 768], P('dp')
- out_master_new: float32 [768, 768], P('dp')
- up_first_new: float32 [768, 3072], P('dp')
- up_second_new: float32 [768, 3072], P('dp')
- up_master_new: float32 [768, 3072], P('dp')
- down_first_new: float32 [3072, 768], P('dp')
- down_second_new: float32 [3072, 768], P('dp')
- down_master_new: float32 [3072, 768], P('dp')
- vector_first_new: float32 [13, 768], replicated
- vector_second_new: float32 [13, 768], replicated
- vector_master_new: float32 [13, 768], replicated
The draws below stay inside these ranges and needn't reach their ends.
Inputs may be any that keep to these rules, and one draw needn't show every extreme that they name: `lengths`: each group of 2048 tokens holds 2 sequences in the order given; a sequence takes its length rounded up to a multiple of 64 rows, and these rows fill the group exactly; rows past a sequence's length are padding.
All inputs are finite; a program needn't handle non-finite values.
Results may differ from the reference program's by a relative error of at most 0.02.
Values may be sent and summed in bfloat16 or wider, within the bound.
A program may use at most 256 MiB of HBM per device.

```python
import math
import jax
import jax.numpy as jnp
from jax import lax

D = 768
H = 12
HD = 64
FF = 3072
SPAN = 64
MIN_LEN = 128
MAX_LEN = 2048
STEP = 10
TOKENS = 16384
GROUP = 2048
NSEQ = 2
SEQS_ALL = 16
OUT_FAN = 1


def group_lengths_draw(key):
    seq_count = NSEQ
    span_total = GROUP // SPAN
    least = MIN_LEN // SPAN
    most = MAX_LEN // SPAN
    longest = min(most, span_total - (seq_count - 1) * least)
    remaining = span_total - longest - (seq_count - 1) * least
    key_pert, key_pad, key_order = jax.random.split(key, 3)
    pieces = [jnp.array([longest], jnp.int32), jnp.array([least], jnp.int32)]
    if seq_count > 2:
        others = seq_count - 2
        base_share = remaining // others
        extras = base_share + (jnp.arange(others) < remaining % others).astype(jnp.int32)
        reach_max = max(0, min(base_share, most - least - base_share - 1))
        pair_count = others // 2
        if pair_count > 0:
            moves = jax.random.randint(key_pert, (pair_count,), -reach_max, reach_max + 1)
            offsets_pair = jnp.stack([moves, -moves], axis=1).reshape(-1)
            offsets_pair = jnp.concatenate([offsets_pair, jnp.zeros((others - 2 * pair_count,), jnp.int32)])
            extras = extras + offsets_pair
        pieces.append((least + extras).astype(jnp.int32))
    counts = jnp.concatenate(pieces).astype(jnp.int32)
    pad_sizes = jax.random.randint(key_pad, (seq_count,), 0, SPAN)
    pad_sizes = pad_sizes * (counts > least).astype(jnp.int32) * (jnp.arange(seq_count) > 0).astype(jnp.int32)
    seq_sizes = counts * SPAN - pad_sizes
    scores = jax.random.randint(key_order, (seq_count,), 0, 4096) * seq_count + jnp.arange(seq_count)
    return seq_sizes[jnp.argsort(scores)].astype(jnp.int32)


def draw_lengths(key, part):
    key = jax.random.fold_in(key, 7)
    group_keys = jax.random.split(key, SEQS_ALL // NSEQ)
    return jax.vmap(group_lengths_draw)(group_keys).reshape(-1).astype(jnp.int32)


def draw_vector_master(key, part):
    key = jax.random.fold_in(key, 3)
    noise = jnp.clip(jax.random.normal(key, (13, D), jnp.float32), -3.0, 3.0)
    row_ids = jnp.arange(13)[:, None]
    gain_rows = (row_ids == 0) | (row_ids == 2)
    return jnp.where(gain_rows, 1.0 + 0.2 * noise, 0.3 * noise).astype(jnp.float32)


def steps_of(rng, dims, cuts, low, high):
    loudness = 1.0
    for dim, parts in cuts:
        steps = jax.random.uniform(jax.random.fold_in(jax.random.fold_in(rng, 6), dim), (parts,), jnp.float32, low / len(cuts), high / len(cuts))
        loudness = loudness * jnp.repeat(jnp.exp(steps), dims[dim] // parts).reshape((-1,) + (1,) * (len(dims) - 1 - dim))
    return loudness


def gaussian(own_key, extent, deviation, most, cuts=(), kind=jnp.bfloat16):
    level = steps_of(own_key, extent, cuts, -0.22, 0.18) if cuts else 1.0
    entries = jax.random.normal(own_key, extent, jnp.float32) * deviation * level
    return jnp.minimum(jnp.maximum(entries, -most), most).astype(kind)


def setup_inputs(seed: int = 0) -> dict:
    splits = jax.random.split(jax.random.key(seed), 19)
    tokens = gaussian(splits[0], (TOKENS, D), 1.0, 6.0, ((0, 32),))
    cotangent = gaussian(splits[1], (TOKENS, D), 1.0, 6.0, ((0, 32),), jnp.float32)
    lengths = draw_lengths(jax.random.fold_in(splits[18], 71), 0)
    qkv_master = gaussian(splits[3], (D, 3 * D), D ** -0.5, 0.21875, ((0, 8),), jnp.float32)
    out_master = gaussian(splits[4], (D, D), OUT_FAN ** -0.5, 6.0, ((0, 8),), jnp.float32)
    up_master = gaussian(splits[5], (D, FF), D ** -0.5, 0.21875, ((0, 8),), jnp.float32)
    down_master = gaussian(splits[6], (FF, D), FF ** -0.5, 0.109375, ((0, 8),), jnp.float32)
    vector_master = draw_vector_master(jax.random.fold_in(splits[18], 71), 0)
    qkv_first = gaussian(splits[8], (D, 3 * D), (0.033 * TOKENS ** 0.5), 24.0, ((0, 8),), jnp.float32)
    qkv_second = jnp.clip(jnp.exp(math.log(5.89824) - 1.3862944 * jax.random.uniform(splits[9], (D, 3 * D), jnp.float32) ** steps_of(splits[9], (D, 3 * D), ((0, 8),), -0.2, 0.2)), 1.47456, 5.89824)
    out_first = gaussian(splits[10], (D, D), (0.044 * (8 * TOKENS / MAX_LEN) ** 0.5), 4.0, ((0, 8),), jnp.float32)
    out_second = jnp.clip(jnp.exp(math.log(0.04096) - 1.3862944 * jax.random.uniform(splits[11], (D, D), jnp.float32) ** steps_of(splits[11], (D, D), ((0, 8),), -0.2, 0.2)), 0.01024, 0.04096)
    up_first = gaussian(splits[12], (D, FF), (0.022 * TOKENS ** 0.5), 16.0, ((0, 8),), jnp.float32)
    up_second = jnp.clip(jnp.exp(math.log(2.62144) - 1.3862944 * jax.random.uniform(splits[13], (D, FF), jnp.float32) ** steps_of(splits[13], (D, FF), ((0, 8),), -0.2, 0.2)), 0.65536, 2.62144)
    down_first = gaussian(splits[14], (FF, D), (0.044 * TOKENS ** 0.5), 32.0, ((0, 8),), jnp.float32)
    down_second = jnp.clip(jnp.exp(math.log(10.48576) - 1.3862944 * jax.random.uniform(splits[15], (FF, D), jnp.float32) ** steps_of(splits[15], (FF, D), ((0, 8),), -0.2, 0.2)), 2.62144, 10.48576)
    vector_first = gaussian(splits[16], (13, D), (0.055 * TOKENS ** 0.5), 40.0, (), jnp.float32)
    vector_second = jnp.clip(jnp.exp(jax.random.uniform(splits[17], (13, D), jnp.float32, math.log(4.096), math.log(16.384))), 4.096, 16.384)
    return {"tokens": tokens, "cotangent": cotangent, "lengths": lengths, "qkv_master": qkv_master, "out_master": out_master, "up_master": up_master, "down_master": down_master, "vector_master": vector_master, "qkv_first": qkv_first, "qkv_second": qkv_second, "out_first": out_first, "out_second": out_second, "up_first": up_first, "up_second": up_second, "down_first": down_first, "down_second": down_second, "vector_first": vector_first, "vector_second": vector_second}


highest = lax.Precision.HIGHEST
norm_epsilon = 1e-05
first_decay = 0.9
second_decay = 0.999
adam_epsilon = 1e-08
weight_decay = 0.01
vector_rate = 0.2

@jax.custom_vjp
def low(v):
    return lax.optimization_barrier(v.astype(jnp.bfloat16)).astype(jnp.float32)

@jax.custom_vjp
def low_back(v):
    return v

def low_keep(v):
    return (low(v), None)

def low_pass(kept, grad):
    return (grad,)

def back_keep(v):
    return (v, None)

def back_low(kept, grad):
    return (low(grad),)
low.defvjp(low_keep, low_pass)
low_back.defvjp(back_keep, back_low)

def layer_norm(residual, gain_row, shift_row):
    center = residual - lax.optimization_barrier(jnp.mean(residual, axis=-1, keepdims=True))
    spread = lax.optimization_barrier(jnp.mean(center * center, axis=-1, keepdims=True))
    return center * lax.rsqrt(spread + norm_epsilon) * gain_row + shift_row

def exact_gelu(upper_pre):
    return jax.nn.gelu(upper_pre, approximate=False)

def group_layout(group_lengths, row_count):
    group_lengths = group_lengths.astype(jnp.int32)
    slot_sizes = ((group_lengths + SPAN - 1) // SPAN * SPAN).astype(jnp.int32)
    slot_ends = jnp.cumsum(slot_sizes).astype(jnp.int32)
    slot_starts = (slot_ends - slot_sizes).astype(jnp.int32)
    positions = jnp.arange(row_count, dtype=jnp.int32)
    member = (positions[:, None] >= slot_starts[None, :]) & (positions[:, None] < slot_ends[None, :])
    seq_first = lax.optimization_barrier(jnp.sum(jnp.where(member, slot_starts[None, :], 0), axis=1)).astype(jnp.int32)
    length = lax.optimization_barrier(jnp.sum(jnp.where(member, group_lengths[None, :], 0), axis=1)).astype(jnp.int32)
    seq_numbers = jnp.arange(group_lengths.shape[0], dtype=jnp.int32)
    owners = lax.optimization_barrier(jnp.sum(jnp.where(member, seq_numbers[None, :], 0), axis=1)).astype(jnp.int32)
    offset = positions - seq_first
    live_rows = (offset < length).astype(jnp.float32)
    angles = 0.5 * math.pi * offset.astype(jnp.float32) / length.astype(jnp.float32)
    cosine = jnp.cos(angles)
    sine_part = jnp.sin(angles)
    span_owner = owners[::SPAN]
    span_order = jnp.arange(span_owner.shape[0], dtype=jnp.int32)
    same_seq = span_owner[None, :] == span_owner[:, None]
    earlier = (same_seq & (span_order[None, :] < span_order[:, None])).astype(jnp.float32)
    return (cosine, sine_part, live_rows, earlier)

def attend(query_rows, key_rows, value_rows, cosine, sine_part, live_rows, earlier):
    row_count = query_rows.shape[0]
    blocks = row_count // SPAN
    soft_query = jax.nn.softplus(query_rows)
    soft_key = jax.nn.softplus(key_rows)
    feat_query = jnp.concatenate([soft_query * cosine[:, None], soft_query * sine_part[:, None]], axis=1) * live_rows[:, None]
    feat_key = jnp.concatenate([soft_key * cosine[:, None], soft_key * sine_part[:, None]], axis=1) * live_rows[:, None]
    block_query = feat_query.reshape(blocks, SPAN, -1)
    block_key = feat_key.reshape(blocks, SPAN, -1)
    block_value = value_rows.reshape(blocks, SPAN, -1)
    lower_mask = (jnp.arange(SPAN)[:, None] >= jnp.arange(SPAN)[None, :]).astype(jnp.float32)
    scores = jnp.einsum('cik,cjk->cij', block_query, block_key, precision=highest) * lower_mask
    inner_sum = jnp.einsum('cij,cjd->cid', scores, block_value, precision=highest)
    inner_den = lax.optimization_barrier(jnp.sum(scores, axis=2))
    states = jnp.einsum('cjk,cjd->ckd', block_key, block_value, precision=highest)
    key_sums = lax.optimization_barrier(jnp.sum(block_key, axis=1))
    before = jnp.einsum('ce,ekd->ckd', earlier, states, precision=highest)
    before_sums = jnp.einsum('ce,ek->ck', earlier, key_sums, precision=highest)
    outer_sum = jnp.einsum('cik,ckd->cid', block_query, before, precision=highest)
    outer_den = jnp.einsum('cik,ck->ci', block_query, before_sums, precision=highest)
    numerator = (inner_sum + outer_sum).reshape(row_count, -1)
    denominator = (inner_den + outer_den).reshape(row_count) + (1.0 - live_rows)
    return numerator / denominator[:, None]

def block_forward(inputs, group_lengths, lowered, vectors):
    mix_weight, out_weight, up_weight, down_weight = lowered
    row_count = inputs.shape[0]
    cosine, sine_part, live_rows, earlier = group_layout(group_lengths, row_count)
    mixed_all = low_back(jnp.dot(inputs, mix_weight, precision=highest)) + vectors[6:9].reshape(-1)
    queries = low(mixed_all[:, :D])
    key_block = low(mixed_all[:, D:2 * D])
    values = low_back(low(mixed_all[:, 2 * D:]))
    query_items = low_back(jnp.repeat(queries.reshape(row_count, H, HD), 2, axis=1))
    key_items = low_back(jnp.repeat(key_block.reshape(row_count, H, HD), 2, axis=1))
    value_items = values.reshape(row_count, 2 * H, HD // 2)

    def single(query_rows, key_rows, value_rows):
        return attend(query_rows, key_rows, value_rows, cosine, sine_part, live_rows, earlier)
    attended = jax.vmap(single, in_axes=1, out_axes=1)(query_items, key_items, value_items)
    heads = low_back(low(attended.reshape(row_count, D)))
    projected = low_back(jnp.dot(heads, out_weight, precision=highest)) + vectors[4]
    hidden = layer_norm(inputs + projected, vectors[0], vectors[1])
    upper_pre = low_back(jnp.dot(low(hidden), up_weight, precision=highest)) + vectors[9:13].reshape(-1)
    active = low(exact_gelu(upper_pre))
    lowered_out = low_back(jnp.dot(active, down_weight, precision=highest)) + vectors[5]
    return layer_norm(hidden + lowered_out, vectors[2], vectors[3])

def adam_update(master, first, second, gradient, rate, decay):
    first_new = first_decay * first + (1.0 - first_decay) * gradient
    second_new = second_decay * second + (1.0 - second_decay) * gradient * gradient
    first_hat = first_new / (1.0 - first_decay ** STEP)
    second_hat = second_new / (1.0 - second_decay ** STEP)
    master_new = master - rate * (first_hat / (jnp.sqrt(second_hat) + adam_epsilon) + decay * master)
    return (first_new, second_new, master_new)

def reference(tokens, cotangent, lengths, qkv_master, out_master, up_master, down_master, vector_master, qkv_first, qkv_second, out_first, out_second, up_first, up_second, down_first, down_second, vector_first, vector_second):
    masters = (qkv_master, out_master, up_master, down_master)

    def forward(inputs, weights, vectors):
        lowered = tuple((low(weight) for weight in weights))

        def one_group(bundle):
            return block_forward(bundle[0], bundle[1], lowered, vectors)
        group_count = lengths.shape[0] // NSEQ
        results = lax.map(jax.checkpoint(one_group), (inputs.reshape(group_count, GROUP, D), lengths.reshape(group_count, NSEQ)))
        return results.reshape(TOKENS, D)
    output, pullback = jax.vjp(forward, tokens.astype(jnp.float32), masters, vector_master)
    input_grad, weight_grads, vector_grad = pullback(cotangent)
    qkv_new = adam_update(qkv_master, qkv_first, qkv_second, weight_grads[0], 1.0 / math.sqrt(D), weight_decay)
    out_new = adam_update(out_master, out_first, out_second, weight_grads[1], 1.0 / math.sqrt(OUT_FAN), weight_decay)
    up_new = adam_update(up_master, up_first, up_second, weight_grads[2], 1.0 / math.sqrt(D), weight_decay)
    down_new = adam_update(down_master, down_first, down_second, weight_grads[3], 1.0 / math.sqrt(FF), weight_decay)
    vector_new = adam_update(vector_master, vector_first, vector_second, vector_grad, vector_rate, 0.0)
    return (output.astype(jnp.bfloat16), input_grad, qkv_new[0], qkv_new[1], qkv_new[2], out_new[0], out_new[1], out_new[2], up_new[0], up_new[1], up_new[2], down_new[0], down_new[1], down_new[2], vector_new[0], vector_new[1], vector_new[2])
```

```python
import functools
import math

import jax
import jax.numpy as jnp
from jax import lax
from jax.experimental import pallas as pl
from jax.experimental.pallas import tpu as pltpu
from jax.sharding import PartitionSpec as P

D = 768
H = 12
HD = 64
FF = 3072
SPAN = 64
STEP = 10
OUT_FAN = 1


highest = lax.Precision.HIGHEST
norm_epsilon = 1e-05
first_decay = 0.9
second_decay = 0.999
adam_epsilon = 1e-08
weight_decay = 0.01
vector_rate = 0.2


def layer_norm(residual, gain_row, shift_row):
    center = residual - jnp.mean(residual, axis=-1, keepdims=True)
    spread = jnp.mean(center * center, axis=-1, keepdims=True)
    return center * lax.rsqrt(spread + norm_epsilon) * gain_row + shift_row


def exact_gelu(upper_pre):
    return jax.nn.gelu(upper_pre, approximate=False)


def group_layout(group_lengths, row_count):
    slot_sizes = (group_lengths + SPAN - 1) // SPAN * SPAN
    slot_ends = jnp.cumsum(slot_sizes)
    slot_starts = slot_ends - slot_sizes
    positions = jnp.arange(row_count, dtype=jnp.int32)
    member = (positions[:, None] >= slot_starts[None, :]) & (
        positions[:, None] < slot_ends[None, :]
    )
    seq_first = jnp.sum(jnp.where(member, slot_starts[None, :], 0), axis=1)
    length = jnp.sum(jnp.where(member, group_lengths[None, :], 0), axis=1)
    seq_numbers = jnp.arange(group_lengths.shape[0], dtype=jnp.int32)
    owners = jnp.sum(jnp.where(member, seq_numbers[None, :], 0), axis=1)
    offset = positions - seq_first
    live_rows = (offset < length).astype(jnp.float32)
    angles = 0.5 * math.pi * offset.astype(jnp.float32) / length.astype(jnp.float32)
    cosine = jnp.cos(angles)
    sine_part = jnp.sin(angles)
    span_owner = owners[::SPAN]
    span_order = jnp.arange(span_owner.shape[0], dtype=jnp.int32)
    same_seq = span_owner[None, :] == span_owner[:, None]
    earlier = (same_seq & (span_order[None, :] < span_order[:, None])).astype(jnp.float32)
    return (cosine, sine_part, live_rows, earlier)


def attend(query_rows, key_rows, value_rows, cosine, sine_part, live_rows, earlier):
    row_count = query_rows.shape[0]
    blocks = row_count // SPAN
    soft_query = jax.nn.softplus(query_rows)
    soft_key = jax.nn.softplus(key_rows)
    feat_query = (
        jnp.concatenate([soft_query * cosine[:, None], soft_query * sine_part[:, None]], axis=1)
        * live_rows[:, None]
    )
    feat_key = (
        jnp.concatenate([soft_key * cosine[:, None], soft_key * sine_part[:, None]], axis=1)
        * live_rows[:, None]
    )
    block_query = feat_query.reshape(blocks, SPAN, -1)
    block_key = feat_key.reshape(blocks, SPAN, -1)
    block_value = value_rows.reshape(blocks, SPAN, -1)
    lower_mask = (jnp.arange(SPAN)[:, None] >= jnp.arange(SPAN)[None, :]).astype(jnp.float32)
    scores = jnp.einsum("cik,cjk->cij", block_query, block_key, precision=highest) * lower_mask
    inner_sum = jnp.einsum("cij,cjd->cid", scores, block_value, precision=highest)
    inner_den = jnp.sum(scores, axis=2)
    states = jnp.einsum("cjk,cjd->ckd", block_key, block_value, precision=highest)
    key_sums = jnp.sum(block_key, axis=1)
    before = jnp.einsum("ce,ekd->ckd", earlier, states, precision=highest)
    before_sums = jnp.einsum("ce,ek->ck", earlier, key_sums, precision=highest)
    outer_sum = jnp.einsum("cik,ckd->cid", block_query, before, precision=highest)
    outer_den = jnp.einsum("cik,ck->ci", block_query, before_sums, precision=highest)
    numerator = (inner_sum + outer_sum).reshape(row_count, -1)
    denominator = (inner_den + outer_den).reshape(row_count) + (1.0 - live_rows)
    return numerator / denominator[:, None]


def contract_rows(left, right):
    return lax.dot_general(
        left, right, (((0,), (0,)), ((), ())), preferred_element_type=jnp.float32
    )


def contract_cols(left, right):
    return lax.dot_general(
        left, right, (((1,), (1,)), ((), ())), preferred_element_type=jnp.float32
    )


def adam_update(master, first, second, gradient, rate, decay):
    first_new = first_decay * first + (1.0 - first_decay) * gradient
    second_new = second_decay * second + (1.0 - second_decay) * gradient * gradient
    first_hat = first_new / (1.0 - first_decay**STEP)
    second_hat = second_new / (1.0 - second_decay**STEP)
    master_new = master - rate * (
        first_hat / (jnp.sqrt(second_hat) + adam_epsilon) + decay * master
    )
    return (first_new, second_new, master_new)


def shards(
    tokens,
    cotangent,
    lengths,
    qkv_master,
    out_master,
    up_master,
    down_master,
    vector_master,
    qkv_first,
    qkv_second,
    out_first,
    out_second,
    up_first,
    up_second,
    down_first,
    down_second,
    vector_first,
    vector_second,
):
    mix_weight, out_weight, up_weight, down_weight = (
        lax.all_gather(qkv_master.astype(jnp.bfloat16), "dp", axis=0, tiled=True),
        lax.all_gather(out_master.astype(jnp.bfloat16), "dp", axis=0, tiled=True),
        lax.all_gather(up_master.astype(jnp.bfloat16), "dp", axis=0, tiled=True),
        lax.all_gather(down_master.astype(jnp.bfloat16), "dp", axis=0, tiled=True),
    )
    tok_count = tokens.shape[0]
    width = tokens.shape[1]
    mixed_all = jnp.dot(tokens, mix_weight, preferred_element_type=jnp.float32) + vector_master[
        6:9
    ].reshape(-1)
    mixed_low = mixed_all.astype(jnp.bfloat16)
    query_part = mixed_low[:, :width].reshape(tok_count, H, 1, HD)
    key_part = mixed_low[:, width : 2 * width].reshape(tok_count, H, 1, HD)
    paired = jnp.concatenate([query_part, key_part], axis=2)
    paired = jnp.repeat(paired[:, :, None], 2, axis=2).reshape(tok_count, 4 * width)
    value_part = mixed_low[:, 2 * width :]
    paired_in, values_in = (
        lax.all_to_all(paired, "head", split_axis=1, concat_axis=0, tiled=True),
        lax.all_to_all(value_part, "head", split_axis=1, concat_axis=0, tiled=True),
    )
    group_rows = paired_in.shape[0]
    item_count = paired_in.shape[1] // (2 * HD)
    cosine, sine_part, live_rows, earlier = group_layout(lengths, group_rows)
    stacked = paired_in.reshape(group_rows, item_count, 2, HD).astype(jnp.float32)
    query_items = stacked[:, :, 0]
    key_items = stacked[:, :, 1]
    value_items = values_in.reshape(group_rows, item_count, HD // 2).astype(jnp.float32)

    def mix_items(query_set, key_set, value_set):

        def single(query_rows, key_rows, value_rows):
            return attend(query_rows, key_rows, value_rows, cosine, sine_part, live_rows, earlier)

        return jax.vmap(single, in_axes=1, out_axes=1)(query_set, key_set, value_set)

    attended, mix_back = jax.vjp(mix_items, query_items, key_items, value_items)
    heads_out = attended.reshape(group_rows, item_count * (HD // 2)).astype(jnp.bfloat16)
    heads = lax.all_to_all(heads_out, "head", split_axis=0, concat_axis=1, tiled=True)
    projected = jnp.dot(heads, out_weight, preferred_element_type=jnp.float32) + vector_master[4]
    resid_one = tokens.astype(jnp.float32) + projected
    hidden, norm_one_back = jax.vjp(layer_norm, resid_one, vector_master[0], vector_master[1])
    hidden_low = hidden.astype(jnp.bfloat16)
    upper_pre = jnp.dot(hidden_low, up_weight, preferred_element_type=jnp.float32) + vector_master[
        9:13
    ].reshape(-1)
    active, gelu_back = jax.vjp(exact_gelu, upper_pre)
    active_low = active.astype(jnp.bfloat16)
    lowered = (
        jnp.dot(active_low, down_weight, preferred_element_type=jnp.float32) + vector_master[5]
    )
    output, norm_two_back = jax.vjp(
        layer_norm, hidden + lowered, vector_master[2], vector_master[3]
    )
    grad_two, gain_two, shift_two = norm_two_back(cotangent)
    grad_two_low = grad_two.astype(jnp.bfloat16)
    down_grad = contract_rows(active_low, grad_two_low)
    (upper_grad,) = gelu_back(contract_cols(grad_two_low, down_weight))
    upper_low = upper_grad.astype(jnp.bfloat16)
    up_grad = contract_rows(hidden_low, upper_low)
    hidden_grad = grad_two + contract_cols(upper_low, up_weight)
    grad_one, gain_one, shift_one = norm_one_back(hidden_grad)
    grad_one_low = grad_one.astype(jnp.bfloat16)
    out_grad = contract_rows(heads, grad_one_low)
    heads_grad = contract_cols(grad_one_low, out_weight).astype(jnp.bfloat16)
    heads_back = lax.all_to_all(heads_grad, "head", split_axis=1, concat_axis=0, tiled=True)
    query_back, key_back, value_back = mix_back(
        heads_back.reshape(group_rows, item_count, HD // 2).astype(jnp.float32)
    )
    pair_back = (
        jnp.stack([query_back, key_back], axis=2)
        .astype(jnp.bfloat16)
        .reshape(group_rows, item_count * 2 * HD)
    )
    value_low = value_back.astype(jnp.bfloat16).reshape(group_rows, item_count * (HD // 2))
    pair_home, value_home = (
        lax.all_to_all(pair_back, "head", split_axis=0, concat_axis=1, tiled=True),
        lax.all_to_all(value_low, "head", split_axis=0, concat_axis=1, tiled=True),
    )
    summed = jnp.sum(pair_home.astype(jnp.float32).reshape(tok_count, H, 2, 2, HD), axis=2)
    mixed_grad = jnp.concatenate(
        [
            summed[:, :, 0].reshape(tok_count, width),
            summed[:, :, 1].reshape(tok_count, width),
            value_home.astype(jnp.float32),
        ],
        axis=1,
    )
    mixed_low_grad = mixed_grad.astype(jnp.bfloat16)
    mix_grad = contract_rows(tokens, mixed_low_grad)
    input_grad = grad_one + contract_cols(mixed_low_grad, mix_weight)
    vector_grad = jnp.concatenate(
        [
            jnp.stack(
                [
                    gain_one,
                    shift_one,
                    gain_two,
                    shift_two,
                    jnp.sum(grad_one, axis=0),
                    jnp.sum(grad_two, axis=0),
                ]
            ),
            jnp.sum(mixed_grad, axis=0).reshape(3, width),
            jnp.sum(upper_grad, axis=0).reshape(4, width),
        ],
        axis=0,
    )
    local_grads = (mix_grad, out_grad, up_grad, down_grad)
    row_parts = (
        lax.psum_scatter(
            local_grads[0].astype(jnp.bfloat16), "dp", scatter_dimension=0, tiled=True
        ).astype(jnp.float32),
        lax.psum_scatter(
            local_grads[1].astype(jnp.bfloat16), "dp", scatter_dimension=0, tiled=True
        ).astype(jnp.float32),
        lax.psum_scatter(
            local_grads[2].astype(jnp.bfloat16), "dp", scatter_dimension=0, tiled=True
        ).astype(jnp.float32),
        lax.psum_scatter(
            local_grads[3].astype(jnp.bfloat16), "dp", scatter_dimension=0, tiled=True
        ).astype(jnp.float32),
    )
    reduced = (
        lax.psum(row_parts[0].astype(jnp.bfloat16), "head").astype(jnp.float32),
        lax.psum(row_parts[1].astype(jnp.bfloat16), "head").astype(jnp.float32),
        lax.psum(row_parts[2].astype(jnp.bfloat16), "head").astype(jnp.float32),
        lax.psum(row_parts[3].astype(jnp.bfloat16), "head").astype(jnp.float32),
    )
    vector_total = lax.psum(vector_grad, ("dp", "head"))
    qkv_new = adam_update(
        qkv_master, qkv_first, qkv_second, reduced[0], 1.0 / math.sqrt(D), weight_decay
    )
    out_new = adam_update(
        out_master, out_first, out_second, reduced[1], 1.0 / math.sqrt(OUT_FAN), weight_decay
    )
    up_new = adam_update(
        up_master, up_first, up_second, reduced[2], 1.0 / math.sqrt(D), weight_decay
    )
    down_new = adam_update(
        down_master, down_first, down_second, reduced[3], 1.0 / math.sqrt(FF), weight_decay
    )
    vector_new = adam_update(
        vector_master, vector_first, vector_second, vector_total, vector_rate, 0.0
    )
    return (
        output.astype(jnp.bfloat16),
        input_grad,
        qkv_new[0],
        qkv_new[1],
        qkv_new[2],
        out_new[0],
        out_new[1],
        out_new[2],
        up_new[0],
        up_new[1],
        up_new[2],
        down_new[0],
        down_new[1],
        down_new[2],
        vector_new[0],
        vector_new[1],
        vector_new[2],
    )


PAIRS = H // 2
LANES = 2 * HD
SLABS = PAIRS + 1
FF_TILE = 512
ROW_TILE = 128
MESH = pl.DeviceIdType.MESH


def mm(left, right):
    return jnp.dot(left, right, preferred_element_type=jnp.float32)


def mm_cols(left, right):
    return lax.dot_general(
        left, right, (((1,), (1,)), ((), ())), preferred_element_type=jnp.float32
    )


def mm_rows(left, right):
    return lax.dot_general(
        left, right, (((0,), (0,)), ((), ())), preferred_element_type=jnp.float32
    )


def swap_halves(slab):
    return pltpu.roll(slab, HD, 1)


def low_cast(value):
    return value.astype(jnp.bfloat16)


def gelu_parts(z):
    x = jnp.abs(z) * (1.0 / math.sqrt(2.0))
    t = 1.0 / (1.0 + 0.3275911 * x)
    bell = jnp.exp(-0.5 * z * z)
    poly = t * (
        0.254829592
        + t * (-0.284496736 + t * (1.421413741 + t * (-1.453152027 + t * 1.061405429)))
    )
    upper_tail = 0.5 * poly * bell
    phi = jnp.where(z >= 0, 1.0 - upper_tail, upper_tail)
    return z * phi, phi + z * (bell * (1.0 / math.sqrt(2.0 * math.pi)))


def layer_kernel(
    n_dp,
    n_head,
    n_seq,
    lens_ref,
    tok_ref,
    cot_ref,
    qkv_f,
    out_f,
    up_f,
    down_f,
    vec_ref,
    y_ref,
    ig_ref,
    w_qkv,
    w_out,
    w_up,
    w_down,
    vg_ref,
    mixed,
    feat_q,
    feat_k,
    val_a,
    grad_a,
    num_a,
    heads,
    norm_one,
    rstd_one,
    hid,
    hid_low,
    hid_t,
    act,
    gel,
    two_low,
    one_low,
    d_heads,
    mask,
    mask_t,
    cs_ref,
    rows_ref,
    keeps,
    state_own,
    state_in,
    back_own,
    back_in,
    state_h,
    back_h,
    zcol,
    tok_t,
    g_send,
    g_recv,
    s_send,
    s_recv,
):
    T = tok_ref.shape[0]
    dp = lax.axis_index("dp")
    z = lax.axis_index("head")
    core = dp % 2
    xx = (dp // 2) % 2
    yy = dp // 4
    sib = dp + 1 - 2 * core
    xn = dp + 2 - 4 * xx
    yn = dp + 4 - 8 * yy
    dg = xn + 4 - 8 * yy

    barrier = pltpu.get_barrier_semaphore()
    for peer in (sib, xn, yn, dg):
        pl.semaphore_signal(barrier, inc=1, device_id=(peer, z), device_id_type=MESH)
    for k in range(1, n_head):
        pl.semaphore_signal(
            barrier, inc=1, device_id=(dp, (z + k) % n_head), device_id_type=MESH
        )

    weights = (w_qkv, w_out, w_up, w_down)
    masters = (qkv_f, out_f, up_f, down_f)
    depth = tuple(f.shape[0] for f in masters)

    def block(m, who):
        return pl.ds(pl.multiple_of(who * depth[m], depth[m]), depth[m])

    for m in range(4):
        weights[m][block(m, dp), :] = low_cast(masters[m][...])

    pl.semaphore_wait(barrier, 4 + n_head - 1)

    def gather_copy(m, kind, who, target):
        ref = weights[m].at[block(m, who), :]
        return pltpu.make_async_remote_copy(
            src_ref=ref,
            dst_ref=ref,
            send_sem=g_send.at[m, kind],
            recv_sem=g_recv.at[m, kind],
            device_id=(target, z),
            device_id_type=MESH,
        )

    def send_own(m):
        for kind, target in ((1, xn), (2, yn), (3, dg), (0, sib)):
            gather_copy(m, kind, dp, target).start()

    def hand_over(m):
        for kind, who in ((1, xn), (2, yn), (3, dg)):
            gather_copy(m, kind, who, who).wait_recv()
            gather_copy(m, kind + 3, who, sib).start()

    def all_here(m):
        for kind in (0, 4, 5, 6):
            gather_copy(m, kind, dp, sib).wait_recv()

    def all_sent(m):
        for kind in range(7):
            gather_copy(m, kind, dp, sib).wait_send()

    for m in range(4):
        send_own(m)

    lens = [lens_ref[s] for s in range(n_seq)]
    ends = []
    total = 0
    for s in range(n_seq):
        total = total + ((lens[s] + (SPAN - 1)) // SPAN) * SPAN
        ends.append(total)
    starts = [0] + ends[:-1]

    def owner_of(row):
        found = jnp.zeros_like(row)
        for s in range(n_seq):
            found = found + (row >= ends[s]).astype(jnp.int32)
        return found

    lane = lax.broadcasted_iota(jnp.int32, (T, LANES), 1)
    row = z * T + lax.broadcasted_iota(jnp.int32, (T, LANES), 0)
    first = jnp.zeros_like(row)
    length = jnp.ones_like(row)
    for s in range(n_seq):
        inside = (row >= starts[s]) & (row < ends[s])
        first = jnp.where(inside, starts[s], first)
        length = jnp.where(inside, lens[s], length)
    offset = row - first
    live = (offset < length).astype(jnp.float32)
    angle = 0.5 * math.pi * offset.astype(jnp.float32) / length.astype(jnp.float32)
    angle = jnp.where(lane < HD, angle, 0.5 * math.pi - angle)
    cs_ref[...] = jnp.cos(angle) * live
    owners = owner_of(row)
    next_owner = owner_of(jnp.full((1, 1), (z + 1) * T, jnp.int32))
    last_owner = owner_of(jnp.full((1, 1), z * T - 1, jnp.int32))
    my_first = owner_of(jnp.full((1, 1), z * T, jnp.int32))
    my_last = owner_of(jnp.full((1, 1), (z + 1) * T - 1, jnp.int32))
    rows_ref[...] = live
    for i, edge in enumerate((next_owner, last_owner, my_first, my_last)):
        keeps[i] = low_cast((owners == edge).astype(jnp.float32))

    def fill_masks(i, carry):
        r0 = pl.multiple_of(i * ROW_TILE, ROW_TILE)
        t_i = r0 + lax.broadcasted_iota(jnp.int32, (ROW_TILE, T), 0)
        u_i = lax.broadcasted_iota(jnp.int32, (ROW_TILE, T), 1)
        same = owner_of(t_i + z * T) == owner_of(u_i + z * T)
        mask[pl.ds(r0, ROW_TILE), :] = (same & (u_i <= t_i)).astype(jnp.float32)
        mask_t[pl.ds(r0, ROW_TILE), :] = (same & (u_i >= t_i)).astype(jnp.float32)
        return carry

    lax.fori_loop(0, T // ROW_TILE, fill_masks, 0)

    hand_over(0)
    all_here(0)
    for j in range(3):
        cols = slice(j * D, (j + 1) * D)
        part = mm(tok_ref[...], w_qkv[:, cols])
        if j < 2:
            part = part + vec_ref[6 + j : 7 + j, :]
        mixed[:, cols] = low_cast(part)
    hand_over(1)

    half_lane = lax.broadcasted_iota(jnp.int32, (T, LANES), 1)
    sq_lane = lax.broadcasted_iota(jnp.int32, (LANES, LANES), 1)
    ones_lane = ((half_lane == HD) | (half_lane == HD + 1)).astype(jnp.float32)

    def softplus(v):
        return jnp.maximum(v, 0.0) + jnp.log1p(jnp.exp(-jnp.abs(v)))

    def pair_cols(p, part):
        return pl.ds(pl.multiple_of(part * D + p * LANES, LANES), LANES)

    def split(slab):
        other = swap_halves(slab)
        return jnp.where(half_lane < HD, slab, other), jnp.where(half_lane < HD, other, slab)

    def join(left, right):
        return jnp.where(half_lane < HD, left, swap_halves(right))

    def pack_states(p, low, high, own, n_ones):
        own[p] = low_cast(jnp.where(sq_lane < HD, low, swap_halves(high)))
        for side, part in ((0, low), (1, high)):
            column = part[:, HD : HD + 1]
            if n_ones == 2:
                column = column + part[:, HD + 1 : HD + 2]
            zcol[...] = jnp.where(sq_lane == 2 * p + side, column, zcol[...])

    zcol[...] = jnp.zeros_like(zcol)

    def make_features(p, carry):
        cs = cs_ref[...]
        for part, store in ((0, feat_q), (1, feat_k)):
            low, high = split(softplus(mixed[:, pair_cols(p, part)].astype(jnp.float32)))
            store[2 * p] = low_cast(low * cs)
            store[2 * p + 1] = low_cast(high * cs)
        v_pair = mixed[:, pair_cols(p, 2)].astype(jnp.float32)
        val_a[2 * p] = low_cast(jnp.where(half_lane < HD, v_pair, ones_lane))
        val_a[2 * p + 1] = low_cast(jnp.where(half_lane < HD, swap_halves(v_pair), ones_lane))
        keep = keeps[0]
        low = mm_rows(feat_k[2 * p] * keep, val_a[2 * p])
        high = mm_rows(feat_k[2 * p + 1] * keep, val_a[2 * p + 1])
        pack_states(p, low, high, state_own, 1)
        return carry

    lax.fori_loop(0, PAIRS, make_features, 0)
    state_own[PAIRS] = low_cast(zcol[...])

    def exchange(which, own, landed, k):
        return pltpu.make_async_remote_copy(
            src_ref=own,
            dst_ref=landed.at[z],
            send_sem=s_send.at[which, k],
            recv_sem=s_recv.at[which, k],
            device_id=(dp, (z + k) % n_head),
            device_id_type=MESH,
        )

    for k in range(1, n_head):
        exchange(0, state_own, state_in, k).start()

    def local_attend(h, carry):
        scores = mm_cols(feat_q[h], feat_k[h]) * mask[...]
        num_a[h] = mm(low_cast(scores), val_a[h])
        return carry

    lax.fori_loop(0, H, local_attend, 0)
    hand_over(2)

    def gather_states(which, own, landed, weight_of, out, n_ones):
        for k in range(1, n_head):
            exchange(which, own, landed, k).wait_recv()

        def unpack(p, carry):
            packed = jnp.zeros((LANES, LANES), jnp.float32)
            ends_col = jnp.zeros((LANES, LANES), jnp.float32)
            for k in range(1, n_head):
                src = (z + n_head - k) % n_head
                weight = weight_of(src)
                packed = packed + weight * landed[src, p].astype(jnp.float32)
                ends_col = ends_col + weight * landed[src, PAIRS].astype(jnp.float32)
            for side in (0, 1):
                column = jnp.sum(
                    jnp.where(sq_lane == 2 * p + side, ends_col, 0.0), axis=1, keepdims=True
                )
                slab = packed if side == 0 else swap_halves(packed)
                wide = (sq_lane >= HD) & (sq_lane < HD + n_ones)
                out[2 * p + side] = low_cast(
                    jnp.where(sq_lane < HD, slab, jnp.where(wide, column, 0.0))
                )
            return carry

        lax.fori_loop(0, PAIRS, unpack, 0)

    def forward_weight(src):
        edge = owner_of(jnp.full((1, 1), (src + 1) * T, jnp.int32))
        return ((edge == my_first) & (src < z)).astype(jnp.float32)

    def backward_weight(src):
        edge = owner_of(jnp.full((1, 1), src * T - 1, jnp.int32))
        return ((edge == my_last) & (src > z)).astype(jnp.float32)

    gather_states(0, state_own, state_in, forward_weight, state_h, 2)

    def finish_heads(p, carry):
        att = []
        for side in (0, 1):
            h = 2 * p + side
            total = num_a[h] + mm(feat_q[h] * keeps[2], state_h[h])
            den = total[:, HD : HD + 1] + (1.0 - rows_ref[...])
            inverse = 1.0 / den
            got = total * inverse
            num_a[h] = jnp.where(half_lane < HD, got, inverse)
            att.append(got)
        joined = join(att[0], att[1])
        shift = vec_ref[8:9, pl.ds(pl.multiple_of(p * LANES, LANES), LANES)]
        heads[:, pair_cols(p, 0)] = low_cast(joined + shift * rows_ref[...])
        return carry

    lax.fori_loop(0, PAIRS, finish_heads, 0)

    all_here(1)

    def first_norm(i, carry):
        r = pl.ds(pl.multiple_of(i * ROW_TILE, ROW_TILE), ROW_TILE)
        residual = tok_ref[r, :].astype(jnp.float32) + (mm(heads[r, :], w_out[...]) + vec_ref[4:5, :])
        center = residual - jnp.mean(residual, axis=-1, keepdims=True)
        rstd = lax.rsqrt(jnp.mean(center * center, axis=-1, keepdims=True) + norm_epsilon)
        normed = center * rstd
        norm_one[r, :] = normed
        rstd_one[r, :] = jnp.broadcast_to(rstd, (ROW_TILE, LANES))
        hidden = normed * vec_ref[0:1, :] + vec_ref[1:2, :]
        hid[r, :] = hidden
        hid_low[r, :] = low_cast(hidden)
        return carry

    lax.fori_loop(0, T // ROW_TILE, first_norm, 0)

    hand_over(3)
    all_here(2)

    def ff_up(j, carry):
        cols = pl.ds(pl.multiple_of(j * FF_TILE, FF_TILE), FF_TILE)
        upper = mm(hid_low[...], w_up[:, cols]) + vg_ref[0:1, cols]
        value, slope = gelu_parts(upper)
        act[:, cols] = low_cast(value)
        gel[:, cols] = low_cast(slope)
        return carry

    for j in range(4):
        vg_ref[0:1, j * D : (j + 1) * D] = vec_ref[9 + j : 10 + j, :]
    lax.fori_loop(0, FF // FF_TILE, ff_up, 0)

    all_here(3)

    def row_sum(value):
        return jnp.sum(value, axis=0, keepdims=True)

    def second_norm(i, sums):
        r = pl.ds(pl.multiple_of(i * ROW_TILE, ROW_TILE), ROW_TILE)
        residual = hid[r, :] + (mm(act[r, :], w_down[...]) + vec_ref[5:6, :])
        center = residual - jnp.mean(residual, axis=-1, keepdims=True)
        rstd = lax.rsqrt(jnp.mean(center * center, axis=-1, keepdims=True) + norm_epsilon)
        normed = center * rstd
        y_ref[r, :] = low_cast(normed * vec_ref[2:3, :] + vec_ref[3:4, :])
        dy = cot_ref[r, :]
        e = dy * vec_ref[2:3, :]
        d_two = rstd * (
            e
            - jnp.mean(e, axis=-1, keepdims=True)
            - normed * jnp.mean(e * normed, axis=-1, keepdims=True)
        )
        hid[r, :] = d_two
        two_low[r, :] = low_cast(d_two)
        return sums[0] + row_sum(dy * normed), sums[1] + row_sum(dy), sums[2] + row_sum(d_two)

    zero_row = jnp.zeros((1, D), jnp.float32)
    gain_two, shift_two, bias_down = lax.fori_loop(
        0, T // ROW_TILE, second_norm, (zero_row, zero_row, zero_row)
    )

    def ff_back(j, carry):
        cols = pl.ds(pl.multiple_of(j * FF_TILE, FF_TILE), FF_TILE)
        d_upper = mm_cols(two_low[...], w_down[cols, :]) * gel[:, cols].astype(jnp.float32)
        gel[:, cols] = low_cast(d_upper)
        vg_ref[1:2, cols] = row_sum(d_upper)
        return carry

    lax.fori_loop(0, FF // FF_TILE, ff_back, 0)
    all_sent(3)

    def grad_down(j, carry):
        cols = pl.ds(pl.multiple_of(j * FF_TILE, FF_TILE), FF_TILE)
        w_down[cols, :] = low_cast(mm_rows(act[:, cols], two_low[...]))
        return carry

    lax.fori_loop(0, FF // FF_TILE, grad_down, 0)

    def norm_back(i, sums):
        r = pl.ds(pl.multiple_of(i * ROW_TILE, ROW_TILE), ROW_TILE)
        dy = hid[r, :] + mm_cols(gel[r, :], w_up[...])
        normed = norm_one[r, :]
        rstd = rstd_one[r, 0:1]
        e = dy * vec_ref[0:1, :]
        d_one = rstd * (
            e
            - jnp.mean(e, axis=-1, keepdims=True)
            - normed * jnp.mean(e * normed, axis=-1, keepdims=True)
        )
        ig_ref[r, :] = d_one
        one_low[r, :] = low_cast(d_one)
        return sums[0] + row_sum(dy * normed), sums[1] + row_sum(dy), sums[2] + row_sum(d_one)

    gain_one, shift_one, bias_out = lax.fori_loop(
        0, T // ROW_TILE, norm_back, (zero_row, zero_row, zero_row)
    )
    all_sent(2)
    hid_t[...] = hid_low[...].T

    def grad_up(j, carry):
        cols = pl.ds(pl.multiple_of(j * FF_TILE, FF_TILE), FF_TILE)
        w_up[:, cols] = low_cast(mm(hid_t[...], gel[:, cols]))
        return carry

    lax.fori_loop(0, FF // FF_TILE, grad_up, 0)

    d_heads[...] = low_cast(mm_cols(one_low[...], w_out[...]))
    all_sent(1)
    w_out[...] = low_cast(mm_rows(heads[...], one_low[...]))

    zcol[...] = jnp.zeros_like(zcol)

    def back_states(p, carry):
        g_pair = d_heads[:, pair_cols(p, 0)].astype(jnp.float32)
        parts = []
        for side in (0, 1):
            h = 2 * p + side
            saved = num_a[h]
            g = g_pair if side == 0 else swap_halves(g_pair)
            gn = jnp.where(half_lane < HD, g * swap_halves(saved), 0.0)
            gd = -jnp.sum(gn * saved, axis=1, keepdims=True)
            gd_high = low_cast(gd).astype(jnp.float32)
            gn = jnp.where(
                half_lane == HD, gd_high, jnp.where(half_lane == HD + 1, gd - gd_high, gn)
            )
            grad_a[h] = low_cast(gn)
            parts.append(mm_rows(feat_q[h] * keeps[1], grad_a[h]))
        pack_states(p, parts[0], parts[1], back_own, 2)
        return carry

    lax.fori_loop(0, PAIRS, back_states, 0)
    back_own[PAIRS] = low_cast(zcol[...])
    for k in range(1, n_head):
        exchange(1, back_own, back_in, k).start()
    gather_states(1, back_own, back_in, backward_weight, back_h, 1)

    def mix_back(p, carry):
        cs = cs_ref[...]
        got = []
        for side in (0, 1):
            h = 2 * p + side
            fq, fk, va, ga = feat_q[h], feat_k[h], val_a[h], grad_a[h]
            d_scores = low_cast(mm_cols(ga, va) * mask[...])
            dq = mm(d_scores, fk) + mm_cols(ga * keeps[2], state_h[h])
            d_scores_t = low_cast(mm_cols(va, ga) * mask_t[...])
            dk = mm(d_scores_t, fq) + mm_cols(va * keeps[3], back_h[h])
            scores_t = low_cast(mm_cols(fk, fq) * mask_t[...])
            dv = mm(scores_t, ga) + mm(fk * keeps[3], back_h[h])
            dq = dq * cs
            dk = dk * cs
            got.append((dq + swap_halves(dq), dk + swap_halves(dk), dv))
        for part in (0, 1):
            value = mixed[:, pair_cols(p, part)].astype(jnp.float32)
            e = jnp.exp(-jnp.abs(value))
            sigma = jnp.where(value >= 0, 1.0, e) / (1.0 + e)
            d_part = sigma * jnp.where(half_lane < HD, got[0][part], got[1][part])
            mixed[:, pair_cols(p, part)] = low_cast(d_part)
            vg_ref[2:3, pair_cols(p, part)] = row_sum(d_part)
        d_part = join(got[0][2], got[1][2])
        mixed[:, pair_cols(p, 2)] = low_cast(d_part)
        vg_ref[2:3, pair_cols(p, 2)] = row_sum(d_part)
        return carry

    lax.fori_loop(0, PAIRS, mix_back, 0)

    for j in range(3):
        cols = slice(j * D, (j + 1) * D)
        ig_ref[...] += mm_cols(mixed[:, cols], w_qkv[:, cols])
    all_sent(0)
    tok_t[...] = tok_ref[...].T
    for j in range(3):
        cols = slice(j * D, (j + 1) * D)
        w_qkv[:, cols] = low_cast(mm(tok_t[...], mixed[:, cols]))
    for k in range(1, n_head):
        exchange(0, state_own, state_in, k).wait_send()
        exchange(1, back_own, back_in, k).wait_send()

    ups = [vg_ref[1:2, j * D : (j + 1) * D] for j in range(4)]
    mix = [vg_ref[2:3, j * D : (j + 1) * D] for j in range(3)]
    vg_rows = [gain_one, shift_one, gain_two, shift_two, bias_out, bias_down] + mix + ups
    for i, value in enumerate(vg_rows):
        vg_ref[i : i + 1, 0:D] = value


def fits(mesh):
    return mesh.shape["dp"] == 8


def fused_layer(n_dp, n_head, lengths, tokens, cotangent, masters, vector_master):
    T = tokens.shape[0]
    bf, f32 = jnp.bfloat16, jnp.float32
    vm = pl.BlockSpec(memory_space=pltpu.VMEM)
    out_shape = (
        jax.ShapeDtypeStruct((T, D), bf),
        jax.ShapeDtypeStruct((T, D), f32),
        jax.ShapeDtypeStruct((D, 3 * D), bf),
        jax.ShapeDtypeStruct((D, D), bf),
        jax.ShapeDtypeStruct((D, FF), bf),
        jax.ShapeDtypeStruct((FF, D), bf),
        jax.ShapeDtypeStruct((16, FF), f32),
    )
    V = pltpu.VMEM
    scratch = [
        V((T, 3 * D), bf),
        V((H, T, LANES), bf),
        V((H, T, LANES), bf),
        V((H, T, LANES), bf),
        V((H, T, LANES), bf),
        V((H, T, LANES), f32),
        V((T, D), bf),
        V((T, D), f32),
        V((T, LANES), f32),
        V((T, D), f32),
        V((T, D), bf),
        V((D, T), bf),
        V((T, FF), bf),
        V((T, FF), bf),
        V((T, D), bf),
        V((T, D), bf),
        V((T, D), bf),
        V((T, T), f32),
        V((T, T), f32),
        V((T, LANES), f32),
        V((T, LANES), f32),
        V((4, T, LANES), bf),
        V((SLABS, LANES, LANES), bf),
        V((n_head, SLABS, LANES, LANES), bf),
        V((SLABS, LANES, LANES), bf),
        V((n_head, SLABS, LANES, LANES), bf),
        V((H, LANES, LANES), bf),
        V((H, LANES, LANES), bf),
        V((LANES, LANES), f32),
        V((D, T), bf),
        pltpu.SemaphoreType.DMA((4, 7)),
        pltpu.SemaphoreType.DMA((4, 7)),
        pltpu.SemaphoreType.DMA((2, n_head)),
        pltpu.SemaphoreType.DMA((2, n_head)),
    ]
    return pl.pallas_call(
        functools.partial(layer_kernel, n_dp, n_head, lengths.shape[0]),
        out_shape=out_shape,
        in_specs=[pl.BlockSpec(memory_space=pltpu.SMEM)] + [vm] * 7,
        out_specs=[vm] * 7,
        scratch_shapes=scratch,
        compiler_params=pltpu.CompilerParams(
            collective_id=0, has_side_effects=True, vmem_limit_bytes=62 * 1024 * 1024
        ),
        name="layer",
    )(lengths, tokens, cotangent, *masters, vector_master)


def fused_shards(
    tokens,
    cotangent,
    lengths,
    qkv_master,
    out_master,
    up_master,
    down_master,
    vector_master,
    qkv_first,
    qkv_second,
    out_first,
    out_second,
    up_first,
    up_second,
    down_first,
    down_second,
    vector_first,
    vector_second,
):
    n_dp, n_head = lax.axis_size("dp"), lax.axis_size("head")
    masters = (qkv_master, out_master, up_master, down_master)
    output, input_grad, *grads, vector_grad = fused_layer(
        n_dp, n_head, lengths, tokens, cotangent, masters, vector_master
    )
    parts = [lax.psum_scatter(g, "dp", scatter_dimension=0, tiled=True) for g in grads]
    reduced = [g.astype(jnp.float32) for g in lax.psum(tuple(parts), "head")]
    vector_total = lax.psum(vector_grad[:13, :D], ("dp", "head"))
    rates = (1.0 / math.sqrt(D), 1.0 / math.sqrt(OUT_FAN), 1.0 / math.sqrt(D), 1.0 / math.sqrt(FF))
    firsts = (qkv_first, out_first, up_first, down_first)
    seconds = (qkv_second, out_second, up_second, down_second)
    news = []
    for i in range(4):
        news.extend(
            adam_update(masters[i], firsts[i], seconds[i], reduced[i], rates[i], weight_decay)
        )
    vector_new = adam_update(
        vector_master, vector_first, vector_second, vector_total, vector_rate, 0.0
    )
    return (output, input_grad, *news, *vector_new)


def solution(mesh):
    return jax.shard_map(
        fused_shards if fits(mesh) else shards,
        mesh=mesh,
        in_specs=(
            P(("dp", "head"), None),
            P(("dp", "head"), None),
            P("dp"),
            P("dp", None),
            P("dp", None),
            P("dp", None),
            P("dp", None),
            P(),
            P("dp", None),
            P("dp", None),
            P("dp", None),
            P("dp", None),
            P("dp", None),
            P("dp", None),
            P("dp", None),
            P("dp", None),
            P(),
            P(),
        ),
        out_specs=(
            P(("dp", "head"), None),
            P(("dp", "head"), None),
            P("dp", None),
            P("dp", None),
            P("dp", None),
            P("dp", None),
            P("dp", None),
            P("dp", None),
            P("dp", None),
            P("dp", None),
            P("dp", None),
            P("dp", None),
            P("dp", None),
            P("dp", None),
            P(),
            P(),
            P(),
        ),
        check_vma=False,
    )
```

```python
import functools
import math

import jax
import jax.numpy as jnp
from jax import lax
from jax.experimental import pallas as pl
from jax.experimental.pallas import tpu as pltpu
from jax.sharding import PartitionSpec as P

D = 768
H = 12
HD = 64
FF = 3072
SPAN = 64
STEP = 10
OUT_FAN = 1


highest = lax.Precision.HIGHEST
norm_epsilon = 1e-05
first_decay = 0.9
second_decay = 0.999
adam_epsilon = 1e-08
weight_decay = 0.01
vector_rate = 0.2


def layer_norm(residual, gain_row, shift_row):
    center = residual - jnp.mean(residual, axis=-1, keepdims=True)
    spread = jnp.mean(center * center, axis=-1, keepdims=True)
    return center * lax.rsqrt(spread + norm_epsilon) * gain_row + shift_row


def exact_gelu(upper_pre):
    return jax.nn.gelu(upper_pre, approximate=False)


def group_layout(group_lengths, row_count):
    slot_sizes = (group_lengths + SPAN - 1) // SPAN * SPAN
    slot_ends = jnp.cumsum(slot_sizes)
    slot_starts = slot_ends - slot_sizes
    positions = jnp.arange(row_count, dtype=jnp.int32)
    member = (positions[:, None] >= slot_starts[None, :]) & (
        positions[:, None] < slot_ends[None, :]
    )
    seq_first = jnp.sum(jnp.where(member, slot_starts[None, :], 0), axis=1)
    length = jnp.sum(jnp.where(member, group_lengths[None, :], 0), axis=1)
    seq_numbers = jnp.arange(group_lengths.shape[0], dtype=jnp.int32)
    owners = jnp.sum(jnp.where(member, seq_numbers[None, :], 0), axis=1)
    offset = positions - seq_first
    live_rows = (offset < length).astype(jnp.float32)
    angles = 0.5 * math.pi * offset.astype(jnp.float32) / length.astype(jnp.float32)
    cosine = jnp.cos(angles)
    sine_part = jnp.sin(angles)
    span_owner = owners[::SPAN]
    span_order = jnp.arange(span_owner.shape[0], dtype=jnp.int32)
    same_seq = span_owner[None, :] == span_owner[:, None]
    earlier = (same_seq & (span_order[None, :] < span_order[:, None])).astype(jnp.float32)
    return (cosine, sine_part, live_rows, earlier)


def attend(query_rows, key_rows, value_rows, cosine, sine_part, live_rows, earlier):
    row_count = query_rows.shape[0]
    blocks = row_count // SPAN
    soft_query = jax.nn.softplus(query_rows)
    soft_key = jax.nn.softplus(key_rows)
    feat_query = (
        jnp.concatenate([soft_query * cosine[:, None], soft_query * sine_part[:, None]], axis=1)
        * live_rows[:, None]
    )
    feat_key = (
        jnp.concatenate([soft_key * cosine[:, None], soft_key * sine_part[:, None]], axis=1)
        * live_rows[:, None]
    )
    block_query = feat_query.reshape(blocks, SPAN, -1)
    block_key = feat_key.reshape(blocks, SPAN, -1)
    block_value = value_rows.reshape(blocks, SPAN, -1)
    lower_mask = (jnp.arange(SPAN)[:, None] >= jnp.arange(SPAN)[None, :]).astype(jnp.float32)
    scores = jnp.einsum("cik,cjk->cij", block_query, block_key, precision=highest) * lower_mask
    inner_sum = jnp.einsum("cij,cjd->cid", scores, block_value, precision=highest)
    inner_den = jnp.sum(scores, axis=2)
    states = jnp.einsum("cjk,cjd->ckd", block_key, block_value, precision=highest)
    key_sums = jnp.sum(block_key, axis=1)
    before = jnp.einsum("ce,ekd->ckd", earlier, states, precision=highest)
    before_sums = jnp.einsum("ce,ek->ck", earlier, key_sums, precision=highest)
    outer_sum = jnp.einsum("cik,ckd->cid", block_query, before, precision=highest)
    outer_den = jnp.einsum("cik,ck->ci", block_query, before_sums, precision=highest)
    numerator = (inner_sum + outer_sum).reshape(row_count, -1)
    denominator = (inner_den + outer_den).reshape(row_count) + (1.0 - live_rows)
    return numerator / denominator[:, None]


def contract_rows(left, right):
    return lax.dot_general(
        left, right, (((0,), (0,)), ((), ())), preferred_element_type=jnp.float32
    )


def contract_cols(left, right):
    return lax.dot_general(
        left, right, (((1,), (1,)), ((), ())), preferred_element_type=jnp.float32
    )


def adam_update(master, first, second, gradient, rate, decay):
    first_new = first_decay * first + (1.0 - first_decay) * gradient
    second_new = second_decay * second + (1.0 - second_decay) * gradient * gradient
    first_hat = first_new / (1.0 - first_decay**STEP)
    second_hat = second_new / (1.0 - second_decay**STEP)
    master_new = master - rate * (
        first_hat / (jnp.sqrt(second_hat) + adam_epsilon) + decay * master
    )
    return (first_new, second_new, master_new)


def shards(
    tokens,
    cotangent,
    lengths,
    qkv_master,
    out_master,
    up_master,
    down_master,
    vector_master,
    qkv_first,
    qkv_second,
    out_first,
    out_second,
    up_first,
    up_second,
    down_first,
    down_second,
    vector_first,
    vector_second,
):
    mix_weight, out_weight, up_weight, down_weight = (
        lax.all_gather(qkv_master.astype(jnp.bfloat16), "dp", axis=0, tiled=True),
        lax.all_gather(out_master.astype(jnp.bfloat16), "dp", axis=0, tiled=True),
        lax.all_gather(up_master.astype(jnp.bfloat16), "dp", axis=0, tiled=True),
        lax.all_gather(down_master.astype(jnp.bfloat16), "dp", axis=0, tiled=True),
    )
    tok_count = tokens.shape[0]
    width = tokens.shape[1]
    mixed_all = jnp.dot(tokens, mix_weight, preferred_element_type=jnp.float32) + vector_master[
        6:9
    ].reshape(-1)
    mixed_low = mixed_all.astype(jnp.bfloat16)
    query_part = mixed_low[:, :width].reshape(tok_count, H, 1, HD)
    key_part = mixed_low[:, width : 2 * width].reshape(tok_count, H, 1, HD)
    paired = jnp.concatenate([query_part, key_part], axis=2)
    paired = jnp.repeat(paired[:, :, None], 2, axis=2).reshape(tok_count, 4 * width)
    value_part = mixed_low[:, 2 * width :]
    paired_in, values_in = (
        lax.all_to_all(paired, "head", split_axis=1, concat_axis=0, tiled=True),
        lax.all_to_all(value_part, "head", split_axis=1, concat_axis=0, tiled=True),
    )
    group_rows = paired_in.shape[0]
    item_count = paired_in.shape[1] // (2 * HD)
    cosine, sine_part, live_rows, earlier = group_layout(lengths, group_rows)
    stacked = paired_in.reshape(group_rows, item_count, 2, HD).astype(jnp.float32)
    query_items = stacked[:, :, 0]
    key_items = stacked[:, :, 1]
    value_items = values_in.reshape(group_rows, item_count, HD // 2).astype(jnp.float32)

    def mix_items(query_set, key_set, value_set):

        def single(query_rows, key_rows, value_rows):
            return attend(query_rows, key_rows, value_rows, cosine, sine_part, live_rows, earlier)

        return jax.vmap(single, in_axes=1, out_axes=1)(query_set, key_set, value_set)

    attended, mix_back = jax.vjp(mix_items, query_items, key_items, value_items)
    heads_out = attended.reshape(group_rows, item_count * (HD // 2)).astype(jnp.bfloat16)
    heads = lax.all_to_all(heads_out, "head", split_axis=0, concat_axis=1, tiled=True)
    projected = jnp.dot(heads, out_weight, preferred_element_type=jnp.float32) + vector_master[4]
    resid_one = tokens.astype(jnp.float32) + projected
    hidden, norm_one_back = jax.vjp(layer_norm, resid_one, vector_master[0], vector_master[1])
    hidden_low = hidden.astype(jnp.bfloat16)
    upper_pre = jnp.dot(hidden_low, up_weight, preferred_element_type=jnp.float32) + vector_master[
        9:13
    ].reshape(-1)
    active, gelu_back = jax.vjp(exact_gelu, upper_pre)
    active_low = active.astype(jnp.bfloat16)
    lowered = (
        jnp.dot(active_low, down_weight, preferred_element_type=jnp.float32) + vector_master[5]
    )
    output, norm_two_back = jax.vjp(
        layer_norm, hidden + lowered, vector_master[2], vector_master[3]
    )
    grad_two, gain_two, shift_two = norm_two_back(cotangent)
    grad_two_low = grad_two.astype(jnp.bfloat16)
    down_grad = contract_rows(active_low, grad_two_low)
    (upper_grad,) = gelu_back(contract_cols(grad_two_low, down_weight))
    upper_low = upper_grad.astype(jnp.bfloat16)
    up_grad = contract_rows(hidden_low, upper_low)
    hidden_grad = grad_two + contract_cols(upper_low, up_weight)
    grad_one, gain_one, shift_one = norm_one_back(hidden_grad)
    grad_one_low = grad_one.astype(jnp.bfloat16)
    out_grad = contract_rows(heads, grad_one_low)
    heads_grad = contract_cols(grad_one_low, out_weight).astype(jnp.bfloat16)
    heads_back = lax.all_to_all(heads_grad, "head", split_axis=1, concat_axis=0, tiled=True)
    query_back, key_back, value_back = mix_back(
        heads_back.reshape(group_rows, item_count, HD // 2).astype(jnp.float32)
    )
    pair_back = (
        jnp.stack([query_back, key_back], axis=2)
        .astype(jnp.bfloat16)
        .reshape(group_rows, item_count * 2 * HD)
    )
    value_low = value_back.astype(jnp.bfloat16).reshape(group_rows, item_count * (HD // 2))
    pair_home, value_home = (
        lax.all_to_all(pair_back, "head", split_axis=0, concat_axis=1, tiled=True),
        lax.all_to_all(value_low, "head", split_axis=0, concat_axis=1, tiled=True),
    )
    summed = jnp.sum(pair_home.astype(jnp.float32).reshape(tok_count, H, 2, 2, HD), axis=2)
    mixed_grad = jnp.concatenate(
        [
            summed[:, :, 0].reshape(tok_count, width),
            summed[:, :, 1].reshape(tok_count, width),
            value_home.astype(jnp.float32),
        ],
        axis=1,
    )
    mixed_low_grad = mixed_grad.astype(jnp.bfloat16)
    mix_grad = contract_rows(tokens, mixed_low_grad)
    input_grad = grad_one + contract_cols(mixed_low_grad, mix_weight)
    vector_grad = jnp.concatenate(
        [
            jnp.stack(
                [
                    gain_one,
                    shift_one,
                    gain_two,
                    shift_two,
                    jnp.sum(grad_one, axis=0),
                    jnp.sum(grad_two, axis=0),
                ]
            ),
            jnp.sum(mixed_grad, axis=0).reshape(3, width),
            jnp.sum(upper_grad, axis=0).reshape(4, width),
        ],
        axis=0,
    )
    local_grads = (mix_grad, out_grad, up_grad, down_grad)
    row_parts = (
        lax.psum_scatter(
            local_grads[0].astype(jnp.bfloat16), "dp", scatter_dimension=0, tiled=True
        ).astype(jnp.float32),
        lax.psum_scatter(
            local_grads[1].astype(jnp.bfloat16), "dp", scatter_dimension=0, tiled=True
        ).astype(jnp.float32),
        lax.psum_scatter(
            local_grads[2].astype(jnp.bfloat16), "dp", scatter_dimension=0, tiled=True
        ).astype(jnp.float32),
        lax.psum_scatter(
            local_grads[3].astype(jnp.bfloat16), "dp", scatter_dimension=0, tiled=True
        ).astype(jnp.float32),
    )
    reduced = (
        lax.psum(row_parts[0].astype(jnp.bfloat16), "head").astype(jnp.float32),
        lax.psum(row_parts[1].astype(jnp.bfloat16), "head").astype(jnp.float32),
        lax.psum(row_parts[2].astype(jnp.bfloat16), "head").astype(jnp.float32),
        lax.psum(row_parts[3].astype(jnp.bfloat16), "head").astype(jnp.float32),
    )
    vector_total = lax.psum(vector_grad, ("dp", "head"))
    qkv_new = adam_update(
        qkv_master, qkv_first, qkv_second, reduced[0], 1.0 / math.sqrt(D), weight_decay
    )
    out_new = adam_update(
        out_master, out_first, out_second, reduced[1], 1.0 / math.sqrt(OUT_FAN), weight_decay
    )
    up_new = adam_update(
        up_master, up_first, up_second, reduced[2], 1.0 / math.sqrt(D), weight_decay
    )
    down_new = adam_update(
        down_master, down_first, down_second, reduced[3], 1.0 / math.sqrt(FF), weight_decay
    )
    vector_new = adam_update(
        vector_master, vector_first, vector_second, vector_total, vector_rate, 0.0
    )
    return (
        output.astype(jnp.bfloat16),
        input_grad,
        qkv_new[0],
        qkv_new[1],
        qkv_new[2],
        out_new[0],
        out_new[1],
        out_new[2],
        up_new[0],
        up_new[1],
        up_new[2],
        down_new[0],
        down_new[1],
        down_new[2],
        vector_new[0],
        vector_new[1],
        vector_new[2],
    )


PAIRS = H // 2
LANES = 2 * HD
SLABS = PAIRS + 1
GROUPS = 3
WIDE = D // GROUPS
TILES = FF // D
ROW_TILE = 128
MESH = pl.DeviceIdType.MESH
DOWN, UP, OUT, MIX = 0, TILES, 2 * TILES, 2 * TILES + 1
UNITS = 2 * TILES + 1 + GROUPS


def mm(left, right):
    return jnp.dot(left, right, preferred_element_type=jnp.float32)


def mm_cols(left, right):
    return lax.dot_general(
        left, right, (((1,), (1,)), ((), ())), preferred_element_type=jnp.float32
    )


def mm_rows(left, right):
    return lax.dot_general(
        left, right, (((0,), (0,)), ((), ())), preferred_element_type=jnp.float32
    )


def swap_halves(slab):
    return pltpu.roll(slab, HD, 1)


def low_cast(value):
    return value.astype(jnp.bfloat16)


def row_sum(value):
    return jnp.sum(value, axis=0, keepdims=True)


def gelu_parts(z):
    x = jnp.abs(z) * (1.0 / math.sqrt(2.0))
    t = 1.0 / (1.0 + 0.3275911 * x)
    bell = jnp.exp(-0.5 * z * z)
    poly = t * (
        0.254829592
        + t * (-0.284496736 + t * (1.421413741 + t * (-1.453152027 + t * 1.061405429)))
    )
    upper_tail = 0.5 * poly * bell
    phi = jnp.where(z >= 0, 1.0 - upper_tail, upper_tail)
    return z * phi, phi + z * (bell * (1.0 / math.sqrt(2.0 * math.pi)))


def norm_rows(residual):
    center = residual - jnp.mean(residual, axis=-1, keepdims=True)
    rstd = lax.rsqrt(jnp.mean(center * center, axis=-1, keepdims=True) + norm_epsilon)
    return center * rstd, rstd


def norm_rows_back(dy, normed, rstd, gain):
    e = dy * gain
    return rstd * (
        e
        - jnp.mean(e, axis=-1, keepdims=True)
        - normed * jnp.mean(e * normed, axis=-1, keepdims=True)
    )


def layer_kernel(
    n_head,
    n_seq,
    lens_ref,
    tok_hbm,
    cot_hbm,
    qkv_f,
    out_f,
    up_f,
    down_f,
    vec_ref,
    y_hbm,
    ig_ref,
    g_qkv,
    g_out,
    g_up,
    g_down,
    vg_ref,
    w_qkv,
    w_out,
    w_up,
    w_down,
    tok,
    mixed,
    feat_q,
    feat_k,
    val_a,
    num_a,
    heads,
    norm_one,
    rstd_one,
    hid,
    hid_low,
    turned,
    act,
    gel,
    two_low,
    one_low,
    mask,
    mask_t,
    cs_ref,
    live_ref,
    keeps,
    state_own,
    state_in,
    back_own,
    back_in,
    state_sum,
    state_h,
    back_h,
    zcol,
    red_a,
    red_b,
    red_c,
    red_e,
    vec_land,
    load_sem,
    g_send,
    g_recv,
    s_send,
    s_recv,
    r_send,
    r_recv,
    v_send,
    v_recv,
):
    T = tok.shape[0]
    rows = w_out.shape[3]
    half = rows // 2
    dp = lax.axis_index("dp")
    z = lax.axis_index("head")
    core = dp % 2
    xx = (dp // 2) % 2
    yy = dp // 4
    color = z % 2
    sib = (dp + 1 - 2 * core, z)
    xn = (dp + 2 - 4 * xx, z)
    yn = (dp + 4 - 8 * yy, z)
    z_one = (dp, z + 1 - 2 * color)
    z_two = (dp, (z + 3 + 2 * color) % n_head)

    def load(i, src, dst):
        return pltpu.make_async_copy(src, dst, load_sem.at[i])

    def spot(ref, i):
        return ref.at[pl.ds(i * rows, rows), :]

    loads = []
    for g in range(GROUPS):
        for part in range(3):
            loads.append(
                load(
                    len(loads),
                    qkv_f.at[:, pl.ds(part * D + g * WIDE, WIDE)],
                    hid.at[pl.ds(g * rows, rows), pl.ds(part * WIDE, WIDE)],
                )
            )
    loads.append(load(len(loads), out_f, spot(hid, GROUPS)))
    for j in range(TILES):
        loads.append(load(len(loads), up_f.at[:, pl.ds(j * D, D)], spot(norm_one, j)))
    loads.append(load(len(loads), down_f, ig_ref.at[pl.ds(0, TILES * rows), :]))
    load_tok = load(len(loads), tok_hbm, tok)
    load_cot = load(len(loads) + 1, cot_hbm, ig_ref)
    save_y = load(len(loads) + 2, one_low, y_hbm)
    for copy in loads:
        copy.start()
    load_tok.start()

    barrier = pltpu.get_barrier_semaphore()
    peers = [sib, xn, yn]
    for k in range(1, n_head):
        peers.append((dp, (z + k) % n_head))
    for peer in peers:
        pl.semaphore_signal(barrier, inc=1, device_id=peer, device_id_type=MESH)

    def remote(src, dst, send, recv, target):
        return pltpu.make_async_remote_copy(
            src_ref=src,
            dst_ref=dst,
            send_sem=send,
            recv_sem=recv,
            device_id=target,
            device_id_type=MESH,
        )

    GATHERS = GROUPS + 1 + TILES // 2 + 2

    def piece(g, y, x, c, which):
        if g < GROUPS:
            ref, size, base = w_qkv.at[g, y, x, c], rows, 0
        elif g == GROUPS:
            ref, size, base = w_out.at[y, x, c], rows, 0
        elif g < GROUPS + 1 + TILES // 2:
            i = g - GROUPS - 1
            if which is None:
                return w_up.at[pl.ds(2 * i, 2), y, x, c]
            return w_up.at[
                pl.ds(2 * i, 2), y, x, c, pl.ds(pl.multiple_of(which * half, half), half), :
            ]
        else:
            i = g - GROUPS - 1 - TILES // 2
            ref, size, base = w_down.at[y, x, c], 2 * rows, 2 * rows * i
        if which is None:
            return ref.at[pl.ds(base, size), :]
        return ref.at[pl.ds(pl.multiple_of(base + which * (size // 2), size // 2), size // 2), :]

    def own_masters(g):
        if g < GROUPS:
            for part in range(3):
                loads[3 * g + part].wait()
            w_qkv[g, yy, xx, core] = low_cast(hid[g * rows : (g + 1) * rows, :])
        elif g == GROUPS:
            loads[9].wait()
            w_out[yy, xx, core] = low_cast(hid[g * rows : (g + 1) * rows, :])
        elif g < GROUPS + 1 + TILES // 2:
            for j in range(2 * (g - GROUPS - 1), 2 * (g - GROUPS)):
                loads[10 + j].wait()
                w_up[j, yy, xx, core] = low_cast(norm_one[j * rows : (j + 1) * rows, :])
        else:
            i = g - GROUPS - 1 - TILES // 2
            if i == 0:
                loads[10 + TILES].wait()
            span = slice(2 * rows * i, 2 * rows * (i + 1))
            w_down[yy, xx, core, span, :] = low_cast(ig_ref[span, :])

    here, mine_x, mine_y, mine_d = (yy, xx), (yy, 1 - xx), (1 - yy, xx), (1 - yy, 1 - xx)
    other = 1 - color

    def gcopy(g, kind, chip, which, target, c=None):
        ref = piece(g, chip[0], chip[1], core if c is None else c, which)
        return remote(ref, ref, g_send.at[g, kind], g_recv.at[g, kind], target)

    def z_target(g):
        return z_one if (g // 2) % 2 == 0 else z_two

    def g_own(g):
        own_masters(g)
        gcopy(g, 0, here, color, xn).start()
        gcopy(g, 1, here, color, yn).start()
        gcopy(g, 2, here, None, sib).start()

    def g_first(g):
        gcopy(g, 0, mine_x, color, xn).wait_recv()
        gcopy(g, 1, mine_y, color, yn).wait_recv()
        if g % 2 == 0:
            gcopy(g, 3, mine_x, color, yn).start()
        else:
            gcopy(g, 3, mine_y, color, xn).start()
        gcopy(g, 4, mine_x, color, z_one).start()
        gcopy(g, 5, mine_y, color, z_two).start()
        gcopy(g, 7, mine_x, color, sib).start()
        gcopy(g, 8, mine_y, color, sib).start()

    def g_second(g):
        gcopy(g, 3, mine_d, color, yn).wait_recv()
        gcopy(g, 6, mine_d, color, z_target(g)).start()
        gcopy(g, 9, mine_d, color, sib).start()
        gcopy(g, 4, mine_x, other, z_one).wait_recv()
        gcopy(g, 10, mine_x, other, sib).start()
        gcopy(g, 5, mine_y, other, z_two).wait_recv()
        gcopy(g, 11, mine_y, other, sib).start()

    def g_third(g):
        gcopy(g, 6, mine_d, other, z_one).wait_recv()
        gcopy(g, 12, mine_d, other, sib).start()

    def g_last(g):
        for kind, chip, which in (
            (2, here, None),
            (7, mine_x, color),
            (8, mine_y, color),
            (9, mine_d, color),
            (10, mine_x, other),
            (11, mine_y, other),
            (12, mine_d, other),
        ):
            gcopy(g, kind, chip, which, sib, 1 - core).wait_recv()

    def g_sent(g):
        for kind, chip, which in (
            (0, here, color),
            (1, here, color),
            (2, here, None),
            (3, mine_x, color),
            (4, mine_x, color),
            (5, mine_y, color),
            (6, mine_d, color),
            (7, mine_x, color),
            (8, mine_y, color),
            (9, mine_d, color),
            (10, mine_x, other),
            (11, mine_y, other),
            (12, mine_d, other),
        ):
            gcopy(g, kind, chip, which, sib).wait_send()

    plan = []
    for step in range(GATHERS + 3):
        for stage, act_of in ((2, g_third), (1, g_second), (0, g_first)):
            g = step - stage
            if 0 <= g < GATHERS:
                plan.append((act_of, g))
        if step + GATHER_AHEAD < GATHERS:
            plan.append((g_own, step + GATHER_AHEAD))
    done = []

    def gather_some(count):
        while plan and count > 0:
            act_of, g = plan.pop(0)
            act_of(g)
            done.append((act_of, g))
            count -= 1

    def gather_until(g):
        while (g_third, g) not in done:
            gather_some(1)
        g_last(g)

    def unit_ref(k):
        if k < UP:
            return w_down.at[:, :, :, pl.ds(k * rows, rows), :]
        if k < OUT:
            return w_up.at[k - UP]
        if k < MIX:
            return w_out
        return w_qkv.at[k - MIX]

    def kept_of(k):
        kept = (z // 2 + color * (1 - 2 * (z // 2))) if k % 2 == 0 else z // 2
        return kept

    def kept_rows(k):
        return pl.ds(pl.multiple_of(kept_of(k) * half, half), half)

    def gone_rows(k):
        return pl.ds(pl.multiple_of((1 - kept_of(k)) * half, half), half)

    top, low_part = pl.ds(0, half), pl.ds(half, half)

    def finals(k):
        span = kept_rows(k)
        if k < UP:
            base = pl.multiple_of(k * rows + span.start, half)
            return [(None, g_down.at[pl.ds(base, half), :])]
        if k < OUT:
            return [(None, g_up.at[span, pl.ds((k - UP) * D, D)])]
        if k < MIX:
            return [(None, g_out.at[span, :])]
        return [
            (part * WIDE, g_qkv.at[span, pl.ds(part * D + (k - MIX) * WIDE, WIDE)])
            for part in range(3)
        ]

    def r_final(k, i):
        mine = red_a.at[k, yy, xx]
        col, dst = finals(k)[i]
        cols = slice(None) if col is None else pl.ds(col, WIDE)
        return mine.at[kept_rows(k), cols], dst

    def r_copy(k, kind):
        mine = red_a.at[k, yy, xx]
        one, two = (z_one, z_two) if k % 2 == 0 else (z_two, z_one)
        if kind == 0:
            src, dst, target = unit_ref(k).at[:, :, 1 - core], red_a.at[k], sib
        elif kind == 1:
            src, dst, target = red_a.at[k, :, 1 - xx, top, :], red_b.at[k, 0], xn
        elif kind == 2:
            src, dst, target = red_a.at[k, 1 - yy, :, low_part, :], red_b.at[k, 1], yn
        elif kind == 3:
            src, dst, target = red_a.at[k, 1 - yy, xx, top, :], red_c.at[k, 0], yn
        elif kind == 4:
            src, dst, target = red_a.at[k, yy, 1 - xx, low_part, :], red_c.at[k, 1], xn
        elif kind == 5:
            src, dst, target = mine.at[gone_rows(k), :], red_e.at[k, 0], one
        elif kind == 6:
            src, dst, target = mine.at[kept_rows(k), :], red_e.at[k, 1], two
        else:
            src, dst = r_final(k, kind - 7)
            target = one
        return remote(src, dst, r_send.at[k, kind], r_recv.at[k, kind], target)

    def r_local(k, i):
        src, dst = r_final(k, i)
        return pltpu.make_async_copy(src, dst, r_recv.at[k, 10 + i])

    def added(one, two):
        return low_cast(one.astype(jnp.float32) + two.astype(jnp.float32))

    def r_start(k):
        r_copy(k, 0).start()

    def r_pair(k):
        r_copy(k, 0).wait_recv()
        for y in range(2):
            for x in range(2):
                mine = unit_ref(k)[y, x, core] if k >= UP else None
                if k < UP:
                    mine = w_down[y, x, core, k * rows : (k + 1) * rows, :]
                red_a[k, y, x] = added(mine, red_a[k, y, x])
        r_copy(k, 1).start()
        r_copy(k, 2).start()

    def r_plane(k):
        r_copy(k, 1).wait_recv()
        red_a[k, 1 - yy, xx, top, :] = added(red_a[k, 1 - yy, xx, top, :], red_b[k, 0, 1 - yy])
        r_copy(k, 3).start()
        r_copy(k, 2).wait_recv()
        red_a[k, yy, 1 - xx, low_part, :] = added(
            red_a[k, yy, 1 - xx, low_part, :], red_b[k, 1, 1 - xx]
        )
        r_copy(k, 4).start()
        red_a[k, yy, xx, top, :] = added(red_a[k, yy, xx, top, :], red_b[k, 0, yy])
        red_a[k, yy, xx, low_part, :] = added(red_a[k, yy, xx, low_part, :], red_b[k, 1, xx])

    def r_whole(k):
        r_copy(k, 3).wait_recv()
        r_copy(k, 4).wait_recv()
        red_a[k, yy, xx, top, :] = added(red_a[k, yy, xx, top, :], red_c[k, 0])
        red_a[k, yy, xx, low_part, :] = added(red_a[k, yy, xx, low_part, :], red_c[k, 1])
        r_copy(k, 5).start()

    def r_z_first(k):
        r_copy(k, 5).wait_recv()
        red_a[k, yy, xx, kept_rows(k), :] = added(red_a[k, yy, xx, kept_rows(k), :], red_e[k, 0])
        r_copy(k, 6).start()

    def r_z_second(k):
        r_copy(k, 6).wait_recv()
        r_copy(k, 6).wait_send()
        red_a[k, yy, xx, kept_rows(k), :] = added(red_a[k, yy, xx, kept_rows(k), :], red_e[k, 1])
        for i in range(len(finals(k))):
            r_copy(k, 7 + i).start()
            r_local(k, i).start()

    def r_end(k):
        for i in range(len(finals(k))):
            r_copy(k, 7 + i).wait()
            r_local(k, i).wait()
        for kind in range(6):
            r_copy(k, kind).wait_send()

    stages = (r_pair, r_plane, r_whole, r_z_first, r_z_second)
    r_plan = []
    for tick in range(UNITS + len(stages)):
        for stage in reversed(range(len(stages))):
            if 0 <= tick - stage < UNITS:
                r_plan.append((stages[stage], tick - stage))
    started = []

    def reduce_start(k):
        r_start(k)
        started.append(k)

    def reduce_some(count):
        while r_plan and count > 0 and r_plan[0][1] in started:
            act_of, k = r_plan.pop(0)
            act_of(k)
            count -= 1

    for g in range(min(GATHER_AHEAD, GATHERS)):
        own_masters(g)
    pl.semaphore_wait(barrier, len(peers))
    for g in range(min(GATHER_AHEAD, GATHERS)):
        gcopy(g, 0, here, color, xn).start()
        gcopy(g, 1, here, color, yn).start()
        gcopy(g, 2, here, None, sib).start()

    lens = [lens_ref[s] for s in range(n_seq)]
    ends = []
    total = 0
    for s in range(n_seq):
        total = total + ((lens[s] + (SPAN - 1)) // SPAN) * SPAN
        ends.append(total)
    starts = [0] + ends[:-1]

    def owner_of(row):
        found = jnp.zeros_like(row)
        for s in range(n_seq):
            found = found + (row >= ends[s]).astype(jnp.int32)
        return found

    half_lane = lax.broadcasted_iota(jnp.int32, (T, LANES), 1)
    row = z * T + lax.broadcasted_iota(jnp.int32, (T, LANES), 0)
    first = jnp.zeros_like(row)
    length = jnp.ones_like(row)
    for s in range(n_seq):
        inside = (row >= starts[s]) & (row < ends[s])
        first = jnp.where(inside, starts[s], first)
        length = jnp.where(inside, lens[s], length)
    offset = row - first
    live = (offset < length).astype(jnp.float32)
    angle = 0.5 * math.pi * offset.astype(jnp.float32) / length.astype(jnp.float32)
    angle = jnp.where(half_lane < HD, angle, 0.5 * math.pi - angle)
    cs_ref[...] = jnp.cos(angle) * live
    live_ref[...] = live
    owners = owner_of(row)
    next_owner = owner_of(jnp.full((1, 1), (z + 1) * T, jnp.int32))
    last_owner = owner_of(jnp.full((1, 1), z * T - 1, jnp.int32))
    my_first = owner_of(jnp.full((1, 1), z * T, jnp.int32))
    my_last = owner_of(jnp.full((1, 1), (z + 1) * T - 1, jnp.int32))
    for i, edge in enumerate((next_owner, last_owner, my_first, my_last)):
        keeps[i] = low_cast((owners == edge).astype(jnp.float32))

    def fill_masks(i, carry):
        r0 = pl.multiple_of(i * ROW_TILE, ROW_TILE)
        t_i = r0 + lax.broadcasted_iota(jnp.int32, (ROW_TILE, T), 0)
        u_i = lax.broadcasted_iota(jnp.int32, (ROW_TILE, T), 1)
        same = owner_of(t_i + z * T) == owner_of(u_i + z * T)
        mask[pl.ds(r0, ROW_TILE), :] = (same & (u_i <= t_i)).astype(jnp.float32)
        mask_t[pl.ds(r0, ROW_TILE), :] = (same & (u_i >= t_i)).astype(jnp.float32)
        return carry

    lax.fori_loop(0, T // ROW_TILE, fill_masks, 0)

    sq_lane = lax.broadcasted_iota(jnp.int32, (LANES, LANES), 1)
    ones_lane = ((half_lane == HD) | (half_lane == HD + 1)).astype(jnp.float32)

    def softplus(v):
        return jnp.maximum(v, 0.0) + jnp.log1p(jnp.exp(-jnp.abs(v)))

    def slab(p, part):
        return p // 2, slice(None), pl.ds(pl.multiple_of(part * WIDE + (p % 2) * LANES, LANES), LANES)

    def pair_cols(p):
        return pl.ds(pl.multiple_of(p * LANES, LANES), LANES)

    def split(value):
        swapped = swap_halves(value)
        return jnp.where(half_lane < HD, value, swapped), jnp.where(half_lane < HD, swapped, value)

    def join(left, right):
        return jnp.where(half_lane < HD, left, swap_halves(right))

    def pack_states(p, left, right, own, n_ones):
        own[p] = low_cast(jnp.where(sq_lane < HD, left, swap_halves(right)))
        for side, part in ((0, left), (1, right)):
            column = part[:, HD : HD + 1]
            if n_ones == 2:
                column = column + part[:, HD + 1 : HD + 2]
            zcol[...] = jnp.where(sq_lane == 2 * p + side, column, zcol[...])

    zcol[...] = jnp.zeros_like(zcol)

    def make_features(p, carry):
        cs = cs_ref[...]
        for part, store in ((0, feat_q), (1, feat_k)):
            left, right = split(softplus(mixed[slab(p, part)].astype(jnp.float32)))
            store[2 * p] = low_cast(left * cs)
            store[2 * p + 1] = low_cast(right * cs)
        v_pair = mixed[slab(p, 2)].astype(jnp.float32)
        val_a[2 * p] = low_cast(jnp.where(half_lane < HD, v_pair, ones_lane))
        val_a[2 * p + 1] = low_cast(jnp.where(half_lane < HD, swap_halves(v_pair), ones_lane))
        left = mm_rows(feat_k[2 * p] * keeps[0], val_a[2 * p])
        right = mm_rows(feat_k[2 * p + 1] * keeps[0], val_a[2 * p + 1])
        pack_states(p, left, right, state_own, 1)
        return carry

    load_tok.wait()
    for g in range(GROUPS):
        gather_until(g)
        part = mm(tok[...], w_qkv[g].reshape(D, D))
        mixed[g, :, 0:WIDE] = low_cast(part[:, 0:WIDE] + vec_ref[6:7, g * WIDE : (g + 1) * WIDE])
        mixed[g, :, WIDE : 2 * WIDE] = low_cast(
            part[:, WIDE : 2 * WIDE] + vec_ref[7:8, g * WIDE : (g + 1) * WIDE]
        )
        mixed[g, :, 2 * WIDE :] = low_cast(part[:, 2 * WIDE :])
        lax.fori_loop(2 * g, 2 * g + 2, make_features, 0)
        gather_some(2)
    state_own[PAIRS] = low_cast(zcol[...])

    def exchange(which, own, landed, k):
        target = (z + k) % n_head if which == 0 else (z + n_head - k) % n_head
        return remote(
            own, landed.at[k - 1], s_send.at[which, k], s_recv.at[which, k], (dp, target)
        )

    def may_send(which, k):
        return z + k < n_head if which == 0 else z >= k

    def may_receive(which, k):
        return z >= k if which == 0 else z + k < n_head

    def exchange_start(which, own, landed):
        for k in range(1, n_head):

            @pl.when(may_send(which, k))
            def _(k=k):
                exchange(which, own, landed, k).start()

    def exchange_sent(which, own, landed):
        for k in range(1, n_head):

            @pl.when(may_send(which, k))
            def _(k=k):
                exchange(which, own, landed, k).wait_send()

    def exchange_end(which, own, landed, weight_of, out, n_ones):
        state_sum[...] = jnp.zeros_like(state_sum)
        for k in range(1, n_head):

            @pl.when(may_receive(which, k))
            def _(k=k):
                exchange(which, own, landed, k).wait_recv()
                weight = weight_of(k).reshape(1, 1, 1)
                state_sum[...] += weight * landed[k - 1].astype(jnp.float32)

        def unpack(p, carry):
            packed = state_sum[p]
            ends_col = state_sum[PAIRS]
            for side in (0, 1):
                column = jnp.sum(
                    jnp.where(sq_lane == 2 * p + side, ends_col, 0.0), axis=1, keepdims=True
                )
                part = packed if side == 0 else swap_halves(packed)
                wide = (sq_lane >= HD) & (sq_lane < HD + n_ones)
                out[2 * p + side] = low_cast(
                    jnp.where(sq_lane < HD, part, jnp.where(wide, column, 0.0))
                )
            return carry

        lax.fori_loop(0, PAIRS, unpack, 0)

    def forward_weight(k):
        edge = owner_of(jnp.full((1, 1), (z - k + 1) * T, jnp.int32))
        return (edge == my_first).astype(jnp.float32)

    def backward_weight(k):
        edge = owner_of(jnp.full((1, 1), (z + k) * T - 1, jnp.int32))
        return (edge == my_last).astype(jnp.float32)

    exchange_start(0, state_own, state_in)

    def local_attend(h, carry):
        scores = mm_cols(feat_q[h], feat_k[h]) * mask[...]
        num_a[h] = mm(low_cast(scores), val_a[h])
        return carry

    gather_some(2)
    for part in range(3):
        lax.fori_loop(4 * part, 4 * part + 4, local_attend, 0)
        gather_some(2)

    exchange_end(0, state_own, state_in, forward_weight, state_h, 2)

    def finish_heads(p, carry):
        att = []
        for side in (0, 1):
            h = 2 * p + side
            whole = num_a[h] + mm(feat_q[h] * keeps[2], state_h[h])
            den = whole[:, HD : HD + 1] + (1.0 - live_ref[...])
            inverse = 1.0 / den
            got = whole * inverse
            num_a[h] = jnp.where(half_lane < HD, got, inverse)
            att.append(got)
        shift = vec_ref[8:9, pair_cols(p)]
        heads[:, pair_cols(p)] = low_cast(join(att[0], att[1]) + shift * live_ref[...])
        return carry

    lax.fori_loop(0, PAIRS, finish_heads, 0)

    gather_until(GROUPS)

    def tile_rows(i):
        return pl.ds(pl.multiple_of(i * ROW_TILE, ROW_TILE), ROW_TILE)

    def first_norm(i, carry):
        r = tile_rows(i)
        w = w_out[...].reshape(D, D)
        residual = tok[r, :].astype(jnp.float32) + (mm(heads[r, :], w) + vec_ref[4:5, :])
        normed, rstd = norm_rows(residual)
        norm_one[r, :] = normed
        rstd_one[r, :] = jnp.broadcast_to(rstd, (ROW_TILE, LANES))
        hidden = normed * vec_ref[0:1, :] + vec_ref[1:2, :]
        hid[r, :] = hidden
        hid_low[r, :] = low_cast(hidden)
        return carry

    gather_some(3)

    while any(act_of is g_own for act_of, _ in plan):
        gather_some(1)
    load_cot.start()
    lax.fori_loop(0, T // ROW_TILE, first_norm, 0)

    for j in range(TILES):
        if j % 2 == 0:
            gather_until(GROUPS + 1 + j // 2)

        def ff_up(i, carry, j=j):
            r = tile_rows(i)
            upper = mm(hid_low[r, :], w_up[j].reshape(D, D)) + vec_ref[9 + j : 10 + j, :]
            value, slope = gelu_parts(upper)
            act[r, j * D : (j + 1) * D] = low_cast(value)
            gel[r, j * D : (j + 1) * D] = low_cast(slope)
            return carry

        lax.fori_loop(0, T // ROW_TILE, ff_up, 0)
        gather_some(2)

    gather_until(GATHERS - 2)
    gather_until(GATHERS - 1)
    load_cot.wait()

    def second_norm(i, sums):
        r = tile_rows(i)
        lowered = mm(act[r, :], w_down[...].reshape(FF, D))
        normed, rstd = norm_rows(hid[r, :] + (lowered + vec_ref[5:6, :]))
        one_low[r, :] = low_cast(normed * vec_ref[2:3, :] + vec_ref[3:4, :])
        dy = ig_ref[r, :]
        d_two = norm_rows_back(dy, normed, rstd, vec_ref[2:3, :])
        hid[r, :] = d_two
        two_low[r, :] = low_cast(d_two)
        return sums[0] + row_sum(dy * normed), sums[1] + row_sum(dy), sums[2] + row_sum(d_two)

    zero_row = jnp.zeros((1, D), jnp.float32)
    gain_two, shift_two, bias_down = lax.fori_loop(
        0, T // ROW_TILE, second_norm, (zero_row, zero_row, zero_row)
    )
    save_y.start()
    vg_ref[2:3, :] = gain_two
    vg_ref[3:4, :] = shift_two
    vg_ref[5:6, :] = bias_down

    for j in range(TILES):

        def ff_back(i, total, j=j):
            r = tile_rows(i)
            d_act = mm_cols(two_low[r, :], w_down[j // 2, j % 2].reshape(D, D))
            d_upper = d_act * gel[r, j * D : (j + 1) * D].astype(jnp.float32)
            gel[r, j * D : (j + 1) * D] = low_cast(d_upper)
            return total + row_sum(d_upper)

        vg_ref[9 + j : 10 + j, :] = lax.fori_loop(0, T // ROW_TILE, ff_back, zero_row)

    for g in (GATHERS - 2, GATHERS - 1):
        g_sent(g)
    for j in range(TILES):
        got = low_cast(mm_rows(act[:, j * D : (j + 1) * D], two_low[...]))
        w_down[j // 2, j % 2] = got.reshape(2, TILES * rows, D)
    for k in range(UP):
        reduce_start(k)

    save_y.wait()

    def first_norm_back(i, sums):
        r = tile_rows(i)
        dy = hid[r, :]
        for j in range(TILES):
            dy = dy + mm_cols(gel[r, j * D : (j + 1) * D], w_up[j].reshape(D, D))
        normed = norm_one[r, :]
        d_one = norm_rows_back(dy, normed, rstd_one[r, 0:1], vec_ref[0:1, :])
        ig_ref[r, :] = d_one
        one_low[r, :] = low_cast(d_one)
        return sums[0] + row_sum(dy * normed), sums[1] + row_sum(dy), sums[2] + row_sum(d_one)

    sums = (zero_row, zero_row, zero_row)
    steps = T // ROW_TILE
    sums = lax.fori_loop(0, steps // 2, first_norm_back, sums)
    reduce_some(1)
    sums = lax.fori_loop(steps // 2, steps, first_norm_back, sums)
    reduce_some(2)
    vg_ref[0:1, :] = sums[0]
    vg_ref[1:2, :] = sums[1]
    vg_ref[4:5, :] = sums[2]

    d_heads = two_low
    d_heads[...] = low_cast(mm_cols(one_low[...], w_out[...].reshape(D, D)))

    zcol[...] = jnp.zeros_like(zcol)

    def grad_slot(h):
        return slice(None), pl.ds(pl.multiple_of(h * LANES, LANES), LANES)

    def back_states(p, carry):
        g_pair = d_heads[:, pair_cols(p)].astype(jnp.float32)
        parts = []
        for side in (0, 1):
            h = 2 * p + side
            saved = num_a[h]
            g = g_pair if side == 0 else swap_halves(g_pair)
            gn = jnp.where(half_lane < HD, g * swap_halves(saved), 0.0)
            gd = -jnp.sum(gn * saved, axis=1, keepdims=True)
            gd_high = low_cast(gd).astype(jnp.float32)
            gn = jnp.where(
                half_lane == HD, gd_high, jnp.where(half_lane == HD + 1, gd - gd_high, gn)
            )
            gn = low_cast(gn)
            act[grad_slot(h)] = gn
            parts.append(mm_rows(feat_q[h] * keeps[1], gn))
        pack_states(p, parts[0], parts[1], back_own, 2)
        return carry

    lax.fori_loop(0, PAIRS, back_states, 0)
    back_own[PAIRS] = low_cast(zcol[...])
    exchange_start(1, back_own, back_in)
    reduce_some(3)

    for g in range(GROUPS + 1, GATHERS - 2):
        g_sent(g)
    turned[...] = hid_low[...].T
    for j in range(TILES):
        got = low_cast(mm(turned[...], gel[:, j * D : (j + 1) * D]))
        w_up[j] = got.reshape(2, 2, 2, rows, D)
        reduce_start(UP + j)
    reduce_some(3)
    g_sent(GROUPS)
    w_out[...] = low_cast(mm_rows(heads[...], one_low[...])).reshape(2, 2, 2, rows, D)
    reduce_start(OUT)
    reduce_some(2)

    def sigmoid(v):
        e = jnp.exp(-jnp.abs(v))
        return jnp.where(v >= 0, 1.0, e) / (1.0 + e)

    def fold(value):
        value = value * cs_ref[...]
        return value + swap_halves(value)

    def through_features(p, part, left, right):
        value = mixed[slab(p, part)].astype(jnp.float32)
        d_part = sigmoid(value) * jnp.where(half_lane < HD, fold(left), fold(right))
        mixed[slab(p, part)] = low_cast(d_part)
        vg_ref[6 + part : 7 + part, pair_cols(p)] = row_sum(d_part)

    def query_back(p, carry):
        got = []
        for side in (0, 1):
            h = 2 * p + side
            ga = act[grad_slot(h)]
            d_scores = low_cast(mm_cols(ga, val_a[h]) * mask[...])
            got.append(mm(d_scores, feat_k[h]) + mm_cols(ga * keeps[2], state_h[h]))
        through_features(p, 0, got[0], got[1])
        return carry

    for part in range(3):
        lax.fori_loop(2 * part, 2 * part + 2, query_back, 0)
        reduce_some(2)

    exchange_end(1, back_own, back_in, backward_weight, back_h, 1)

    def key_value_back(p, carry):
        keys, values = [], []
        for side in (0, 1):
            h = 2 * p + side
            fq, fk, va, ga = feat_q[h], feat_k[h], val_a[h], act[grad_slot(h)]
            d_scores_t = low_cast(mm_cols(va, ga) * mask_t[...])
            keys.append(mm(d_scores_t, fq) + mm_cols(va * keeps[3], back_h[h]))
            scores_t = low_cast(mm_cols(fk, fq) * mask_t[...])
            values.append(mm(scores_t, ga) + mm(fk * keeps[3], back_h[h]))
        through_features(p, 1, keys[0], keys[1])
        d_part = join(values[0], values[1])
        mixed[slab(p, 2)] = low_cast(d_part)
        vg_ref[8:9, pair_cols(p)] = row_sum(d_part)
        return carry

    turned[...] = tok[...].T
    for g in range(GROUPS):
        lax.fori_loop(2 * g, 2 * g + 2, key_value_back, 0)
        ig_ref[...] += mm_cols(mixed[g], w_qkv[g].reshape(D, D))
        g_sent(g)
        w_qkv[g] = low_cast(mm(turned[...], mixed[g])).reshape(2, 2, 2, rows, D)
        reduce_start(MIX + g)
        reduce_some(4)

    def vcopy(level):
        target = (sib, xn, yn, z_one, z_two)[level]
        return remote(vg_ref, vec_land.at[level], v_send.at[level], v_recv.at[level], target)

    vg_ref[13:16, :] = jnp.zeros((3, D), jnp.float32)
    vcopy(0).start()
    for level in range(5):
        reduce_some(3)
        vcopy(level).wait()
        vg_ref[...] += vec_land[level]
        if level < 4:
            vcopy(level + 1).start()
    reduce_some(len(r_plan))
    for k in range(UNITS):
        r_end(k)
    exchange_sent(0, state_own, state_in)
    exchange_sent(1, back_own, back_in)


GATHER_AHEAD = 3


def fits(mesh):
    return mesh.shape["dp"] == 8 and mesh.shape["head"] == 4


def fused_layer(lengths, tokens, cotangent, masters, vector_master):
    n_head = lax.axis_size("head")
    T = tokens.shape[0]
    rows = masters[1].shape[0]
    bf, f32 = jnp.bfloat16, jnp.float32
    V, S = pltpu.VMEM, jax.ShapeDtypeStruct
    vm, anywhere = pl.BlockSpec(memory_space=pltpu.VMEM), pl.BlockSpec(memory_space=pl.ANY)
    out_shape = (S((T, D), bf), S((T, D), f32)) + tuple(S(m.shape, bf) for m in masters)
    out_shape += (S((16, D), f32),)
    shard = (2, 2, 2, rows, D)
    scratch = [
        V((GROUPS, *shard), bf),
        V(shard, bf),
        V((TILES, *shard), bf),
        V((2, 2, 2, TILES * rows, D), bf),
        V((T, D), bf),
        V((GROUPS, T, D), bf),
        V((H, T, LANES), bf),
        V((H, T, LANES), bf),
        V((H, T, LANES), bf),
        V((H, T, LANES), f32),
        V((T, D), bf),
        V((T, D), f32),
        V((T, LANES), f32),
        V((T, D), f32),
        V((T, D), bf),
        V((D, T), bf),
        V((T, FF), bf),
        V((T, FF), bf),
        V((T, D), bf),
        V((T, D), bf),
        V((T, T), f32),
        V((T, T), f32),
        V((T, LANES), f32),
        V((T, LANES), f32),
        V((4, T, LANES), bf),
        V((SLABS, LANES, LANES), bf),
        V((n_head - 1, SLABS, LANES, LANES), bf),
        V((SLABS, LANES, LANES), bf),
        V((n_head - 1, SLABS, LANES, LANES), bf),
        V((SLABS, LANES, LANES), f32),
        V((H, LANES, LANES), bf),
        V((H, LANES, LANES), bf),
        V((LANES, LANES), f32),
        V((UNITS, 2, 2, rows, D), bf),
        V((UNITS, 2, 2, rows // 2, D), bf),
        V((UNITS, 2, rows // 2, D), bf),
        V((UNITS, 2, rows // 2, D), bf),
        V((5, 16, D), f32),
        pltpu.SemaphoreType.DMA((18,)),
        pltpu.SemaphoreType.DMA((8, 13)),
        pltpu.SemaphoreType.DMA((8, 13)),
        pltpu.SemaphoreType.DMA((2, n_head)),
        pltpu.SemaphoreType.DMA((2, n_head)),
        pltpu.SemaphoreType.DMA((UNITS, 13)),
        pltpu.SemaphoreType.DMA((UNITS, 13)),
        pltpu.SemaphoreType.DMA((5,)),
        pltpu.SemaphoreType.DMA((5,)),
    ]
    return pl.pallas_call(
        functools.partial(layer_kernel, n_head, lengths.shape[0]),
        out_shape=out_shape,
        in_specs=[pl.BlockSpec(memory_space=pltpu.SMEM)] + [anywhere] * 6 + [vm],
        out_specs=[anywhere, vm] + [anywhere] * 4 + [vm],
        scratch_shapes=scratch,
        compiler_params=pltpu.CompilerParams(
            collective_id=0, has_side_effects=True, vmem_limit_bytes=VMEM_BYTES
        ),
        name="layer",
    )(lengths, tokens, cotangent, *masters, vector_master)


VMEM_BYTES = 63 * 1024 * 1024


def fused_shards(
    tokens,
    cotangent,
    lengths,
    qkv_master,
    out_master,
    up_master,
    down_master,
    vector_master,
    qkv_first,
    qkv_second,
    out_first,
    out_second,
    up_first,
    up_second,
    down_first,
    down_second,
    vector_first,
    vector_second,
):
    masters = (qkv_master, out_master, up_master, down_master)
    output, input_grad, *grads, vector_grad = fused_layer(
        lengths, tokens, cotangent, masters, vector_master
    )
    rates = (1.0 / math.sqrt(D), 1.0 / math.sqrt(OUT_FAN), 1.0 / math.sqrt(D), 1.0 / math.sqrt(FF))
    firsts = (qkv_first, out_first, up_first, down_first)
    seconds = (qkv_second, out_second, up_second, down_second)
    news = []
    for i in range(4):
        news.extend(
            adam_update(
                masters[i],
                firsts[i],
                seconds[i],
                grads[i].astype(jnp.float32),
                rates[i],
                weight_decay,
            )
        )
    vector_new = adam_update(
        vector_master, vector_first, vector_second, vector_grad[:13], vector_rate, 0.0
    )
    return (output, input_grad, *news, *vector_new)


def solution(mesh):
    return jax.shard_map(
        fused_shards if fits(mesh) else shards,
        mesh=mesh,
        in_specs=(
            P(("dp", "head"), None),
            P(("dp", "head"), None),
            P("dp"),
            P("dp", None),
            P("dp", None),
            P("dp", None),
            P("dp", None),
            P(),
            P("dp", None),
            P("dp", None),
            P("dp", None),
            P("dp", None),
            P("dp", None),
            P("dp", None),
            P("dp", None),
            P("dp", None),
            P(),
            P(),
        ),
        out_specs=(
            P(("dp", "head"), None),
            P(("dp", "head"), None),
            P("dp", None),
            P("dp", None),
            P("dp", None),
            P("dp", None),
            P("dp", None),
            P("dp", None),
            P("dp", None),
            P("dp", None),
            P("dp", None),
            P("dp", None),
            P("dp", None),
            P("dp", None),
            P(),
            P(),
            P(),
        ),
        check_vma=False,
    )
```

```python
import functools
import math

import jax
import jax.numpy as jnp
from jax import lax
from jax.experimental import pallas as pl
from jax.experimental.pallas import tpu as pltpu
from jax.sharding import PartitionSpec as P

D = 768
H = 12
HD = 64
FF = 3072
SPAN = 64
STEP = 10
OUT_FAN = 1


highest = lax.Precision.HIGHEST
norm_epsilon = 1e-05
first_decay = 0.9
second_decay = 0.999
adam_epsilon = 1e-08
weight_decay = 0.01
vector_rate = 0.2


def layer_norm(residual, gain_row, shift_row):
    center = residual - jnp.mean(residual, axis=-1, keepdims=True)
    spread = jnp.mean(center * center, axis=-1, keepdims=True)
    return center * lax.rsqrt(spread + norm_epsilon) * gain_row + shift_row


def exact_gelu(upper_pre):
    return jax.nn.gelu(upper_pre, approximate=False)


def group_layout(group_lengths, row_count):
    slot_sizes = (group_lengths + SPAN - 1) // SPAN * SPAN
    slot_ends = jnp.cumsum(slot_sizes)
    slot_starts = slot_ends - slot_sizes
    positions = jnp.arange(row_count, dtype=jnp.int32)
    member = (positions[:, None] >= slot_starts[None, :]) & (
        positions[:, None] < slot_ends[None, :]
    )
    seq_first = jnp.sum(jnp.where(member, slot_starts[None, :], 0), axis=1)
    length = jnp.sum(jnp.where(member, group_lengths[None, :], 0), axis=1)
    seq_numbers = jnp.arange(group_lengths.shape[0], dtype=jnp.int32)
    owners = jnp.sum(jnp.where(member, seq_numbers[None, :], 0), axis=1)
    offset = positions - seq_first
    live_rows = (offset < length).astype(jnp.float32)
    angles = 0.5 * math.pi * offset.astype(jnp.float32) / length.astype(jnp.float32)
    cosine = jnp.cos(angles)
    sine_part = jnp.sin(angles)
    span_owner = owners[::SPAN]
    span_order = jnp.arange(span_owner.shape[0], dtype=jnp.int32)
    same_seq = span_owner[None, :] == span_owner[:, None]
    earlier = (same_seq & (span_order[None, :] < span_order[:, None])).astype(jnp.float32)
    return (cosine, sine_part, live_rows, earlier)


def attend(query_rows, key_rows, value_rows, cosine, sine_part, live_rows, earlier):
    row_count = query_rows.shape[0]
    blocks = row_count // SPAN
    soft_query = jax.nn.softplus(query_rows)
    soft_key = jax.nn.softplus(key_rows)
    feat_query = (
        jnp.concatenate([soft_query * cosine[:, None], soft_query * sine_part[:, None]], axis=1)
        * live_rows[:, None]
    )
    feat_key = (
        jnp.concatenate([soft_key * cosine[:, None], soft_key * sine_part[:, None]], axis=1)
        * live_rows[:, None]
    )
    block_query = feat_query.reshape(blocks, SPAN, -1)
    block_key = feat_key.reshape(blocks, SPAN, -1)
    block_value = value_rows.reshape(blocks, SPAN, -1)
    lower_mask = (jnp.arange(SPAN)[:, None] >= jnp.arange(SPAN)[None, :]).astype(jnp.float32)
    scores = jnp.einsum("cik,cjk->cij", block_query, block_key, precision=highest) * lower_mask
    inner_sum = jnp.einsum("cij,cjd->cid", scores, block_value, precision=highest)
    inner_den = jnp.sum(scores, axis=2)
    states = jnp.einsum("cjk,cjd->ckd", block_key, block_value, precision=highest)
    key_sums = jnp.sum(block_key, axis=1)
    before = jnp.einsum("ce,ekd->ckd", earlier, states, precision=highest)
    before_sums = jnp.einsum("ce,ek->ck", earlier, key_sums, precision=highest)
    outer_sum = jnp.einsum("cik,ckd->cid", block_query, before, precision=highest)
    outer_den = jnp.einsum("cik,ck->ci", block_query, before_sums, precision=highest)
    numerator = (inner_sum + outer_sum).reshape(row_count, -1)
    denominator = (inner_den + outer_den).reshape(row_count) + (1.0 - live_rows)
    return numerator / denominator[:, None]


def contract_rows(left, right):
    return lax.dot_general(
        left, right, (((0,), (0,)), ((), ())), preferred_element_type=jnp.float32
    )


def contract_cols(left, right):
    return lax.dot_general(
        left, right, (((1,), (1,)), ((), ())), preferred_element_type=jnp.float32
    )


def adam_update(master, first, second, gradient, rate, decay):
    first_new = first_decay * first + (1.0 - first_decay) * gradient
    second_new = second_decay * second + (1.0 - second_decay) * gradient * gradient
    first_hat = first_new / (1.0 - first_decay**STEP)
    second_hat = second_new / (1.0 - second_decay**STEP)
    master_new = master - rate * (
        first_hat / (jnp.sqrt(second_hat) + adam_epsilon) + decay * master
    )
    return (first_new, second_new, master_new)


def shards(
    tokens,
    cotangent,
    lengths,
    qkv_master,
    out_master,
    up_master,
    down_master,
    vector_master,
    qkv_first,
    qkv_second,
    out_first,
    out_second,
    up_first,
    up_second,
    down_first,
    down_second,
    vector_first,
    vector_second,
):
    mix_weight, out_weight, up_weight, down_weight = (
        lax.all_gather(qkv_master.astype(jnp.bfloat16), "dp", axis=0, tiled=True),
        lax.all_gather(out_master.astype(jnp.bfloat16), "dp", axis=0, tiled=True),
        lax.all_gather(up_master.astype(jnp.bfloat16), "dp", axis=0, tiled=True),
        lax.all_gather(down_master.astype(jnp.bfloat16), "dp", axis=0, tiled=True),
    )
    tok_count = tokens.shape[0]
    width = tokens.shape[1]
    mixed_all = jnp.dot(tokens, mix_weight, preferred_element_type=jnp.float32) + vector_master[
        6:9
    ].reshape(-1)
    mixed_low = mixed_all.astype(jnp.bfloat16)
    query_part = mixed_low[:, :width].reshape(tok_count, H, 1, HD)
    key_part = mixed_low[:, width : 2 * width].reshape(tok_count, H, 1, HD)
    paired = jnp.concatenate([query_part, key_part], axis=2)
    paired = jnp.repeat(paired[:, :, None], 2, axis=2).reshape(tok_count, 4 * width)
    value_part = mixed_low[:, 2 * width :]
    paired_in, values_in = (
        lax.all_to_all(paired, "head", split_axis=1, concat_axis=0, tiled=True),
        lax.all_to_all(value_part, "head", split_axis=1, concat_axis=0, tiled=True),
    )
    group_rows = paired_in.shape[0]
    item_count = paired_in.shape[1] // (2 * HD)
    cosine, sine_part, live_rows, earlier = group_layout(lengths, group_rows)
    stacked = paired_in.reshape(group_rows, item_count, 2, HD).astype(jnp.float32)
    query_items = stacked[:, :, 0]
    key_items = stacked[:, :, 1]
    value_items = values_in.reshape(group_rows, item_count, HD // 2).astype(jnp.float32)

    def mix_items(query_set, key_set, value_set):

        def single(query_rows, key_rows, value_rows):
            return attend(query_rows, key_rows, value_rows, cosine, sine_part, live_rows, earlier)

        return jax.vmap(single, in_axes=1, out_axes=1)(query_set, key_set, value_set)

    attended, mix_back = jax.vjp(mix_items, query_items, key_items, value_items)
    heads_out = attended.reshape(group_rows, item_count * (HD // 2)).astype(jnp.bfloat16)
    heads = lax.all_to_all(heads_out, "head", split_axis=0, concat_axis=1, tiled=True)
    projected = jnp.dot(heads, out_weight, preferred_element_type=jnp.float32) + vector_master[4]
    resid_one = tokens.astype(jnp.float32) + projected
    hidden, norm_one_back = jax.vjp(layer_norm, resid_one, vector_master[0], vector_master[1])
    hidden_low = hidden.astype(jnp.bfloat16)
    upper_pre = jnp.dot(hidden_low, up_weight, preferred_element_type=jnp.float32) + vector_master[
        9:13
    ].reshape(-1)
    active, gelu_back = jax.vjp(exact_gelu, upper_pre)
    active_low = active.astype(jnp.bfloat16)
    lowered = (
        jnp.dot(active_low, down_weight, preferred_element_type=jnp.float32) + vector_master[5]
    )
    output, norm_two_back = jax.vjp(
        layer_norm, hidden + lowered, vector_master[2], vector_master[3]
    )
    grad_two, gain_two, shift_two = norm_two_back(cotangent)
    grad_two_low = grad_two.astype(jnp.bfloat16)
    down_grad = contract_rows(active_low, grad_two_low)
    (upper_grad,) = gelu_back(contract_cols(grad_two_low, down_weight))
    upper_low = upper_grad.astype(jnp.bfloat16)
    up_grad = contract_rows(hidden_low, upper_low)
    hidden_grad = grad_two + contract_cols(upper_low, up_weight)
    grad_one, gain_one, shift_one = norm_one_back(hidden_grad)
    grad_one_low = grad_one.astype(jnp.bfloat16)
    out_grad = contract_rows(heads, grad_one_low)
    heads_grad = contract_cols(grad_one_low, out_weight).astype(jnp.bfloat16)
    heads_back = lax.all_to_all(heads_grad, "head", split_axis=1, concat_axis=0, tiled=True)
    query_back, key_back, value_back = mix_back(
        heads_back.reshape(group_rows, item_count, HD // 2).astype(jnp.float32)
    )
    pair_back = (
        jnp.stack([query_back, key_back], axis=2)
        .astype(jnp.bfloat16)
        .reshape(group_rows, item_count * 2 * HD)
    )
    value_low = value_back.astype(jnp.bfloat16).reshape(group_rows, item_count * (HD // 2))
    pair_home, value_home = (
        lax.all_to_all(pair_back, "head", split_axis=0, concat_axis=1, tiled=True),
        lax.all_to_all(value_low, "head", split_axis=0, concat_axis=1, tiled=True),
    )
    summed = jnp.sum(pair_home.astype(jnp.float32).reshape(tok_count, H, 2, 2, HD), axis=2)
    mixed_grad = jnp.concatenate(
        [
            summed[:, :, 0].reshape(tok_count, width),
            summed[:, :, 1].reshape(tok_count, width),
            value_home.astype(jnp.float32),
        ],
        axis=1,
    )
    mixed_low_grad = mixed_grad.astype(jnp.bfloat16)
    mix_grad = contract_rows(tokens, mixed_low_grad)
    input_grad = grad_one + contract_cols(mixed_low_grad, mix_weight)
    vector_grad = jnp.concatenate(
        [
            jnp.stack(
                [
                    gain_one,
                    shift_one,
                    gain_two,
                    shift_two,
                    jnp.sum(grad_one, axis=0),
                    jnp.sum(grad_two, axis=0),
                ]
            ),
            jnp.sum(mixed_grad, axis=0).reshape(3, width),
            jnp.sum(upper_grad, axis=0).reshape(4, width),
        ],
        axis=0,
    )
    local_grads = (mix_grad, out_grad, up_grad, down_grad)
    row_parts = (
        lax.psum_scatter(
            local_grads[0].astype(jnp.bfloat16), "dp", scatter_dimension=0, tiled=True
        ).astype(jnp.float32),
        lax.psum_scatter(
            local_grads[1].astype(jnp.bfloat16), "dp", scatter_dimension=0, tiled=True
        ).astype(jnp.float32),
        lax.psum_scatter(
            local_grads[2].astype(jnp.bfloat16), "dp", scatter_dimension=0, tiled=True
        ).astype(jnp.float32),
        lax.psum_scatter(
            local_grads[3].astype(jnp.bfloat16), "dp", scatter_dimension=0, tiled=True
        ).astype(jnp.float32),
    )
    reduced = (
        lax.psum(row_parts[0].astype(jnp.bfloat16), "head").astype(jnp.float32),
        lax.psum(row_parts[1].astype(jnp.bfloat16), "head").astype(jnp.float32),
        lax.psum(row_parts[2].astype(jnp.bfloat16), "head").astype(jnp.float32),
        lax.psum(row_parts[3].astype(jnp.bfloat16), "head").astype(jnp.float32),
    )
    vector_total = lax.psum(vector_grad, ("dp", "head"))
    qkv_new = adam_update(
        qkv_master, qkv_first, qkv_second, reduced[0], 1.0 / math.sqrt(D), weight_decay
    )
    out_new = adam_update(
        out_master, out_first, out_second, reduced[1], 1.0 / math.sqrt(OUT_FAN), weight_decay
    )
    up_new = adam_update(
        up_master, up_first, up_second, reduced[2], 1.0 / math.sqrt(D), weight_decay
    )
    down_new = adam_update(
        down_master, down_first, down_second, reduced[3], 1.0 / math.sqrt(FF), weight_decay
    )
    vector_new = adam_update(
        vector_master, vector_first, vector_second, vector_total, vector_rate, 0.0
    )
    return (
        output.astype(jnp.bfloat16),
        input_grad,
        qkv_new[0],
        qkv_new[1],
        qkv_new[2],
        out_new[0],
        out_new[1],
        out_new[2],
        up_new[0],
        up_new[1],
        up_new[2],
        down_new[0],
        down_new[1],
        down_new[2],
        vector_new[0],
        vector_new[1],
        vector_new[2],
    )


PAIRS = H // 2
LANES = 2 * HD
SLABS = PAIRS + 1
GROUPS = 3
WIDE = D // GROUPS
TILES = FF // D
ROW_TILE = 128
MESH = pl.DeviceIdType.MESH
DOWN, UP, OUT, MIX = 0, TILES, 2 * TILES, 2 * TILES + 1
UNITS = 2 * TILES + 1 + GROUPS


def mm(left, right):
    return jnp.dot(left, right, preferred_element_type=jnp.float32)


def mm_cols(left, right):
    return lax.dot_general(
        left, right, (((1,), (1,)), ((), ())), preferred_element_type=jnp.float32
    )


def mm_rows(left, right):
    return lax.dot_general(
        left, right, (((0,), (0,)), ((), ())), preferred_element_type=jnp.float32
    )


def swap_halves(slab):
    return pltpu.roll(slab, HD, 1)


def low_cast(value):
    return value.astype(jnp.bfloat16)


def row_sum(value):
    return jnp.sum(value, axis=0, keepdims=True)


def gelu_parts(z):
    x = jnp.abs(z) * (1.0 / math.sqrt(2.0))
    t = 1.0 / (1.0 + 0.3275911 * x)
    bell = jnp.exp(-0.5 * z * z)
    poly = t * (
        0.254829592
        + t * (-0.284496736 + t * (1.421413741 + t * (-1.453152027 + t * 1.061405429)))
    )
    upper_tail = 0.5 * poly * bell
    phi = jnp.where(z >= 0, 1.0 - upper_tail, upper_tail)
    return z * phi, phi + z * (bell * (1.0 / math.sqrt(2.0 * math.pi)))


def norm_rows(residual):
    center = residual - jnp.mean(residual, axis=-1, keepdims=True)
    rstd = lax.rsqrt(jnp.mean(center * center, axis=-1, keepdims=True) + norm_epsilon)
    return center * rstd, rstd


def norm_rows_back(dy, normed, rstd, gain):
    e = dy * gain
    return rstd * (
        e
        - jnp.mean(e, axis=-1, keepdims=True)
        - normed * jnp.mean(e * normed, axis=-1, keepdims=True)
    )


def layer_kernel(
    n_head,
    n_seq,
    lens_ref,
    tok_hbm,
    cot_hbm,
    qkv_f,
    out_f,
    up_f,
    down_f,
    vec_ref,
    y_hbm,
    ig_ref,
    g_qkv,
    g_out,
    g_up,
    g_down,
    vg_ref,
    w_qkv,
    w_out,
    w_up,
    w_down,
    tok,
    mixed,
    feat_q,
    feat_k,
    val_a,
    num_a,
    heads,
    norm_one,
    rstd_one,
    hid,
    hid_low,
    turned,
    act,
    gel,
    two_low,
    one_low,
    mask,
    mask_t,
    cs_ref,
    live_ref,
    keeps,
    state_own,
    state_in,
    back_own,
    back_in,
    state_sum,
    state_h,
    back_h,
    zcol,
    red_a,
    red_b,
    red_c,
    red_e,
    vec_land,
    load_sem,
    g_send,
    g_recv,
    s_send,
    s_recv,
    r_send,
    r_recv,
    v_send,
    v_recv,
):
    T = tok.shape[0]
    rows = w_out.shape[3]
    half = rows // 2
    dp = lax.axis_index("dp")
    z = lax.axis_index("head")
    core = dp % 2
    xx = (dp // 2) % 2
    yy = dp // 4
    color = z % 2
    sib = (dp + 1 - 2 * core, z)
    xn = (dp + 2 - 4 * xx, z)
    yn = (dp + 4 - 8 * yy, z)
    z_one = (dp, z + 1 - 2 * color)
    z_two = (dp, (z + 3 + 2 * color) % n_head)

    def load(i, src, dst):
        return pltpu.make_async_copy(src, dst, load_sem.at[i])

    def spot(ref, i):
        return ref.at[pl.ds(i * rows, rows), :]

    loads = []
    for g in range(GROUPS):
        for part in range(3):
            loads.append(
                load(
                    len(loads),
                    qkv_f.at[:, pl.ds(part * D + g * WIDE, WIDE)],
                    hid.at[pl.ds(g * rows, rows), pl.ds(part * WIDE, WIDE)],
                )
            )
    loads.append(load(len(loads), out_f, spot(hid, GROUPS)))
    for j in range(TILES):
        loads.append(load(len(loads), up_f.at[:, pl.ds(j * D, D)], spot(norm_one, j)))
    loads.append(load(len(loads), down_f, ig_ref.at[pl.ds(0, TILES * rows), :]))
    load_tok = load(len(loads), tok_hbm, tok)
    load_cot = load(len(loads) + 1, cot_hbm, ig_ref)
    save_y = load(len(loads) + 2, one_low, y_hbm)
    for copy in loads:
        copy.start()
    load_tok.start()

    barrier = pltpu.get_barrier_semaphore()
    peers = [sib, xn, yn]
    for k in range(1, n_head):
        peers.append((dp, (z + k) % n_head))
    for peer in peers:
        pl.semaphore_signal(barrier, inc=1, device_id=peer, device_id_type=MESH)

    def remote(src, dst, send, recv, target):
        return pltpu.make_async_remote_copy(
            src_ref=src,
            dst_ref=dst,
            send_sem=send,
            recv_sem=recv,
            device_id=target,
            device_id_type=MESH,
        )

    GATHERS = GROUPS + 1 + TILES // 2 + 2

    def piece(g, y, x, c, which):
        if g < GROUPS:
            ref, size, base = w_qkv.at[g, y, x, c], rows, 0
        elif g == GROUPS:
            ref, size, base = w_out.at[y, x, c], rows, 0
        elif g < GROUPS + 1 + TILES // 2:
            i = g - GROUPS - 1
            if which is None:
                return w_up.at[pl.ds(2 * i, 2), y, x, c]
            return w_up.at[
                pl.ds(2 * i, 2), y, x, c, pl.ds(pl.multiple_of(which * half, half), half), :
            ]
        else:
            i = g - GROUPS - 1 - TILES // 2
            ref, size, base = w_down.at[y, x, c], 2 * rows, 2 * rows * i
        if which is None:
            return ref.at[pl.ds(base, size), :]
        return ref.at[pl.ds(pl.multiple_of(base + which * (size // 2), size // 2), size // 2), :]

    def own_masters(g):
        if g < GROUPS:
            for part in range(3):
                loads[3 * g + part].wait()
            w_qkv[g, yy, xx, core] = low_cast(hid[g * rows : (g + 1) * rows, :])
        elif g == GROUPS:
            loads[9].wait()
            w_out[yy, xx, core] = low_cast(hid[g * rows : (g + 1) * rows, :])
        elif g < GROUPS + 1 + TILES // 2:
            for j in range(2 * (g - GROUPS - 1), 2 * (g - GROUPS)):
                loads[10 + j].wait()
                w_up[j, yy, xx, core] = low_cast(norm_one[j * rows : (j + 1) * rows, :])
        else:
            i = g - GROUPS - 1 - TILES // 2
            if i == 0:
                loads[10 + TILES].wait()
            span = slice(2 * rows * i, 2 * rows * (i + 1))
            w_down[yy, xx, core, span, :] = low_cast(ig_ref[span, :])

    here, mine_x, mine_y, mine_d = (yy, xx), (yy, 1 - xx), (1 - yy, xx), (1 - yy, 1 - xx)

    def gcopy(g, kind, chip, which, target, lands):
        ref = piece(g, chip[0], chip[1], core, which)
        return remote(ref, ref, g_send.at[g, kind], g_recv.at[g, lands], target)

    def landed(g, chip, which, lands):
        gcopy(g, 0, chip, which, sib, lands).wait_recv()

    blocks = ((mine_x, 0), (mine_x, 1), (mine_y, 0), (mine_y, 1), (mine_d, 0), (mine_d, 1))

    def hand_over(g, lands):
        chip, which = blocks[lands]
        gcopy(g, 10 + lands, chip, which, sib, 7 + lands).start()

    def arrived(g, lands):
        chip, which = blocks[lands]
        landed(g, chip, which, lands)

    def g_start(g):
        gcopy(g, 0, here, 0, xn, 0).start()
        gcopy(g, 1, here, 1, yn, 3).start()

        @pl.when(color == 0)
        def _():
            gcopy(g, 2, here, 1, xn, 1).start()
            gcopy(g, 3, here, 0, yn, 2).start()

        gcopy(g, 9, here, None, sib, 6).start()

    def g_own(g):
        own_masters(g)
        g_start(g)

    def g_first(g):
        arrived(g, 0)

        @pl.when(color == 1)
        def _():
            gcopy(g, 4, mine_x, 0, yn, 4).start()

        arrived(g, 3)

        @pl.when(color == 1)
        def _():
            gcopy(g, 5, mine_y, 1, xn, 5).start()

        hand_over(g, 0)
        hand_over(g, 3)

        @pl.when(color == 0)
        def _():
            arrived(g, 1)
            gcopy(g, 6, mine_x, 1, z_one, 1).start()
            arrived(g, 2)
            gcopy(g, 7, mine_y, 0, z_one, 2).start()
            hand_over(g, 1)
            hand_over(g, 2)

    def g_second(g):
        @pl.when(color == 1)
        def _():
            arrived(g, 4)
            gcopy(g, 8, mine_d, 0, z_one, 4).start()
            arrived(g, 5)
            gcopy(g, 16, mine_d, 1, z_one, 5).start()
            hand_over(g, 4)
            hand_over(g, 5)
            arrived(g, 1)
            hand_over(g, 1)
            arrived(g, 2)
            hand_over(g, 2)

    def g_third(g):
        @pl.when(color == 0)
        def _():
            arrived(g, 4)
            hand_over(g, 4)
            arrived(g, 5)
            hand_over(g, 5)

    def g_last(g):
        landed(g, here, None, 6)
        for lands in range(6):
            chip, which = blocks[lands]
            landed(g, chip, which, 7 + lands)

    def g_sent(g):
        def sent(kind, chip, which):
            gcopy(g, kind, chip, which, sib, 0).wait_send()

        sent(0, here, 0)
        sent(1, here, 1)
        sent(9, here, None)
        for lands in range(6):
            sent(10 + lands, *blocks[lands])

        @pl.when(color == 0)
        def _():
            sent(2, here, 1)
            sent(3, here, 0)
            sent(6, mine_x, 1)
            sent(7, mine_y, 0)

        @pl.when(color == 1)
        def _():
            sent(4, mine_x, 0)
            sent(5, mine_y, 1)
            sent(8, mine_d, 0)
            sent(16, mine_d, 1)

    plan = []
    for step in range(GATHERS + 2):
        acts = [(f, step - lag) for f, lag in ((g_third, 2), (g_second, 1), (g_first, 0))]
        acts = [(f, g) for f, g in acts if 0 <= g < GATHERS]
        if step + GATHER_AHEAD < GATHERS:
            acts.append((g_own, step + GATHER_AHEAD))
        plan.append(acts)

    def gather_step():
        if plan:
            for act_of, g in plan.pop(0):
                act_of(g)

    def gather_until(g):
        while any((g_third, g) in acts for acts in plan):
            gather_step()
        g_last(g)

    def unit_ref(k):
        if k < UP:
            return w_down.at[:, :, :, pl.ds(k * rows, rows), :]
        if k < OUT:
            return w_up.at[k - UP]
        if k < MIX:
            return w_out
        return w_qkv.at[k - MIX]

    middle = (z > 0) & (z < n_head - 1)
    top, low_part = pl.ds(0, half), pl.ds(half, half)

    def finals(k):
        if k < UP:
            return [(None, g_down.at[pl.ds(k * rows, rows), :])]
        if k < OUT:
            return [(None, g_up.at[:, pl.ds((k - UP) * D, D)])]
        if k < MIX:
            return [(None, g_out)]
        return [
            (part * WIDE, g_qkv.at[:, pl.ds(part * D + (k - MIX) * WIDE, WIDE)])
            for part in range(3)
        ]

    def r_final(k, i):
        mine = red_a.at[k, yy, xx]
        col, dst = finals(k)[i]
        return mine if col is None else mine.at[:, pl.ds(col, WIDE)], dst

    def r_copy(k, kind):
        mine = red_a.at[k, yy, xx]
        if kind == 0:
            src, dst, target = unit_ref(k).at[:, :, 1 - core], red_a.at[k], sib
        elif kind == 1:
            src, dst, target = red_a.at[k, :, 1 - xx, top, :], red_b.at[k, 0], xn
        elif kind == 2:
            src, dst, target = red_a.at[k, 1 - yy, :, low_part, :], red_b.at[k, 1], yn
        elif kind == 3:
            src, dst, target = red_a.at[k, 1 - yy, xx, top, :], red_c.at[k, 0], yn
        elif kind == 4:
            src, dst, target = red_a.at[k, yy, 1 - xx, low_part, :], red_c.at[k, 1], xn
        elif kind == 5:
            src, dst, target = mine, red_e.at[k, 0], z_one
        elif kind == 6:
            src, dst, target = mine, red_e.at[k, 1], z_two
        else:
            src, dst = r_final(k, kind - 7)
            target = z_one
        return remote(src, dst, r_send.at[k, kind], r_recv.at[k, kind], target)

    def r_local(k, i):
        src, dst = r_final(k, i)
        return pltpu.make_async_copy(src, dst, r_recv.at[k, 10 + i])

    def added(one, two):
        return low_cast(one.astype(jnp.float32) + two.astype(jnp.float32))

    def r_start(k):
        r_copy(k, 0).start()

    def r_pair(k):
        r_copy(k, 0).wait_recv()
        for y in range(2):
            for x in range(2):
                mine = unit_ref(k)[y, x, core] if k >= UP else None
                if k < UP:
                    mine = w_down[y, x, core, k * rows : (k + 1) * rows, :]
                red_a[k, y, x] = added(mine, red_a[k, y, x])
        r_copy(k, 1).start()
        r_copy(k, 2).start()

    def r_plane(k):
        r_copy(k, 1).wait_recv()
        red_a[k, 1 - yy, xx, top, :] = added(red_a[k, 1 - yy, xx, top, :], red_b[k, 0, 1 - yy])
        r_copy(k, 3).start()
        r_copy(k, 2).wait_recv()
        red_a[k, yy, 1 - xx, low_part, :] = added(
            red_a[k, yy, 1 - xx, low_part, :], red_b[k, 1, 1 - xx]
        )
        r_copy(k, 4).start()
        red_a[k, yy, xx, top, :] = added(red_a[k, yy, xx, top, :], red_b[k, 0, yy])
        red_a[k, yy, xx, low_part, :] = added(red_a[k, yy, xx, low_part, :], red_b[k, 1, xx])

    def r_whole(k):
        r_copy(k, 3).wait_recv()
        r_copy(k, 4).wait_recv()
        red_a[k, yy, xx, top, :] = added(red_a[k, yy, xx, top, :], red_c[k, 0])
        red_a[k, yy, xx, low_part, :] = added(red_a[k, yy, xx, low_part, :], red_c[k, 1])

        @pl.when(~middle)
        def _():
            r_copy(k, 5).start()

    def r_z_first(k):
        @pl.when(middle)
        def _():
            r_copy(k, 5).wait_recv()
            red_a[k, yy, xx] = added(red_a[k, yy, xx], red_e[k, 0])
            r_copy(k, 6).start()

    def r_z_second(k):
        @pl.when(middle)
        def _():
            r_copy(k, 6).wait()
            red_a[k, yy, xx] = added(red_a[k, yy, xx], red_e[k, 1])
            for i in range(len(finals(k))):
                r_copy(k, 7 + i).start()
                r_local(k, i).start()

    def r_end(k):
        for kind in range(5):
            r_copy(k, kind).wait_send()

        @pl.when(middle)
        def _():
            for i in range(len(finals(k))):
                r_copy(k, 7 + i).wait_send()
                r_local(k, i).wait()

        @pl.when(~middle)
        def _():
            r_copy(k, 5).wait_send()
            for i in range(len(finals(k))):
                r_copy(k, 7 + i).wait_recv()

    stages = (r_pair, r_plane, r_whole, r_z_first, r_z_second)
    r_plan = []
    for tick in range(UNITS + len(stages)):
        for stage in reversed(range(len(stages))):
            if 0 <= tick - stage < UNITS:
                r_plan.append((stages[stage], tick - stage))
    started = []

    def reduce_start(k):
        r_start(k)
        started.append(k)

    def reduce_some(count):
        while r_plan and count > 0 and r_plan[0][1] in started:
            act_of, k = r_plan.pop(0)
            act_of(k)
            count -= 1

    for g in range(min(GATHER_AHEAD, GATHERS)):
        own_masters(g)
    pl.semaphore_wait(barrier, len(peers))
    for g in range(min(GATHER_AHEAD, GATHERS)):
        g_start(g)

    lens = [lens_ref[s] for s in range(n_seq)]
    ends = []
    total = 0
    for s in range(n_seq):
        total = total + ((lens[s] + (SPAN - 1)) // SPAN) * SPAN
        ends.append(total)
    starts = [0] + ends[:-1]

    def owner_of(row):
        found = jnp.zeros_like(row)
        for s in range(n_seq):
            found = found + (row >= ends[s]).astype(jnp.int32)
        return found

    half_lane = lax.broadcasted_iota(jnp.int32, (T, LANES), 1)
    row = z * T + lax.broadcasted_iota(jnp.int32, (T, LANES), 0)
    first = jnp.zeros_like(row)
    length = jnp.ones_like(row)
    for s in range(n_seq):
        inside = (row >= starts[s]) & (row < ends[s])
        first = jnp.where(inside, starts[s], first)
        length = jnp.where(inside, lens[s], length)
    offset = row - first
    live = (offset < length).astype(jnp.float32)
    angle = 0.5 * math.pi * offset.astype(jnp.float32) / length.astype(jnp.float32)
    angle = jnp.where(half_lane < HD, angle, 0.5 * math.pi - angle)
    cs_ref[...] = jnp.cos(angle) * live
    live_ref[...] = live
    owners = owner_of(row)
    next_owner = owner_of(jnp.full((1, 1), (z + 1) * T, jnp.int32))
    last_owner = owner_of(jnp.full((1, 1), z * T - 1, jnp.int32))
    my_first = owner_of(jnp.full((1, 1), z * T, jnp.int32))
    my_last = owner_of(jnp.full((1, 1), (z + 1) * T - 1, jnp.int32))
    for i, edge in enumerate((next_owner, last_owner, my_first, my_last)):
        keeps[i] = low_cast((owners == edge).astype(jnp.float32))

    def fill_masks(i, carry):
        r0 = pl.multiple_of(i * ROW_TILE, ROW_TILE)
        t_i = r0 + lax.broadcasted_iota(jnp.int32, (ROW_TILE, T), 0)
        u_i = lax.broadcasted_iota(jnp.int32, (ROW_TILE, T), 1)
        same = owner_of(t_i + z * T) == owner_of(u_i + z * T)
        mask[pl.ds(r0, ROW_TILE), :] = low_cast((same & (u_i <= t_i)).astype(jnp.float32))
        mask_t[pl.ds(r0, ROW_TILE), :] = low_cast((same & (u_i >= t_i)).astype(jnp.float32))
        return carry

    lax.fori_loop(0, T // ROW_TILE, fill_masks, 0)

    sq_lane = lax.broadcasted_iota(jnp.int32, (LANES, LANES), 1)
    ones_lane = ((half_lane == HD) | (half_lane == HD + 1)).astype(jnp.float32)

    def softplus(v):
        return jnp.maximum(v, 0.0) + jnp.log1p(jnp.exp(-jnp.abs(v)))

    def slab(p, part):
        return p // 2, slice(None), pl.ds(pl.multiple_of(part * WIDE + (p % 2) * LANES, LANES), LANES)

    def pair_cols(p):
        return pl.ds(pl.multiple_of(p * LANES, LANES), LANES)

    def split(value):
        swapped = swap_halves(value)
        return jnp.where(half_lane < HD, value, swapped), jnp.where(half_lane < HD, swapped, value)

    def join(left, right):
        return jnp.where(half_lane < HD, left, swap_halves(right))

    def pack_states(p, left, right, own, n_ones):
        own[p] = low_cast(jnp.where(sq_lane < HD, left, swap_halves(right)))
        for side, part in ((0, left), (1, right)):
            column = part[:, HD : HD + 1]
            if n_ones == 2:
                column = column + part[:, HD + 1 : HD + 2]
            zcol[...] = jnp.where(sq_lane == 2 * p + side, column, zcol[...])

    zcol[...] = jnp.zeros_like(zcol)

    def features_of(p, part, store):
        cs = cs_ref[...]
        left, right = split(softplus(mixed[slab(p, part)].astype(jnp.float32)))
        store[2 * p] = low_cast(left * cs)
        store[2 * p + 1] = low_cast(right * cs)

    def make_keys(p, carry):
        features_of(p, 1, feat_k)
        v_pair = mixed[slab(p, 2)].astype(jnp.float32)
        val_a[2 * p] = low_cast(jnp.where(half_lane < HD, v_pair, ones_lane))
        val_a[2 * p + 1] = low_cast(jnp.where(half_lane < HD, swap_halves(v_pair), ones_lane))
        left = mm_rows(feat_k[2 * p] * keeps[0], val_a[2 * p])
        right = mm_rows(feat_k[2 * p + 1] * keeps[0], val_a[2 * p + 1])
        pack_states(p, left, right, state_own, 1)
        return carry

    def make_queries(p, carry):
        features_of(p, 0, feat_q)
        return carry

    load_tok.wait()
    for g in range(GROUPS):
        gather_until(g)
        part = mm(tok[...], w_qkv[g].reshape(D, D))
        mixed[g, :, 0:WIDE] = low_cast(part[:, 0:WIDE] + vec_ref[6:7, g * WIDE : (g + 1) * WIDE])
        mixed[g, :, WIDE : 2 * WIDE] = low_cast(
            part[:, WIDE : 2 * WIDE] + vec_ref[7:8, g * WIDE : (g + 1) * WIDE]
        )
        mixed[g, :, 2 * WIDE :] = low_cast(part[:, 2 * WIDE :])
        lax.fori_loop(2 * g, 2 * g + 2, make_keys, 0)
    state_own[PAIRS] = low_cast(zcol[...])

    def exchange(which, own, landed, k):
        target = (z + k) % n_head if which == 0 else (z + n_head - k) % n_head
        return remote(
            own, landed.at[k - 1], s_send.at[which, k], s_recv.at[which, k], (dp, target)
        )

    def may_send(which, k):
        return z + k < n_head if which == 0 else z >= k

    def may_receive(which, k):
        return z >= k if which == 0 else z + k < n_head

    def exchange_start(which, own, landed):
        for k in range(1, n_head):

            @pl.when(may_send(which, k))
            def _(k=k):
                exchange(which, own, landed, k).start()

    def exchange_sent(which, own, landed):
        for k in range(1, n_head):

            @pl.when(may_send(which, k))
            def _(k=k):
                exchange(which, own, landed, k).wait_send()

    def exchange_end(which, own, landed, weight_of, out, n_ones):
        state_sum[...] = jnp.zeros_like(state_sum)
        for k in range(1, n_head):

            @pl.when(may_receive(which, k))
            def _(k=k):
                exchange(which, own, landed, k).wait_recv()
                weight = weight_of(k).reshape(1, 1, 1)
                state_sum[...] += weight * landed[k - 1].astype(jnp.float32)

        def unpack(p, carry):
            packed = state_sum[p]
            ends_col = state_sum[PAIRS]
            for side in (0, 1):
                column = jnp.sum(
                    jnp.where(sq_lane == 2 * p + side, ends_col, 0.0), axis=1, keepdims=True
                )
                part = packed if side == 0 else swap_halves(packed)
                wide = (sq_lane >= HD) & (sq_lane < HD + n_ones)
                out[2 * p + side] = low_cast(
                    jnp.where(sq_lane < HD, part, jnp.where(wide, column, 0.0))
                )
            return carry

        lax.fori_loop(0, PAIRS, unpack, 0)

    def forward_weight(k):
        edge = owner_of(jnp.full((1, 1), (z - k + 1) * T, jnp.int32))
        return (edge == my_first).astype(jnp.float32)

    def backward_weight(k):
        edge = owner_of(jnp.full((1, 1), (z + k) * T - 1, jnp.int32))
        return (edge == my_last).astype(jnp.float32)

    exchange_start(0, state_own, state_in)

    def local_attend(h, carry):
        scores = low_cast(mm_cols(feat_q[h], feat_k[h])) * mask[...]
        num_a[h] = mm(scores, val_a[h])
        return carry

    gather_step()
    for part in range(3):
        lax.fori_loop(2 * part, 2 * part + 2, make_queries, 0)
        lax.fori_loop(4 * part, 4 * part + 4, local_attend, 0)
        gather_step()

    exchange_end(0, state_own, state_in, forward_weight, state_h, 2)

    def finish_heads(p, carry):
        att = []
        for side in (0, 1):
            h = 2 * p + side
            whole = num_a[h] + mm(feat_q[h] * keeps[2], state_h[h])
            den = whole[:, HD : HD + 1] + (1.0 - live_ref[...])
            inverse = 1.0 / den
            got = whole * inverse
            num_a[h] = jnp.where(half_lane < HD, got, inverse)
            att.append(got)
        shift = vec_ref[8:9, pair_cols(p)]
        heads[:, pair_cols(p)] = low_cast(join(att[0], att[1]) + shift * live_ref[...])
        return carry

    lax.fori_loop(0, PAIRS, finish_heads, 0)

    gather_until(GROUPS)

    def tile_rows(i):
        return pl.ds(pl.multiple_of(i * ROW_TILE, ROW_TILE), ROW_TILE)

    def first_norm(i, carry):
        r = tile_rows(i)
        w = w_out[...].reshape(D, D)
        residual = tok[r, :].astype(jnp.float32) + (mm(heads[r, :], w) + vec_ref[4:5, :])
        normed, rstd = norm_rows(residual)
        norm_one[r, :] = normed
        rstd_one[r, :] = jnp.broadcast_to(rstd, (ROW_TILE, LANES))
        hidden = normed * vec_ref[0:1, :] + vec_ref[1:2, :]
        hid[r, :] = hidden
        hid_low[r, :] = low_cast(hidden)
        return carry

    while any(act_of is g_own for acts in plan for act_of, _ in acts):
        gather_step()
    load_cot.start()
    lax.fori_loop(0, T // ROW_TILE, first_norm, 0)

    for j in range(TILES):
        if j % 2 == 0:
            gather_until(GROUPS + 1 + j // 2)

        def ff_up(i, carry, j=j):
            r = tile_rows(i)
            upper = mm(hid_low[r, :], w_up[j].reshape(D, D)) + vec_ref[9 + j : 10 + j, :]
            value, slope = gelu_parts(upper)
            act[r, j * D : (j + 1) * D] = low_cast(value)
            gel[r, j * D : (j + 1) * D] = low_cast(slope)
            return carry

        lax.fori_loop(0, T // ROW_TILE, ff_up, 0)
        gather_step()

    gather_until(GATHERS - 2)
    gather_until(GATHERS - 1)
    load_cot.wait()

    def second_norm(i, sums):
        r = tile_rows(i)
        lowered = mm(act[r, :], w_down[...].reshape(FF, D))
        normed, rstd = norm_rows(hid[r, :] + (lowered + vec_ref[5:6, :]))
        one_low[r, :] = low_cast(normed * vec_ref[2:3, :] + vec_ref[3:4, :])
        dy = ig_ref[r, :]
        d_two = norm_rows_back(dy, normed, rstd, vec_ref[2:3, :])
        hid[r, :] = d_two
        two_low[r, :] = low_cast(d_two)
        return sums[0] + row_sum(dy * normed), sums[1] + row_sum(dy), sums[2] + row_sum(d_two)

    zero_row = jnp.zeros((1, D), jnp.float32)
    gain_two, shift_two, bias_down = lax.fori_loop(
        0, T // ROW_TILE, second_norm, (zero_row, zero_row, zero_row)
    )
    save_y.start()
    vg_ref[2:3, :] = gain_two
    vg_ref[3:4, :] = shift_two
    vg_ref[5:6, :] = bias_down

    for j in range(TILES):

        def ff_back(i, total, j=j):
            r = tile_rows(i)
            d_act = mm_cols(two_low[r, :], w_down[j // 2, j % 2].reshape(D, D))
            d_upper = d_act * gel[r, j * D : (j + 1) * D].astype(jnp.float32)
            gel[r, j * D : (j + 1) * D] = low_cast(d_upper)
            return total + row_sum(d_upper)

        vg_ref[9 + j : 10 + j, :] = lax.fori_loop(0, T // ROW_TILE, ff_back, zero_row)

    for g in (GATHERS - 2, GATHERS - 1):
        g_sent(g)
    for j in range(TILES):
        got = low_cast(mm_rows(act[:, j * D : (j + 1) * D], two_low[...]))
        w_down[j // 2, j % 2] = got.reshape(2, TILES * rows, D)
    for k in range(UP):
        reduce_start(k)

    save_y.wait()

    def first_norm_back(i, sums):
        r = tile_rows(i)
        dy = hid[r, :]
        for j in range(TILES):
            dy = dy + mm_cols(gel[r, j * D : (j + 1) * D], w_up[j].reshape(D, D))
        normed = norm_one[r, :]
        d_one = norm_rows_back(dy, normed, rstd_one[r, 0:1], vec_ref[0:1, :])
        ig_ref[r, :] = d_one
        one_low[r, :] = low_cast(d_one)
        return sums[0] + row_sum(dy * normed), sums[1] + row_sum(dy), sums[2] + row_sum(d_one)

    sums = (zero_row, zero_row, zero_row)
    steps = T // ROW_TILE
    sums = lax.fori_loop(0, steps // 2, first_norm_back, sums)
    reduce_some(1)
    sums = lax.fori_loop(steps // 2, steps, first_norm_back, sums)
    reduce_some(2)
    vg_ref[0:1, :] = sums[0]
    vg_ref[1:2, :] = sums[1]
    vg_ref[4:5, :] = sums[2]

    d_heads = two_low
    d_heads[...] = low_cast(mm_cols(one_low[...], w_out[...].reshape(D, D)))

    zcol[...] = jnp.zeros_like(zcol)

    def grad_slot(h):
        return slice(None), pl.ds(pl.multiple_of(h * LANES, LANES), LANES)

    def back_states(p, carry):
        g_pair = d_heads[:, pair_cols(p)].astype(jnp.float32)
        parts = []
        for side in (0, 1):
            h = 2 * p + side
            saved = num_a[h]
            g = g_pair if side == 0 else swap_halves(g_pair)
            gn = jnp.where(half_lane < HD, g * swap_halves(saved), 0.0)
            gd = -jnp.sum(gn * saved, axis=1, keepdims=True)
            gd_high = low_cast(gd).astype(jnp.float32)
            gn = jnp.where(
                half_lane == HD, gd_high, jnp.where(half_lane == HD + 1, gd - gd_high, gn)
            )
            gn = low_cast(gn)
            act[grad_slot(h)] = gn
            parts.append(mm_rows(feat_q[h] * keeps[1], gn))
        pack_states(p, parts[0], parts[1], back_own, 2)
        return carry

    lax.fori_loop(0, PAIRS, back_states, 0)
    back_own[PAIRS] = low_cast(zcol[...])
    exchange_start(1, back_own, back_in)
    reduce_some(3)

    for g in range(GROUPS + 1, GATHERS - 2):
        g_sent(g)
    turned[...] = hid_low[...].T
    for j in range(TILES):
        got = low_cast(mm(turned[...], gel[:, j * D : (j + 1) * D]))
        w_up[j] = got.reshape(2, 2, 2, rows, D)
        reduce_start(UP + j)
    reduce_some(3)
    g_sent(GROUPS)
    w_out[...] = low_cast(mm_rows(heads[...], one_low[...])).reshape(2, 2, 2, rows, D)
    reduce_start(OUT)
    reduce_some(2)

    def sigmoid(v):
        e = jnp.exp(-jnp.abs(v))
        return jnp.where(v >= 0, 1.0, e) / (1.0 + e)

    def fold(value):
        value = value * cs_ref[...]
        return value + swap_halves(value)

    def through_features(p, part, left, right):
        value = mixed[slab(p, part)].astype(jnp.float32)
        d_part = sigmoid(value) * jnp.where(half_lane < HD, fold(left), fold(right))
        mixed[slab(p, part)] = low_cast(d_part)
        vg_ref[6 + part : 7 + part, pair_cols(p)] = row_sum(d_part)

    def query_back(p, carry):
        got = []
        for side in (0, 1):
            h = 2 * p + side
            ga = act[grad_slot(h)]
            d_scores = low_cast(mm_cols(ga, val_a[h])) * mask[...]
            got.append(mm(d_scores, feat_k[h]) + mm_cols(ga * keeps[2], state_h[h]))
        through_features(p, 0, got[0], got[1])
        return carry

    for part in range(3):
        lax.fori_loop(2 * part, 2 * part + 2, query_back, 0)
        reduce_some(2)

    exchange_end(1, back_own, back_in, backward_weight, back_h, 1)

    def key_value_back(p, carry):
        keys, values = [], []
        for side in (0, 1):
            h = 2 * p + side
            fq, fk, va, ga = feat_q[h], feat_k[h], val_a[h], act[grad_slot(h)]
            d_scores_t = low_cast(mm_cols(va, ga)) * mask_t[...]
            keys.append(mm(d_scores_t, fq) + mm_cols(va * keeps[3], back_h[h]))
            scores_t = low_cast(mm_cols(fk, fq)) * mask_t[...]
            values.append(mm(scores_t, ga) + mm(fk * keeps[3], back_h[h]))
        through_features(p, 1, keys[0], keys[1])
        d_part = join(values[0], values[1])
        mixed[slab(p, 2)] = low_cast(d_part)
        vg_ref[8:9, pair_cols(p)] = row_sum(d_part)
        return carry

    turned[...] = tok[...].T
    for g in range(GROUPS):
        lax.fori_loop(2 * g, 2 * g + 2, key_value_back, 0)
        ig_ref[...] += mm_cols(mixed[g], w_qkv[g].reshape(D, D))
        g_sent(g)
        w_qkv[g] = low_cast(mm(turned[...], mixed[g])).reshape(2, 2, 2, rows, D)
        reduce_start(MIX + g)
        reduce_some(4)

    def vcopy(level):
        target = (sib, xn, yn, z_one, z_two)[level]
        return remote(vg_ref, vec_land.at[level], v_send.at[level], v_recv.at[level], target)

    vg_ref[13:16, :] = jnp.zeros((3, D), jnp.float32)
    vcopy(0).start()
    for level in range(5):
        reduce_some(3)
        vcopy(level).wait()
        vg_ref[...] += vec_land[level]
        if level < 4:
            vcopy(level + 1).start()
    reduce_some(len(r_plan))
    for k in range(UNITS):
        r_end(k)
    exchange_sent(0, state_own, state_in)
    exchange_sent(1, back_own, back_in)


GATHER_AHEAD = 3


def fits(mesh):
    return mesh.shape["dp"] == 8 and mesh.shape["head"] == 4


def fused_layer(lengths, tokens, cotangent, masters, vector_master):
    n_head = lax.axis_size("head")
    T = tokens.shape[0]
    rows = masters[1].shape[0]
    bf, f32 = jnp.bfloat16, jnp.float32
    V, S = pltpu.VMEM, jax.ShapeDtypeStruct
    vm, anywhere = pl.BlockSpec(memory_space=pltpu.VMEM), pl.BlockSpec(memory_space=pl.ANY)
    out_shape = (S((T, D), bf), S((T, D), f32)) + tuple(S(m.shape, bf) for m in masters)
    out_shape += (S((16, D), f32),)
    shard = (2, 2, 2, rows, D)
    scratch = [
        V((GROUPS, *shard), bf),
        V(shard, bf),
        V((TILES, *shard), bf),
        V((2, 2, 2, TILES * rows, D), bf),
        V((T, D), bf),
        V((GROUPS, T, D), bf),
        V((H, T, LANES), bf),
        V((H, T, LANES), bf),
        V((H, T, LANES), bf),
        V((H, T, LANES), f32),
        V((T, D), bf),
        V((T, D), f32),
        V((T, LANES), f32),
        V((T, D), f32),
        V((T, D), bf),
        V((D, T), bf),
        V((T, FF), bf),
        V((T, FF), bf),
        V((T, D), bf),
        V((T, D), bf),
        V((T, T), bf),
        V((T, T), bf),
        V((T, LANES), f32),
        V((T, LANES), f32),
        V((4, T, LANES), bf),
        V((SLABS, LANES, LANES), bf),
        V((n_head - 1, SLABS, LANES, LANES), bf),
        V((SLABS, LANES, LANES), bf),
        V((n_head - 1, SLABS, LANES, LANES), bf),
        V((SLABS, LANES, LANES), f32),
        V((H, LANES, LANES), bf),
        V((H, LANES, LANES), bf),
        V((LANES, LANES), f32),
        V((UNITS, 2, 2, rows, D), bf),
        V((UNITS, 2, 2, rows // 2, D), bf),
        V((UNITS, 2, rows // 2, D), bf),
        V((UNITS, 2, rows, D), bf),
        V((5, 16, D), f32),
        pltpu.SemaphoreType.DMA((18,)),
        pltpu.SemaphoreType.DMA((8, 17)),
        pltpu.SemaphoreType.DMA((8, 17)),
        pltpu.SemaphoreType.DMA((2, n_head)),
        pltpu.SemaphoreType.DMA((2, n_head)),
        pltpu.SemaphoreType.DMA((UNITS, 13)),
        pltpu.SemaphoreType.DMA((UNITS, 13)),
        pltpu.SemaphoreType.DMA((5,)),
        pltpu.SemaphoreType.DMA((5,)),
    ]
    return pl.pallas_call(
        functools.partial(layer_kernel, n_head, lengths.shape[0]),
        out_shape=out_shape,
        in_specs=[pl.BlockSpec(memory_space=pltpu.SMEM)] + [anywhere] * 6 + [vm],
        out_specs=[anywhere, vm] + [anywhere] * 4 + [vm],
        scratch_shapes=scratch,
        compiler_params=pltpu.CompilerParams(
            collective_id=0, has_side_effects=True, vmem_limit_bytes=VMEM_BYTES
        ),
        name="layer",
    )(lengths, tokens, cotangent, *masters, vector_master)


VMEM_BYTES = 63 * 1024 * 1024


def fused_shards(
    tokens,
    cotangent,
    lengths,
    qkv_master,
    out_master,
    up_master,
    down_master,
    vector_master,
    qkv_first,
    qkv_second,
    out_first,
    out_second,
    up_first,
    up_second,
    down_first,
    down_second,
    vector_first,
    vector_second,
):
    masters = (qkv_master, out_master, up_master, down_master)
    output, input_grad, *grads, vector_grad = fused_layer(
        lengths, tokens, cotangent, masters, vector_master
    )
    rates = (1.0 / math.sqrt(D), 1.0 / math.sqrt(OUT_FAN), 1.0 / math.sqrt(D), 1.0 / math.sqrt(FF))
    firsts = (qkv_first, out_first, up_first, down_first)
    seconds = (qkv_second, out_second, up_second, down_second)
    news = []
    for i in range(4):
        news.extend(
            adam_update(
                masters[i],
                firsts[i],
                seconds[i],
                grads[i].astype(jnp.float32),
                rates[i],
                weight_decay,
            )
        )
    vector_new = adam_update(
        vector_master, vector_first, vector_second, vector_grad[:13], vector_rate, 0.0
    )
    return (output, input_grad, *news, *vector_new)


def solution(mesh):
    return jax.shard_map(
        fused_shards if fits(mesh) else shards,
        mesh=mesh,
        in_specs=(
            P(("dp", "head"), None),
            P(("dp", "head"), None),
            P("dp"),
            P("dp", None),
            P("dp", None),
            P("dp", None),
            P("dp", None),
            P(),
            P("dp", None),
            P("dp", None),
            P("dp", None),
            P("dp", None),
            P("dp", None),
            P("dp", None),
            P("dp", None),
            P("dp", None),
            P(),
            P(),
        ),
        out_specs=(
            P(("dp", "head"), None),
            P(("dp", "head"), None),
            P("dp", None),
            P("dp", None),
            P("dp", None),
            P("dp", None),
            P("dp", None),
            P("dp", None),
            P("dp", None),
            P("dp", None),
            P("dp", None),
            P("dp", None),
            P("dp", None),
            P("dp", None),
            P(),
            P(),
            P(),
        ),
        check_vma=False,
    )
```

```python
import functools
import math

import jax
import jax.numpy as jnp
from jax import lax
from jax.experimental import pallas as pl
from jax.experimental.pallas import tpu as pltpu
from jax.sharding import PartitionSpec as P

D = 768
H = 12
HD = 64
FF = 3072
SPAN = 64
STEP = 10
OUT_FAN = 1


highest = lax.Precision.HIGHEST
norm_epsilon = 1e-05
first_decay = 0.9
second_decay = 0.999
adam_epsilon = 1e-08
weight_decay = 0.01
vector_rate = 0.2


def layer_norm(residual, gain_row, shift_row):
    center = residual - jnp.mean(residual, axis=-1, keepdims=True)
    spread = jnp.mean(center * center, axis=-1, keepdims=True)
    return center * lax.rsqrt(spread + norm_epsilon) * gain_row + shift_row


def exact_gelu(upper_pre):
    return jax.nn.gelu(upper_pre, approximate=False)


def group_layout(group_lengths, row_count):
    slot_sizes = (group_lengths + SPAN - 1) // SPAN * SPAN
    slot_ends = jnp.cumsum(slot_sizes)
    slot_starts = slot_ends - slot_sizes
    positions = jnp.arange(row_count, dtype=jnp.int32)
    member = (positions[:, None] >= slot_starts[None, :]) & (
        positions[:, None] < slot_ends[None, :]
    )
    seq_first = jnp.sum(jnp.where(member, slot_starts[None, :], 0), axis=1)
    length = jnp.sum(jnp.where(member, group_lengths[None, :], 0), axis=1)
    seq_numbers = jnp.arange(group_lengths.shape[0], dtype=jnp.int32)
    owners = jnp.sum(jnp.where(member, seq_numbers[None, :], 0), axis=1)
    offset = positions - seq_first
    live_rows = (offset < length).astype(jnp.float32)
    angles = 0.5 * math.pi * offset.astype(jnp.float32) / length.astype(jnp.float32)
    cosine = jnp.cos(angles)
    sine_part = jnp.sin(angles)
    span_owner = owners[::SPAN]
    span_order = jnp.arange(span_owner.shape[0], dtype=jnp.int32)
    same_seq = span_owner[None, :] == span_owner[:, None]
    earlier = (same_seq & (span_order[None, :] < span_order[:, None])).astype(jnp.float32)
    return (cosine, sine_part, live_rows, earlier)


def attend(query_rows, key_rows, value_rows, cosine, sine_part, live_rows, earlier):
    row_count = query_rows.shape[0]
    blocks = row_count // SPAN
    soft_query = jax.nn.softplus(query_rows)
    soft_key = jax.nn.softplus(key_rows)
    feat_query = (
        jnp.concatenate([soft_query * cosine[:, None], soft_query * sine_part[:, None]], axis=1)
        * live_rows[:, None]
    )
    feat_key = (
        jnp.concatenate([soft_key * cosine[:, None], soft_key * sine_part[:, None]], axis=1)
        * live_rows[:, None]
    )
    block_query = feat_query.reshape(blocks, SPAN, -1)
    block_key = feat_key.reshape(blocks, SPAN, -1)
    block_value = value_rows.reshape(blocks, SPAN, -1)
    lower_mask = (jnp.arange(SPAN)[:, None] >= jnp.arange(SPAN)[None, :]).astype(jnp.float32)
    scores = jnp.einsum("cik,cjk->cij", block_query, block_key, precision=highest) * lower_mask
    inner_sum = jnp.einsum("cij,cjd->cid", scores, block_value, precision=highest)
    inner_den = jnp.sum(scores, axis=2)
    states = jnp.einsum("cjk,cjd->ckd", block_key, block_value, precision=highest)
    key_sums = jnp.sum(block_key, axis=1)
    before = jnp.einsum("ce,ekd->ckd", earlier, states, precision=highest)
    before_sums = jnp.einsum("ce,ek->ck", earlier, key_sums, precision=highest)
    outer_sum = jnp.einsum("cik,ckd->cid", block_query, before, precision=highest)
    outer_den = jnp.einsum("cik,ck->ci", block_query, before_sums, precision=highest)
    numerator = (inner_sum + outer_sum).reshape(row_count, -1)
    denominator = (inner_den + outer_den).reshape(row_count) + (1.0 - live_rows)
    return numerator / denominator[:, None]


def contract_rows(left, right):
    return lax.dot_general(
        left, right, (((0,), (0,)), ((), ())), preferred_element_type=jnp.float32
    )


def contract_cols(left, right):
    return lax.dot_general(
        left, right, (((1,), (1,)), ((), ())), preferred_element_type=jnp.float32
    )


def adam_update(master, first, second, gradient, rate, decay):
    first_new = first_decay * first + (1.0 - first_decay) * gradient
    second_new = second_decay * second + (1.0 - second_decay) * gradient * gradient
    first_hat = first_new / (1.0 - first_decay**STEP)
    second_hat = second_new / (1.0 - second_decay**STEP)
    master_new = master - rate * (
        first_hat / (jnp.sqrt(second_hat) + adam_epsilon) + decay * master
    )
    return (first_new, second_new, master_new)


def shards(
    tokens,
    cotangent,
    lengths,
    qkv_master,
    out_master,
    up_master,
    down_master,
    vector_master,
    qkv_first,
    qkv_second,
    out_first,
    out_second,
    up_first,
    up_second,
    down_first,
    down_second,
    vector_first,
    vector_second,
):
    mix_weight, out_weight, up_weight, down_weight = (
        lax.all_gather(qkv_master.astype(jnp.bfloat16), "dp", axis=0, tiled=True),
        lax.all_gather(out_master.astype(jnp.bfloat16), "dp", axis=0, tiled=True),
        lax.all_gather(up_master.astype(jnp.bfloat16), "dp", axis=0, tiled=True),
        lax.all_gather(down_master.astype(jnp.bfloat16), "dp", axis=0, tiled=True),
    )
    tok_count = tokens.shape[0]
    width = tokens.shape[1]
    mixed_all = jnp.dot(tokens, mix_weight, preferred_element_type=jnp.float32) + vector_master[
        6:9
    ].reshape(-1)
    mixed_low = mixed_all.astype(jnp.bfloat16)
    query_part = mixed_low[:, :width].reshape(tok_count, H, 1, HD)
    key_part = mixed_low[:, width : 2 * width].reshape(tok_count, H, 1, HD)
    paired = jnp.concatenate([query_part, key_part], axis=2)
    paired = jnp.repeat(paired[:, :, None], 2, axis=2).reshape(tok_count, 4 * width)
    value_part = mixed_low[:, 2 * width :]
    paired_in, values_in = (
        lax.all_to_all(paired, "head", split_axis=1, concat_axis=0, tiled=True),
        lax.all_to_all(value_part, "head", split_axis=1, concat_axis=0, tiled=True),
    )
    group_rows = paired_in.shape[0]
    item_count = paired_in.shape[1] // (2 * HD)
    cosine, sine_part, live_rows, earlier = group_layout(lengths, group_rows)
    stacked = paired_in.reshape(group_rows, item_count, 2, HD).astype(jnp.float32)
    query_items = stacked[:, :, 0]
    key_items = stacked[:, :, 1]
    value_items = values_in.reshape(group_rows, item_count, HD // 2).astype(jnp.float32)

    def mix_items(query_set, key_set, value_set):

        def single(query_rows, key_rows, value_rows):
            return attend(query_rows, key_rows, value_rows, cosine, sine_part, live_rows, earlier)

        return jax.vmap(single, in_axes=1, out_axes=1)(query_set, key_set, value_set)

    attended, mix_back = jax.vjp(mix_items, query_items, key_items, value_items)
    heads_out = attended.reshape(group_rows, item_count * (HD // 2)).astype(jnp.bfloat16)
    heads = lax.all_to_all(heads_out, "head", split_axis=0, concat_axis=1, tiled=True)
    projected = jnp.dot(heads, out_weight, preferred_element_type=jnp.float32) + vector_master[4]
    resid_one = tokens.astype(jnp.float32) + projected
    hidden, norm_one_back = jax.vjp(layer_norm, resid_one, vector_master[0], vector_master[1])
    hidden_low = hidden.astype(jnp.bfloat16)
    upper_pre = jnp.dot(hidden_low, up_weight, preferred_element_type=jnp.float32) + vector_master[
        9:13
    ].reshape(-1)
    active, gelu_back = jax.vjp(exact_gelu, upper_pre)
    active_low = active.astype(jnp.bfloat16)
    lowered = (
        jnp.dot(active_low, down_weight, preferred_element_type=jnp.float32) + vector_master[5]
    )
    output, norm_two_back = jax.vjp(
        layer_norm, hidden + lowered, vector_master[2], vector_master[3]
    )
    grad_two, gain_two, shift_two = norm_two_back(cotangent)
    grad_two_low = grad_two.astype(jnp.bfloat16)
    down_grad = contract_rows(active_low, grad_two_low)
    (upper_grad,) = gelu_back(contract_cols(grad_two_low, down_weight))
    upper_low = upper_grad.astype(jnp.bfloat16)
    up_grad = contract_rows(hidden_low, upper_low)
    hidden_grad = grad_two + contract_cols(upper_low, up_weight)
    grad_one, gain_one, shift_one = norm_one_back(hidden_grad)
    grad_one_low = grad_one.astype(jnp.bfloat16)
    out_grad = contract_rows(heads, grad_one_low)
    heads_grad = contract_cols(grad_one_low, out_weight).astype(jnp.bfloat16)
    heads_back = lax.all_to_all(heads_grad, "head", split_axis=1, concat_axis=0, tiled=True)
    query_back, key_back, value_back = mix_back(
        heads_back.reshape(group_rows, item_count, HD // 2).astype(jnp.float32)
    )
    pair_back = (
        jnp.stack([query_back, key_back], axis=2)
        .astype(jnp.bfloat16)
        .reshape(group_rows, item_count * 2 * HD)
    )
    value_low = value_back.astype(jnp.bfloat16).reshape(group_rows, item_count * (HD // 2))
    pair_home, value_home = (
        lax.all_to_all(pair_back, "head", split_axis=0, concat_axis=1, tiled=True),
        lax.all_to_all(value_low, "head", split_axis=0, concat_axis=1, tiled=True),
    )
    summed = jnp.sum(pair_home.astype(jnp.float32).reshape(tok_count, H, 2, 2, HD), axis=2)
    mixed_grad = jnp.concatenate(
        [
            summed[:, :, 0].reshape(tok_count, width),
            summed[:, :, 1].reshape(tok_count, width),
            value_home.astype(jnp.float32),
        ],
        axis=1,
    )
    mixed_low_grad = mixed_grad.astype(jnp.bfloat16)
    mix_grad = contract_rows(tokens, mixed_low_grad)
    input_grad = grad_one + contract_cols(mixed_low_grad, mix_weight)
    vector_grad = jnp.concatenate(
        [
            jnp.stack(
                [
                    gain_one,
                    shift_one,
                    gain_two,
                    shift_two,
                    jnp.sum(grad_one, axis=0),
                    jnp.sum(grad_two, axis=0),
                ]
            ),
            jnp.sum(mixed_grad, axis=0).reshape(3, width),
            jnp.sum(upper_grad, axis=0).reshape(4, width),
        ],
        axis=0,
    )
    local_grads = (mix_grad, out_grad, up_grad, down_grad)
    row_parts = (
        lax.psum_scatter(
            local_grads[0].astype(jnp.bfloat16), "dp", scatter_dimension=0, tiled=True
        ).astype(jnp.float32),
        lax.psum_scatter(
            local_grads[1].astype(jnp.bfloat16), "dp", scatter_dimension=0, tiled=True
        ).astype(jnp.float32),
        lax.psum_scatter(
            local_grads[2].astype(jnp.bfloat16), "dp", scatter_dimension=0, tiled=True
        ).astype(jnp.float32),
        lax.psum_scatter(
            local_grads[3].astype(jnp.bfloat16), "dp", scatter_dimension=0, tiled=True
        ).astype(jnp.float32),
    )
    reduced = (
        lax.psum(row_parts[0].astype(jnp.bfloat16), "head").astype(jnp.float32),
        lax.psum(row_parts[1].astype(jnp.bfloat16), "head").astype(jnp.float32),
        lax.psum(row_parts[2].astype(jnp.bfloat16), "head").astype(jnp.float32),
        lax.psum(row_parts[3].astype(jnp.bfloat16), "head").astype(jnp.float32),
    )
    vector_total = lax.psum(vector_grad, ("dp", "head"))
    qkv_new = adam_update(
        qkv_master, qkv_first, qkv_second, reduced[0], 1.0 / math.sqrt(D), weight_decay
    )
    out_new = adam_update(
        out_master, out_first, out_second, reduced[1], 1.0 / math.sqrt(OUT_FAN), weight_decay
    )
    up_new = adam_update(
        up_master, up_first, up_second, reduced[2], 1.0 / math.sqrt(D), weight_decay
    )
    down_new = adam_update(
        down_master, down_first, down_second, reduced[3], 1.0 / math.sqrt(FF), weight_decay
    )
    vector_new = adam_update(
        vector_master, vector_first, vector_second, vector_total, vector_rate, 0.0
    )
    return (
        output.astype(jnp.bfloat16),
        input_grad,
        qkv_new[0],
        qkv_new[1],
        qkv_new[2],
        out_new[0],
        out_new[1],
        out_new[2],
        up_new[0],
        up_new[1],
        up_new[2],
        down_new[0],
        down_new[1],
        down_new[2],
        vector_new[0],
        vector_new[1],
        vector_new[2],
    )


PAIRS = H // 2
LANES = 2 * HD
GROUPS = 3
STATE_ROWS = (PAIRS // GROUPS) * LANES + 16
WIDE = D // GROUPS
TILES = FF // D
ROW_TILE = 128
MESH = pl.DeviceIdType.MESH
DOWN, UP, OUT, MIX = 0, TILES, 2 * TILES, 2 * TILES + 1
UNITS = 2 * TILES + 1 + GROUPS


def mm(left, right):
    return jnp.dot(left, right, preferred_element_type=jnp.float32)


def mm_cols(left, right):
    return lax.dot_general(
        left, right, (((1,), (1,)), ((), ())), preferred_element_type=jnp.float32
    )


def mm_rows(left, right):
    return lax.dot_general(
        left, right, (((0,), (0,)), ((), ())), preferred_element_type=jnp.float32
    )


def swap_halves(slab):
    return pltpu.roll(slab, HD, 1)


def low_cast(value):
    return value.astype(jnp.bfloat16)


def row_sum(value):
    return jnp.sum(value, axis=0, keepdims=True)


def gelu_parts(z):
    x = jnp.abs(z) * (1.0 / math.sqrt(2.0))
    t = 1.0 / (1.0 + 0.3275911 * x)
    bell = jnp.exp(-0.5 * z * z)
    poly = t * (
        0.254829592
        + t * (-0.284496736 + t * (1.421413741 + t * (-1.453152027 + t * 1.061405429)))
    )
    upper_tail = 0.5 * poly * bell
    phi = jnp.where(z >= 0, 1.0 - upper_tail, upper_tail)
    return z * phi, phi + z * (bell * (1.0 / math.sqrt(2.0 * math.pi)))


def over_rows(count, body, carry, start=0):
    for i in range(start, count):
        carry = body(i, carry)
    return carry


def norm_rows(residual):
    center = residual - jnp.mean(residual, axis=-1, keepdims=True)
    rstd = lax.rsqrt(jnp.mean(center * center, axis=-1, keepdims=True) + norm_epsilon)
    return center * rstd, rstd


def norm_rows_back(dy, normed, rstd, gain):
    e = dy * gain
    return rstd * (
        e
        - jnp.mean(e, axis=-1, keepdims=True)
        - normed * jnp.mean(e * normed, axis=-1, keepdims=True)
    )


def layer_kernel(
    n_head,
    n_seq,
    lens_ref,
    tok_hbm,
    cot_hbm,
    qkv_f,
    out_f,
    up_f,
    down_f,
    vec_ref,
    y_hbm,
    ig_ref,
    g_qkv,
    g_out,
    g_up,
    g_down,
    vg_ref,
    w_qkv,
    w_out,
    w_up,
    w_down,
    tok,
    mixed,
    feat_q,
    feat_k,
    val_a,
    num_a,
    heads,
    norm_one,
    rstd_one,
    hid,
    hid_low,
    turned,
    act,
    gel,
    two_low,
    one_low,
    mask,
    mask_t,
    cs_ref,
    live_ref,
    keeps,
    state_own,
    state_in,
    back_own,
    back_in,
    state_sum,
    state_h,
    back_h,
    zcol,
    red_a,
    red_b,
    red_c,
    red_e,
    vec_land,
    load_sem,
    g_send,
    g_recv,
    s_send,
    s_recv,
    r_send,
    r_recv,
    v_send,
    v_recv,
):
    T = tok.shape[0]
    rows = w_out.shape[3]
    half = rows // 2
    dp = lax.axis_index("dp")
    z = lax.axis_index("head")
    core = dp % 2
    xx = (dp // 2) % 2
    yy = dp // 4
    color = z % 2
    sib = (dp + 1 - 2 * core, z)
    xn = (dp + 2 - 4 * xx, z)
    yn = (dp + 4 - 8 * yy, z)
    z_one = (dp, z + 1 - 2 * color)
    z_two = (dp, (z + 3 + 2 * color) % n_head)

    def load(i, src, dst):
        return pltpu.make_async_copy(src, dst, load_sem.at[i])

    def spot(ref, i):
        return ref.at[pl.ds(i * rows, rows), :]

    loads = []
    for g in range(GROUPS):
        for part in range(3):
            loads.append(
                load(
                    len(loads),
                    qkv_f.at[:, pl.ds(part * D + g * WIDE, WIDE)],
                    hid.at[pl.ds(g * rows, rows), pl.ds(part * WIDE, WIDE)],
                )
            )
    loads.append(load(len(loads), out_f, spot(hid, GROUPS)))
    for j in range(TILES):
        loads.append(load(len(loads), up_f.at[:, pl.ds(j * D, D)], spot(norm_one, j)))
    loads.append(load(len(loads), down_f, ig_ref.at[pl.ds(0, TILES * rows), :]))
    load_tok = load(len(loads), tok_hbm, tok)
    load_cot = load(len(loads) + 1, cot_hbm, ig_ref)
    save_y = load(len(loads) + 2, one_low, y_hbm)
    for copy in loads:
        copy.start()
    load_tok.start()

    barrier = pltpu.get_barrier_semaphore()
    peers = [sib, xn, yn]
    for k in range(1, n_head):
        peers.append((dp, (z + k) % n_head))
    for peer in peers:
        pl.semaphore_signal(barrier, inc=1, device_id=peer, device_id_type=MESH)

    def remote(src, dst, send, recv, target):
        return pltpu.make_async_remote_copy(
            src_ref=src,
            dst_ref=dst,
            send_sem=send,
            recv_sem=recv,
            device_id=target,
            device_id_type=MESH,
        )

    GATHERS = GROUPS + 1 + TILES // 2 + 2

    def piece(g, y, x, c, which):
        if g < GROUPS:
            ref, size, base = w_qkv.at[g, y, x, c], rows, 0
        elif g == GROUPS:
            ref, size, base = w_out.at[y, x, c], rows, 0
        elif g < GROUPS + 1 + TILES // 2:
            i = g - GROUPS - 1
            if which is None:
                return w_up.at[pl.ds(2 * i, 2), y, x, c]
            return w_up.at[
                pl.ds(2 * i, 2), y, x, c, pl.ds(pl.multiple_of(which * half, half), half), :
            ]
        else:
            i = g - GROUPS - 1 - TILES // 2
            ref, size, base = w_down.at[y, x, c], 2 * rows, 2 * rows * i
        if which is None:
            return ref.at[pl.ds(base, size), :]
        return ref.at[pl.ds(pl.multiple_of(base + which * (size // 2), size // 2), size // 2), :]

    def own_masters(g):
        if g < GROUPS:
            for part in range(3):
                loads[3 * g + part].wait()
            w_qkv[g, yy, xx, core] = low_cast(hid[g * rows : (g + 1) * rows, :])
        elif g == GROUPS:
            loads[9].wait()
            w_out[yy, xx, core] = low_cast(hid[g * rows : (g + 1) * rows, :])
        elif g < GROUPS + 1 + TILES // 2:
            for j in range(2 * (g - GROUPS - 1), 2 * (g - GROUPS)):
                loads[10 + j].wait()
                w_up[j, yy, xx, core] = low_cast(norm_one[j * rows : (j + 1) * rows, :])
        else:
            i = g - GROUPS - 1 - TILES // 2
            if i == 0:
                loads[10 + TILES].wait()
            span = slice(2 * rows * i, 2 * rows * (i + 1))
            w_down[yy, xx, core, span, :] = low_cast(ig_ref[span, :])

    here, mine_x, mine_y, mine_d = (yy, xx), (yy, 1 - xx), (1 - yy, xx), (1 - yy, 1 - xx)

    def gcopy(g, kind, chip, which, target, lands):
        ref = piece(g, chip[0], chip[1], core, which)
        return remote(ref, ref, g_send.at[g, kind], g_recv.at[g, lands], target)

    def landed(g, chip, which, lands):
        gcopy(g, 0, chip, which, sib, lands).wait_recv()

    blocks = ((mine_x, 0), (mine_x, 1), (mine_y, 0), (mine_y, 1), (mine_d, 0), (mine_d, 1))

    def hand_over(g, lands):
        chip, which = blocks[lands]
        gcopy(g, 10 + lands, chip, which, sib, 7 + lands).start()

    def arrived(g, lands):
        chip, which = blocks[lands]
        landed(g, chip, which, lands)

    def g_start(g):
        gcopy(g, 0, here, 0, xn, 0).start()
        gcopy(g, 1, here, 1, yn, 3).start()

        @pl.when(color == 0)
        def _():
            gcopy(g, 2, here, 1, xn, 1).start()
            gcopy(g, 3, here, 0, yn, 2).start()

        gcopy(g, 9, here, None, sib, 6).start()

    def g_own(g):
        own_masters(g)
        g_start(g)

    def g_first(g):
        arrived(g, 0)

        @pl.when(color == 1)
        def _():
            gcopy(g, 4, mine_x, 0, yn, 4).start()

        arrived(g, 3)

        @pl.when(color == 1)
        def _():
            gcopy(g, 5, mine_y, 1, xn, 5).start()

        hand_over(g, 0)
        hand_over(g, 3)

        @pl.when(color == 0)
        def _():
            arrived(g, 1)
            gcopy(g, 6, mine_x, 1, z_one, 1).start()
            arrived(g, 2)
            gcopy(g, 7, mine_y, 0, z_one, 2).start()
            hand_over(g, 1)
            hand_over(g, 2)

    def g_second(g):
        @pl.when(color == 1)
        def _():
            arrived(g, 4)
            gcopy(g, 8, mine_d, 0, z_one, 4).start()
            arrived(g, 5)
            gcopy(g, 16, mine_d, 1, z_one, 5).start()
            hand_over(g, 4)
            hand_over(g, 5)
            arrived(g, 1)
            hand_over(g, 1)
            arrived(g, 2)
            hand_over(g, 2)

    def g_third(g):
        @pl.when(color == 0)
        def _():
            arrived(g, 4)
            hand_over(g, 4)
            arrived(g, 5)
            hand_over(g, 5)

    def g_last(g):
        landed(g, here, None, 6)
        for lands in range(6):
            chip, which = blocks[lands]
            landed(g, chip, which, 7 + lands)

    def g_sent(g):
        def sent(kind, chip, which):
            gcopy(g, kind, chip, which, sib, 0).wait_send()

        sent(0, here, 0)
        sent(1, here, 1)
        sent(9, here, None)
        for lands in range(6):
            sent(10 + lands, *blocks[lands])

        @pl.when(color == 0)
        def _():
            sent(2, here, 1)
            sent(3, here, 0)
            sent(6, mine_x, 1)
            sent(7, mine_y, 0)

        @pl.when(color == 1)
        def _():
            sent(4, mine_x, 0)
            sent(5, mine_y, 1)
            sent(8, mine_d, 0)
            sent(16, mine_d, 1)

    plan = []
    for step in range(GATHERS + 2):
        acts = [(f, step - lag) for f, lag in ((g_third, 2), (g_second, 1), (g_first, 0))]
        acts = [(f, g) for f, g in acts if 0 <= g < GATHERS]
        if step + GATHER_AHEAD < GATHERS:
            acts.append((g_own, step + GATHER_AHEAD))
        plan.append(acts)

    def gather_step():
        if plan:
            for act_of, g in plan.pop(0):
                act_of(g)

    def gather_until(g):
        while any((g_third, g) in acts for acts in plan):
            gather_step()
        g_last(g)

    def unit_ref(k):
        if k < UP:
            return w_down.at[:, :, :, pl.ds(k * rows, rows), :]
        if k < OUT:
            return w_up.at[k - UP]
        if k < MIX:
            return w_out
        return w_qkv.at[k - MIX]

    middle = (z > 0) & (z < n_head - 1)
    top, low_part = pl.ds(0, half), pl.ds(half, half)

    def finals(k):
        if k < UP:
            return [(None, g_down.at[pl.ds(k * rows, rows), :])]
        if k < OUT:
            return [(None, g_up.at[:, pl.ds((k - UP) * D, D)])]
        if k < MIX:
            return [(None, g_out)]
        return [
            (part * WIDE, g_qkv.at[:, pl.ds(part * D + (k - MIX) * WIDE, WIDE)])
            for part in range(3)
        ]

    def r_final(k, i):
        mine = red_a.at[k, yy, xx]
        col, dst = finals(k)[i]
        return mine if col is None else mine.at[:, pl.ds(col, WIDE)], dst

    def r_copy(k, kind):
        mine = red_a.at[k, yy, xx]
        if kind == 0:
            src, dst, target = unit_ref(k).at[:, :, 1 - core], red_a.at[k], sib
        elif kind == 1:
            src, dst, target = red_a.at[k, :, 1 - xx, top, :], red_b.at[k, 0], xn
        elif kind == 2:
            src, dst, target = red_a.at[k, 1 - yy, :, low_part, :], red_b.at[k, 1], yn
        elif kind == 3:
            src, dst, target = red_a.at[k, 1 - yy, xx, top, :], red_c.at[k, 0], yn
        elif kind == 4:
            src, dst, target = red_a.at[k, yy, 1 - xx, low_part, :], red_c.at[k, 1], xn
        elif kind == 5:
            src, dst, target = mine, red_e.at[k, 0], z_one
        elif kind == 6:
            src, dst, target = mine, red_e.at[k, 1], z_two
        else:
            src, dst = r_final(k, kind - 7)
            target = z_one
        return remote(src, dst, r_send.at[k, kind], r_recv.at[k, kind], target)

    def r_local(k, i):
        src, dst = r_final(k, i)
        return pltpu.make_async_copy(src, dst, r_recv.at[k, 10 + i])

    def added(one, two):
        return low_cast(one.astype(jnp.float32) + two.astype(jnp.float32))

    def r_start(k):
        r_copy(k, 0).start()

    def r_pair(k):
        r_copy(k, 0).wait_recv()
        for y in range(2):
            for x in range(2):
                mine = unit_ref(k)[y, x, core] if k >= UP else None
                if k < UP:
                    mine = w_down[y, x, core, k * rows : (k + 1) * rows, :]
                red_a[k, y, x] = added(mine, red_a[k, y, x])
        r_copy(k, 1).start()
        r_copy(k, 2).start()

    def r_plane(k):
        r_copy(k, 1).wait_recv()
        red_a[k, 1 - yy, xx, top, :] = added(red_a[k, 1 - yy, xx, top, :], red_b[k, 0, 1 - yy])
        r_copy(k, 3).start()
        r_copy(k, 2).wait_recv()
        red_a[k, yy, 1 - xx, low_part, :] = added(
            red_a[k, yy, 1 - xx, low_part, :], red_b[k, 1, 1 - xx]
        )
        r_copy(k, 4).start()
        red_a[k, yy, xx, top, :] = added(red_a[k, yy, xx, top, :], red_b[k, 0, yy])
        red_a[k, yy, xx, low_part, :] = added(red_a[k, yy, xx, low_part, :], red_b[k, 1, xx])

    def r_whole(k):
        r_copy(k, 3).wait_recv()
        r_copy(k, 4).wait_recv()
        red_a[k, yy, xx, top, :] = added(red_a[k, yy, xx, top, :], red_c[k, 0])
        red_a[k, yy, xx, low_part, :] = added(red_a[k, yy, xx, low_part, :], red_c[k, 1])

        @pl.when(~middle)
        def _():
            r_copy(k, 5).start()

    def r_z_first(k):
        @pl.when(middle)
        def _():
            r_copy(k, 5).wait_recv()
            red_a[k, yy, xx] = added(red_a[k, yy, xx], red_e[k, 0])
            r_copy(k, 6).start()

    def r_z_second(k):
        @pl.when(middle)
        def _():
            r_copy(k, 6).wait()
            red_a[k, yy, xx] = added(red_a[k, yy, xx], red_e[k, 1])
            for i in range(len(finals(k))):
                r_copy(k, 7 + i).start()
                r_local(k, i).start()

    def r_end(k):
        for kind in range(5):
            r_copy(k, kind).wait_send()

        @pl.when(middle)
        def _():
            for i in range(len(finals(k))):
                r_copy(k, 7 + i).wait_send()
                r_local(k, i).wait()

        @pl.when(~middle)
        def _():
            r_copy(k, 5).wait_send()
            for i in range(len(finals(k))):
                r_copy(k, 7 + i).wait_recv()

    stages = (r_pair, r_plane, r_whole, r_z_first, r_z_second)
    r_plan = []
    for tick in range(UNITS + len(stages)):
        acts = [(stages[s], tick - s) for s in reversed(range(1, len(stages)))]
        acts += [(r_pair, tick + 1)] if tick else [(r_pair, 0), (r_pair, 1)]
        r_plan.append([(f, k) for f, k in acts if 0 <= k < UNITS])
    started = []

    def reduce_start(k):
        r_start(k)
        started.append(k)

    def reduce_tick():
        if r_plan and all(k in started for _, k in r_plan[0]):
            for act_of, k in r_plan.pop(0):
                act_of(k)

    for g in range(min(GATHER_AHEAD, GATHERS)):
        own_masters(g)
    pl.semaphore_wait(barrier, len(peers))
    for g in range(min(GATHER_AHEAD, GATHERS)):
        g_start(g)

    lens = [lens_ref[s] for s in range(n_seq)]
    ends = []
    total = 0
    for s in range(n_seq):
        total = total + ((lens[s] + (SPAN - 1)) // SPAN) * SPAN
        ends.append(total)
    starts = [0] + ends[:-1]

    def owner_of(row):
        found = jnp.zeros_like(row)
        for s in range(n_seq):
            found = found + (row >= ends[s]).astype(jnp.int32)
        return found

    half_lane = lax.broadcasted_iota(jnp.int32, (T, LANES), 1)
    row = z * T + lax.broadcasted_iota(jnp.int32, (T, LANES), 0)
    first = jnp.zeros_like(row)
    length = jnp.ones_like(row)
    for s in range(n_seq):
        inside = (row >= starts[s]) & (row < ends[s])
        first = jnp.where(inside, starts[s], first)
        length = jnp.where(inside, lens[s], length)
    offset = row - first
    live = (offset < length).astype(jnp.float32)
    angle = 0.5 * math.pi * offset.astype(jnp.float32) / length.astype(jnp.float32)
    angle = jnp.where(half_lane < HD, angle, 0.5 * math.pi - angle)
    cs_ref[...] = jnp.cos(angle) * live
    live_ref[...] = live
    owners = owner_of(row)
    next_owner = owner_of(jnp.full((1, 1), (z + 1) * T, jnp.int32))
    last_owner = owner_of(jnp.full((1, 1), z * T - 1, jnp.int32))
    my_first = owner_of(jnp.full((1, 1), z * T, jnp.int32))
    my_last = owner_of(jnp.full((1, 1), (z + 1) * T - 1, jnp.int32))
    for i, edge in enumerate((next_owner, last_owner, my_first, my_last)):
        keeps[i] = low_cast((owners == edge).astype(jnp.float32))

    def fill_masks(i, carry):
        r0 = pl.multiple_of(i * ROW_TILE, ROW_TILE)
        t_i = r0 + lax.broadcasted_iota(jnp.int32, (ROW_TILE, T), 0)
        u_i = lax.broadcasted_iota(jnp.int32, (ROW_TILE, T), 1)
        same = owner_of(t_i + z * T) == owner_of(u_i + z * T)
        mask[pl.ds(r0, ROW_TILE), :] = low_cast((same & (u_i <= t_i)).astype(jnp.float32))
        mask_t[pl.ds(r0, ROW_TILE), :] = low_cast((same & (u_i >= t_i)).astype(jnp.float32))
        return carry

    lax.fori_loop(0, T // ROW_TILE, fill_masks, 0)

    sq_lane = lax.broadcasted_iota(jnp.int32, (LANES, LANES), 1)
    ones_lane = ((half_lane == HD) | (half_lane == HD + 1)).astype(jnp.float32)

    def softplus(v):
        return jnp.maximum(v, 0.0) + jnp.log1p(jnp.exp(-jnp.abs(v)))

    def slab(p, part):
        return p // 2, slice(None), pl.ds(pl.multiple_of(part * WIDE + (p % 2) * LANES, LANES), LANES)

    def pair_cols(p):
        return pl.ds(pl.multiple_of(p * LANES, LANES), LANES)

    def split(value):
        swapped = swap_halves(value)
        return jnp.where(half_lane < HD, value, swapped), jnp.where(half_lane < HD, swapped, value)

    def join(left, right):
        return jnp.where(half_lane < HD, left, swap_halves(right))

    def pack_states(p, left, right, own, n_ones):
        place = pl.ds(pl.multiple_of((p % 2) * LANES, LANES), LANES)
        own[p // 2, place, :] = low_cast(jnp.where(sq_lane < HD, left, swap_halves(right)))
        for side, part in ((0, left), (1, right)):
            column = part[:, HD : HD + 1]
            if n_ones == 2:
                column = column + part[:, HD + 1 : HD + 2]
            zcol[...] = jnp.where(sq_lane == 2 * (p % 2) + side, column, zcol[...])

    def exchange(which, own, landed, g):
        target = z + 1 - 2 * which
        target = (target + n_head) % n_head
        return remote(
            own.at[g], landed.at[g], s_send.at[which, g], s_recv.at[which, g], (dp, target)
        )

    def place_of(which):
        return z if which == 0 else n_head - 1 - z

    def send_states(which, own, landed, g):
        own[g, 2 * LANES : STATE_ROWS, :] = low_cast(zcol[...].T[0:16, :])

        @pl.when(place_of(which) == 0)
        def _():
            exchange(which, own, landed, g).start()

    def pass_on(which, own, landed, out, n_ones, point):
        for place in range(1, n_head):
            g = point - place
            if 0 <= g < GROUPS:

                @pl.when(place_of(which) == place)
                def _(g=g, place=place):
                    exchange(which, own, landed, g).wait_recv()
                    state_sum[0:STATE_ROWS, :] = landed[g].astype(jnp.float32)
                    if place < n_head - 1:
                        through = (my_first == next_owner) if which == 0 else (my_last == last_owner)
                        own[g] = low_cast(
                            own[g].astype(jnp.float32)
                            + through.astype(jnp.float32) * state_sum[0:STATE_ROWS, :]
                        )
                        exchange(which, own, landed, g).start()
                    unpack(out, n_ones, g)

    def unpack(out, n_ones, g):
        columns = state_sum[2 * LANES : 3 * LANES, :].T
        wide = (sq_lane >= HD) & (sq_lane < HD + n_ones)
        for i in range(2):
            packed = state_sum[i * LANES : (i + 1) * LANES, :]
            for side in (0, 1):
                part = packed if side == 0 else swap_halves(packed)
                column = columns[:, 2 * i + side : 2 * i + side + 1]
                out[4 * g + 2 * i + side] = low_cast(
                    jnp.where(sq_lane < HD, part, jnp.where(wide, column, 0.0))
                )

    def exchange_sent(which, own, landed):
        @pl.when(place_of(which) < n_head - 1)
        def _():
            for g in range(GROUPS):
                exchange(which, own, landed, g).wait_send()

    state_sum[...] = jnp.zeros_like(state_sum)
    state_h[...] = jnp.zeros_like(state_h)
    back_h[...] = jnp.zeros_like(back_h)

    def pass_forward(point):
        pass_on(0, state_own, state_in, state_h, 2, point)

    def pass_backward(point):
        pass_on(1, back_own, back_in, back_h, 1, point)

    zcol[...] = jnp.zeros_like(zcol)

    def features_of(p, part, store):
        cs = cs_ref[...]
        left, right = split(softplus(mixed[slab(p, part)].astype(jnp.float32)))
        store[2 * p] = low_cast(left * cs)
        store[2 * p + 1] = low_cast(right * cs)

    def make_keys(p, carry):
        features_of(p, 1, feat_k)
        v_pair = mixed[slab(p, 2)].astype(jnp.float32)
        val_a[2 * p] = low_cast(jnp.where(half_lane < HD, v_pair, ones_lane))
        val_a[2 * p + 1] = low_cast(jnp.where(half_lane < HD, swap_halves(v_pair), ones_lane))
        left = mm_rows(feat_k[2 * p] * keeps[0], val_a[2 * p])
        right = mm_rows(feat_k[2 * p + 1] * keeps[0], val_a[2 * p + 1])
        pack_states(p, left, right, state_own, 1)
        return carry

    def make_queries(p, carry):
        features_of(p, 0, feat_q)
        return carry

    load_tok.wait()
    for g in range(GROUPS):
        gather_until(g)
        part = mm(tok[...], w_qkv[g].reshape(D, D))
        mixed[g, :, 0:WIDE] = low_cast(part[:, 0:WIDE] + vec_ref[6:7, g * WIDE : (g + 1) * WIDE])
        mixed[g, :, WIDE : 2 * WIDE] = low_cast(
            part[:, WIDE : 2 * WIDE] + vec_ref[7:8, g * WIDE : (g + 1) * WIDE]
        )
        mixed[g, :, 2 * WIDE :] = low_cast(part[:, 2 * WIDE :])
        lax.fori_loop(2 * g, 2 * g + 2, make_keys, 0)
        send_states(0, state_own, state_in, g)
        if g:
            pass_forward(g)

    def local_attend(h, carry):
        scores = low_cast(mm_cols(feat_q[h], feat_k[h])) * mask[...]
        num_a[h] = mm(scores, val_a[h])
        return carry

    gather_step()
    for part in range(3):
        lax.fori_loop(2 * part, 2 * part + 2, make_queries, 0)
        lax.fori_loop(4 * part, 4 * part + 4, local_attend, 0)
        gather_step()
        pass_forward(3 + part)

    def finish_heads(p, carry):
        att = []
        for side in (0, 1):
            h = 2 * p + side
            whole = num_a[h] + mm(feat_q[h] * keeps[2], state_h[h])
            den = whole[:, HD : HD + 1] + (1.0 - live_ref[...])
            inverse = 1.0 / den
            got = whole * inverse
            num_a[h] = jnp.where(half_lane < HD, got, inverse)
            att.append(got)
        shift = vec_ref[8:9, pair_cols(p)]
        heads[:, pair_cols(p)] = low_cast(join(att[0], att[1]) + shift * live_ref[...])
        return carry

    for g in range(GROUPS):
        lax.fori_loop(2 * g, 2 * g + 2, finish_heads, 0)

    gather_until(GROUPS)

    def tile_rows(i):
        return slice(i * ROW_TILE, (i + 1) * ROW_TILE)

    def first_norm(i, carry):
        r = tile_rows(i)
        w = w_out[...].reshape(D, D)
        residual = tok[r, :].astype(jnp.float32) + (mm(heads[r, :], w) + vec_ref[4:5, :])
        normed, rstd = norm_rows(residual)
        norm_one[r, :] = normed
        rstd_one[r, :] = jnp.broadcast_to(rstd, (ROW_TILE, LANES))
        hidden = normed * vec_ref[0:1, :] + vec_ref[1:2, :]
        hid[r, :] = hidden
        hid_low[r, :] = low_cast(hidden)
        return carry

    while any(act_of is g_own for acts in plan for act_of, _ in acts):
        gather_step()
    load_cot.start()
    over_rows(T // ROW_TILE, first_norm, 0)

    for j in range(TILES):
        if j % 2 == 0:
            gather_until(GROUPS + 1 + j // 2)

        def ff_up(i, carry, j=j):
            r = tile_rows(i)
            upper = mm(hid_low[r, :], w_up[j].reshape(D, D)) + vec_ref[9 + j : 10 + j, :]
            value, slope = gelu_parts(upper)
            act[r, j * D : (j + 1) * D] = low_cast(value)
            gel[r, j * D : (j + 1) * D] = low_cast(slope)
            return carry

        over_rows(T // ROW_TILE, ff_up, 0)
        gather_step()

    gather_until(GATHERS - 2)
    gather_until(GATHERS - 1)
    load_cot.wait()

    def second_norm(i, sums):
        r = tile_rows(i)
        lowered = mm(act[r, :], w_down[...].reshape(FF, D))
        normed, rstd = norm_rows(hid[r, :] + (lowered + vec_ref[5:6, :]))
        one_low[r, :] = low_cast(normed * vec_ref[2:3, :] + vec_ref[3:4, :])
        dy = ig_ref[r, :]
        d_two = norm_rows_back(dy, normed, rstd, vec_ref[2:3, :])
        hid[r, :] = d_two
        two_low[r, :] = low_cast(d_two)
        return sums[0] + row_sum(dy * normed), sums[1] + row_sum(dy), sums[2] + row_sum(d_two)

    zero_row = jnp.zeros((1, D), jnp.float32)
    gain_two, shift_two, bias_down = over_rows(
        T // ROW_TILE, second_norm, (zero_row, zero_row, zero_row)
    )
    save_y.start()
    vg_ref[2:3, :] = gain_two
    vg_ref[3:4, :] = shift_two
    vg_ref[5:6, :] = bias_down

    for j in range(TILES):

        def ff_back(i, total, j=j):
            r = tile_rows(i)
            d_act = mm_cols(two_low[r, :], w_down[j // 2, j % 2].reshape(D, D))
            d_upper = d_act * gel[r, j * D : (j + 1) * D].astype(jnp.float32)
            gel[r, j * D : (j + 1) * D] = low_cast(d_upper)
            return total + row_sum(d_upper)

        vg_ref[9 + j : 10 + j, :] = over_rows(T // ROW_TILE, ff_back, zero_row)

    for g in (GATHERS - 2, GATHERS - 1):
        g_sent(g)
    for j in range(TILES):
        got = low_cast(mm_rows(act[:, j * D : (j + 1) * D], two_low[...]))
        w_down[j // 2, j % 2] = got.reshape(2, TILES * rows, D)
    for k in range(UP):
        reduce_start(k)

    save_y.wait()

    def first_norm_back(i, sums):
        r = tile_rows(i)
        dy = hid[r, :]
        for j in range(TILES):
            dy = dy + mm_cols(gel[r, j * D : (j + 1) * D], w_up[j].reshape(D, D))
        normed = norm_one[r, :]
        d_one = norm_rows_back(dy, normed, rstd_one[r, 0:1], vec_ref[0:1, :])
        ig_ref[r, :] = d_one
        one_low[r, :] = low_cast(d_one)
        return sums[0] + row_sum(dy * normed), sums[1] + row_sum(dy), sums[2] + row_sum(d_one)

    sums = (zero_row, zero_row, zero_row)
    steps = T // ROW_TILE
    sums = over_rows(steps // 2, first_norm_back, sums)
    reduce_tick()
    sums = over_rows(steps, first_norm_back, sums, steps // 2)
    reduce_tick()
    vg_ref[0:1, :] = sums[0]
    vg_ref[1:2, :] = sums[1]
    vg_ref[4:5, :] = sums[2]

    d_heads = two_low
    d_heads[...] = low_cast(mm_cols(one_low[...], w_out[...].reshape(D, D)))

    zcol[...] = jnp.zeros_like(zcol)

    def grad_slot(h):
        return slice(None), pl.ds(pl.multiple_of(h * LANES, LANES), LANES)

    def back_states(p, carry):
        g_pair = d_heads[:, pair_cols(p)].astype(jnp.float32)
        parts = []
        for side in (0, 1):
            h = 2 * p + side
            saved = num_a[h]
            g = g_pair if side == 0 else swap_halves(g_pair)
            gn = jnp.where(half_lane < HD, g * swap_halves(saved), 0.0)
            gd = -jnp.sum(gn * saved, axis=1, keepdims=True)
            gd_high = low_cast(gd).astype(jnp.float32)
            gn = jnp.where(
                half_lane == HD, gd_high, jnp.where(half_lane == HD + 1, gd - gd_high, gn)
            )
            gn = low_cast(gn)
            act[grad_slot(h)] = gn
            parts.append(mm_rows(feat_q[h] * keeps[1], gn))
        pack_states(p, parts[0], parts[1], back_own, 2)
        return carry

    for g in range(GROUPS):
        lax.fori_loop(2 * g, 2 * g + 2, back_states, 0)
        send_states(1, back_own, back_in, g)
        if g:
            pass_backward(g)
        if g == 1:
            reduce_tick()

    for g in range(GROUPS + 1, GATHERS - 2):
        g_sent(g)
    turned[...] = hid_low[...].T
    for j in range(TILES):
        got = low_cast(mm(turned[...], gel[:, j * D : (j + 1) * D]))
        w_up[j] = got.reshape(2, 2, 2, rows, D)
        reduce_start(UP + j)
    reduce_tick()
    g_sent(GROUPS)
    w_out[...] = low_cast(mm_rows(heads[...], one_low[...])).reshape(2, 2, 2, rows, D)
    reduce_start(OUT)
    pass_backward(3)

    def sigmoid(v):
        e = jnp.exp(-jnp.abs(v))
        return jnp.where(v >= 0, 1.0, e) / (1.0 + e)

    def fold(value):
        value = value * cs_ref[...]
        return value + swap_halves(value)

    def through_features(p, part, left, right):
        value = mixed[slab(p, part)].astype(jnp.float32)
        d_part = sigmoid(value) * jnp.where(half_lane < HD, fold(left), fold(right))
        mixed[slab(p, part)] = low_cast(d_part)
        vg_ref[6 + part : 7 + part, pair_cols(p)] = row_sum(d_part)

    def query_back(p, carry):
        got = []
        for side in (0, 1):
            h = 2 * p + side
            ga = act[grad_slot(h)]
            d_scores = low_cast(mm_cols(ga, val_a[h])) * mask[...]
            got.append(mm(d_scores, feat_k[h]) + mm_cols(ga * keeps[2], state_h[h]))
        through_features(p, 0, got[0], got[1])
        return carry

    for part in range(3):
        lax.fori_loop(2 * part, 2 * part + 2, query_back, 0)
        if part == 0:
            pass_backward(4)
        if part == 1:
            reduce_tick()
            pass_backward(5)

    def key_value_back(p, carry):
        keys, values = [], []
        for side in (0, 1):
            h = 2 * p + side
            fq, fk, va, ga = feat_q[h], feat_k[h], val_a[h], act[grad_slot(h)]
            d_scores_t = low_cast(mm_cols(va, ga)) * mask_t[...]
            keys.append(mm(d_scores_t, fq) + mm_cols(va * keeps[3], back_h[h]))
            scores_t = low_cast(mm_cols(fk, fq)) * mask_t[...]
            values.append(mm(scores_t, ga) + mm(fk * keeps[3], back_h[h]))
        through_features(p, 1, keys[0], keys[1])
        d_part = join(values[0], values[1])
        mixed[slab(p, 2)] = low_cast(d_part)
        vg_ref[8:9, pair_cols(p)] = row_sum(d_part)
        return carry

    turned[...] = tok[...].T
    for g in range(GROUPS):
        lax.fori_loop(2 * g, 2 * g + 2, key_value_back, 0)
        ig_ref[...] += mm_cols(mixed[g], w_qkv[g].reshape(D, D))
        g_sent(g)
        w_qkv[g] = low_cast(mm(turned[...], mixed[g])).reshape(2, 2, 2, rows, D)
        reduce_start(MIX + g)
        reduce_tick()

    def vcopy(level):
        target = (sib, xn, yn, z_one, z_two)[level]
        return remote(vg_ref, vec_land.at[level], v_send.at[level], v_recv.at[level], target)

    vg_ref[13:16, :] = jnp.zeros((3, D), jnp.float32)
    vcopy(0).start()
    for level in range(5):
        reduce_tick()
        vcopy(level).wait()
        vg_ref[...] += vec_land[level]
        if level < 4:
            vcopy(level + 1).start()
    while r_plan:
        reduce_tick()
    for k in range(UNITS):
        r_end(k)
    exchange_sent(0, state_own, state_in)
    exchange_sent(1, back_own, back_in)


GATHER_AHEAD = 3


def fits(mesh):
    return mesh.shape["dp"] == 8 and mesh.shape["head"] == 4


def fused_layer(lengths, tokens, cotangent, masters, vector_master):
    n_head = lax.axis_size("head")
    T = tokens.shape[0]
    rows = masters[1].shape[0]
    bf, f32 = jnp.bfloat16, jnp.float32
    V, S = pltpu.VMEM, jax.ShapeDtypeStruct
    vm, anywhere = pl.BlockSpec(memory_space=pltpu.VMEM), pl.BlockSpec(memory_space=pl.ANY)
    out_shape = (S((T, D), bf), S((T, D), f32)) + tuple(S(m.shape, bf) for m in masters)
    out_shape += (S((16, D), f32),)
    shard = (2, 2, 2, rows, D)
    scratch = [
        V((GROUPS, *shard), bf),
        V(shard, bf),
        V((TILES, *shard), bf),
        V((2, 2, 2, TILES * rows, D), bf),
        V((T, D), bf),
        V((GROUPS, T, D), bf),
        V((H, T, LANES), bf),
        V((H, T, LANES), bf),
        V((H, T, LANES), bf),
        V((H, T, LANES), f32),
        V((T, D), bf),
        V((T, D), f32),
        V((T, LANES), f32),
        V((T, D), f32),
        V((T, D), bf),
        V((D, T), bf),
        V((T, FF), bf),
        V((T, FF), bf),
        V((T, D), bf),
        V((T, D), bf),
        V((T, T), bf),
        V((T, T), bf),
        V((T, LANES), f32),
        V((T, LANES), f32),
        V((4, T, LANES), bf),
        V((GROUPS, STATE_ROWS, LANES), bf),
        V((GROUPS, STATE_ROWS, LANES), bf),
        V((GROUPS, STATE_ROWS, LANES), bf),
        V((GROUPS, STATE_ROWS, LANES), bf),
        V((3 * LANES, LANES), f32),
        V((H, LANES, LANES), bf),
        V((H, LANES, LANES), bf),
        V((LANES, LANES), f32),
        V((UNITS, 2, 2, rows, D), bf),
        V((UNITS, 2, 2, rows // 2, D), bf),
        V((UNITS, 2, rows // 2, D), bf),
        V((UNITS, 2, rows, D), bf),
        V((5, 16, D), f32),
        pltpu.SemaphoreType.DMA((18,)),
        pltpu.SemaphoreType.DMA((8, 17)),
        pltpu.SemaphoreType.DMA((8, 17)),
        pltpu.SemaphoreType.DMA((2, GROUPS)),
        pltpu.SemaphoreType.DMA((2, GROUPS)),
        pltpu.SemaphoreType.DMA((UNITS, 13)),
        pltpu.SemaphoreType.DMA((UNITS, 13)),
        pltpu.SemaphoreType.DMA((5,)),
        pltpu.SemaphoreType.DMA((5,)),
    ]
    return pl.pallas_call(
        functools.partial(layer_kernel, n_head, lengths.shape[0]),
        out_shape=out_shape,
        in_specs=[pl.BlockSpec(memory_space=pltpu.SMEM)] + [anywhere] * 6 + [vm],
        out_specs=[anywhere, vm] + [anywhere] * 4 + [vm],
        scratch_shapes=scratch,
        compiler_params=pltpu.CompilerParams(
            collective_id=0, has_side_effects=True, vmem_limit_bytes=VMEM_BYTES
        ),
        name="layer",
    )(lengths, tokens, cotangent, *masters, vector_master)


VMEM_BYTES = 63 * 1024 * 1024


def fused_shards(
    tokens,
    cotangent,
    lengths,
    qkv_master,
    out_master,
    up_master,
    down_master,
    vector_master,
    qkv_first,
    qkv_second,
    out_first,
    out_second,
    up_first,
    up_second,
    down_first,
    down_second,
    vector_first,
    vector_second,
):
    masters = (qkv_master, out_master, up_master, down_master)
    output, input_grad, *grads, vector_grad = fused_layer(
        lengths, tokens, cotangent, masters, vector_master
    )
    rates = (1.0 / math.sqrt(D), 1.0 / math.sqrt(OUT_FAN), 1.0 / math.sqrt(D), 1.0 / math.sqrt(FF))
    firsts = (qkv_first, out_first, up_first, down_first)
    seconds = (qkv_second, out_second, up_second, down_second)
    news = []
    for i in range(4):
        news.extend(
            adam_update(
                masters[i],
                firsts[i],
                seconds[i],
                grads[i].astype(jnp.float32),
                rates[i],
                weight_decay,
            )
        )
    vector_new = adam_update(
        vector_master, vector_first, vector_second, vector_grad[:13], vector_rate, 0.0
    )
    return (output, input_grad, *news, *vector_new)


def solution(mesh):
    return jax.shard_map(
        fused_shards if fits(mesh) else shards,
        mesh=mesh,
        in_specs=(
            P(("dp", "head"), None),
            P(("dp", "head"), None),
            P("dp"),
            P("dp", None),
            P("dp", None),
            P("dp", None),
            P("dp", None),
            P(),
            P("dp", None),
            P("dp", None),
            P("dp", None),
            P("dp", None),
            P("dp", None),
            P("dp", None),
            P("dp", None),
            P("dp", None),
            P(),
            P(),
        ),
        out_specs=(
            P(("dp", "head"), None),
            P(("dp", "head"), None),
            P("dp", None),
            P("dp", None),
            P("dp", None),
            P("dp", None),
            P("dp", None),
            P("dp", None),
            P("dp", None),
            P("dp", None),
            P("dp", None),
            P("dp", None),
            P("dp", None),
            P("dp", None),
            P(),
            P(),
            P(),
        ),
        check_vma=False,
    )
```

```python
import functools
import math

import jax
import jax.numpy as jnp
from jax import lax
from jax.experimental import pallas as pl
from jax.experimental.pallas import tpu as pltpu
from jax.sharding import PartitionSpec as P

D = 768
H = 12
HD = 64
FF = 3072
SPAN = 64
STEP = 10
OUT_FAN = 1


highest = lax.Precision.HIGHEST
norm_epsilon = 1e-05
first_decay = 0.9
second_decay = 0.999
adam_epsilon = 1e-08
weight_decay = 0.01
vector_rate = 0.2


def layer_norm(residual, gain_row, shift_row):
    center = residual - jnp.mean(residual, axis=-1, keepdims=True)
    spread = jnp.mean(center * center, axis=-1, keepdims=True)
    return center * lax.rsqrt(spread + norm_epsilon) * gain_row + shift_row


def exact_gelu(upper_pre):
    return jax.nn.gelu(upper_pre, approximate=False)


def group_layout(group_lengths, row_count):
    slot_sizes = (group_lengths + SPAN - 1) // SPAN * SPAN
    slot_ends = jnp.cumsum(slot_sizes)
    slot_starts = slot_ends - slot_sizes
    positions = jnp.arange(row_count, dtype=jnp.int32)
    member = (positions[:, None] >= slot_starts[None, :]) & (
        positions[:, None] < slot_ends[None, :]
    )
    seq_first = jnp.sum(jnp.where(member, slot_starts[None, :], 0), axis=1)
    length = jnp.sum(jnp.where(member, group_lengths[None, :], 0), axis=1)
    seq_numbers = jnp.arange(group_lengths.shape[0], dtype=jnp.int32)
    owners = jnp.sum(jnp.where(member, seq_numbers[None, :], 0), axis=1)
    offset = positions - seq_first
    live_rows = (offset < length).astype(jnp.float32)
    angles = 0.5 * math.pi * offset.astype(jnp.float32) / length.astype(jnp.float32)
    cosine = jnp.cos(angles)
    sine_part = jnp.sin(angles)
    span_owner = owners[::SPAN]
    span_order = jnp.arange(span_owner.shape[0], dtype=jnp.int32)
    same_seq = span_owner[None, :] == span_owner[:, None]
    earlier = (same_seq & (span_order[None, :] < span_order[:, None])).astype(jnp.float32)
    return (cosine, sine_part, live_rows, earlier)


def attend(query_rows, key_rows, value_rows, cosine, sine_part, live_rows, earlier):
    row_count = query_rows.shape[0]
    blocks = row_count // SPAN
    soft_query = jax.nn.softplus(query_rows)
    soft_key = jax.nn.softplus(key_rows)
    feat_query = (
        jnp.concatenate([soft_query * cosine[:, None], soft_query * sine_part[:, None]], axis=1)
        * live_rows[:, None]
    )
    feat_key = (
        jnp.concatenate([soft_key * cosine[:, None], soft_key * sine_part[:, None]], axis=1)
        * live_rows[:, None]
    )
    block_query = feat_query.reshape(blocks, SPAN, -1)
    block_key = feat_key.reshape(blocks, SPAN, -1)
    block_value = value_rows.reshape(blocks, SPAN, -1)
    lower_mask = (jnp.arange(SPAN)[:, None] >= jnp.arange(SPAN)[None, :]).astype(jnp.float32)
    scores = jnp.einsum("cik,cjk->cij", block_query, block_key, precision=highest) * lower_mask
    inner_sum = jnp.einsum("cij,cjd->cid", scores, block_value, precision=highest)
    inner_den = jnp.sum(scores, axis=2)
    states = jnp.einsum("cjk,cjd->ckd", block_key, block_value, precision=highest)
    key_sums = jnp.sum(block_key, axis=1)
    before = jnp.einsum("ce,ekd->ckd", earlier, states, precision=highest)
    before_sums = jnp.einsum("ce,ek->ck", earlier, key_sums, precision=highest)
    outer_sum = jnp.einsum("cik,ckd->cid", block_query, before, precision=highest)
    outer_den = jnp.einsum("cik,ck->ci", block_query, before_sums, precision=highest)
    numerator = (inner_sum + outer_sum).reshape(row_count, -1)
    denominator = (inner_den + outer_den).reshape(row_count) + (1.0 - live_rows)
    return numerator / denominator[:, None]


def contract_rows(left, right):
    return lax.dot_general(
        left, right, (((0,), (0,)), ((), ())), preferred_element_type=jnp.float32
    )


def contract_cols(left, right):
    return lax.dot_general(
        left, right, (((1,), (1,)), ((), ())), preferred_element_type=jnp.float32
    )


def adam_update(master, first, second, gradient, rate, decay):
    first_new = first_decay * first + (1.0 - first_decay) * gradient
    second_new = second_decay * second + (1.0 - second_decay) * gradient * gradient
    first_hat = first_new / (1.0 - first_decay**STEP)
    second_hat = second_new / (1.0 - second_decay**STEP)
    master_new = master - rate * (
        first_hat / (jnp.sqrt(second_hat) + adam_epsilon) + decay * master
    )
    return (first_new, second_new, master_new)


def shards(
    tokens,
    cotangent,
    lengths,
    qkv_master,
    out_master,
    up_master,
    down_master,
    vector_master,
    qkv_first,
    qkv_second,
    out_first,
    out_second,
    up_first,
    up_second,
    down_first,
    down_second,
    vector_first,
    vector_second,
):
    mix_weight, out_weight, up_weight, down_weight = (
        lax.all_gather(qkv_master.astype(jnp.bfloat16), "dp", axis=0, tiled=True),
        lax.all_gather(out_master.astype(jnp.bfloat16), "dp", axis=0, tiled=True),
        lax.all_gather(up_master.astype(jnp.bfloat16), "dp", axis=0, tiled=True),
        lax.all_gather(down_master.astype(jnp.bfloat16), "dp", axis=0, tiled=True),
    )
    tok_count = tokens.shape[0]
    width = tokens.shape[1]
    mixed_all = jnp.dot(tokens, mix_weight, preferred_element_type=jnp.float32) + vector_master[
        6:9
    ].reshape(-1)
    mixed_low = mixed_all.astype(jnp.bfloat16)
    query_part = mixed_low[:, :width].reshape(tok_count, H, 1, HD)
    key_part = mixed_low[:, width : 2 * width].reshape(tok_count, H, 1, HD)
    paired = jnp.concatenate([query_part, key_part], axis=2)
    paired = jnp.repeat(paired[:, :, None], 2, axis=2).reshape(tok_count, 4 * width)
    value_part = mixed_low[:, 2 * width :]
    paired_in, values_in = (
        lax.all_to_all(paired, "head", split_axis=1, concat_axis=0, tiled=True),
        lax.all_to_all(value_part, "head", split_axis=1, concat_axis=0, tiled=True),
    )
    group_rows = paired_in.shape[0]
    item_count = paired_in.shape[1] // (2 * HD)
    cosine, sine_part, live_rows, earlier = group_layout(lengths, group_rows)
    stacked = paired_in.reshape(group_rows, item_count, 2, HD).astype(jnp.float32)
    query_items = stacked[:, :, 0]
    key_items = stacked[:, :, 1]
    value_items = values_in.reshape(group_rows, item_count, HD // 2).astype(jnp.float32)

    def mix_items(query_set, key_set, value_set):

        def single(query_rows, key_rows, value_rows):
            return attend(query_rows, key_rows, value_rows, cosine, sine_part, live_rows, earlier)

        return jax.vmap(single, in_axes=1, out_axes=1)(query_set, key_set, value_set)

    attended, mix_back = jax.vjp(mix_items, query_items, key_items, value_items)
    heads_out = attended.reshape(group_rows, item_count * (HD // 2)).astype(jnp.bfloat16)
    heads = lax.all_to_all(heads_out, "head", split_axis=0, concat_axis=1, tiled=True)
    projected = jnp.dot(heads, out_weight, preferred_element_type=jnp.float32) + vector_master[4]
    resid_one = tokens.astype(jnp.float32) + projected
    hidden, norm_one_back = jax.vjp(layer_norm, resid_one, vector_master[0], vector_master[1])
    hidden_low = hidden.astype(jnp.bfloat16)
    upper_pre = jnp.dot(hidden_low, up_weight, preferred_element_type=jnp.float32) + vector_master[
        9:13
    ].reshape(-1)
    active, gelu_back = jax.vjp(exact_gelu, upper_pre)
    active_low = active.astype(jnp.bfloat16)
    lowered = (
        jnp.dot(active_low, down_weight, preferred_element_type=jnp.float32) + vector_master[5]
    )
    output, norm_two_back = jax.vjp(
        layer_norm, hidden + lowered, vector_master[2], vector_master[3]
    )
    grad_two, gain_two, shift_two = norm_two_back(cotangent)
    grad_two_low = grad_two.astype(jnp.bfloat16)
    down_grad = contract_rows(active_low, grad_two_low)
    (upper_grad,) = gelu_back(contract_cols(grad_two_low, down_weight))
    upper_low = upper_grad.astype(jnp.bfloat16)
    up_grad = contract_rows(hidden_low, upper_low)
    hidden_grad = grad_two + contract_cols(upper_low, up_weight)
    grad_one, gain_one, shift_one = norm_one_back(hidden_grad)
    grad_one_low = grad_one.astype(jnp.bfloat16)
    out_grad = contract_rows(heads, grad_one_low)
    heads_grad = contract_cols(grad_one_low, out_weight).astype(jnp.bfloat16)
    heads_back = lax.all_to_all(heads_grad, "head", split_axis=1, concat_axis=0, tiled=True)
    query_back, key_back, value_back = mix_back(
        heads_back.reshape(group_rows, item_count, HD // 2).astype(jnp.float32)
    )
    pair_back = (
        jnp.stack([query_back, key_back], axis=2)
        .astype(jnp.bfloat16)
        .reshape(group_rows, item_count * 2 * HD)
    )
    value_low = value_back.astype(jnp.bfloat16).reshape(group_rows, item_count * (HD // 2))
    pair_home, value_home = (
        lax.all_to_all(pair_back, "head", split_axis=0, concat_axis=1, tiled=True),
        lax.all_to_all(value_low, "head", split_axis=0, concat_axis=1, tiled=True),
    )
    summed = jnp.sum(pair_home.astype(jnp.float32).reshape(tok_count, H, 2, 2, HD), axis=2)
    mixed_grad = jnp.concatenate(
        [
            summed[:, :, 0].reshape(tok_count, width),
            summed[:, :, 1].reshape(tok_count, width),
            value_home.astype(jnp.float32),
        ],
        axis=1,
    )
    mixed_low_grad = mixed_grad.astype(jnp.bfloat16)
    mix_grad = contract_rows(tokens, mixed_low_grad)
    input_grad = grad_one + contract_cols(mixed_low_grad, mix_weight)
    vector_grad = jnp.concatenate(
        [
            jnp.stack(
                [
                    gain_one,
                    shift_one,
                    gain_two,
                    shift_two,
                    jnp.sum(grad_one, axis=0),
                    jnp.sum(grad_two, axis=0),
                ]
            ),
            jnp.sum(mixed_grad, axis=0).reshape(3, width),
            jnp.sum(upper_grad, axis=0).reshape(4, width),
        ],
        axis=0,
    )
    local_grads = (mix_grad, out_grad, up_grad, down_grad)
    row_parts = (
        lax.psum_scatter(
            local_grads[0].astype(jnp.bfloat16), "dp", scatter_dimension=0, tiled=True
        ).astype(jnp.float32),
        lax.psum_scatter(
            local_grads[1].astype(jnp.bfloat16), "dp", scatter_dimension=0, tiled=True
        ).astype(jnp.float32),
        lax.psum_scatter(
            local_grads[2].astype(jnp.bfloat16), "dp", scatter_dimension=0, tiled=True
        ).astype(jnp.float32),
        lax.psum_scatter(
            local_grads[3].astype(jnp.bfloat16), "dp", scatter_dimension=0, tiled=True
        ).astype(jnp.float32),
    )
    reduced = (
        lax.psum(row_parts[0].astype(jnp.bfloat16), "head").astype(jnp.float32),
        lax.psum(row_parts[1].astype(jnp.bfloat16), "head").astype(jnp.float32),
        lax.psum(row_parts[2].astype(jnp.bfloat16), "head").astype(jnp.float32),
        lax.psum(row_parts[3].astype(jnp.bfloat16), "head").astype(jnp.float32),
    )
    vector_total = lax.psum(vector_grad, ("dp", "head"))
    qkv_new = adam_update(
        qkv_master, qkv_first, qkv_second, reduced[0], 1.0 / math.sqrt(D), weight_decay
    )
    out_new = adam_update(
        out_master, out_first, out_second, reduced[1], 1.0 / math.sqrt(OUT_FAN), weight_decay
    )
    up_new = adam_update(
        up_master, up_first, up_second, reduced[2], 1.0 / math.sqrt(D), weight_decay
    )
    down_new = adam_update(
        down_master, down_first, down_second, reduced[3], 1.0 / math.sqrt(FF), weight_decay
    )
    vector_new = adam_update(
        vector_master, vector_first, vector_second, vector_total, vector_rate, 0.0
    )
    return (
        output.astype(jnp.bfloat16),
        input_grad,
        qkv_new[0],
        qkv_new[1],
        qkv_new[2],
        out_new[0],
        out_new[1],
        out_new[2],
        up_new[0],
        up_new[1],
        up_new[2],
        down_new[0],
        down_new[1],
        down_new[2],
        vector_new[0],
        vector_new[1],
        vector_new[2],
    )


PAIRS = H // 2
LANES = 2 * HD
GROUPS = 3
STATE_ROWS = (PAIRS // GROUPS) * LANES + 16
WIDE = D // GROUPS
TILES = FF // D
ROW_TILE = 256
MESH = pl.DeviceIdType.MESH
DOWN, UP, OUT, MIX = 0, TILES, 2 * TILES, 2 * TILES + 1
UNITS = 2 * TILES + 1 + GROUPS


def mm(left, right):
    return jnp.dot(left, right, preferred_element_type=jnp.float32)


def mm_cols(left, right):
    return lax.dot_general(
        left, right, (((1,), (1,)), ((), ())), preferred_element_type=jnp.float32
    )


def mm_rows(left, right):
    return lax.dot_general(
        left, right, (((0,), (0,)), ((), ())), preferred_element_type=jnp.float32
    )


def swap_halves(slab):
    return pltpu.roll(slab, HD, 1)


def low_cast(value):
    return value.astype(jnp.bfloat16)


def row_sum(value):
    return jnp.sum(value, axis=0, keepdims=True)


def gelu_parts(z):
    x = jnp.abs(z) * (1.0 / math.sqrt(2.0))
    t = 1.0 / (1.0 + 0.3275911 * x)
    bell = jnp.exp(-0.5 * z * z)
    poly = t * (
        0.254829592
        + t * (-0.284496736 + t * (1.421413741 + t * (-1.453152027 + t * 1.061405429)))
    )
    upper_tail = 0.5 * poly * bell
    phi = jnp.where(z >= 0, 1.0 - upper_tail, upper_tail)
    return z * phi, phi + z * (bell * (1.0 / math.sqrt(2.0 * math.pi)))


def over_rows(count, body, carry, start=0):
    for i in range(start, count):
        carry = body(i, carry)
    return carry


def norm_rows(residual):
    center = residual - jnp.mean(residual, axis=-1, keepdims=True)
    rstd = lax.rsqrt(jnp.mean(center * center, axis=-1, keepdims=True) + norm_epsilon)
    return center * rstd, rstd


def norm_rows_back(dy, normed, rstd, gain):
    e = dy * gain
    return rstd * (
        e
        - jnp.mean(e, axis=-1, keepdims=True)
        - normed * jnp.mean(e * normed, axis=-1, keepdims=True)
    )


def layer_kernel(
    n_head,
    n_seq,
    lens_ref,
    tok_hbm,
    cot_hbm,
    qkv_f,
    out_f,
    up_f,
    down_f,
    vec_ref,
    y_hbm,
    ig_ref,
    g_qkv,
    g_out,
    g_up,
    g_down,
    vg_ref,
    w_qkv,
    w_out,
    w_up,
    w_down,
    tok,
    mixed,
    feat_q,
    feat_k,
    val_a,
    num_a,
    heads,
    norm_one,
    rstd_one,
    hid,
    hid_low,
    turned,
    act,
    gel,
    two_low,
    one_low,
    mask,
    mask_t,
    cs_ref,
    live_ref,
    keeps,
    state_own,
    state_in,
    back_own,
    back_in,
    state_sum,
    state_h,
    back_h,
    zcol,
    red_a,
    red_b,
    red_c,
    red_e,
    vec_land,
    load_sem,
    g_send,
    g_recv,
    s_send,
    s_recv,
    r_send,
    r_recv,
    v_send,
    v_recv,
    free_sem,
):
    T = tok.shape[0]
    rows = w_out.shape[3]
    half = rows // 2
    dp = lax.axis_index("dp")
    z = lax.axis_index("head")
    core = dp % 2
    xx = (dp // 2) % 2
    yy = dp // 4
    color = z % 2
    sib = (dp + 1 - 2 * core, z)
    xn = (dp + 2 - 4 * xx, z)
    yn = (dp + 4 - 8 * yy, z)
    z_one = (dp, z + 1 - 2 * color)
    z_two = (dp, (z + 3 + 2 * color) % n_head)

    def load(i, src, dst):
        return pltpu.make_async_copy(src, dst, load_sem.at[i])

    def spot(ref, i):
        return ref.at[pl.ds(i * rows, rows), :]

    loads = []
    for g in range(GROUPS):
        for part in range(3):
            loads.append(
                load(
                    len(loads),
                    qkv_f.at[:, pl.ds(part * D + g * WIDE, WIDE)],
                    hid.at[pl.ds(g * rows, rows), pl.ds(part * WIDE, WIDE)],
                )
            )
    loads.append(load(len(loads), out_f, spot(hid, GROUPS)))
    for j in range(TILES):
        loads.append(load(len(loads), up_f.at[:, pl.ds(j * D, D)], spot(norm_one, j)))
    loads.append(load(len(loads), down_f, ig_ref.at[pl.ds(0, TILES * rows), :]))
    load_tok = load(len(loads), tok_hbm, tok)
    load_cot = load(len(loads) + 1, cot_hbm, ig_ref)
    save_y = load(len(loads) + 2, one_low, y_hbm)
    for copy in loads:
        copy.start()
    load_tok.start()

    barrier = pltpu.get_barrier_semaphore()
    peers = [sib, xn, yn]
    for k in range(1, n_head):
        peers.append((dp, (z + k) % n_head))
    for peer in peers:
        pl.semaphore_signal(barrier, inc=1, device_id=peer, device_id_type=MESH)

    def remote(src, dst, send, recv, target):
        return pltpu.make_async_remote_copy(
            src_ref=src,
            dst_ref=dst,
            send_sem=send,
            recv_sem=recv,
            device_id=target,
            device_id_type=MESH,
        )

    GATHERS = GROUPS + 1 + TILES // 2 + 2

    def piece(g, y, x, c, which):
        if g < GROUPS:
            ref, size, base = w_qkv.at[g, y, x, c], rows, 0
        elif g == GROUPS:
            ref, size, base = w_out.at[y, x, c], rows, 0
        elif g < GROUPS + 1 + TILES // 2:
            i = g - GROUPS - 1
            if which is None:
                return w_up.at[pl.ds(2 * i, 2), y, x, c]
            return w_up.at[
                pl.ds(2 * i, 2), y, x, c, pl.ds(pl.multiple_of(which * half, half), half), :
            ]
        else:
            i = g - GROUPS - 1 - TILES // 2
            ref, size, base = w_down.at[y, x, c], 2 * rows, 2 * rows * i
        if which is None:
            return ref.at[pl.ds(base, size), :]
        return ref.at[pl.ds(pl.multiple_of(base + which * (size // 2), size // 2), size // 2), :]

    def own_masters(g):
        if g < GROUPS:
            for part in range(3):
                loads[3 * g + part].wait()
            w_qkv[g, yy, xx, core] = low_cast(hid[g * rows : (g + 1) * rows, :])
        elif g == GROUPS:
            loads[9].wait()
            w_out[yy, xx, core] = low_cast(hid[g * rows : (g + 1) * rows, :])
        elif g < GROUPS + 1 + TILES // 2:
            for j in range(2 * (g - GROUPS - 1), 2 * (g - GROUPS)):
                loads[10 + j].wait()
                w_up[j, yy, xx, core] = low_cast(norm_one[j * rows : (j + 1) * rows, :])
        else:
            i = g - GROUPS - 1 - TILES // 2
            if i == 0:
                loads[10 + TILES].wait()
            span = slice(2 * rows * i, 2 * rows * (i + 1))
            w_down[yy, xx, core, span, :] = low_cast(ig_ref[span, :])

    here, mine_x, mine_y, mine_d = (yy, xx), (yy, 1 - xx), (1 - yy, xx), (1 - yy, 1 - xx)

    def gcopy(g, kind, chip, which, target, lands):
        ref = piece(g, chip[0], chip[1], core, which)
        return remote(ref, ref, g_send.at[g, kind], g_recv.at[g, lands], target)

    def landed(g, chip, which, lands):
        gcopy(g, 0, chip, which, sib, lands).wait_recv()

    blocks = ((mine_x, 0), (mine_x, 1), (mine_y, 0), (mine_y, 1), (mine_d, 0), (mine_d, 1))

    def hand_over(g, lands):
        chip, which = blocks[lands]
        gcopy(g, 10 + lands, chip, which, sib, 7 + lands).start()

    def arrived(g, lands):
        chip, which = blocks[lands]
        landed(g, chip, which, lands)

    def g_start(g):
        gcopy(g, 0, here, 0, xn, 0).start()
        gcopy(g, 1, here, 1, yn, 3).start()

        @pl.when(color == 0)
        def _():
            gcopy(g, 2, here, 1, xn, 1).start()
            gcopy(g, 3, here, 0, yn, 2).start()

        gcopy(g, 9, here, None, sib, 6).start()

    def g_own(g):
        own_masters(g)
        g_start(g)

    def g_first(g):
        arrived(g, 0)

        @pl.when(color == 1)
        def _():
            gcopy(g, 4, mine_x, 0, yn, 4).start()

        arrived(g, 3)

        @pl.when(color == 1)
        def _():
            gcopy(g, 5, mine_y, 1, xn, 5).start()

        hand_over(g, 0)
        hand_over(g, 3)

        @pl.when(color == 0)
        def _():
            arrived(g, 1)
            gcopy(g, 6, mine_x, 1, z_one, 1).start()
            arrived(g, 2)
            gcopy(g, 7, mine_y, 0, z_one, 2).start()
            hand_over(g, 1)
            hand_over(g, 2)

    def g_second(g):
        @pl.when(color == 1)
        def _():
            arrived(g, 4)
            gcopy(g, 8, mine_d, 0, z_one, 4).start()
            arrived(g, 5)
            gcopy(g, 16, mine_d, 1, z_one, 5).start()
            hand_over(g, 4)
            hand_over(g, 5)
            arrived(g, 1)
            hand_over(g, 1)
            arrived(g, 2)
            hand_over(g, 2)

    def g_third(g):
        @pl.when(color == 0)
        def _():
            arrived(g, 4)
            hand_over(g, 4)
            arrived(g, 5)
            hand_over(g, 5)

    def g_last(g):
        landed(g, here, None, 6)
        for lands in range(6):
            chip, which = blocks[lands]
            landed(g, chip, which, 7 + lands)

    def g_sent(g):
        def sent(kind, chip, which):
            gcopy(g, kind, chip, which, sib, 0).wait_send()

        sent(0, here, 0)
        sent(1, here, 1)
        sent(9, here, None)
        for lands in range(6):
            sent(10 + lands, *blocks[lands])

        @pl.when(color == 0)
        def _():
            sent(2, here, 1)
            sent(3, here, 0)
            sent(6, mine_x, 1)
            sent(7, mine_y, 0)

        @pl.when(color == 1)
        def _():
            sent(4, mine_x, 0)
            sent(5, mine_y, 1)
            sent(8, mine_d, 0)
            sent(16, mine_d, 1)

    plan = []
    for step in range(GATHERS + 2):
        acts = [(f, step - lag) for f, lag in ((g_third, 2), (g_second, 1), (g_first, 0))]
        acts = [(f, g) for f, g in acts if 0 <= g < GATHERS]
        if step + GATHER_AHEAD < GATHERS:
            acts.append((g_own, step + GATHER_AHEAD))
        plan.append(acts)

    def gather_step():
        if plan:
            for act_of, g in plan.pop(0):
                act_of(g)

    def gather_until(g):
        while any((g_third, g) in acts for acts in plan):
            gather_step()
        g_last(g)

    def unit_ref(k):
        if k < OUT:
            return w_up.at[k - UP]
        if k < MIX:
            return w_out
        return w_qkv.at[k - MIX]

    def own_half(k, y, x):
        return red_a[OUT + k, y, x] if k < UP else unit_ref(k)[y, x, core]

    middle = (z > 0) & (z < n_head - 1)
    top, low_part = pl.ds(0, half), pl.ds(half, half)

    def finals(k):
        if k < UP:
            return [(None, g_down.at[pl.ds(k * rows, rows), :])]
        if k < OUT:
            return [(None, g_up.at[:, pl.ds((k - UP) * D, D)])]
        if k < MIX:
            return [(None, g_out)]
        return [
            (part * WIDE, g_qkv.at[:, pl.ds(part * D + (k - MIX) * WIDE, WIDE)])
            for part in range(3)
        ]

    def r_final(k, i):
        mine = red_a.at[k, yy, xx]
        col, dst = finals(k)[i]
        return mine if col is None else mine.at[:, pl.ds(col, WIDE)], dst

    def r_copy(k, kind):
        mine = red_a.at[k, yy, xx]
        if kind == 0:
            src = red_a.at[UP + k] if k < UP else unit_ref(k).at[:, :, 1 - core]
            dst, target = red_a.at[k], sib
        elif kind == 1:
            src, dst, target = red_a.at[k, :, 1 - xx, top, :], red_b.at[k, 0], xn
        elif kind == 2:
            src, dst, target = red_a.at[k, 1 - yy, :, low_part, :], red_b.at[k, 1], yn
        elif kind == 3:
            src, dst, target = red_a.at[k, 1 - yy, xx, top, :], red_c.at[k, 0], yn
        elif kind == 4:
            src, dst, target = red_a.at[k, yy, 1 - xx, low_part, :], red_c.at[k, 1], xn
        elif kind == 5:
            src, dst, target = mine, red_e.at[k, 0], z_one
        elif kind == 6:
            src, dst, target = mine, red_e.at[k, 1], z_two
        else:
            src, dst = r_final(k, kind - 7)
            target = z_one
        return remote(src, dst, r_send.at[k, kind], r_recv.at[k, kind], target)

    def r_local(k, i):
        src, dst = r_final(k, i)
        return pltpu.make_async_copy(src, dst, r_recv.at[k, 10 + i])

    def added(one, two):
        return low_cast(one.astype(jnp.float32) + two.astype(jnp.float32))

    def r_start(k):
        r_copy(k, 0).start()

    def r_pair(k):
        r_copy(k, 0).wait_recv()
        for y in range(2):
            for x in range(2):
                red_a[k, y, x] = added(own_half(k, y, x), red_a[k, y, x])
        r_copy(k, 1).start()
        r_copy(k, 2).start()
        if k == UP - 1:
            for i in range(UP):
                r_copy(i, 0).wait_send()
            pl.semaphore_signal(free_sem, inc=1, device_id=sib, device_id_type=MESH)

    def r_plane(k):
        r_copy(k, 1).wait_recv()
        red_a[k, 1 - yy, xx, top, :] = added(red_a[k, 1 - yy, xx, top, :], red_b[k, 0, 1 - yy])
        r_copy(k, 3).start()
        r_copy(k, 2).wait_recv()
        red_a[k, yy, 1 - xx, low_part, :] = added(
            red_a[k, yy, 1 - xx, low_part, :], red_b[k, 1, 1 - xx]
        )
        r_copy(k, 4).start()
        red_a[k, yy, xx, top, :] = added(red_a[k, yy, xx, top, :], red_b[k, 0, yy])
        red_a[k, yy, xx, low_part, :] = added(red_a[k, yy, xx, low_part, :], red_b[k, 1, xx])

    def r_whole(k):
        r_copy(k, 3).wait_recv()
        r_copy(k, 4).wait_recv()
        red_a[k, yy, xx, top, :] = added(red_a[k, yy, xx, top, :], red_c[k, 0])
        red_a[k, yy, xx, low_part, :] = added(red_a[k, yy, xx, low_part, :], red_c[k, 1])

        @pl.when(~middle)
        def _():
            r_copy(k, 5).start()

    def r_z_first(k):
        @pl.when(middle)
        def _():
            r_copy(k, 5).wait_recv()
            red_a[k, yy, xx] = added(red_a[k, yy, xx], red_e[k, 0])
            r_copy(k, 6).start()

    def r_z_second(k):
        @pl.when(middle)
        def _():
            r_copy(k, 6).wait()
            red_a[k, yy, xx] = added(red_a[k, yy, xx], red_e[k, 1])
            for i in range(len(finals(k))):
                r_copy(k, 7 + i).start()
                r_local(k, i).start()

    def r_end(k):
        for kind in range(1 if k < UP else 0, 5):
            r_copy(k, kind).wait_send()

        @pl.when(middle)
        def _():
            for i in range(len(finals(k))):
                r_copy(k, 7 + i).wait_send()
                r_local(k, i).wait()

        @pl.when(~middle)
        def _():
            r_copy(k, 5).wait_send()
            for i in range(len(finals(k))):
                r_copy(k, 7 + i).wait_recv()

    stages = (r_pair, r_plane, r_whole, r_z_first, r_z_second)
    r_plan = []
    for tick in range(UNITS + len(stages)):
        acts = [(stages[s], tick - s) for s in reversed(range(1, len(stages)))]
        acts += [(r_pair, tick + 1)] if tick else [(r_pair, 0), (r_pair, 1)]
        r_plan.append([(f, k) for f, k in acts if 0 <= k < UNITS])
    started = []

    def reduce_start(k):
        if k == UP:
            pl.semaphore_wait(free_sem, 1)
        r_start(k)
        started.append(k)

    def reduce_tick():
        if r_plan and all(k in started for _, k in r_plan[0]):
            for act_of, k in r_plan.pop(0):
                act_of(k)

    for g in range(min(GATHER_AHEAD, GATHERS)):
        own_masters(g)
    pl.semaphore_wait(barrier, len(peers))
    for g in range(min(GATHER_AHEAD, GATHERS)):
        g_start(g)

    lens = [lens_ref[s] for s in range(n_seq)]
    ends = []
    total = 0
    for s in range(n_seq):
        total = total + ((lens[s] + (SPAN - 1)) // SPAN) * SPAN
        ends.append(total)
    starts = [0] + ends[:-1]

    def owner_of(row):
        found = jnp.zeros_like(row)
        for s in range(n_seq):
            found = found + (row >= ends[s]).astype(jnp.int32)
        return found

    half_lane = lax.broadcasted_iota(jnp.int32, (T, LANES), 1)
    row = z * T + lax.broadcasted_iota(jnp.int32, (T, LANES), 0)
    first = jnp.zeros_like(row)
    length = jnp.ones_like(row)
    for s in range(n_seq):
        inside = (row >= starts[s]) & (row < ends[s])
        first = jnp.where(inside, starts[s], first)
        length = jnp.where(inside, lens[s], length)
    offset = row - first
    live = (offset < length).astype(jnp.float32)
    angle = 0.5 * math.pi * offset.astype(jnp.float32) / length.astype(jnp.float32)
    angle = jnp.where(half_lane < HD, angle, 0.5 * math.pi - angle)
    cs_ref[...] = jnp.cos(angle) * live
    live_ref[...] = live
    owners = owner_of(row)
    next_owner = owner_of(jnp.full((1, 1), (z + 1) * T, jnp.int32))
    last_owner = owner_of(jnp.full((1, 1), z * T - 1, jnp.int32))
    my_first = owner_of(jnp.full((1, 1), z * T, jnp.int32))
    my_last = owner_of(jnp.full((1, 1), (z + 1) * T - 1, jnp.int32))
    for i, edge in enumerate((next_owner, last_owner, my_first, my_last)):
        keeps[i] = low_cast((owners == edge).astype(jnp.float32))

    def fill_masks(i, carry):
        r0 = pl.multiple_of(i * ROW_TILE, ROW_TILE)
        t_i = r0 + lax.broadcasted_iota(jnp.int32, (ROW_TILE, T), 0)
        u_i = lax.broadcasted_iota(jnp.int32, (ROW_TILE, T), 1)
        same = owner_of(t_i + z * T) == owner_of(u_i + z * T)
        mask[pl.ds(r0, ROW_TILE), :] = low_cast((same & (u_i <= t_i)).astype(jnp.float32))
        mask_t[pl.ds(r0, ROW_TILE), :] = low_cast((same & (u_i >= t_i)).astype(jnp.float32))
        return carry

    lax.fori_loop(0, T // ROW_TILE, fill_masks, 0)

    sq_lane = lax.broadcasted_iota(jnp.int32, (LANES, LANES), 1)
    ones_lane = ((half_lane == HD) | (half_lane == HD + 1)).astype(jnp.float32)

    def softplus(v):
        return jnp.maximum(v, 0.0) + jnp.log1p(jnp.exp(-jnp.abs(v)))

    def slab(p, part):
        return p // 2, slice(None), pl.ds(part * WIDE + (p % 2) * LANES, LANES)

    def pair_cols(p):
        return pl.ds(p * LANES, LANES)

    def split(value):
        swapped = swap_halves(value)
        return jnp.where(half_lane < HD, value, swapped), jnp.where(half_lane < HD, swapped, value)

    def join(left, right):
        return jnp.where(half_lane < HD, left, swap_halves(right))

    def pack_states(p, left, right, own, n_ones):
        place = pl.ds((p % 2) * LANES, LANES)
        own[p // 2, place, :] = low_cast(jnp.where(sq_lane < HD, left, swap_halves(right)))
        for side, part in ((0, left), (1, right)):
            column = part[:, HD : HD + 1]
            if n_ones == 2:
                column = column + part[:, HD + 1 : HD + 2]
            zcol[...] = jnp.where(sq_lane == 2 * (p % 2) + side, column, zcol[...])

    def exchange(which, own, landed, g):
        target = z + 1 - 2 * which
        target = (target + n_head) % n_head
        return remote(
            own.at[g], landed.at[g], s_send.at[which, g], s_recv.at[which, g], (dp, target)
        )

    def place_of(which):
        return z if which == 0 else n_head - 1 - z

    def send_states(which, own, landed, g):
        own[g, 2 * LANES : STATE_ROWS, :] = low_cast(zcol[...].T[0:16, :])

        @pl.when(place_of(which) == 0)
        def _():
            exchange(which, own, landed, g).start()

    def pass_on(which, own, landed, out, n_ones, point):
        for place in range(1, n_head):
            g = point - place
            if 0 <= g < GROUPS:

                @pl.when(place_of(which) == place)
                def _(g=g, place=place):
                    exchange(which, own, landed, g).wait_recv()
                    state_sum[0:STATE_ROWS, :] = landed[g].astype(jnp.float32)
                    if place < n_head - 1:
                        through = (my_first == next_owner) if which == 0 else (my_last == last_owner)
                        own[g] = low_cast(
                            own[g].astype(jnp.float32)
                            + through.astype(jnp.float32) * state_sum[0:STATE_ROWS, :]
                        )
                        exchange(which, own, landed, g).start()
                    unpack(out, n_ones, g)

    def unpack(out, n_ones, g):
        columns = state_sum[2 * LANES : 3 * LANES, :].T
        wide = (sq_lane >= HD) & (sq_lane < HD + n_ones)
        for i in range(2):
            packed = state_sum[i * LANES : (i + 1) * LANES, :]
            for side in (0, 1):
                part = packed if side == 0 else swap_halves(packed)
                column = columns[:, 2 * i + side : 2 * i + side + 1]
                out[4 * g + 2 * i + side] = low_cast(
                    jnp.where(sq_lane < HD, part, jnp.where(wide, column, 0.0))
                )

    def exchange_sent(which, own, landed):
        @pl.when(place_of(which) < n_head - 1)
        def _():
            for g in range(GROUPS):
                exchange(which, own, landed, g).wait_send()

    state_sum[...] = jnp.zeros_like(state_sum)
    state_h[...] = jnp.zeros_like(state_h)
    back_h[...] = jnp.zeros_like(back_h)

    def pass_forward(point):
        pass_on(0, state_own, state_in, state_h, 2, point)

    def pass_backward(point):
        pass_on(1, back_own, back_in, back_h, 1, point)

    zcol[...] = jnp.zeros_like(zcol)

    def features_of(p, part, store):
        cs = cs_ref[...]
        left, right = split(softplus(mixed[slab(p, part)].astype(jnp.float32)))
        store[2 * p] = low_cast(left * cs)
        store[2 * p + 1] = low_cast(right * cs)

    def make_keys(p, carry):
        features_of(p, 1, feat_k)
        v_pair = mixed[slab(p, 2)].astype(jnp.float32)
        val_a[2 * p] = low_cast(jnp.where(half_lane < HD, v_pair, ones_lane))
        val_a[2 * p + 1] = low_cast(jnp.where(half_lane < HD, swap_halves(v_pair), ones_lane))
        left = mm_rows(feat_k[2 * p] * keeps[0], val_a[2 * p])
        right = mm_rows(feat_k[2 * p + 1] * keeps[0], val_a[2 * p + 1])
        pack_states(p, left, right, state_own, 1)
        return carry

    def make_queries(p, carry):
        features_of(p, 0, feat_q)
        return carry

    load_tok.wait()
    for g in range(GROUPS):
        gather_until(g)
        part = mm(tok[...], w_qkv[g].reshape(D, D))
        mixed[g, :, 0:WIDE] = low_cast(part[:, 0:WIDE] + vec_ref[6:7, g * WIDE : (g + 1) * WIDE])
        mixed[g, :, WIDE : 2 * WIDE] = low_cast(
            part[:, WIDE : 2 * WIDE] + vec_ref[7:8, g * WIDE : (g + 1) * WIDE]
        )
        mixed[g, :, 2 * WIDE :] = low_cast(part[:, 2 * WIDE :])
        over_rows(2 * g + 2, make_keys, 0, 2 * g)
        send_states(0, state_own, state_in, g)
        if g:
            pass_forward(g)

    def local_attend(h, carry):
        scores = low_cast(mm_cols(feat_q[h], feat_k[h])) * mask[...]
        num_a[h] = mm(scores, val_a[h])
        return carry

    gather_step()
    for part in range(3):
        over_rows(2 * part + 2, make_queries, 0, 2 * part)
        over_rows(4 * part + 4, local_attend, 0, 4 * part)
        gather_step()
        pass_forward(3 + part)

    def finish_heads(p, carry):
        att = []
        for side in (0, 1):
            h = 2 * p + side
            whole = num_a[h] + mm(feat_q[h] * keeps[2], state_h[h])
            den = whole[:, HD : HD + 1] + (1.0 - live_ref[...])
            inverse = 1.0 / den
            got = whole * inverse
            num_a[h] = jnp.where(half_lane < HD, got, inverse)
            att.append(got)
        shift = vec_ref[8:9, pair_cols(p)]
        heads[:, pair_cols(p)] = low_cast(join(att[0], att[1]) + shift * live_ref[...])
        return carry

    for g in range(GROUPS):
        over_rows(2 * g + 2, finish_heads, 0, 2 * g)

    gather_until(GROUPS)

    def tile_rows(i):
        return slice(i * ROW_TILE, (i + 1) * ROW_TILE)

    def first_norm(i, carry):
        r = tile_rows(i)
        w = w_out[...].reshape(D, D)
        residual = tok[r, :].astype(jnp.float32) + (mm(heads[r, :], w) + vec_ref[4:5, :])
        normed, rstd = norm_rows(residual)
        norm_one[r, :] = normed
        rstd_one[r, :] = jnp.broadcast_to(rstd, (ROW_TILE, LANES))
        hidden = normed * vec_ref[0:1, :] + vec_ref[1:2, :]
        hid[r, :] = hidden
        hid_low[r, :] = low_cast(hidden)
        return carry

    while any(act_of is g_own for acts in plan for act_of, _ in acts):
        gather_step()
    load_cot.start()
    over_rows(T // ROW_TILE, first_norm, 0)

    for j in range(TILES):
        if j % 2 == 0:
            gather_until(GROUPS + 1 + j // 2)

        def ff_up(i, carry, j=j):
            r = tile_rows(i)
            upper = mm(hid_low[r, :], w_up[j].reshape(D, D)) + vec_ref[9 + j : 10 + j, :]
            value, slope = gelu_parts(upper)
            act[r, j * D : (j + 1) * D] = low_cast(value)
            gel[r, j * D : (j + 1) * D] = low_cast(slope)
            return carry

        over_rows(T // ROW_TILE, ff_up, 0)
        gather_step()

    gather_until(GATHERS - 2)
    gather_until(GATHERS - 1)
    load_cot.wait()

    def second_norm(i, sums):
        r = tile_rows(i)
        lowered = mm(act[r, :], w_down[...].reshape(FF, D))
        normed, rstd = norm_rows(hid[r, :] + (lowered + vec_ref[5:6, :]))
        one_low[r, :] = low_cast(normed * vec_ref[2:3, :] + vec_ref[3:4, :])
        dy = ig_ref[r, :]
        d_two = norm_rows_back(dy, normed, rstd, vec_ref[2:3, :])
        hid[r, :] = d_two
        two_low[r, :] = low_cast(d_two)
        return sums[0] + row_sum(dy * normed), sums[1] + row_sum(dy), sums[2] + row_sum(d_two)

    zero_row = jnp.zeros((1, D), jnp.float32)
    gain_two, shift_two, bias_down = over_rows(
        T // ROW_TILE, second_norm, (zero_row, zero_row, zero_row)
    )
    save_y.start()
    vg_ref[2:3, :] = gain_two
    vg_ref[3:4, :] = shift_two
    vg_ref[5:6, :] = bias_down

    for j in range(TILES):
        got = low_cast(mm_rows(act[:, j * D : (j + 1) * D], two_low[...]))
        got = got.reshape(2, TILES, rows, D)
        for k in range(TILES):
            red_a[UP + k, j // 2, j % 2] = jnp.where(core == 0, got[1, k], got[0, k])
            red_a[OUT + k, j // 2, j % 2] = jnp.where(core == 0, got[0, k], got[1, k])
    for k in range(UP):
        reduce_start(k)

    for j in range(TILES):

        def ff_back(i, total, j=j):
            r = tile_rows(i)
            d_act = mm_cols(two_low[r, :], w_down[j // 2, j % 2].reshape(D, D))
            d_upper = d_act * gel[r, j * D : (j + 1) * D].astype(jnp.float32)
            gel[r, j * D : (j + 1) * D] = low_cast(d_upper)
            return total + row_sum(d_upper)

        vg_ref[9 + j : 10 + j, :] = over_rows(T // ROW_TILE, ff_back, zero_row)
    reduce_tick()

    save_y.wait()

    def first_norm_back(i, sums):
        r = tile_rows(i)
        dy = hid[r, :]
        for j in range(TILES):
            dy = dy + mm_cols(gel[r, j * D : (j + 1) * D], w_up[j].reshape(D, D))
        normed = norm_one[r, :]
        d_one = norm_rows_back(dy, normed, rstd_one[r, 0:1], vec_ref[0:1, :])
        ig_ref[r, :] = d_one
        one_low[r, :] = low_cast(d_one)
        return sums[0] + row_sum(dy * normed), sums[1] + row_sum(dy), sums[2] + row_sum(d_one)

    sums = (zero_row, zero_row, zero_row)
    steps = T // ROW_TILE
    sums = over_rows(steps // 2, first_norm_back, sums)
    reduce_tick()
    sums = over_rows(steps, first_norm_back, sums, steps // 2)
    vg_ref[0:1, :] = sums[0]
    vg_ref[1:2, :] = sums[1]
    vg_ref[4:5, :] = sums[2]

    for g in range(GROUPS + 1, GATHERS - 2):
        g_sent(g)
    turned[...] = hid_low[...].T
    for j in range(TILES):
        got = low_cast(mm(turned[...], gel[:, j * D : (j + 1) * D]))
        w_up[j] = got.reshape(2, 2, 2, rows, D)
    reduce_tick()

    d_heads = two_low
    d_heads[...] = low_cast(mm_cols(one_low[...], w_out[...].reshape(D, D)))
    g_sent(GROUPS)
    w_out[...] = low_cast(mm_rows(heads[...], one_low[...])).reshape(2, 2, 2, rows, D)

    zcol[...] = jnp.zeros_like(zcol)

    def grad_slot(h):
        return slice(None), pl.ds(h * LANES, LANES)

    def back_states(p, carry):
        g_pair = d_heads[:, pair_cols(p)].astype(jnp.float32)
        parts = []
        for side in (0, 1):
            h = 2 * p + side
            saved = num_a[h]
            g = g_pair if side == 0 else swap_halves(g_pair)
            gn = jnp.where(half_lane < HD, g * swap_halves(saved), 0.0)
            gd = -jnp.sum(gn * saved, axis=1, keepdims=True)
            gd_high = low_cast(gd).astype(jnp.float32)
            gn = jnp.where(
                half_lane == HD, gd_high, jnp.where(half_lane == HD + 1, gd - gd_high, gn)
            )
            gn = low_cast(gn)
            act[grad_slot(h)] = gn
            parts.append(mm_rows(feat_q[h] * keeps[1], gn))
        pack_states(p, parts[0], parts[1], back_own, 2)
        return carry

    for g in range(GROUPS):
        over_rows(2 * g + 2, back_states, 0, 2 * g)
        send_states(1, back_own, back_in, g)
        if g:
            pass_backward(g)
        if g == 0:
            reduce_tick()
            for k in range(UP, MIX):
                reduce_start(k)
        if g == 2:
            reduce_tick()

    def sigmoid(v):
        e = jnp.exp(-jnp.abs(v))
        return jnp.where(v >= 0, 1.0, e) / (1.0 + e)

    def fold(value):
        value = value * cs_ref[...]
        return value + swap_halves(value)

    def through_features(p, part, left, right):
        value = mixed[slab(p, part)].astype(jnp.float32)
        d_part = sigmoid(value) * jnp.where(half_lane < HD, fold(left), fold(right))
        mixed[slab(p, part)] = low_cast(d_part)
        vg_ref[6 + part : 7 + part, pair_cols(p)] = row_sum(d_part)

    def query_back(p, carry):
        got = []
        for side in (0, 1):
            h = 2 * p + side
            ga = act[grad_slot(h)]
            d_scores = low_cast(mm_cols(ga, val_a[h])) * mask[...]
            got.append(mm(d_scores, feat_k[h]) + mm_cols(ga * keeps[2], state_h[h]))
        through_features(p, 0, got[0], got[1])
        return carry

    for part in range(3):
        over_rows(2 * part + 2, query_back, 0, 2 * part)
        pass_backward(3 + part)
        if part == 1:
            reduce_tick()

    def key_value_back(p, carry):
        keys, values = [], []
        for side in (0, 1):
            h = 2 * p + side
            fq, fk, va, ga = feat_q[h], feat_k[h], val_a[h], act[grad_slot(h)]
            d_scores_t = low_cast(mm_cols(va, ga)) * mask_t[...]
            keys.append(mm(d_scores_t, fq) + mm_cols(va * keeps[3], back_h[h]))
            scores_t = low_cast(mm_cols(fk, fq)) * mask_t[...]
            values.append(mm(scores_t, ga) + mm(fk * keeps[3], back_h[h]))
        through_features(p, 1, keys[0], keys[1])
        d_part = join(values[0], values[1])
        mixed[slab(p, 2)] = low_cast(d_part)
        vg_ref[8:9, pair_cols(p)] = row_sum(d_part)
        return carry

    turned[...] = tok[...].T
    reduce_tick()
    for g in range(GROUPS):
        over_rows(2 * g + 2, key_value_back, 0, 2 * g)
        ig_ref[...] += mm_cols(mixed[g], w_qkv[g].reshape(D, D))
        g_sent(g)
        w_qkv[g] = low_cast(mm(turned[...], mixed[g])).reshape(2, 2, 2, rows, D)
        reduce_start(MIX + g)
        reduce_tick()

    def vcopy(level):
        target = (sib, xn, yn, z_one, z_two)[level]
        return remote(vg_ref, vec_land.at[level], v_send.at[level], v_recv.at[level], target)

    vg_ref[13:16, :] = jnp.zeros((3, D), jnp.float32)
    vcopy(0).start()
    for level in range(5):
        reduce_tick()
        vcopy(level).wait()
        vg_ref[...] += vec_land[level]
        if level < 4:
            vcopy(level + 1).start()
    while r_plan:
        reduce_tick()
    for k in range(UNITS):
        r_end(k)
    for g in (GATHERS - 2, GATHERS - 1):
        g_sent(g)
    exchange_sent(0, state_own, state_in)
    exchange_sent(1, back_own, back_in)


GATHER_AHEAD = 3


def fits(mesh):
    return mesh.shape["dp"] == 8 and mesh.shape["head"] == 4


def fused_layer(lengths, tokens, cotangent, masters, vector_master):
    n_head = lax.axis_size("head")
    T = tokens.shape[0]
    rows = masters[1].shape[0]
    bf, f32 = jnp.bfloat16, jnp.float32
    V, S = pltpu.VMEM, jax.ShapeDtypeStruct
    vm, anywhere = pl.BlockSpec(memory_space=pltpu.VMEM), pl.BlockSpec(memory_space=pl.ANY)
    out_shape = (S((T, D), bf), S((T, D), f32)) + tuple(S(m.shape, bf) for m in masters)
    out_shape += (S((16, D), f32),)
    shard = (2, 2, 2, rows, D)
    scratch = [
        V((GROUPS, *shard), bf),
        V(shard, bf),
        V((TILES, *shard), bf),
        V((2, 2, 2, TILES * rows, D), bf),
        V((T, D), bf),
        V((GROUPS, T, D), bf),
        V((H, T, LANES), bf),
        V((H, T, LANES), bf),
        V((H, T, LANES), bf),
        V((H, T, LANES), f32),
        V((T, D), bf),
        V((T, D), f32),
        V((T, LANES), f32),
        V((T, D), f32),
        V((T, D), bf),
        V((D, T), bf),
        V((T, FF), bf),
        V((T, FF), bf),
        V((T, D), bf),
        V((T, D), bf),
        V((T, T), bf),
        V((T, T), bf),
        V((T, LANES), f32),
        V((T, LANES), f32),
        V((4, T, LANES), bf),
        V((GROUPS, STATE_ROWS, LANES), bf),
        V((GROUPS, STATE_ROWS, LANES), bf),
        V((GROUPS, STATE_ROWS, LANES), bf),
        V((GROUPS, STATE_ROWS, LANES), bf),
        V((3 * LANES, LANES), f32),
        V((H, LANES, LANES), bf),
        V((H, LANES, LANES), bf),
        V((LANES, LANES), f32),
        V((UNITS, 2, 2, rows, D), bf),
        V((UNITS, 2, 2, rows // 2, D), bf),
        V((UNITS, 2, rows // 2, D), bf),
        V((UNITS, 2, rows, D), bf),
        V((5, 16, D), f32),
        pltpu.SemaphoreType.DMA((18,)),
        pltpu.SemaphoreType.DMA((8, 17)),
        pltpu.SemaphoreType.DMA((8, 17)),
        pltpu.SemaphoreType.DMA((2, GROUPS)),
        pltpu.SemaphoreType.DMA((2, GROUPS)),
        pltpu.SemaphoreType.DMA((UNITS, 13)),
        pltpu.SemaphoreType.DMA((UNITS, 13)),
        pltpu.SemaphoreType.DMA((5,)),
        pltpu.SemaphoreType.DMA((5,)),
        pltpu.SemaphoreType.REGULAR,
    ]
    return pl.pallas_call(
        functools.partial(layer_kernel, n_head, lengths.shape[0]),
        out_shape=out_shape,
        in_specs=[pl.BlockSpec(memory_space=pltpu.SMEM)] + [anywhere] * 6 + [vm],
        out_specs=[anywhere, vm] + [anywhere] * 4 + [vm],
        scratch_shapes=scratch,
        compiler_params=pltpu.CompilerParams(
            collective_id=0, has_side_effects=True, vmem_limit_bytes=VMEM_BYTES
        ),
        name="layer",
    )(lengths, tokens, cotangent, *masters, vector_master)


VMEM_BYTES = 63 * 1024 * 1024


def fused_shards(
    tokens,
    cotangent,
    lengths,
    qkv_master,
    out_master,
    up_master,
    down_master,
    vector_master,
    qkv_first,
    qkv_second,
    out_first,
    out_second,
    up_first,
    up_second,
    down_first,
    down_second,
    vector_first,
    vector_second,
):
    masters = (qkv_master, out_master, up_master, down_master)
    output, input_grad, *grads, vector_grad = fused_layer(
        lengths, tokens, cotangent, masters, vector_master
    )
    rates = (1.0 / math.sqrt(D), 1.0 / math.sqrt(OUT_FAN), 1.0 / math.sqrt(D), 1.0 / math.sqrt(FF))
    firsts = (qkv_first, out_first, up_first, down_first)
    seconds = (qkv_second, out_second, up_second, down_second)
    news = []
    for i in range(4):
        news.extend(
            adam_update(
                masters[i],
                firsts[i],
                seconds[i],
                grads[i].astype(jnp.float32),
                rates[i],
                weight_decay,
            )
        )
    vector_new = adam_update(
        vector_master, vector_first, vector_second, vector_grad[:13], vector_rate, 0.0
    )
    return (output, input_grad, *news, *vector_new)


def solution(mesh):
    return jax.shard_map(
        fused_shards if fits(mesh) else shards,
        mesh=mesh,
        in_specs=(
            P(("dp", "head"), None),
            P(("dp", "head"), None),
            P("dp"),
            P("dp", None),
            P("dp", None),
            P("dp", None),
            P("dp", None),
            P(),
            P("dp", None),
            P("dp", None),
            P("dp", None),
            P("dp", None),
            P("dp", None),
            P("dp", None),
            P("dp", None),
            P("dp", None),
            P(),
            P(),
        ),
        out_specs=(
            P(("dp", "head"), None),
            P(("dp", "head"), None),
            P("dp", None),
            P("dp", None),
            P("dp", None),
            P("dp", None),
            P("dp", None),
            P("dp", None),
            P("dp", None),
            P("dp", None),
            P("dp", None),
            P("dp", None),
            P("dp", None),
            P("dp", None),
            P(),
            P(),
            P(),
        ),
        check_vma=False,
    )
```

```python
import functools
import math

import jax
import jax.numpy as jnp
from jax import lax
from jax.experimental import pallas as pl
from jax.experimental.pallas import tpu as pltpu
from jax.sharding import PartitionSpec as P

D = 768
H = 12
HD = 64
FF = 3072
SPAN = 64
STEP = 10
OUT_FAN = 1


highest = lax.Precision.HIGHEST
norm_epsilon = 1e-05
first_decay = 0.9
second_decay = 0.999
adam_epsilon = 1e-08
weight_decay = 0.01
vector_rate = 0.2


def layer_norm(residual, gain_row, shift_row):
    center = residual - jnp.mean(residual, axis=-1, keepdims=True)
    spread = jnp.mean(center * center, axis=-1, keepdims=True)
    return center * lax.rsqrt(spread + norm_epsilon) * gain_row + shift_row


def exact_gelu(upper_pre):
    return jax.nn.gelu(upper_pre, approximate=False)


def group_layout(group_lengths, row_count):
    slot_sizes = (group_lengths + SPAN - 1) // SPAN * SPAN
    slot_ends = jnp.cumsum(slot_sizes)
    slot_starts = slot_ends - slot_sizes
    positions = jnp.arange(row_count, dtype=jnp.int32)
    member = (positions[:, None] >= slot_starts[None, :]) & (
        positions[:, None] < slot_ends[None, :]
    )
    seq_first = jnp.sum(jnp.where(member, slot_starts[None, :], 0), axis=1)
    length = jnp.sum(jnp.where(member, group_lengths[None, :], 0), axis=1)
    seq_numbers = jnp.arange(group_lengths.shape[0], dtype=jnp.int32)
    owners = jnp.sum(jnp.where(member, seq_numbers[None, :], 0), axis=1)
    offset = positions - seq_first
    live_rows = (offset < length).astype(jnp.float32)
    angles = 0.5 * math.pi * offset.astype(jnp.float32) / length.astype(jnp.float32)
    cosine = jnp.cos(angles)
    sine_part = jnp.sin(angles)
    span_owner = owners[::SPAN]
    span_order = jnp.arange(span_owner.shape[0], dtype=jnp.int32)
    same_seq = span_owner[None, :] == span_owner[:, None]
    earlier = (same_seq & (span_order[None, :] < span_order[:, None])).astype(jnp.float32)
    return (cosine, sine_part, live_rows, earlier)


def attend(query_rows, key_rows, value_rows, cosine, sine_part, live_rows, earlier):
    row_count = query_rows.shape[0]
    blocks = row_count // SPAN
    soft_query = jax.nn.softplus(query_rows)
    soft_key = jax.nn.softplus(key_rows)
    feat_query = (
        jnp.concatenate([soft_query * cosine[:, None], soft_query * sine_part[:, None]], axis=1)
        * live_rows[:, None]
    )
    feat_key = (
        jnp.concatenate([soft_key * cosine[:, None], soft_key * sine_part[:, None]], axis=1)
        * live_rows[:, None]
    )
    block_query = feat_query.reshape(blocks, SPAN, -1)
    block_key = feat_key.reshape(blocks, SPAN, -1)
    block_value = value_rows.reshape(blocks, SPAN, -1)
    lower_mask = (jnp.arange(SPAN)[:, None] >= jnp.arange(SPAN)[None, :]).astype(jnp.float32)
    scores = jnp.einsum("cik,cjk->cij", block_query, block_key, precision=highest) * lower_mask
    inner_sum = jnp.einsum("cij,cjd->cid", scores, block_value, precision=highest)
    inner_den = jnp.sum(scores, axis=2)
    states = jnp.einsum("cjk,cjd->ckd", block_key, block_value, precision=highest)
    key_sums = jnp.sum(block_key, axis=1)
    before = jnp.einsum("ce,ekd->ckd", earlier, states, precision=highest)
    before_sums = jnp.einsum("ce,ek->ck", earlier, key_sums, precision=highest)
    outer_sum = jnp.einsum("cik,ckd->cid", block_query, before, precision=highest)
    outer_den = jnp.einsum("cik,ck->ci", block_query, before_sums, precision=highest)
    numerator = (inner_sum + outer_sum).reshape(row_count, -1)
    denominator = (inner_den + outer_den).reshape(row_count) + (1.0 - live_rows)
    return numerator / denominator[:, None]


def contract_rows(left, right):
    return lax.dot_general(
        left, right, (((0,), (0,)), ((), ())), preferred_element_type=jnp.float32
    )


def contract_cols(left, right):
    return lax.dot_general(
        left, right, (((1,), (1,)), ((), ())), preferred_element_type=jnp.float32
    )


def adam_update(master, first, second, gradient, rate, decay):
    first_new = first_decay * first + (1.0 - first_decay) * gradient
    second_new = second_decay * second + (1.0 - second_decay) * gradient * gradient
    first_hat = first_new / (1.0 - first_decay**STEP)
    second_hat = second_new / (1.0 - second_decay**STEP)
    master_new = master - rate * (
        first_hat / (jnp.sqrt(second_hat) + adam_epsilon) + decay * master
    )
    return (first_new, second_new, master_new)


def shards(
    tokens,
    cotangent,
    lengths,
    qkv_master,
    out_master,
    up_master,
    down_master,
    vector_master,
    qkv_first,
    qkv_second,
    out_first,
    out_second,
    up_first,
    up_second,
    down_first,
    down_second,
    vector_first,
    vector_second,
):
    mix_weight, out_weight, up_weight, down_weight = (
        lax.all_gather(qkv_master.astype(jnp.bfloat16), "dp", axis=0, tiled=True),
        lax.all_gather(out_master.astype(jnp.bfloat16), "dp", axis=0, tiled=True),
        lax.all_gather(up_master.astype(jnp.bfloat16), "dp", axis=0, tiled=True),
        lax.all_gather(down_master.astype(jnp.bfloat16), "dp", axis=0, tiled=True),
    )
    tok_count = tokens.shape[0]
    width = tokens.shape[1]
    mixed_all = jnp.dot(tokens, mix_weight, preferred_element_type=jnp.float32) + vector_master[
        6:9
    ].reshape(-1)
    mixed_low = mixed_all.astype(jnp.bfloat16)
    query_part = mixed_low[:, :width].reshape(tok_count, H, 1, HD)
    key_part = mixed_low[:, width : 2 * width].reshape(tok_count, H, 1, HD)
    paired = jnp.concatenate([query_part, key_part], axis=2)
    paired = jnp.repeat(paired[:, :, None], 2, axis=2).reshape(tok_count, 4 * width)
    value_part = mixed_low[:, 2 * width :]
    paired_in, values_in = (
        lax.all_to_all(paired, "head", split_axis=1, concat_axis=0, tiled=True),
        lax.all_to_all(value_part, "head", split_axis=1, concat_axis=0, tiled=True),
    )
    group_rows = paired_in.shape[0]
    item_count = paired_in.shape[1] // (2 * HD)
    cosine, sine_part, live_rows, earlier = group_layout(lengths, group_rows)
    stacked = paired_in.reshape(group_rows, item_count, 2, HD).astype(jnp.float32)
    query_items = stacked[:, :, 0]
    key_items = stacked[:, :, 1]
    value_items = values_in.reshape(group_rows, item_count, HD // 2).astype(jnp.float32)

    def mix_items(query_set, key_set, value_set):

        def single(query_rows, key_rows, value_rows):
            return attend(query_rows, key_rows, value_rows, cosine, sine_part, live_rows, earlier)

        return jax.vmap(single, in_axes=1, out_axes=1)(query_set, key_set, value_set)

    attended, mix_back = jax.vjp(mix_items, query_items, key_items, value_items)
    heads_out = attended.reshape(group_rows, item_count * (HD // 2)).astype(jnp.bfloat16)
    heads = lax.all_to_all(heads_out, "head", split_axis=0, concat_axis=1, tiled=True)
    projected = jnp.dot(heads, out_weight, preferred_element_type=jnp.float32) + vector_master[4]
    resid_one = tokens.astype(jnp.float32) + projected
    hidden, norm_one_back = jax.vjp(layer_norm, resid_one, vector_master[0], vector_master[1])
    hidden_low = hidden.astype(jnp.bfloat16)
    upper_pre = jnp.dot(hidden_low, up_weight, preferred_element_type=jnp.float32) + vector_master[
        9:13
    ].reshape(-1)
    active, gelu_back = jax.vjp(exact_gelu, upper_pre)
    active_low = active.astype(jnp.bfloat16)
    lowered = (
        jnp.dot(active_low, down_weight, preferred_element_type=jnp.float32) + vector_master[5]
    )
    output, norm_two_back = jax.vjp(
        layer_norm, hidden + lowered, vector_master[2], vector_master[3]
    )
    grad_two, gain_two, shift_two = norm_two_back(cotangent)
    grad_two_low = grad_two.astype(jnp.bfloat16)
    down_grad = contract_rows(active_low, grad_two_low)
    (upper_grad,) = gelu_back(contract_cols(grad_two_low, down_weight))
    upper_low = upper_grad.astype(jnp.bfloat16)
    up_grad = contract_rows(hidden_low, upper_low)
    hidden_grad = grad_two + contract_cols(upper_low, up_weight)
    grad_one, gain_one, shift_one = norm_one_back(hidden_grad)
    grad_one_low = grad_one.astype(jnp.bfloat16)
    out_grad = contract_rows(heads, grad_one_low)
    heads_grad = contract_cols(grad_one_low, out_weight).astype(jnp.bfloat16)
    heads_back = lax.all_to_all(heads_grad, "head", split_axis=1, concat_axis=0, tiled=True)
    query_back, key_back, value_back = mix_back(
        heads_back.reshape(group_rows, item_count, HD // 2).astype(jnp.float32)
    )
    pair_back = (
        jnp.stack([query_back, key_back], axis=2)
        .astype(jnp.bfloat16)
        .reshape(group_rows, item_count * 2 * HD)
    )
    value_low = value_back.astype(jnp.bfloat16).reshape(group_rows, item_count * (HD // 2))
    pair_home, value_home = (
        lax.all_to_all(pair_back, "head", split_axis=0, concat_axis=1, tiled=True),
        lax.all_to_all(value_low, "head", split_axis=0, concat_axis=1, tiled=True),
    )
    summed = jnp.sum(pair_home.astype(jnp.float32).reshape(tok_count, H, 2, 2, HD), axis=2)
    mixed_grad = jnp.concatenate(
        [
            summed[:, :, 0].reshape(tok_count, width),
            summed[:, :, 1].reshape(tok_count, width),
            value_home.astype(jnp.float32),
        ],
        axis=1,
    )
    mixed_low_grad = mixed_grad.astype(jnp.bfloat16)
    mix_grad = contract_rows(tokens, mixed_low_grad)
    input_grad = grad_one + contract_cols(mixed_low_grad, mix_weight)
    vector_grad = jnp.concatenate(
        [
            jnp.stack(
                [
                    gain_one,
                    shift_one,
                    gain_two,
                    shift_two,
                    jnp.sum(grad_one, axis=0),
                    jnp.sum(grad_two, axis=0),
                ]
            ),
            jnp.sum(mixed_grad, axis=0).reshape(3, width),
            jnp.sum(upper_grad, axis=0).reshape(4, width),
        ],
        axis=0,
    )
    local_grads = (mix_grad, out_grad, up_grad, down_grad)
    row_parts = (
        lax.psum_scatter(
            local_grads[0].astype(jnp.bfloat16), "dp", scatter_dimension=0, tiled=True
        ).astype(jnp.float32),
        lax.psum_scatter(
            local_grads[1].astype(jnp.bfloat16), "dp", scatter_dimension=0, tiled=True
        ).astype(jnp.float32),
        lax.psum_scatter(
            local_grads[2].astype(jnp.bfloat16), "dp", scatter_dimension=0, tiled=True
        ).astype(jnp.float32),
        lax.psum_scatter(
            local_grads[3].astype(jnp.bfloat16), "dp", scatter_dimension=0, tiled=True
        ).astype(jnp.float32),
    )
    reduced = (
        lax.psum(row_parts[0].astype(jnp.bfloat16), "head").astype(jnp.float32),
        lax.psum(row_parts[1].astype(jnp.bfloat16), "head").astype(jnp.float32),
        lax.psum(row_parts[2].astype(jnp.bfloat16), "head").astype(jnp.float32),
        lax.psum(row_parts[3].astype(jnp.bfloat16), "head").astype(jnp.float32),
    )
    vector_total = lax.psum(vector_grad, ("dp", "head"))
    qkv_new = adam_update(
        qkv_master, qkv_first, qkv_second, reduced[0], 1.0 / math.sqrt(D), weight_decay
    )
    out_new = adam_update(
        out_master, out_first, out_second, reduced[1], 1.0 / math.sqrt(OUT_FAN), weight_decay
    )
    up_new = adam_update(
        up_master, up_first, up_second, reduced[2], 1.0 / math.sqrt(D), weight_decay
    )
    down_new = adam_update(
        down_master, down_first, down_second, reduced[3], 1.0 / math.sqrt(FF), weight_decay
    )
    vector_new = adam_update(
        vector_master, vector_first, vector_second, vector_total, vector_rate, 0.0
    )
    return (
        output.astype(jnp.bfloat16),
        input_grad,
        qkv_new[0],
        qkv_new[1],
        qkv_new[2],
        out_new[0],
        out_new[1],
        out_new[2],
        up_new[0],
        up_new[1],
        up_new[2],
        down_new[0],
        down_new[1],
        down_new[2],
        vector_new[0],
        vector_new[1],
        vector_new[2],
    )


PAIRS = H // 2
LANES = 2 * HD
GROUPS = 3
STATE_ROWS = (PAIRS // GROUPS) * LANES + 16
WIDE = D // GROUPS
TILES = FF // D
ROW_TILE = 256
MESH = pl.DeviceIdType.MESH
DOWN, UP, OUT, MIX = 0, TILES, 2 * TILES, 2 * TILES + 1
UNITS = 2 * TILES + 1 + GROUPS


def mm(left, right):
    return jnp.dot(left, right, preferred_element_type=jnp.float32)


def mm_cols(left, right):
    return lax.dot_general(
        left, right, (((1,), (1,)), ((), ())), preferred_element_type=jnp.float32
    )


def mm_rows(left, right):
    return lax.dot_general(
        left, right, (((0,), (0,)), ((), ())), preferred_element_type=jnp.float32
    )


def swap_halves(slab):
    return pltpu.roll(slab, HD, 1)


def low_cast(value):
    return value.astype(jnp.bfloat16)


def row_sum(value):
    return jnp.sum(value, axis=0, keepdims=True)


def gelu_parts(z):
    x = jnp.abs(z) * (1.0 / math.sqrt(2.0))
    t = 1.0 / (1.0 + 0.3275911 * x)
    bell = jnp.exp(-0.5 * z * z)
    poly = t * (
        0.254829592
        + t * (-0.284496736 + t * (1.421413741 + t * (-1.453152027 + t * 1.061405429)))
    )
    upper_tail = 0.5 * poly * bell
    phi = jnp.where(z >= 0, 1.0 - upper_tail, upper_tail)
    return z * phi, phi + z * (bell * (1.0 / math.sqrt(2.0 * math.pi)))


def over_rows(count, body, carry, start=0):
    for i in range(start, count):
        carry = body(i, carry)
    return carry


def norm_rows(residual):
    center = residual - jnp.mean(residual, axis=-1, keepdims=True)
    rstd = lax.rsqrt(jnp.mean(center * center, axis=-1, keepdims=True) + norm_epsilon)
    return center * rstd, rstd


def norm_rows_back(dy, normed, rstd, gain):
    e = dy * gain
    return rstd * (
        e
        - jnp.mean(e, axis=-1, keepdims=True)
        - normed * jnp.mean(e * normed, axis=-1, keepdims=True)
    )


def layer_kernel(
    n_head,
    n_seq,
    lens_ref,
    tok_hbm,
    cot_hbm,
    qkv_f,
    out_f,
    up_f,
    down_f,
    vec_ref,
    y_hbm,
    ig_ref,
    g_qkv,
    g_out,
    g_up,
    g_down,
    vg_ref,
    w_qkv,
    w_out,
    w_up,
    w_down,
    tok,
    mixed,
    feat_q,
    feat_k,
    val_a,
    num_a,
    heads,
    norm_one,
    rstd_one,
    hid,
    hid_low,
    turned,
    act,
    gel,
    two_low,
    one_low,
    mask,
    mask_t,
    cs_ref,
    live_ref,
    keeps,
    state_own,
    state_in,
    back_own,
    back_in,
    state_sum,
    state_h,
    back_h,
    zcol,
    red_a,
    red_b,
    red_c,
    red_e,
    vec_land,
    load_sem,
    g_send,
    g_recv,
    s_send,
    s_recv,
    r_send,
    r_recv,
    v_send,
    v_recv,
    free_sem,
):
    T = tok.shape[0]
    rows = w_out.shape[3]
    half = rows // 2
    dp = lax.axis_index("dp")
    z = lax.axis_index("head")
    core = dp % 2
    xx = (dp // 2) % 2
    yy = dp // 4
    color = z % 2
    sib = (dp + 1 - 2 * core, z)
    xn = (dp + 2 - 4 * xx, z)
    yn = (dp + 4 - 8 * yy, z)
    z_one = (dp, z + 1 - 2 * color)
    z_two = (dp, (z + 3 + 2 * color) % n_head)

    def load(i, src, dst):
        return pltpu.make_async_copy(src, dst, load_sem.at[i])

    def spot(ref, i):
        return ref.at[pl.ds(i * rows, rows), :]

    loads = []
    for g in range(GROUPS):
        for part in range(3):
            loads.append(
                load(
                    len(loads),
                    qkv_f.at[:, pl.ds(part * D + g * WIDE, WIDE)],
                    hid.at[pl.ds(g * rows, rows), pl.ds(part * WIDE, WIDE)],
                )
            )
    loads.append(load(len(loads), out_f, spot(hid, GROUPS)))
    for j in range(TILES):
        loads.append(load(len(loads), up_f.at[:, pl.ds(j * D, D)], spot(norm_one, j)))
    loads.append(load(len(loads), down_f, ig_ref.at[pl.ds(0, TILES * rows), :]))
    load_tok = load(len(loads), tok_hbm, tok)
    load_cot = load(len(loads) + 1, cot_hbm, ig_ref)
    save_y = load(len(loads) + 2, one_low, y_hbm)
    for copy in loads:
        copy.start()
    load_tok.start()

    barrier = pltpu.get_barrier_semaphore()
    peers = [sib, xn, yn]
    for k in range(1, n_head):
        peers.append((dp, (z + k) % n_head))
    for peer in peers:
        pl.semaphore_signal(barrier, inc=1, device_id=peer, device_id_type=MESH)

    def remote(src, dst, send, recv, target):
        return pltpu.make_async_remote_copy(
            src_ref=src,
            dst_ref=dst,
            send_sem=send,
            recv_sem=recv,
            device_id=target,
            device_id_type=MESH,
        )

    GATHERS = GROUPS + 1 + TILES // 2 + 2

    def piece(g, y, x, c, which):
        if g < GROUPS:
            ref, size, base = w_qkv.at[g, y, x, c], rows, 0
        elif g == GROUPS:
            ref, size, base = w_out.at[y, x, c], rows, 0
        elif g < GROUPS + 1 + TILES // 2:
            i = g - GROUPS - 1
            if which is None:
                return w_up.at[pl.ds(2 * i, 2), y, x, c]
            return w_up.at[
                pl.ds(2 * i, 2), y, x, c, pl.ds(pl.multiple_of(which * half, half), half), :
            ]
        else:
            i = g - GROUPS - 1 - TILES // 2
            ref, size, base = w_down.at[y, x, c], 2 * rows, 2 * rows * i
        if which is None:
            return ref.at[pl.ds(base, size), :]
        return ref.at[pl.ds(pl.multiple_of(base + which * (size // 2), size // 2), size // 2), :]

    def own_masters(g):
        if g < GROUPS:
            for part in range(3):
                loads[3 * g + part].wait()
            w_qkv[g, yy, xx, core] = low_cast(hid[g * rows : (g + 1) * rows, :])
        elif g == GROUPS:
            loads[9].wait()
            w_out[yy, xx, core] = low_cast(hid[g * rows : (g + 1) * rows, :])
        elif g < GROUPS + 1 + TILES // 2:
            for j in range(2 * (g - GROUPS - 1), 2 * (g - GROUPS)):
                loads[10 + j].wait()
                w_up[j, yy, xx, core] = low_cast(norm_one[j * rows : (j + 1) * rows, :])
        else:
            i = g - GROUPS - 1 - TILES // 2
            if i == 0:
                loads[10 + TILES].wait()
            span = slice(2 * rows * i, 2 * rows * (i + 1))
            w_down[yy, xx, core, span, :] = low_cast(ig_ref[span, :])

    here, mine_x, mine_y, mine_d = (yy, xx), (yy, 1 - xx), (1 - yy, xx), (1 - yy, 1 - xx)

    def gcopy(g, kind, chip, which, target, lands):
        ref = piece(g, chip[0], chip[1], core, which)
        return remote(ref, ref, g_send.at[g, kind], g_recv.at[g, lands], target)

    def landed(g, chip, which, lands):
        gcopy(g, 0, chip, which, sib, lands).wait_recv()

    blocks = ((mine_x, 0), (mine_x, 1), (mine_y, 0), (mine_y, 1), (mine_d, 0), (mine_d, 1))

    def hand_over(g, lands):
        chip, which = blocks[lands]
        gcopy(g, 10 + lands, chip, which, sib, 7 + lands).start()

    def arrived(g, lands):
        chip, which = blocks[lands]
        landed(g, chip, which, lands)

    def g_start(g):
        gcopy(g, 0, here, 0, xn, 0).start()
        gcopy(g, 1, here, 1, yn, 3).start()

        @pl.when(color == 0)
        def _():
            gcopy(g, 2, here, 1, xn, 1).start()
            gcopy(g, 3, here, 0, yn, 2).start()

        gcopy(g, 9, here, None, sib, 6).start()

    def g_own(g):
        own_masters(g)
        g_start(g)

    def g_first(g):
        arrived(g, 0)

        @pl.when(color == 1)
        def _():
            gcopy(g, 4, mine_x, 0, yn, 4).start()

        arrived(g, 3)

        @pl.when(color == 1)
        def _():
            gcopy(g, 5, mine_y, 1, xn, 5).start()

        hand_over(g, 0)
        hand_over(g, 3)

        @pl.when(color == 0)
        def _():
            arrived(g, 1)
            gcopy(g, 6, mine_x, 1, z_one, 1).start()
            arrived(g, 2)
            gcopy(g, 7, mine_y, 0, z_one, 2).start()
            hand_over(g, 1)
            hand_over(g, 2)

    def g_second(g):
        @pl.when(color == 1)
        def _():
            arrived(g, 4)
            gcopy(g, 8, mine_d, 0, z_one, 4).start()
            arrived(g, 5)
            gcopy(g, 16, mine_d, 1, z_one, 5).start()
            hand_over(g, 4)
            hand_over(g, 5)
            arrived(g, 1)
            hand_over(g, 1)
            arrived(g, 2)
            hand_over(g, 2)

    def g_third(g):
        @pl.when(color == 0)
        def _():
            arrived(g, 4)
            hand_over(g, 4)
            arrived(g, 5)
            hand_over(g, 5)

    def g_last(g):
        landed(g, here, None, 6)
        for lands in range(6):
            chip, which = blocks[lands]
            landed(g, chip, which, 7 + lands)

    def g_sent(g):
        def sent(kind, chip, which):
            gcopy(g, kind, chip, which, sib, 0).wait_send()

        sent(0, here, 0)
        sent(1, here, 1)
        sent(9, here, None)
        for lands in range(6):
            sent(10 + lands, *blocks[lands])

        @pl.when(color == 0)
        def _():
            sent(2, here, 1)
            sent(3, here, 0)
            sent(6, mine_x, 1)
            sent(7, mine_y, 0)

        @pl.when(color == 1)
        def _():
            sent(4, mine_x, 0)
            sent(5, mine_y, 1)
            sent(8, mine_d, 0)
            sent(16, mine_d, 1)

    plan = []
    for step in range(GATHERS + 2):
        acts = [(f, step - lag) for f, lag in ((g_third, 2), (g_second, 1), (g_first, 0))]
        acts = [(f, g) for f, g in acts if 0 <= g < GATHERS]
        if step + GATHER_AHEAD < GATHERS:
            acts.append((g_own, step + GATHER_AHEAD))
        plan.append(acts)

    def gather_step():
        if plan:
            for act_of, g in plan.pop(0):
                act_of(g)

    def gather_until(g):
        while any((g_third, g) in acts for acts in plan):
            gather_step()
        g_last(g)

    def unit_ref(k):
        if k < OUT:
            return w_up.at[k - UP]
        if k < MIX:
            return w_out
        return w_qkv.at[k - MIX]

    def own_half(k, y, x):
        return red_a[OUT + k, y, x] if k < UP else unit_ref(k)[y, x, core]

    middle = (z > 0) & (z < n_head - 1)
    top, low_part = pl.ds(0, half), pl.ds(half, half)

    def finals(k):
        if k < UP:
            return [(None, g_down.at[pl.ds(k * rows, rows), :])]
        if k < OUT:
            return [(None, g_up.at[:, pl.ds((k - UP) * D, D)])]
        if k < MIX:
            return [(None, g_out)]
        return [
            (part * WIDE, g_qkv.at[:, pl.ds(part * D + (k - MIX) * WIDE, WIDE)])
            for part in range(3)
        ]

    def r_final(k, i):
        mine = red_a.at[k, yy, xx]
        col, dst = finals(k)[i]
        return mine if col is None else mine.at[:, pl.ds(col, WIDE)], dst

    def r_copy(k, kind):
        mine = red_a.at[k, yy, xx]
        if kind == 0:
            src = red_a.at[UP + k] if k < UP else unit_ref(k).at[:, :, 1 - core]
            dst, target = red_a.at[k], sib
        elif kind == 1:
            src, dst, target = red_a.at[k, :, 1 - xx, top, :], red_b.at[k, 0], xn
        elif kind == 2:
            src, dst, target = red_a.at[k, 1 - yy, :, low_part, :], red_b.at[k, 1], yn
        elif kind == 3:
            src, dst, target = red_a.at[k, 1 - yy, xx, top, :], red_c.at[k, 0], yn
        elif kind == 4:
            src, dst, target = red_a.at[k, yy, 1 - xx, low_part, :], red_c.at[k, 1], xn
        elif kind == 5:
            src, dst, target = mine, red_e.at[k, 0], z_one
        elif kind == 6:
            src, dst, target = mine, red_e.at[k, 1], z_two
        else:
            src, dst = r_final(k, kind - 7)
            target = z_one
        return remote(src, dst, r_send.at[k, kind], r_recv.at[k, kind], target)

    def r_local(k, i):
        src, dst = r_final(k, i)
        return pltpu.make_async_copy(src, dst, r_recv.at[k, 10 + i])

    def added(one, two):
        return low_cast(one.astype(jnp.float32) + two.astype(jnp.float32))

    def r_start(k):
        r_copy(k, 0).start()

    def r_pair(k):
        r_copy(k, 0).wait_recv()
        for y in range(2):
            for x in range(2):
                red_a[k, y, x] = added(own_half(k, y, x), red_a[k, y, x])
        r_copy(k, 1).start()
        r_copy(k, 2).start()
        if k == UP - 1:
            for i in range(UP):
                r_copy(i, 0).wait_send()
            pl.semaphore_signal(free_sem, inc=1, device_id=sib, device_id_type=MESH)

    def r_plane(k):
        r_copy(k, 1).wait_recv()
        red_a[k, 1 - yy, xx, top, :] = added(red_a[k, 1 - yy, xx, top, :], red_b[k, 0, 1 - yy])
        r_copy(k, 3).start()
        r_copy(k, 2).wait_recv()
        red_a[k, yy, 1 - xx, low_part, :] = added(
            red_a[k, yy, 1 - xx, low_part, :], red_b[k, 1, 1 - xx]
        )
        r_copy(k, 4).start()
        red_a[k, yy, xx, top, :] = added(red_a[k, yy, xx, top, :], red_b[k, 0, yy])
        red_a[k, yy, xx, low_part, :] = added(red_a[k, yy, xx, low_part, :], red_b[k, 1, xx])

    def r_whole(k):
        r_copy(k, 3).wait_recv()
        r_copy(k, 4).wait_recv()
        red_a[k, yy, xx, top, :] = added(red_a[k, yy, xx, top, :], red_c[k, 0])
        red_a[k, yy, xx, low_part, :] = added(red_a[k, yy, xx, low_part, :], red_c[k, 1])

        @pl.when(~middle)
        def _():
            r_copy(k, 5).start()

    def r_z_first(k):
        @pl.when(middle)
        def _():
            r_copy(k, 5).wait_recv()
            red_a[k, yy, xx] = added(red_a[k, yy, xx], red_e[k, 0])
            r_copy(k, 6).start()

    def r_z_second(k):
        @pl.when(middle)
        def _():
            r_copy(k, 6).wait()
            red_a[k, yy, xx] = added(red_a[k, yy, xx], red_e[k, 1])
            for i in range(len(finals(k))):
                r_copy(k, 7 + i).start()
                r_local(k, i).start()

    def r_end(k):
        for kind in range(1 if k < UP else 0, 5):
            r_copy(k, kind).wait_send()

        @pl.when(middle)
        def _():
            for i in range(len(finals(k))):
                r_copy(k, 7 + i).wait_send()
                r_local(k, i).wait()

        @pl.when(~middle)
        def _():
            r_copy(k, 5).wait_send()
            for i in range(len(finals(k))):
                r_copy(k, 7 + i).wait_recv()

    stages = (r_pair, r_plane, r_whole, r_z_first, r_z_second)
    r_plan = []
    for tick in range(UNITS + len(stages)):
        acts = [(stages[s], tick - s) for s in reversed(range(1, len(stages)))]
        if tick == 0:
            r_plan.append([(r_pair, 0)])
        acts.append((r_pair, tick + 1))
        r_plan.append([(f, k) for f, k in acts if 0 <= k < UNITS])
    started = []

    def reduce_start(k):
        if k == UP:
            pl.semaphore_wait(free_sem, 1)
        r_start(k)
        started.append(k)

    def reduce_tick():
        if r_plan and all(k in started for _, k in r_plan[0]):
            for act_of, k in r_plan.pop(0):
                act_of(k)

    for g in range(min(GATHER_AHEAD, GATHERS)):
        own_masters(g)
    pl.semaphore_wait(barrier, len(peers))
    for g in range(min(GATHER_AHEAD, GATHERS)):
        g_start(g)

    lens = [lens_ref[s] for s in range(n_seq)]
    ends = []
    total = 0
    for s in range(n_seq):
        total = total + ((lens[s] + (SPAN - 1)) // SPAN) * SPAN
        ends.append(total)
    starts = [0] + ends[:-1]

    def owner_of(row):
        found = jnp.zeros_like(row)
        for s in range(n_seq):
            found = found + (row >= ends[s]).astype(jnp.int32)
        return found

    half_lane = lax.broadcasted_iota(jnp.int32, (T, LANES), 1)
    row = z * T + lax.broadcasted_iota(jnp.int32, (T, LANES), 0)
    first = jnp.zeros_like(row)
    length = jnp.ones_like(row)
    for s in range(n_seq):
        inside = (row >= starts[s]) & (row < ends[s])
        first = jnp.where(inside, starts[s], first)
        length = jnp.where(inside, lens[s], length)
    offset = row - first
    live = (offset < length).astype(jnp.float32)
    angle = 0.5 * math.pi * offset.astype(jnp.float32) / length.astype(jnp.float32)
    angle = jnp.where(half_lane < HD, angle, 0.5 * math.pi - angle)
    cs_ref[...] = jnp.cos(angle) * live
    live_ref[...] = live
    owners = owner_of(row)
    next_owner = owner_of(jnp.full((1, 1), (z + 1) * T, jnp.int32))
    last_owner = owner_of(jnp.full((1, 1), z * T - 1, jnp.int32))
    my_first = owner_of(jnp.full((1, 1), z * T, jnp.int32))
    my_last = owner_of(jnp.full((1, 1), (z + 1) * T - 1, jnp.int32))
    for i, edge in enumerate((next_owner, last_owner, my_first, my_last)):
        keeps[i] = low_cast((owners == edge).astype(jnp.float32))

    def fill_masks(i, carry):
        r0 = pl.multiple_of(i * ROW_TILE, ROW_TILE)
        t_i = r0 + lax.broadcasted_iota(jnp.int32, (ROW_TILE, T), 0)
        u_i = lax.broadcasted_iota(jnp.int32, (ROW_TILE, T), 1)
        same = owner_of(t_i + z * T) == owner_of(u_i + z * T)
        mask[pl.ds(r0, ROW_TILE), :] = low_cast((same & (u_i <= t_i)).astype(jnp.float32))
        mask_t[pl.ds(r0, ROW_TILE), :] = low_cast((same & (u_i >= t_i)).astype(jnp.float32))
        return carry

    lax.fori_loop(0, T // ROW_TILE, fill_masks, 0)

    sq_lane = lax.broadcasted_iota(jnp.int32, (LANES, LANES), 1)
    ones_lane = ((half_lane == HD) | (half_lane == HD + 1)).astype(jnp.float32)

    def softplus(v):
        return jnp.maximum(v, 0.0) + jnp.log1p(jnp.exp(-jnp.abs(v)))

    def slab(p, part):
        return p // 2, slice(None), pl.ds(part * WIDE + (p % 2) * LANES, LANES)

    def pair_cols(p):
        return pl.ds(p * LANES, LANES)

    def split(value):
        swapped = swap_halves(value)
        return jnp.where(half_lane < HD, value, swapped), jnp.where(half_lane < HD, swapped, value)

    def join(left, right):
        return jnp.where(half_lane < HD, left, swap_halves(right))

    def pack_states(p, left, right, own, n_ones):
        place = pl.ds((p % 2) * LANES, LANES)
        own[p // 2, place, :] = low_cast(jnp.where(sq_lane < HD, left, swap_halves(right)))
        for side, part in ((0, left), (1, right)):
            column = part[:, HD : HD + 1]
            if n_ones == 2:
                column = column + part[:, HD + 1 : HD + 2]
            zcol[...] = jnp.where(sq_lane == 2 * (p % 2) + side, column, zcol[...])

    def exchange(which, own, landed, g):
        target = z + 1 - 2 * which
        target = (target + n_head) % n_head
        return remote(
            own.at[g], landed.at[g], s_send.at[which, g], s_recv.at[which, g], (dp, target)
        )

    def place_of(which):
        return z if which == 0 else n_head - 1 - z

    def send_states(which, own, landed, g):
        own[g, 2 * LANES : STATE_ROWS, :] = low_cast(zcol[...].T[0:16, :])

        @pl.when(place_of(which) == 0)
        def _():
            exchange(which, own, landed, g).start()

    def pass_on(which, own, landed, out, n_ones, point):
        for place in range(1, n_head):
            g = point - place
            if 0 <= g < GROUPS:

                @pl.when(place_of(which) == place)
                def _(g=g, place=place):
                    exchange(which, own, landed, g).wait_recv()
                    state_sum[0:STATE_ROWS, :] = landed[g].astype(jnp.float32)
                    if place < n_head - 1:
                        through = (my_first == next_owner) if which == 0 else (my_last == last_owner)
                        own[g] = low_cast(
                            own[g].astype(jnp.float32)
                            + through.astype(jnp.float32) * state_sum[0:STATE_ROWS, :]
                        )
                        exchange(which, own, landed, g).start()
                    unpack(out, n_ones, g)

    def unpack(out, n_ones, g):
        columns = state_sum[2 * LANES : 3 * LANES, :].T
        wide = (sq_lane >= HD) & (sq_lane < HD + n_ones)
        for i in range(2):
            packed = state_sum[i * LANES : (i + 1) * LANES, :]
            for side in (0, 1):
                part = packed if side == 0 else swap_halves(packed)
                column = columns[:, 2 * i + side : 2 * i + side + 1]
                out[4 * g + 2 * i + side] = low_cast(
                    jnp.where(sq_lane < HD, part, jnp.where(wide, column, 0.0))
                )

    def exchange_sent(which, own, landed):
        @pl.when(place_of(which) < n_head - 1)
        def _():
            for g in range(GROUPS):
                exchange(which, own, landed, g).wait_send()

    state_sum[...] = jnp.zeros_like(state_sum)
    state_h[...] = jnp.zeros_like(state_h)
    back_h[...] = jnp.zeros_like(back_h)

    def pass_forward(point):
        pass_on(0, state_own, state_in, state_h, 2, point)

    def pass_backward(point):
        pass_on(1, back_own, back_in, back_h, 1, point)

    zcol[...] = jnp.zeros_like(zcol)

    def features_of(p, part, store):
        cs = cs_ref[...]
        left, right = split(softplus(mixed[slab(p, part)].astype(jnp.float32)))
        store[2 * p] = low_cast(left * cs)
        store[2 * p + 1] = low_cast(right * cs)

    def make_keys(p, carry):
        features_of(p, 1, feat_k)
        v_pair = mixed[slab(p, 2)].astype(jnp.float32)
        val_a[2 * p] = low_cast(jnp.where(half_lane < HD, v_pair, ones_lane))
        val_a[2 * p + 1] = low_cast(jnp.where(half_lane < HD, swap_halves(v_pair), ones_lane))
        left = mm_rows(feat_k[2 * p] * keeps[0], val_a[2 * p])
        right = mm_rows(feat_k[2 * p + 1] * keeps[0], val_a[2 * p + 1])
        pack_states(p, left, right, state_own, 1)
        return carry

    def make_queries(p, carry):
        features_of(p, 0, feat_q)
        return carry

    load_tok.wait()
    for g in range(GROUPS):
        gather_until(g)
        part = mm(tok[...], w_qkv[g].reshape(D, D))
        mixed[g, :, 0:WIDE] = low_cast(part[:, 0:WIDE] + vec_ref[6:7, g * WIDE : (g + 1) * WIDE])
        mixed[g, :, WIDE : 2 * WIDE] = low_cast(
            part[:, WIDE : 2 * WIDE] + vec_ref[7:8, g * WIDE : (g + 1) * WIDE]
        )
        mixed[g, :, 2 * WIDE :] = low_cast(part[:, 2 * WIDE :])
        over_rows(2 * g + 2, make_keys, 0, 2 * g)
        send_states(0, state_own, state_in, g)
        if g:
            pass_forward(g)

    def local_attend(h, carry):
        scores = low_cast(mm_cols(feat_q[h], feat_k[h])) * mask[...]
        num_a[h] = mm(scores, val_a[h])
        return carry

    gather_step()
    for part in range(3):
        over_rows(2 * part + 2, make_queries, 0, 2 * part)
        over_rows(4 * part + 4, local_attend, 0, 4 * part)
        gather_step()
        pass_forward(3 + part)

    def finish_heads(p, carry):
        att = []
        for side in (0, 1):
            h = 2 * p + side
            whole = num_a[h] + mm(feat_q[h] * keeps[2], state_h[h])
            den = whole[:, HD : HD + 1] + (1.0 - live_ref[...])
            inverse = 1.0 / den
            got = whole * inverse
            num_a[h] = jnp.where(half_lane < HD, got, inverse)
            att.append(got)
        shift = vec_ref[8:9, pair_cols(p)]
        heads[:, pair_cols(p)] = low_cast(join(att[0], att[1]) + shift * live_ref[...])
        return carry

    for g in range(GROUPS):
        over_rows(2 * g + 2, finish_heads, 0, 2 * g)

    gather_until(GROUPS)

    def tile_rows(i):
        return slice(i * ROW_TILE, (i + 1) * ROW_TILE)

    def first_norm(i, carry):
        r = tile_rows(i)
        w = w_out[...].reshape(D, D)
        residual = tok[r, :].astype(jnp.float32) + (mm(heads[r, :], w) + vec_ref[4:5, :])
        normed, rstd = norm_rows(residual)
        norm_one[r, :] = normed
        rstd_one[r, :] = jnp.broadcast_to(rstd, (ROW_TILE, LANES))
        hidden = normed * vec_ref[0:1, :] + vec_ref[1:2, :]
        hid[r, :] = hidden
        hid_low[r, :] = low_cast(hidden)
        return carry

    while any(act_of is g_own for acts in plan for act_of, _ in acts):
        gather_step()
    load_cot.start()
    over_rows(T // ROW_TILE, first_norm, 0)

    for j in range(TILES):
        if j % 2 == 0:
            gather_until(GROUPS + 1 + j // 2)

        def ff_up(i, carry, j=j):
            r = tile_rows(i)
            upper = mm(hid_low[r, :], w_up[j].reshape(D, D)) + vec_ref[9 + j : 10 + j, :]
            value, slope = gelu_parts(upper)
            act[r, j * D : (j + 1) * D] = low_cast(value)
            gel[r, j * D : (j + 1) * D] = low_cast(slope)
            return carry

        over_rows(T // ROW_TILE, ff_up, 0)
        gather_step()

    gather_until(GATHERS - 2)
    gather_until(GATHERS - 1)
    load_cot.wait()

    def second_norm(i, sums):
        r = tile_rows(i)
        lowered = mm(act[r, :], w_down[...].reshape(FF, D))
        normed, rstd = norm_rows(hid[r, :] + (lowered + vec_ref[5:6, :]))
        one_low[r, :] = low_cast(normed * vec_ref[2:3, :] + vec_ref[3:4, :])
        dy = ig_ref[r, :]
        d_two = norm_rows_back(dy, normed, rstd, vec_ref[2:3, :])
        hid[r, :] = d_two
        two_low[r, :] = low_cast(d_two)
        return sums[0] + row_sum(dy * normed), sums[1] + row_sum(dy), sums[2] + row_sum(d_two)

    zero_row = jnp.zeros((1, D), jnp.float32)
    gain_two, shift_two, bias_down = over_rows(
        T // ROW_TILE, second_norm, (zero_row, zero_row, zero_row)
    )
    save_y.start()
    vg_ref[2:3, :] = gain_two
    vg_ref[3:4, :] = shift_two
    vg_ref[5:6, :] = bias_down

    for j in range(TILES):
        got = low_cast(mm_rows(act[:, j * D : (j + 1) * D], two_low[...]))
        got = got.reshape(2, TILES, rows, D)
        for k in range(TILES):
            red_a[UP + k, j // 2, j % 2] = jnp.where(core == 0, got[1, k], got[0, k])
            red_a[OUT + k, j // 2, j % 2] = jnp.where(core == 0, got[0, k], got[1, k])
    for k in range(UP):
        reduce_start(k)

    for j in range(TILES):

        def ff_back(i, total, j=j):
            r = tile_rows(i)
            d_act = mm_cols(two_low[r, :], w_down[j // 2, j % 2].reshape(D, D))
            d_upper = d_act * gel[r, j * D : (j + 1) * D].astype(jnp.float32)
            gel[r, j * D : (j + 1) * D] = low_cast(d_upper)
            return total + row_sum(d_upper)

        vg_ref[9 + j : 10 + j, :] = over_rows(T // ROW_TILE, ff_back, zero_row)
        if j % 2 == 1:
            reduce_tick()

    save_y.wait()

    def first_norm_back(i, sums):
        r = tile_rows(i)
        dy = hid[r, :]
        for j in range(TILES):
            dy = dy + mm_cols(gel[r, j * D : (j + 1) * D], w_up[j].reshape(D, D))
        normed = norm_one[r, :]
        d_one = norm_rows_back(dy, normed, rstd_one[r, 0:1], vec_ref[0:1, :])
        ig_ref[r, :] = d_one
        one_low[r, :] = low_cast(d_one)
        return sums[0] + row_sum(dy * normed), sums[1] + row_sum(dy), sums[2] + row_sum(d_one)

    sums = (zero_row, zero_row, zero_row)
    steps = T // ROW_TILE
    sums = over_rows(steps, first_norm_back, sums)
    reduce_tick()
    vg_ref[0:1, :] = sums[0]
    vg_ref[1:2, :] = sums[1]
    vg_ref[4:5, :] = sums[2]

    for g in range(GROUPS + 1, GATHERS - 2):
        g_sent(g)
    turned[...] = hid_low[...].T
    for j in range(TILES):
        got = low_cast(mm(turned[...], gel[:, j * D : (j + 1) * D]))
        w_up[j] = got.reshape(2, 2, 2, rows, D)

    d_heads = two_low
    d_heads[...] = low_cast(mm_cols(one_low[...], w_out[...].reshape(D, D)))
    g_sent(GROUPS)
    w_out[...] = low_cast(mm_rows(heads[...], one_low[...])).reshape(2, 2, 2, rows, D)
    reduce_tick()
    for k in range(UP, MIX):
        reduce_start(k)

    zcol[...] = jnp.zeros_like(zcol)

    def grad_slot(h):
        return slice(None), pl.ds(h * LANES, LANES)

    def back_states(p, carry):
        g_pair = d_heads[:, pair_cols(p)].astype(jnp.float32)
        parts = []
        for side in (0, 1):
            h = 2 * p + side
            saved = num_a[h]
            g = g_pair if side == 0 else swap_halves(g_pair)
            gn = jnp.where(half_lane < HD, g * swap_halves(saved), 0.0)
            gd = -jnp.sum(gn * saved, axis=1, keepdims=True)
            gd_high = low_cast(gd).astype(jnp.float32)
            gn = jnp.where(
                half_lane == HD, gd_high, jnp.where(half_lane == HD + 1, gd - gd_high, gn)
            )
            gn = low_cast(gn)
            act[grad_slot(h)] = gn
            parts.append(mm_rows(feat_q[h] * keeps[1], gn))
        pack_states(p, parts[0], parts[1], back_own, 2)
        return carry

    for g in range(GROUPS):
        over_rows(2 * g + 2, back_states, 0, 2 * g)
        send_states(1, back_own, back_in, g)
        if g == 1:
            reduce_tick()
    pass_backward(1)

    def sigmoid(v):
        e = jnp.exp(-jnp.abs(v))
        return jnp.where(v >= 0, 1.0, e) / (1.0 + e)

    def fold(value):
        value = value * cs_ref[...]
        return value + swap_halves(value)

    def through_features(p, part, left, right):
        value = mixed[slab(p, part)].astype(jnp.float32)
        d_part = sigmoid(value) * jnp.where(half_lane < HD, fold(left), fold(right))
        mixed[slab(p, part)] = low_cast(d_part)
        vg_ref[6 + part : 7 + part, pair_cols(p)] = row_sum(d_part)

    def query_back(p, carry):
        got = []
        for side in (0, 1):
            h = 2 * p + side
            ga = act[grad_slot(h)]
            d_scores = low_cast(mm_cols(ga, val_a[h])) * mask[...]
            got.append(mm(d_scores, feat_k[h]) + mm_cols(ga * keeps[2], state_h[h]))
        through_features(p, 0, got[0], got[1])
        return carry

    for part in range(3):
        over_rows(2 * part + 2, query_back, 0, 2 * part)
        if part == 0:
            reduce_tick()
            pass_backward(2)
    reduce_tick()

    def key_value_back(p, carry):
        keys, values = [], []
        for side in (0, 1):
            h = 2 * p + side
            fq, fk, va, ga = feat_q[h], feat_k[h], val_a[h], act[grad_slot(h)]
            d_scores_t = low_cast(mm_cols(va, ga)) * mask_t[...]
            keys.append(mm(d_scores_t, fq) + mm_cols(va * keeps[3], back_h[h]))
            scores_t = low_cast(mm_cols(fk, fq)) * mask_t[...]
            values.append(mm(scores_t, ga) + mm(fk * keeps[3], back_h[h]))
        through_features(p, 1, keys[0], keys[1])
        d_part = join(values[0], values[1])
        mixed[slab(p, 2)] = low_cast(d_part)
        vg_ref[8:9, pair_cols(p)] = row_sum(d_part)
        return carry

    turned[...] = tok[...].T
    reduce_tick()
    for g in range(GROUPS):
        pass_backward(3 + g)
        over_rows(2 * g + 2, key_value_back, 0, 2 * g)
        ig_ref[...] += mm_cols(mixed[g], w_qkv[g].reshape(D, D))
        g_sent(g)
        w_qkv[g] = low_cast(mm(turned[...], mixed[g])).reshape(2, 2, 2, rows, D)
        reduce_start(MIX + g)
        reduce_tick()

    def vcopy(level):
        target = (sib, xn, yn, z_one, z_two)[level]
        return remote(vg_ref, vec_land.at[level], v_send.at[level], v_recv.at[level], target)

    vg_ref[13:16, :] = jnp.zeros((3, D), jnp.float32)
    vcopy(0).start()
    for level in range(5):
        reduce_tick()
        vcopy(level).wait()
        vg_ref[...] += vec_land[level]
        if level < 4:
            vcopy(level + 1).start()
    while r_plan:
        reduce_tick()
    for k in range(UNITS):
        r_end(k)
    for g in (GATHERS - 2, GATHERS - 1):
        g_sent(g)
    exchange_sent(0, state_own, state_in)
    exchange_sent(1, back_own, back_in)


GATHER_AHEAD = 3


def fits(mesh):
    return mesh.shape["dp"] == 8 and mesh.shape["head"] == 4


def fused_layer(lengths, tokens, cotangent, masters, vector_master):
    n_head = lax.axis_size("head")
    T = tokens.shape[0]
    rows = masters[1].shape[0]
    bf, f32 = jnp.bfloat16, jnp.float32
    V, S = pltpu.VMEM, jax.ShapeDtypeStruct
    vm, anywhere = pl.BlockSpec(memory_space=pltpu.VMEM), pl.BlockSpec(memory_space=pl.ANY)
    out_shape = (S((T, D), bf), S((T, D), f32)) + tuple(S(m.shape, bf) for m in masters)
    out_shape += (S((16, D), f32),)
    shard = (2, 2, 2, rows, D)
    scratch = [
        V((GROUPS, *shard), bf),
        V(shard, bf),
        V((TILES, *shard), bf),
        V((2, 2, 2, TILES * rows, D), bf),
        V((T, D), bf),
        V((GROUPS, T, D), bf),
        V((H, T, LANES), bf),
        V((H, T, LANES), bf),
        V((H, T, LANES), bf),
        V((H, T, LANES), f32),
        V((T, D), bf),
        V((T, D), f32),
        V((T, LANES), f32),
        V((T, D), f32),
        V((T, D), bf),
        V((D, T), bf),
        V((T, FF), bf),
        V((T, FF), bf),
        V((T, D), bf),
        V((T, D), bf),
        V((T, T), bf),
        V((T, T), bf),
        V((T, LANES), f32),
        V((T, LANES), f32),
        V((4, T, LANES), bf),
        V((GROUPS, STATE_ROWS, LANES), bf),
        V((GROUPS, STATE_ROWS, LANES), bf),
        V((GROUPS, STATE_ROWS, LANES), bf),
        V((GROUPS, STATE_ROWS, LANES), bf),
        V((3 * LANES, LANES), f32),
        V((H, LANES, LANES), bf),
        V((H, LANES, LANES), bf),
        V((LANES, LANES), f32),
        V((UNITS, 2, 2, rows, D), bf),
        V((UNITS, 2, 2, rows // 2, D), bf),
        V((UNITS, 2, rows // 2, D), bf),
        V((UNITS, 2, rows, D), bf),
        V((5, 16, D), f32),
        pltpu.SemaphoreType.DMA((18,)),
        pltpu.SemaphoreType.DMA((8, 17)),
        pltpu.SemaphoreType.DMA((8, 17)),
        pltpu.SemaphoreType.DMA((2, GROUPS)),
        pltpu.SemaphoreType.DMA((2, GROUPS)),
        pltpu.SemaphoreType.DMA((UNITS, 13)),
        pltpu.SemaphoreType.DMA((UNITS, 13)),
        pltpu.SemaphoreType.DMA((5,)),
        pltpu.SemaphoreType.DMA((5,)),
        pltpu.SemaphoreType.REGULAR,
    ]
    return pl.pallas_call(
        functools.partial(layer_kernel, n_head, lengths.shape[0]),
        out_shape=out_shape,
        in_specs=[pl.BlockSpec(memory_space=pltpu.SMEM)] + [anywhere] * 6 + [vm],
        out_specs=[anywhere, vm] + [anywhere] * 4 + [vm],
        scratch_shapes=scratch,
        compiler_params=pltpu.CompilerParams(
            collective_id=0, has_side_effects=True, vmem_limit_bytes=VMEM_BYTES
        ),
        name="layer",
    )(lengths, tokens, cotangent, *masters, vector_master)


VMEM_BYTES = 63 * 1024 * 1024


RATES = (1.0 / math.sqrt(D), 1.0 / math.sqrt(OUT_FAN), 1.0 / math.sqrt(D), 1.0 / math.sqrt(FF))
ADAM_ROWS = 32


def adam_step(master, first, second, gradient, rate, decay):
    first_new = first_decay * first + (1.0 - first_decay) * gradient
    second_new = second_decay * second + (1.0 - second_decay) * gradient * gradient
    root = jnp.sqrt(second_new * (1.0 / (1.0 - second_decay**STEP)))
    ratio = (first_new * (rate / (1.0 - first_decay**STEP))) / (root + adam_epsilon)
    return first_new, second_new, master * (1.0 - rate * decay) - ratio


def adam_kernel(*refs):
    ins, outs = refs[:22], refs[22:]
    for i in range(2):
        outs[i][...] = ins[i][...]

    @pl.when(pl.program_id(0) == 0)
    def _():
        vector_new = adam_step(
            ins[18][...], ins[19][...], ins[20][...], ins[21][0:13, :], vector_rate, 0.0
        )
        for i in range(3):
            outs[14 + i][...] = vector_new[i]

    for m in range(4):
        master, first, second, grad = ins[2 + 4 * m : 6 + 4 * m]
        news = adam_step(
            master[...],
            first[...],
            second[...],
            grad[...].astype(jnp.float32),
            RATES[m],
            weight_decay,
        )
        for i in range(3):
            outs[2 + 3 * m + i][...] = news[i]


def adam_all(output, input_grad, masters, firsts, seconds, grads, vectors):
    n_steps = masters[1].shape[0] // ADAM_ROWS

    def rows_of(a):
        return pl.BlockSpec((a.shape[0] // n_steps, a.shape[1]), lambda i: (i, 0))

    def whole(a):
        return pl.BlockSpec(a.shape, lambda i: (0, 0))

    args = [output, input_grad]
    step_rows = pl.cdiv(output.shape[0], n_steps * ADAM_ROWS) * ADAM_ROWS
    in_specs = [pl.BlockSpec((step_rows, D), lambda i: (i, 0))] * 2
    out_shape = [jax.ShapeDtypeStruct(a.shape, a.dtype) for a in args]
    out_specs = list(in_specs)
    for quad in zip(masters, firsts, seconds, grads):
        args += quad
        in_specs += [rows_of(a) for a in quad]
        out_shape += [jax.ShapeDtypeStruct(a.shape, jnp.float32) for a in quad[:3]]
        out_specs += [rows_of(a) for a in quad[:3]]
    args += vectors
    in_specs += [whole(a) for a in vectors]
    out_shape += [jax.ShapeDtypeStruct(a.shape, jnp.float32) for a in vectors[:3]]
    out_specs += [whole(a) for a in vectors[:3]]
    return pl.pallas_call(
        adam_kernel,
        grid=(n_steps,),
        out_shape=out_shape,
        in_specs=in_specs,
        out_specs=out_specs,
        compiler_params=pltpu.CompilerParams(vmem_limit_bytes=VMEM_BYTES),
        name="adam",
    )(*args)


def fused_shards(
    tokens,
    cotangent,
    lengths,
    qkv_master,
    out_master,
    up_master,
    down_master,
    vector_master,
    qkv_first,
    qkv_second,
    out_first,
    out_second,
    up_first,
    up_second,
    down_first,
    down_second,
    vector_first,
    vector_second,
):
    masters = (qkv_master, out_master, up_master, down_master)
    output, input_grad, *grads, vector_grad = fused_layer(
        lengths, tokens, cotangent, masters, vector_master
    )
    firsts = (qkv_first, out_first, up_first, down_first)
    seconds = (qkv_second, out_second, up_second, down_second)
    vectors = [vector_master, vector_first, vector_second, vector_grad]
    return tuple(adam_all(output, input_grad, masters, firsts, seconds, grads, vectors))


def solution(mesh):
    return jax.shard_map(
        fused_shards if fits(mesh) else shards,
        mesh=mesh,
        in_specs=(
            P(("dp", "head"), None),
            P(("dp", "head"), None),
            P("dp"),
            P("dp", None),
            P("dp", None),
            P("dp", None),
            P("dp", None),
            P(),
            P("dp", None),
            P("dp", None),
            P("dp", None),
            P("dp", None),
            P("dp", None),
            P("dp", None),
            P("dp", None),
            P("dp", None),
            P(),
            P(),
        ),
        out_specs=(
            P(("dp", "head"), None),
            P(("dp", "head"), None),
            P("dp", None),
            P("dp", None),
            P("dp", None),
            P("dp", None),
            P("dp", None),
            P("dp", None),
            P("dp", None),
            P("dp", None),
            P("dp", None),
            P("dp", None),
            P("dp", None),
            P("dp", None),
            P(),
            P(),
            P(),
        ),
        check_vma=False,
    )
```

```python
import functools
import math

import jax
import jax.numpy as jnp
from jax import lax
from jax.experimental import pallas as pl
from jax.experimental.pallas import tpu as pltpu
from jax.sharding import PartitionSpec as P

D = 768
H = 12
HD = 64
FF = 3072
SPAN = 64
STEP = 10
OUT_FAN = 1


highest = lax.Precision.HIGHEST
norm_epsilon = 1e-05
first_decay = 0.9
second_decay = 0.999
adam_epsilon = 1e-08
weight_decay = 0.01
vector_rate = 0.2


def layer_norm(residual, gain_row, shift_row):
    center = residual - jnp.mean(residual, axis=-1, keepdims=True)
    spread = jnp.mean(center * center, axis=-1, keepdims=True)
    return center * lax.rsqrt(spread + norm_epsilon) * gain_row + shift_row


def exact_gelu(upper_pre):
    return jax.nn.gelu(upper_pre, approximate=False)


def group_layout(group_lengths, row_count):
    slot_sizes = (group_lengths + SPAN - 1) // SPAN * SPAN
    slot_ends = jnp.cumsum(slot_sizes)
    slot_starts = slot_ends - slot_sizes
    positions = jnp.arange(row_count, dtype=jnp.int32)
    member = (positions[:, None] >= slot_starts[None, :]) & (
        positions[:, None] < slot_ends[None, :]
    )
    seq_first = jnp.sum(jnp.where(member, slot_starts[None, :], 0), axis=1)
    length = jnp.sum(jnp.where(member, group_lengths[None, :], 0), axis=1)
    seq_numbers = jnp.arange(group_lengths.shape[0], dtype=jnp.int32)
    owners = jnp.sum(jnp.where(member, seq_numbers[None, :], 0), axis=1)
    offset = positions - seq_first
    live_rows = (offset < length).astype(jnp.float32)
    angles = 0.5 * math.pi * offset.astype(jnp.float32) / length.astype(jnp.float32)
    cosine = jnp.cos(angles)
    sine_part = jnp.sin(angles)
    span_owner = owners[::SPAN]
    span_order = jnp.arange(span_owner.shape[0], dtype=jnp.int32)
    same_seq = span_owner[None, :] == span_owner[:, None]
    earlier = (same_seq & (span_order[None, :] < span_order[:, None])).astype(jnp.float32)
    return (cosine, sine_part, live_rows, earlier)


def attend(query_rows, key_rows, value_rows, cosine, sine_part, live_rows, earlier):
    row_count = query_rows.shape[0]
    blocks = row_count // SPAN
    soft_query = jax.nn.softplus(query_rows)
    soft_key = jax.nn.softplus(key_rows)
    feat_query = (
        jnp.concatenate([soft_query * cosine[:, None], soft_query * sine_part[:, None]], axis=1)
        * live_rows[:, None]
    )
    feat_key = (
        jnp.concatenate([soft_key * cosine[:, None], soft_key * sine_part[:, None]], axis=1)
        * live_rows[:, None]
    )
    block_query = feat_query.reshape(blocks, SPAN, -1)
    block_key = feat_key.reshape(blocks, SPAN, -1)
    block_value = value_rows.reshape(blocks, SPAN, -1)
    lower_mask = (jnp.arange(SPAN)[:, None] >= jnp.arange(SPAN)[None, :]).astype(jnp.float32)
    scores = jnp.einsum("cik,cjk->cij", block_query, block_key, precision=highest) * lower_mask
    inner_sum = jnp.einsum("cij,cjd->cid", scores, block_value, precision=highest)
    inner_den = jnp.sum(scores, axis=2)
    states = jnp.einsum("cjk,cjd->ckd", block_key, block_value, precision=highest)
    key_sums = jnp.sum(block_key, axis=1)
    before = jnp.einsum("ce,ekd->ckd", earlier, states, precision=highest)
    before_sums = jnp.einsum("ce,ek->ck", earlier, key_sums, precision=highest)
    outer_sum = jnp.einsum("cik,ckd->cid", block_query, before, precision=highest)
    outer_den = jnp.einsum("cik,ck->ci", block_query, before_sums, precision=highest)
    numerator = (inner_sum + outer_sum).reshape(row_count, -1)
    denominator = (inner_den + outer_den).reshape(row_count) + (1.0 - live_rows)
    return numerator / denominator[:, None]


def contract_rows(left, right):
    return lax.dot_general(
        left, right, (((0,), (0,)), ((), ())), preferred_element_type=jnp.float32
    )


def contract_cols(left, right):
    return lax.dot_general(
        left, right, (((1,), (1,)), ((), ())), preferred_element_type=jnp.float32
    )


def adam_update(master, first, second, gradient, rate, decay):
    first_new = first_decay * first + (1.0 - first_decay) * gradient
    second_new = second_decay * second + (1.0 - second_decay) * gradient * gradient
    first_hat = first_new / (1.0 - first_decay**STEP)
    second_hat = second_new / (1.0 - second_decay**STEP)
    master_new = master - rate * (
        first_hat / (jnp.sqrt(second_hat) + adam_epsilon) + decay * master
    )
    return (first_new, second_new, master_new)


def shards(
    tokens,
    cotangent,
    lengths,
    qkv_master,
    out_master,
    up_master,
    down_master,
    vector_master,
    qkv_first,
    qkv_second,
    out_first,
    out_second,
    up_first,
    up_second,
    down_first,
    down_second,
    vector_first,
    vector_second,
):
    mix_weight, out_weight, up_weight, down_weight = (
        lax.all_gather(qkv_master.astype(jnp.bfloat16), "dp", axis=0, tiled=True),
        lax.all_gather(out_master.astype(jnp.bfloat16), "dp", axis=0, tiled=True),
        lax.all_gather(up_master.astype(jnp.bfloat16), "dp", axis=0, tiled=True),
        lax.all_gather(down_master.astype(jnp.bfloat16), "dp", axis=0, tiled=True),
    )
    tok_count = tokens.shape[0]
    width = tokens.shape[1]
    mixed_all = jnp.dot(tokens, mix_weight, preferred_element_type=jnp.float32) + vector_master[
        6:9
    ].reshape(-1)
    mixed_low = mixed_all.astype(jnp.bfloat16)
    query_part = mixed_low[:, :width].reshape(tok_count, H, 1, HD)
    key_part = mixed_low[:, width : 2 * width].reshape(tok_count, H, 1, HD)
    paired = jnp.concatenate([query_part, key_part], axis=2)
    paired = jnp.repeat(paired[:, :, None], 2, axis=2).reshape(tok_count, 4 * width)
    value_part = mixed_low[:, 2 * width :]
    paired_in, values_in = (
        lax.all_to_all(paired, "head", split_axis=1, concat_axis=0, tiled=True),
        lax.all_to_all(value_part, "head", split_axis=1, concat_axis=0, tiled=True),
    )
    group_rows = paired_in.shape[0]
    item_count = paired_in.shape[1] // (2 * HD)
    cosine, sine_part, live_rows, earlier = group_layout(lengths, group_rows)
    stacked = paired_in.reshape(group_rows, item_count, 2, HD).astype(jnp.float32)
    query_items = stacked[:, :, 0]
    key_items = stacked[:, :, 1]
    value_items = values_in.reshape(group_rows, item_count, HD // 2).astype(jnp.float32)

    def mix_items(query_set, key_set, value_set):

        def single(query_rows, key_rows, value_rows):
            return attend(query_rows, key_rows, value_rows, cosine, sine_part, live_rows, earlier)

        return jax.vmap(single, in_axes=1, out_axes=1)(query_set, key_set, value_set)

    attended, mix_back = jax.vjp(mix_items, query_items, key_items, value_items)
    heads_out = attended.reshape(group_rows, item_count * (HD // 2)).astype(jnp.bfloat16)
    heads = lax.all_to_all(heads_out, "head", split_axis=0, concat_axis=1, tiled=True)
    projected = jnp.dot(heads, out_weight, preferred_element_type=jnp.float32) + vector_master[4]
    resid_one = tokens.astype(jnp.float32) + projected
    hidden, norm_one_back = jax.vjp(layer_norm, resid_one, vector_master[0], vector_master[1])
    hidden_low = hidden.astype(jnp.bfloat16)
    upper_pre = jnp.dot(hidden_low, up_weight, preferred_element_type=jnp.float32) + vector_master[
        9:13
    ].reshape(-1)
    active, gelu_back = jax.vjp(exact_gelu, upper_pre)
    active_low = active.astype(jnp.bfloat16)
    lowered = (
        jnp.dot(active_low, down_weight, preferred_element_type=jnp.float32) + vector_master[5]
    )
    output, norm_two_back = jax.vjp(
        layer_norm, hidden + lowered, vector_master[2], vector_master[3]
    )
    grad_two, gain_two, shift_two = norm_two_back(cotangent)
    grad_two_low = grad_two.astype(jnp.bfloat16)
    down_grad = contract_rows(active_low, grad_two_low)
    (upper_grad,) = gelu_back(contract_cols(grad_two_low, down_weight))
    upper_low = upper_grad.astype(jnp.bfloat16)
    up_grad = contract_rows(hidden_low, upper_low)
    hidden_grad = grad_two + contract_cols(upper_low, up_weight)
    grad_one, gain_one, shift_one = norm_one_back(hidden_grad)
    grad_one_low = grad_one.astype(jnp.bfloat16)
    out_grad = contract_rows(heads, grad_one_low)
    heads_grad = contract_cols(grad_one_low, out_weight).astype(jnp.bfloat16)
    heads_back = lax.all_to_all(heads_grad, "head", split_axis=1, concat_axis=0, tiled=True)
    query_back, key_back, value_back = mix_back(
        heads_back.reshape(group_rows, item_count, HD // 2).astype(jnp.float32)
    )
    pair_back = (
        jnp.stack([query_back, key_back], axis=2)
        .astype(jnp.bfloat16)
        .reshape(group_rows, item_count * 2 * HD)
    )
    value_low = value_back.astype(jnp.bfloat16).reshape(group_rows, item_count * (HD // 2))
    pair_home, value_home = (
        lax.all_to_all(pair_back, "head", split_axis=0, concat_axis=1, tiled=True),
        lax.all_to_all(value_low, "head", split_axis=0, concat_axis=1, tiled=True),
    )
    summed = jnp.sum(pair_home.astype(jnp.float32).reshape(tok_count, H, 2, 2, HD), axis=2)
    mixed_grad = jnp.concatenate(
        [
            summed[:, :, 0].reshape(tok_count, width),
            summed[:, :, 1].reshape(tok_count, width),
            value_home.astype(jnp.float32),
        ],
        axis=1,
    )
    mixed_low_grad = mixed_grad.astype(jnp.bfloat16)
    mix_grad = contract_rows(tokens, mixed_low_grad)
    input_grad = grad_one + contract_cols(mixed_low_grad, mix_weight)
    vector_grad = jnp.concatenate(
        [
            jnp.stack(
                [
                    gain_one,
                    shift_one,
                    gain_two,
                    shift_two,
                    jnp.sum(grad_one, axis=0),
                    jnp.sum(grad_two, axis=0),
                ]
            ),
            jnp.sum(mixed_grad, axis=0).reshape(3, width),
            jnp.sum(upper_grad, axis=0).reshape(4, width),
        ],
        axis=0,
    )
    local_grads = (mix_grad, out_grad, up_grad, down_grad)
    row_parts = (
        lax.psum_scatter(
            local_grads[0].astype(jnp.bfloat16), "dp", scatter_dimension=0, tiled=True
        ).astype(jnp.float32),
        lax.psum_scatter(
            local_grads[1].astype(jnp.bfloat16), "dp", scatter_dimension=0, tiled=True
        ).astype(jnp.float32),
        lax.psum_scatter(
            local_grads[2].astype(jnp.bfloat16), "dp", scatter_dimension=0, tiled=True
        ).astype(jnp.float32),
        lax.psum_scatter(
            local_grads[3].astype(jnp.bfloat16), "dp", scatter_dimension=0, tiled=True
        ).astype(jnp.float32),
    )
    reduced = (
        lax.psum(row_parts[0].astype(jnp.bfloat16), "head").astype(jnp.float32),
        lax.psum(row_parts[1].astype(jnp.bfloat16), "head").astype(jnp.float32),
        lax.psum(row_parts[2].astype(jnp.bfloat16), "head").astype(jnp.float32),
        lax.psum(row_parts[3].astype(jnp.bfloat16), "head").astype(jnp.float32),
    )
    vector_total = lax.psum(vector_grad, ("dp", "head"))
    qkv_new = adam_update(
        qkv_master, qkv_first, qkv_second, reduced[0], 1.0 / math.sqrt(D), weight_decay
    )
    out_new = adam_update(
        out_master, out_first, out_second, reduced[1], 1.0 / math.sqrt(OUT_FAN), weight_decay
    )
    up_new = adam_update(
        up_master, up_first, up_second, reduced[2], 1.0 / math.sqrt(D), weight_decay
    )
    down_new = adam_update(
        down_master, down_first, down_second, reduced[3], 1.0 / math.sqrt(FF), weight_decay
    )
    vector_new = adam_update(
        vector_master, vector_first, vector_second, vector_total, vector_rate, 0.0
    )
    return (
        output.astype(jnp.bfloat16),
        input_grad,
        qkv_new[0],
        qkv_new[1],
        qkv_new[2],
        out_new[0],
        out_new[1],
        out_new[2],
        up_new[0],
        up_new[1],
        up_new[2],
        down_new[0],
        down_new[1],
        down_new[2],
        vector_new[0],
        vector_new[1],
        vector_new[2],
    )


PAIRS = H // 2
LANES = 2 * HD
GROUPS = 3
STATE_ROWS = (PAIRS // GROUPS) * LANES + 16
WIDE = D // GROUPS
TILES = FF // D
ROW_TILE = 256
MESH = pl.DeviceIdType.MESH
DOWN, UP, OUT, MIX = 0, TILES, 2 * TILES, 2 * TILES + 1
UNITS = 2 * TILES + 1 + GROUPS


def mm(left, right):
    return jnp.dot(left, right, preferred_element_type=jnp.float32)


def mm_cols(left, right):
    return lax.dot_general(
        left, right, (((1,), (1,)), ((), ())), preferred_element_type=jnp.float32
    )


def mm_rows(left, right):
    return lax.dot_general(
        left, right, (((0,), (0,)), ((), ())), preferred_element_type=jnp.float32
    )


def swap_halves(slab):
    return pltpu.roll(slab, HD, 1)


def low_cast(value):
    return value.astype(jnp.bfloat16)


def row_sum(value):
    return jnp.sum(value, axis=0, keepdims=True)


def gelu_parts(z):
    x = jnp.abs(z) * (1.0 / math.sqrt(2.0))
    t = 1.0 / (1.0 + 0.3275911 * x)
    bell = jnp.exp(-0.5 * z * z)
    poly = t * (
        0.254829592
        + t * (-0.284496736 + t * (1.421413741 + t * (-1.453152027 + t * 1.061405429)))
    )
    upper_tail = 0.5 * poly * bell
    phi = jnp.where(z >= 0, 1.0 - upper_tail, upper_tail)
    return z * phi, phi + z * (bell * (1.0 / math.sqrt(2.0 * math.pi)))


def over_rows(count, body, carry, start=0):
    for i in range(start, count):
        carry = body(i, carry)
    return carry


def norm_rows(residual):
    center = residual - jnp.mean(residual, axis=-1, keepdims=True)
    rstd = lax.rsqrt(jnp.mean(center * center, axis=-1, keepdims=True) + norm_epsilon)
    return center * rstd, rstd


def norm_rows_back(dy, normed, rstd, gain):
    e = dy * gain
    return rstd * (
        e
        - jnp.mean(e, axis=-1, keepdims=True)
        - normed * jnp.mean(e * normed, axis=-1, keepdims=True)
    )


def layer_kernel(
    n_head,
    n_seq,
    lens_ref,
    tok_hbm,
    cot_hbm,
    qkv_f,
    out_f,
    up_f,
    down_f,
    vec_ref,
    y_hbm,
    ig_hbm,
    g_qkv,
    g_out,
    g_up,
    g_down,
    vg_ref,
    w_qkv,
    w_out,
    w_up,
    w_down,
    tok,
    mixed,
    feat_q,
    feat_k,
    val_a,
    num_a,
    heads,
    norm_one,
    rstd_one,
    hid,
    hid_low,
    turned,
    act,
    gel,
    two_low,
    one_low,
    mask,
    mask_t,
    cs_ref,
    live_ref,
    keeps,
    state_own,
    state_in,
    back_own,
    back_in,
    state_sum,
    state_h,
    back_h,
    zcol,
    red_a,
    red_b,
    red_c,
    red_e,
    vec_land,
    load_sem,
    g_send,
    g_recv,
    s_send,
    s_recv,
    r_send,
    r_recv,
    v_send,
    v_recv,
    free_sem,
    ig_ref,
):
    T = tok.shape[0]
    rows = w_out.shape[3]
    half = rows // 2
    dp = lax.axis_index("dp")
    z = lax.axis_index("head")
    core = dp % 2
    xx = (dp // 2) % 2
    yy = dp // 4
    color = z % 2
    sib = (dp + 1 - 2 * core, z)
    xn = (dp + 2 - 4 * xx, z)
    yn = (dp + 4 - 8 * yy, z)
    z_one = (dp, z + 1 - 2 * color)
    z_two = (dp, (z + 3 + 2 * color) % n_head)

    def load(i, src, dst):
        return pltpu.make_async_copy(src, dst, load_sem.at[i])

    def spot(ref, i):
        return ref.at[pl.ds(i * rows, rows), :]

    loads = []
    for g in range(GROUPS):
        for part in range(3):
            loads.append(
                load(
                    len(loads),
                    qkv_f.at[:, pl.ds(part * D + g * WIDE, WIDE)],
                    hid.at[pl.ds(g * rows, rows), pl.ds(part * WIDE, WIDE)],
                )
            )
    loads.append(load(len(loads), out_f, spot(hid, GROUPS)))
    for j in range(TILES):
        loads.append(load(len(loads), up_f.at[:, pl.ds(j * D, D)], spot(norm_one, j)))
    loads.append(load(len(loads), down_f, ig_ref.at[pl.ds(0, TILES * rows), :]))
    load_tok = load(len(loads), tok_hbm, tok)
    load_cot = load(len(loads) + 1, cot_hbm, ig_ref)
    save_y = load(len(loads) + 2, one_low, y_hbm)
    save_ig = load(len(loads) + 3, ig_ref, ig_hbm)
    for copy in loads:
        copy.start()
    load_tok.start()

    barrier = pltpu.get_barrier_semaphore()
    peers = [sib, xn, yn]
    for k in range(1, n_head):
        peers.append((dp, (z + k) % n_head))
    for peer in peers:
        pl.semaphore_signal(barrier, inc=1, device_id=peer, device_id_type=MESH)

    def remote(src, dst, send, recv, target):
        return pltpu.make_async_remote_copy(
            src_ref=src,
            dst_ref=dst,
            send_sem=send,
            recv_sem=recv,
            device_id=target,
            device_id_type=MESH,
        )

    down_parts = ((0, 2), (2, 1), (3, 1))
    FIRST_DOWN = GROUPS + 1 + TILES // 2
    GATHERS = FIRST_DOWN + len(down_parts)

    def piece(g, y, x, c, which):
        if g < GROUPS:
            ref, size, base = w_qkv.at[g, y, x, c], rows, 0
        elif g == GROUPS:
            ref, size, base = w_out.at[y, x, c], rows, 0
        elif g < GROUPS + 1 + TILES // 2:
            i = g - GROUPS - 1
            if which is None:
                return w_up.at[pl.ds(2 * i, 2), y, x, c]
            return w_up.at[
                pl.ds(2 * i, 2), y, x, c, pl.ds(pl.multiple_of(which * half, half), half), :
            ]
        else:
            base, size = (rows * v for v in down_parts[g - FIRST_DOWN])
            ref = w_down.at[y, x, c]
        if which is None:
            return ref.at[pl.ds(base, size), :]
        return ref.at[pl.ds(base + which * (size // 2), size // 2), :]

    def own_masters(g):
        if g < GROUPS:
            for part in range(3):
                loads[3 * g + part].wait()
            w_qkv[g, yy, xx, core] = low_cast(hid[g * rows : (g + 1) * rows, :])
        elif g == GROUPS:
            loads[9].wait()
            w_out[yy, xx, core] = low_cast(hid[g * rows : (g + 1) * rows, :])
        elif g < GROUPS + 1 + TILES // 2:
            for j in range(2 * (g - GROUPS - 1), 2 * (g - GROUPS)):
                loads[10 + j].wait()
                w_up[j, yy, xx, core] = low_cast(norm_one[j * rows : (j + 1) * rows, :])
        else:
            if g == FIRST_DOWN:
                loads[10 + TILES].wait()
            base, size = (rows * v for v in down_parts[g - FIRST_DOWN])
            span = slice(base, base + size)
            w_down[yy, xx, core, span, :] = low_cast(ig_ref[span, :])

    here, mine_x, mine_y, mine_d = (yy, xx), (yy, 1 - xx), (1 - yy, xx), (1 - yy, 1 - xx)

    def gcopy(g, kind, chip, which, target, lands):
        ref = piece(g, chip[0], chip[1], core, which)
        return remote(ref, ref, g_send.at[g, kind], g_recv.at[g, lands], target)

    def landed(g, chip, which, lands):
        gcopy(g, 0, chip, which, sib, lands).wait_recv()

    blocks = ((mine_x, 0), (mine_x, 1), (mine_y, 0), (mine_y, 1), (mine_d, 0), (mine_d, 1))

    def hand_over(g, lands):
        chip, which = blocks[lands]
        gcopy(g, 10 + lands, chip, which, sib, 7 + lands).start()

    def arrived(g, lands):
        chip, which = blocks[lands]
        landed(g, chip, which, lands)

    def g_start(g):
        gcopy(g, 0, here, 0, xn, 0).start()
        gcopy(g, 1, here, 1, yn, 3).start()

        @pl.when(color == 0)
        def _():
            gcopy(g, 2, here, 1, xn, 1).start()
            gcopy(g, 3, here, 0, yn, 2).start()

        gcopy(g, 9, here, None, sib, 6).start()

    def g_own(g):
        own_masters(g)
        g_start(g)

    def g_first(g):
        arrived(g, 0)

        @pl.when(color == 1)
        def _():
            gcopy(g, 4, mine_x, 0, yn, 4).start()

        arrived(g, 3)

        @pl.when(color == 1)
        def _():
            gcopy(g, 5, mine_y, 1, xn, 5).start()

        hand_over(g, 0)
        hand_over(g, 3)

        @pl.when(color == 0)
        def _():
            arrived(g, 1)
            gcopy(g, 6, mine_x, 1, z_one, 1).start()
            arrived(g, 2)
            gcopy(g, 7, mine_y, 0, z_one, 2).start()
            hand_over(g, 1)
            hand_over(g, 2)

    def g_second(g):
        @pl.when(color == 1)
        def _():
            arrived(g, 4)
            gcopy(g, 8, mine_d, 0, z_one, 4).start()
            arrived(g, 5)
            gcopy(g, 16, mine_d, 1, z_one, 5).start()
            hand_over(g, 4)
            hand_over(g, 5)
            arrived(g, 1)
            hand_over(g, 1)
            arrived(g, 2)
            hand_over(g, 2)

    def g_third(g):
        @pl.when(color == 0)
        def _():
            arrived(g, 4)
            hand_over(g, 4)
            arrived(g, 5)
            hand_over(g, 5)

    def g_last(g):
        landed(g, here, None, 6)
        for lands in range(6):
            chip, which = blocks[lands]
            landed(g, chip, which, 7 + lands)

    def g_sent(g):
        def sent(kind, chip, which):
            gcopy(g, kind, chip, which, sib, 0).wait_send()

        sent(0, here, 0)
        sent(1, here, 1)
        sent(9, here, None)
        for lands in range(6):
            sent(10 + lands, *blocks[lands])

        @pl.when(color == 0)
        def _():
            sent(2, here, 1)
            sent(3, here, 0)
            sent(6, mine_x, 1)
            sent(7, mine_y, 0)

        @pl.when(color == 1)
        def _():
            sent(4, mine_x, 0)
            sent(5, mine_y, 1)
            sent(8, mine_d, 0)
            sent(16, mine_d, 1)

    plan = []
    for step in range(GATHERS + 2):
        acts = [(f, step - lag) for f, lag in ((g_third, 2), (g_second, 1), (g_first, 0))]
        acts = [(f, g) for f, g in acts if 0 <= g < GATHERS]
        if step + GATHER_AHEAD < GATHERS:
            acts.append((g_own, step + GATHER_AHEAD))
        plan.append(acts)

    def gather_step():
        if plan:
            for act_of, g in plan.pop(0):
                act_of(g)

    def gather_until(g):
        while any((g_third, g) in acts for acts in plan):
            gather_step()
        g_last(g)

    def unit_ref(k):
        if k < OUT:
            return w_up.at[k - UP]
        if k < MIX:
            return w_out
        return w_qkv.at[k - MIX]

    def own_half(k, y, x):
        return red_a[OUT + k, y, x] if k < UP else unit_ref(k)[y, x, core]

    middle = (z > 0) & (z < n_head - 1)
    top, low_part = pl.ds(0, half), pl.ds(half, half)

    def finals(k):
        if k < UP:
            return [(None, g_down.at[pl.ds(k * rows, rows), :])]
        if k < OUT:
            return [(None, g_up.at[:, pl.ds((k - UP) * D, D)])]
        if k < MIX:
            return [(None, g_out)]
        return [
            (part * WIDE, g_qkv.at[:, pl.ds(part * D + (k - MIX) * WIDE, WIDE)])
            for part in range(3)
        ]

    def r_final(k, i):
        mine = red_a.at[k, yy, xx]
        col, dst = finals(k)[i]
        return mine if col is None else mine.at[:, pl.ds(col, WIDE)], dst

    def r_copy(k, kind):
        mine = red_a.at[k, yy, xx]
        if kind == 0:
            src = red_a.at[UP + k] if k < UP else unit_ref(k).at[:, :, 1 - core]
            dst, target = red_a.at[k], sib
        elif kind == 1:
            src, dst, target = red_a.at[k, :, 1 - xx, top, :], red_b.at[k, 0], xn
        elif kind == 2:
            src, dst, target = red_a.at[k, 1 - yy, :, low_part, :], red_b.at[k, 1], yn
        elif kind == 3:
            src, dst, target = red_a.at[k, 1 - yy, xx, top, :], red_c.at[k, 0], yn
        elif kind == 4:
            src, dst, target = red_a.at[k, yy, 1 - xx, low_part, :], red_c.at[k, 1], xn
        elif kind == 5:
            src, dst, target = mine, red_e.at[k, 0], z_one
        elif kind == 6:
            src, dst, target = mine, red_e.at[k, 1], z_two
        else:
            src, dst = r_final(k, kind - 7)
            target = z_one
        return remote(src, dst, r_send.at[k, kind], r_recv.at[k, kind], target)

    def r_local(k, i):
        src, dst = r_final(k, i)
        return pltpu.make_async_copy(src, dst, r_recv.at[k, 10 + i])

    def added(one, two):
        return low_cast(one.astype(jnp.float32) + two.astype(jnp.float32))

    def r_start(k):
        r_copy(k, 0).start()

    def r_pair(k):
        r_copy(k, 0).wait_recv()
        for y in range(2):
            for x in range(2):
                red_a[k, y, x] = added(own_half(k, y, x), red_a[k, y, x])
        r_copy(k, 1).start()
        r_copy(k, 2).start()
        if k == UP - 1:
            for i in range(UP):
                r_copy(i, 0).wait_send()
            pl.semaphore_signal(free_sem, inc=1, device_id=sib, device_id_type=MESH)

    def r_plane(k):
        r_copy(k, 1).wait_recv()
        red_a[k, 1 - yy, xx, top, :] = added(red_a[k, 1 - yy, xx, top, :], red_b[k, 0, 1 - yy])
        r_copy(k, 3).start()
        r_copy(k, 2).wait_recv()
        red_a[k, yy, 1 - xx, low_part, :] = added(
            red_a[k, yy, 1 - xx, low_part, :], red_b[k, 1, 1 - xx]
        )
        r_copy(k, 4).start()
        red_a[k, yy, xx, top, :] = added(red_a[k, yy, xx, top, :], red_b[k, 0, yy])
        red_a[k, yy, xx, low_part, :] = added(red_a[k, yy, xx, low_part, :], red_b[k, 1, xx])

    def r_whole(k):
        r_copy(k, 3).wait_recv()
        r_copy(k, 4).wait_recv()
        red_a[k, yy, xx, top, :] = added(red_a[k, yy, xx, top, :], red_c[k, 0])
        red_a[k, yy, xx, low_part, :] = added(red_a[k, yy, xx, low_part, :], red_c[k, 1])

        @pl.when(~middle)
        def _():
            r_copy(k, 5).start()

    def r_z_first(k):
        @pl.when(middle)
        def _():
            r_copy(k, 5).wait_recv()
            red_a[k, yy, xx] = added(red_a[k, yy, xx], red_e[k, 0])
            r_copy(k, 6).start()

    def r_z_second(k):
        @pl.when(middle)
        def _():
            r_copy(k, 6).wait()
            red_a[k, yy, xx] = added(red_a[k, yy, xx], red_e[k, 1])
            for i in range(len(finals(k))):
                r_copy(k, 7 + i).start()
                r_local(k, i).start()

    def r_end(k):
        for kind in range(1 if k < UP else 0, 5):
            r_copy(k, kind).wait_send()

        @pl.when(middle)
        def _():
            for i in range(len(finals(k))):
                r_copy(k, 7 + i).wait_send()
                r_local(k, i).wait()

        @pl.when(~middle)
        def _():
            r_copy(k, 5).wait_send()
            for i in range(len(finals(k))):
                r_copy(k, 7 + i).wait_recv()

    stages = (r_pair, r_plane, r_whole, r_z_first, r_z_second)
    r_plan = []
    for tick in range(UNITS + len(stages)):
        acts = [(stages[s], tick - s) for s in reversed(range(1, len(stages)))]
        if tick == 0:
            r_plan.append([(r_pair, 0)])
        acts.append((r_pair, tick + 1))
        r_plan.append([(f, k) for f, k in acts if 0 <= k < UNITS])
    started = []

    def reduce_start(k):
        if k == UP:
            pl.semaphore_wait(free_sem, 1)
        r_start(k)
        started.append(k)

    def reduce_tick():
        if r_plan and all(k in started for _, k in r_plan[0]):
            for act_of, k in r_plan.pop(0):
                act_of(k)

    for g in range(min(GATHER_AHEAD, GATHERS)):
        own_masters(g)
    pl.semaphore_wait(barrier, len(peers))
    for g in range(min(GATHER_AHEAD, GATHERS)):
        g_start(g)

    lens = [lens_ref[s] for s in range(n_seq)]
    ends = []
    total = 0
    for s in range(n_seq):
        total = total + ((lens[s] + (SPAN - 1)) // SPAN) * SPAN
        ends.append(total)
    starts = [0] + ends[:-1]

    def owner_of(row):
        found = jnp.zeros_like(row)
        for s in range(n_seq):
            found = found + (row >= ends[s]).astype(jnp.int32)
        return found

    half_lane = lax.broadcasted_iota(jnp.int32, (T, LANES), 1)
    row = z * T + lax.broadcasted_iota(jnp.int32, (T, LANES), 0)
    first = jnp.zeros_like(row)
    length = jnp.ones_like(row)
    for s in range(n_seq):
        inside = (row >= starts[s]) & (row < ends[s])
        first = jnp.where(inside, starts[s], first)
        length = jnp.where(inside, lens[s], length)
    offset = row - first
    live = (offset < length).astype(jnp.float32)
    angle = 0.5 * math.pi * offset.astype(jnp.float32) / length.astype(jnp.float32)
    angle = jnp.where(half_lane < HD, angle, 0.5 * math.pi - angle)
    cs_ref[...] = jnp.cos(angle) * live
    live_ref[...] = live
    owners = owner_of(row)
    next_owner = owner_of(jnp.full((1, 1), (z + 1) * T, jnp.int32))
    last_owner = owner_of(jnp.full((1, 1), z * T - 1, jnp.int32))
    my_first = owner_of(jnp.full((1, 1), z * T, jnp.int32))
    my_last = owner_of(jnp.full((1, 1), (z + 1) * T - 1, jnp.int32))
    for i, edge in enumerate((next_owner, last_owner, my_first, my_last)):
        keeps[i] = low_cast((owners == edge).astype(jnp.float32))

    def fill_masks(i, carry):
        r0 = pl.multiple_of(i * ROW_TILE, ROW_TILE)
        t_i = r0 + lax.broadcasted_iota(jnp.int32, (ROW_TILE, T), 0)
        u_i = lax.broadcasted_iota(jnp.int32, (ROW_TILE, T), 1)
        same = owner_of(t_i + z * T) == owner_of(u_i + z * T)
        mask[pl.ds(r0, ROW_TILE), :] = low_cast((same & (u_i <= t_i)).astype(jnp.float32))
        mask_t[pl.ds(r0, ROW_TILE), :] = low_cast((same & (u_i >= t_i)).astype(jnp.float32))
        return carry

    lax.fori_loop(0, T // ROW_TILE, fill_masks, 0)

    sq_lane = lax.broadcasted_iota(jnp.int32, (LANES, LANES), 1)
    ones_lane = ((half_lane == HD) | (half_lane == HD + 1)).astype(jnp.float32)

    def softplus(v):
        return jnp.maximum(v, 0.0) + jnp.log1p(jnp.exp(-jnp.abs(v)))

    def slab(p, part):
        return p // 2, slice(None), pl.ds(part * WIDE + (p % 2) * LANES, LANES)

    def pair_cols(p):
        return pl.ds(p * LANES, LANES)

    def split(value):
        swapped = swap_halves(value)
        return jnp.where(half_lane < HD, value, swapped), jnp.where(half_lane < HD, swapped, value)

    def join(left, right):
        return jnp.where(half_lane < HD, left, swap_halves(right))

    def pack_states(p, left, right, own, n_ones):
        place = pl.ds((p % 2) * LANES, LANES)
        own[p // 2, place, :] = low_cast(jnp.where(sq_lane < HD, left, swap_halves(right)))
        for side, part in ((0, left), (1, right)):
            column = part[:, HD : HD + 1]
            if n_ones == 2:
                column = column + part[:, HD + 1 : HD + 2]
            zcol[...] = jnp.where(sq_lane == 2 * (p % 2) + side, column, zcol[...])

    def exchange(which, own, landed, g):
        target = z + 1 - 2 * which
        target = (target + n_head) % n_head
        return remote(
            own.at[g], landed.at[g], s_send.at[which, g], s_recv.at[which, g], (dp, target)
        )

    def place_of(which):
        return z if which == 0 else n_head - 1 - z

    def send_states(which, own, landed, g):
        own[g, 2 * LANES : STATE_ROWS, :] = low_cast(zcol[...].T[0:16, :])

        @pl.when(place_of(which) == 0)
        def _():
            exchange(which, own, landed, g).start()

    def pass_on(which, own, landed, out, n_ones, point):
        for place in range(1, n_head):
            g = point - place
            if 0 <= g < GROUPS:

                @pl.when(place_of(which) == place)
                def _(g=g, place=place):
                    exchange(which, own, landed, g).wait_recv()
                    state_sum[0:STATE_ROWS, :] = landed[g].astype(jnp.float32)
                    if place < n_head - 1:
                        through = (my_first == next_owner) if which == 0 else (my_last == last_owner)
                        own[g] = low_cast(
                            own[g].astype(jnp.float32)
                            + through.astype(jnp.float32) * state_sum[0:STATE_ROWS, :]
                        )
                        exchange(which, own, landed, g).start()
                    unpack(out, n_ones, g)

    def unpack(out, n_ones, g):
        columns = state_sum[2 * LANES : 3 * LANES, :].T
        wide = (sq_lane >= HD) & (sq_lane < HD + n_ones)
        for i in range(2):
            packed = state_sum[i * LANES : (i + 1) * LANES, :]
            for side in (0, 1):
                part = packed if side == 0 else swap_halves(packed)
                column = columns[:, 2 * i + side : 2 * i + side + 1]
                out[4 * g + 2 * i + side] = low_cast(
                    jnp.where(sq_lane < HD, part, jnp.where(wide, column, 0.0))
                )

    def exchange_sent(which, own, landed):
        @pl.when(place_of(which) < n_head - 1)
        def _():
            for g in range(GROUPS):
                exchange(which, own, landed, g).wait_send()

    state_sum[...] = jnp.zeros_like(state_sum)
    state_h[...] = jnp.zeros_like(state_h)
    back_h[...] = jnp.zeros_like(back_h)

    def pass_forward(point):
        pass_on(0, state_own, state_in, state_h, 2, point)

    def pass_backward(point):
        pass_on(1, back_own, back_in, back_h, 1, point)

    zcol[...] = jnp.zeros_like(zcol)

    def features_of(p, part, store):
        cs = cs_ref[...]
        left, right = split(softplus(mixed[slab(p, part)].astype(jnp.float32)))
        store[2 * p] = low_cast(left * cs)
        store[2 * p + 1] = low_cast(right * cs)

    def make_keys(p, carry):
        features_of(p, 1, feat_k)
        v_pair = mixed[slab(p, 2)].astype(jnp.float32)
        val_a[2 * p] = low_cast(jnp.where(half_lane < HD, v_pair, ones_lane))
        val_a[2 * p + 1] = low_cast(jnp.where(half_lane < HD, swap_halves(v_pair), ones_lane))
        left = mm_rows(feat_k[2 * p] * keeps[0], val_a[2 * p])
        right = mm_rows(feat_k[2 * p + 1] * keeps[0], val_a[2 * p + 1])
        pack_states(p, left, right, state_own, 1)
        return carry

    def make_queries(p, carry):
        features_of(p, 0, feat_q)
        return carry

    load_tok.wait()
    for g in range(GROUPS):
        gather_until(g)
        part = mm(tok[...], w_qkv[g].reshape(D, D))
        mixed[g, :, 0:WIDE] = low_cast(part[:, 0:WIDE] + vec_ref[6:7, g * WIDE : (g + 1) * WIDE])
        mixed[g, :, WIDE : 2 * WIDE] = low_cast(
            part[:, WIDE : 2 * WIDE] + vec_ref[7:8, g * WIDE : (g + 1) * WIDE]
        )
        mixed[g, :, 2 * WIDE :] = low_cast(part[:, 2 * WIDE :])
        over_rows(2 * g + 2, make_keys, 0, 2 * g)
        send_states(0, state_own, state_in, g)
        if g:
            pass_forward(g)

    def local_attend(h, carry):
        scores = low_cast(mm_cols(feat_q[h], feat_k[h])) * mask[...]
        num_a[h] = mm(scores, val_a[h])
        return carry

    for part in range(3):
        over_rows(2 * part + 2, make_queries, 0, 2 * part)
        over_rows(4 * part + 4, local_attend, 0, 4 * part)
        gather_step()
        pass_forward(3 + part)

    def finish_heads(p, carry):
        att = []
        for side in (0, 1):
            h = 2 * p + side
            whole = num_a[h] + mm(feat_q[h] * keeps[2], state_h[h])
            den = whole[:, HD : HD + 1] + (1.0 - live_ref[...])
            inverse = 1.0 / den
            got = whole * inverse
            num_a[h] = jnp.where(half_lane < HD, got, inverse)
            att.append(got)
        shift = vec_ref[8:9, pair_cols(p)]
        heads[:, pair_cols(p)] = low_cast(join(att[0], att[1]) + shift * live_ref[...])
        return carry

    for g in range(GROUPS):
        over_rows(2 * g + 2, finish_heads, 0, 2 * g)

    gather_step()

    gather_until(GROUPS)

    def tile_rows(i):
        return slice(i * ROW_TILE, (i + 1) * ROW_TILE)

    def first_norm(i, carry):
        r = tile_rows(i)
        w = w_out[...].reshape(D, D)
        residual = tok[r, :].astype(jnp.float32) + (mm(heads[r, :], w) + vec_ref[4:5, :])
        normed, rstd = norm_rows(residual)
        norm_one[r, :] = normed
        rstd_one[r, :] = jnp.broadcast_to(rstd, (ROW_TILE, LANES))
        hidden = normed * vec_ref[0:1, :] + vec_ref[1:2, :]
        hid[r, :] = hidden
        hid_low[r, :] = low_cast(hidden)
        return carry

    while any(act_of is g_own for acts in plan for act_of, _ in acts):
        gather_step()
    load_cot.start()
    over_rows(T // ROW_TILE, first_norm, 0)

    for j in range(TILES):
        if j % 2 == 0:
            gather_until(GROUPS + 1 + j // 2)

        def ff_up(i, carry, j=j):
            r = tile_rows(i)
            upper = mm(hid_low[r, :], w_up[j].reshape(D, D)) + vec_ref[9 + j : 10 + j, :]
            value, slope = gelu_parts(upper)
            act[r, j * D : (j + 1) * D] = low_cast(value)
            gel[r, j * D : (j + 1) * D] = low_cast(slope)
            return carry

        over_rows(T // ROW_TILE, ff_up, 0)
        gather_step()

    for g in range(FIRST_DOWN, GATHERS):
        gather_until(g)
    load_cot.wait()

    def second_norm(i, sums):
        r = tile_rows(i)
        lowered = mm(act[r, :], w_down[...].reshape(FF, D))
        normed, rstd = norm_rows(hid[r, :] + (lowered + vec_ref[5:6, :]))
        one_low[r, :] = low_cast(normed * vec_ref[2:3, :] + vec_ref[3:4, :])
        dy = ig_ref[r, :]
        d_two = norm_rows_back(dy, normed, rstd, vec_ref[2:3, :])
        hid[r, :] = d_two
        two_low[r, :] = low_cast(d_two)
        return sums[0] + row_sum(dy * normed), sums[1] + row_sum(dy), sums[2] + row_sum(d_two)

    zero_row = jnp.zeros((1, D), jnp.float32)
    gain_two, shift_two, bias_down = over_rows(
        T // ROW_TILE, second_norm, (zero_row, zero_row, zero_row)
    )
    save_y.start()
    vg_ref[2:3, :] = gain_two
    vg_ref[3:4, :] = shift_two
    vg_ref[5:6, :] = bias_down

    for j in range(TILES):
        got = low_cast(mm_rows(act[:, j * D : (j + 1) * D], two_low[...]))
        got = got.reshape(2, TILES, rows, D)
        for k in range(TILES):
            red_a[UP + k, j // 2, j % 2] = jnp.where(core == 0, got[1, k], got[0, k])
            red_a[OUT + k, j // 2, j % 2] = jnp.where(core == 0, got[0, k], got[1, k])
    for k in range(UP):
        reduce_start(k)

    for j in range(TILES):

        def ff_back(i, total, j=j):
            r = tile_rows(i)
            d_act = mm_cols(two_low[r, :], w_down[j // 2, j % 2].reshape(D, D))
            d_upper = d_act * gel[r, j * D : (j + 1) * D].astype(jnp.float32)
            gel[r, j * D : (j + 1) * D] = low_cast(d_upper)
            return total + row_sum(d_upper)

        vg_ref[9 + j : 10 + j, :] = over_rows(T // ROW_TILE, ff_back, zero_row)
        if j % 2 == 1:
            reduce_tick()

    save_y.wait()

    def first_norm_back(i, sums):
        r = tile_rows(i)
        dy = hid[r, :]
        for j in range(TILES):
            dy = dy + mm_cols(gel[r, j * D : (j + 1) * D], w_up[j].reshape(D, D))
        normed = norm_one[r, :]
        d_one = norm_rows_back(dy, normed, rstd_one[r, 0:1], vec_ref[0:1, :])
        ig_ref[r, :] = d_one
        one_low[r, :] = low_cast(d_one)
        return sums[0] + row_sum(dy * normed), sums[1] + row_sum(dy), sums[2] + row_sum(d_one)

    sums = (zero_row, zero_row, zero_row)
    steps = T // ROW_TILE
    sums = over_rows(steps, first_norm_back, sums)
    reduce_tick()
    vg_ref[0:1, :] = sums[0]
    vg_ref[1:2, :] = sums[1]
    vg_ref[4:5, :] = sums[2]

    for g in range(GROUPS + 1, FIRST_DOWN):
        g_sent(g)
    turned[...] = hid_low[...].T
    for j in range(TILES):
        got = low_cast(mm(turned[...], gel[:, j * D : (j + 1) * D]))
        w_up[j] = got.reshape(2, 2, 2, rows, D)

    d_heads = two_low
    d_heads[...] = low_cast(mm_cols(one_low[...], w_out[...].reshape(D, D)))
    g_sent(GROUPS)
    w_out[...] = low_cast(mm_rows(heads[...], one_low[...])).reshape(2, 2, 2, rows, D)
    reduce_tick()
    for k in range(UP, MIX):
        reduce_start(k)

    zcol[...] = jnp.zeros_like(zcol)

    def grad_slot(h):
        return slice(None), pl.ds(h * LANES, LANES)

    def back_states(p, carry):
        g_pair = d_heads[:, pair_cols(p)].astype(jnp.float32)
        parts = []
        for side in (0, 1):
            h = 2 * p + side
            saved = num_a[h]
            g = g_pair if side == 0 else swap_halves(g_pair)
            gn = jnp.where(half_lane < HD, g * swap_halves(saved), 0.0)
            gd = -jnp.sum(gn * saved, axis=1, keepdims=True)
            gd_high = low_cast(gd).astype(jnp.float32)
            gn = jnp.where(
                half_lane == HD, gd_high, jnp.where(half_lane == HD + 1, gd - gd_high, gn)
            )
            gn = low_cast(gn)
            act[grad_slot(h)] = gn
            parts.append(mm_rows(feat_q[h] * keeps[1], gn))
        pack_states(p, parts[0], parts[1], back_own, 2)
        return carry

    for g in range(GROUPS):
        over_rows(2 * g + 2, back_states, 0, 2 * g)
        send_states(1, back_own, back_in, g)
        if g == 1:
            reduce_tick()
    pass_backward(1)

    def sigmoid(v):
        e = jnp.exp(-jnp.abs(v))
        return jnp.where(v >= 0, 1.0, e) / (1.0 + e)

    def fold(value):
        value = value * cs_ref[...]
        return value + swap_halves(value)

    def through_features(p, part, left, right):
        value = mixed[slab(p, part)].astype(jnp.float32)
        d_part = sigmoid(value) * jnp.where(half_lane < HD, fold(left), fold(right))
        mixed[slab(p, part)] = low_cast(d_part)
        vg_ref[6 + part : 7 + part, pair_cols(p)] = row_sum(d_part)

    def query_back(p, carry):
        got = []
        for side in (0, 1):
            h = 2 * p + side
            ga = act[grad_slot(h)]
            d_scores = low_cast(mm_cols(ga, val_a[h])) * mask[...]
            got.append(mm(d_scores, feat_k[h]) + mm_cols(ga * keeps[2], state_h[h]))
        through_features(p, 0, got[0], got[1])
        return carry

    for part in range(3):
        over_rows(2 * part + 2, query_back, 0, 2 * part)
        if part == 0:
            reduce_tick()
            pass_backward(2)
    reduce_tick()

    def key_value_back(p, carry):
        keys, values = [], []
        for side in (0, 1):
            h = 2 * p + side
            fq, fk, va, ga = feat_q[h], feat_k[h], val_a[h], act[grad_slot(h)]
            d_scores_t = low_cast(mm_cols(va, ga)) * mask_t[...]
            keys.append(mm(d_scores_t, fq) + mm_cols(va * keeps[3], back_h[h]))
            scores_t = low_cast(mm_cols(fk, fq)) * mask_t[...]
            values.append(mm(scores_t, ga) + mm(fk * keeps[3], back_h[h]))
        through_features(p, 1, keys[0], keys[1])
        d_part = join(values[0], values[1])
        mixed[slab(p, 2)] = low_cast(d_part)
        vg_ref[8:9, pair_cols(p)] = row_sum(d_part)
        return carry

    turned[...] = tok[...].T
    reduce_tick()
    for g in range(GROUPS):
        pass_backward(3 + g)
        over_rows(2 * g + 2, key_value_back, 0, 2 * g)
        ig_ref[...] += mm_cols(mixed[g], w_qkv[g].reshape(D, D))
        g_sent(g)
        w_qkv[g] = low_cast(mm(turned[...], mixed[g])).reshape(2, 2, 2, rows, D)
        reduce_start(MIX + g)
        reduce_tick()

    save_ig.start()

    def vcopy(level):
        target = (sib, xn, yn, z_one, z_two)[level]
        return remote(vg_ref, vec_land.at[level], v_send.at[level], v_recv.at[level], target)

    vg_ref[13:16, :] = jnp.zeros((3, D), jnp.float32)
    vcopy(0).start()
    for level in range(5):
        reduce_tick()
        vcopy(level).wait()
        vg_ref[...] += vec_land[level]
        if level < 4:
            vcopy(level + 1).start()
    while r_plan:
        reduce_tick()
    for k in range(UNITS):
        r_end(k)
    save_ig.wait()
    for g in range(FIRST_DOWN, GATHERS):
        g_sent(g)
    exchange_sent(0, state_own, state_in)
    exchange_sent(1, back_own, back_in)


GATHER_AHEAD = 3


def fits(mesh):
    return mesh.shape["dp"] == 8 and mesh.shape["head"] == 4


def fused_layer(lengths, tokens, cotangent, masters, vector_master):
    n_head = lax.axis_size("head")
    T = tokens.shape[0]
    rows = masters[1].shape[0]
    bf, f32 = jnp.bfloat16, jnp.float32
    V, S = pltpu.VMEM, jax.ShapeDtypeStruct
    vm, anywhere = pl.BlockSpec(memory_space=pltpu.VMEM), pl.BlockSpec(memory_space=pl.ANY)
    out_shape = (S((T, D), bf), S((T, D), f32)) + tuple(S(m.shape, bf) for m in masters)
    out_shape += (S((16, D), f32),)
    shard = (2, 2, 2, rows, D)
    scratch = [
        V((GROUPS, *shard), bf),
        V(shard, bf),
        V((TILES, *shard), bf),
        V((2, 2, 2, TILES * rows, D), bf),
        V((T, D), bf),
        V((GROUPS, T, D), bf),
        V((H, T, LANES), bf),
        V((H, T, LANES), bf),
        V((H, T, LANES), bf),
        V((H, T, LANES), f32),
        V((T, D), bf),
        V((T, D), f32),
        V((T, LANES), f32),
        V((T, D), f32),
        V((T, D), bf),
        V((D, T), bf),
        V((T, FF), bf),
        V((T, FF), bf),
        V((T, D), bf),
        V((T, D), bf),
        V((T, T), bf),
        V((T, T), bf),
        V((T, LANES), f32),
        V((T, LANES), f32),
        V((4, T, LANES), bf),
        V((GROUPS, STATE_ROWS, LANES), bf),
        V((GROUPS, STATE_ROWS, LANES), bf),
        V((GROUPS, STATE_ROWS, LANES), bf),
        V((GROUPS, STATE_ROWS, LANES), bf),
        V((3 * LANES, LANES), f32),
        V((H, LANES, LANES), bf),
        V((H, LANES, LANES), bf),
        V((LANES, LANES), f32),
        V((UNITS, 2, 2, rows, D), bf),
        V((UNITS, 2, 2, rows // 2, D), bf),
        V((UNITS, 2, rows // 2, D), bf),
        V((UNITS, 2, rows, D), bf),
        V((5, 16, D), f32),
        pltpu.SemaphoreType.DMA((19,)),
        pltpu.SemaphoreType.DMA((9, 17)),
        pltpu.SemaphoreType.DMA((9, 17)),
        pltpu.SemaphoreType.DMA((2, GROUPS)),
        pltpu.SemaphoreType.DMA((2, GROUPS)),
        pltpu.SemaphoreType.DMA((UNITS, 13)),
        pltpu.SemaphoreType.DMA((UNITS, 13)),
        pltpu.SemaphoreType.DMA((5,)),
        pltpu.SemaphoreType.DMA((5,)),
        pltpu.SemaphoreType.REGULAR,
        V((T, D), f32),
    ]
    return pl.pallas_call(
        functools.partial(layer_kernel, n_head, lengths.shape[0]),
        out_shape=out_shape,
        in_specs=[pl.BlockSpec(memory_space=pltpu.SMEM)] + [anywhere] * 6 + [vm],
        out_specs=[anywhere] * 6 + [vm],
        scratch_shapes=scratch,
        compiler_params=pltpu.CompilerParams(
            collective_id=0, has_side_effects=True, vmem_limit_bytes=VMEM_BYTES
        ),
        name="layer",
    )(lengths, tokens, cotangent, *masters, vector_master)


VMEM_BYTES = 63 * 1024 * 1024


RATES = (1.0 / math.sqrt(D), 1.0 / math.sqrt(OUT_FAN), 1.0 / math.sqrt(D), 1.0 / math.sqrt(FF))
ADAM_ROWS = 32


def adam_step(master, first, second, gradient, rate, decay):
    first_new = first_decay * first + (1.0 - first_decay) * gradient
    second_new = second_decay * second + (1.0 - second_decay) * gradient * gradient
    root = jnp.sqrt(second_new * (1.0 / (1.0 - second_decay**STEP)))
    ratio = (first_new * (rate / (1.0 - first_decay**STEP))) / (root + adam_epsilon)
    return first_new, second_new, master * (1.0 - rate * decay) - ratio


def adam_kernel(*refs):
    ins, outs = refs[:22], refs[22:]
    for i in range(2):
        outs[i][...] = ins[i][...]

    @pl.when(pl.program_id(0) == 0)
    def _():
        vector_new = adam_step(
            ins[18][...], ins[19][...], ins[20][...], ins[21][0:13, :], vector_rate, 0.0
        )
        for i in range(3):
            outs[14 + i][...] = vector_new[i]

    for m in range(4):
        master, first, second, grad = ins[2 + 4 * m : 6 + 4 * m]
        news = adam_step(
            master[...],
            first[...],
            second[...],
            grad[...].astype(jnp.float32),
            RATES[m],
            weight_decay,
        )
        for i in range(3):
            outs[2 + 3 * m + i][...] = news[i]


def adam_all(output, input_grad, masters, firsts, seconds, grads, vectors):
    n_steps = masters[1].shape[0] // ADAM_ROWS

    def rows_of(a):
        return pl.BlockSpec((a.shape[0] // n_steps, a.shape[1]), lambda i: (i, 0))

    def whole(a):
        return pl.BlockSpec(a.shape, lambda i: (0, 0))

    args = [output, input_grad]
    step_rows = pl.cdiv(output.shape[0], n_steps * ADAM_ROWS) * ADAM_ROWS
    in_specs = [pl.BlockSpec((step_rows, D), lambda i: (i, 0))] * 2
    out_shape = [jax.ShapeDtypeStruct(a.shape, a.dtype) for a in args]
    out_specs = list(in_specs)
    for quad in zip(masters, firsts, seconds, grads):
        args += quad
        in_specs += [rows_of(a) for a in quad]
        out_shape += [jax.ShapeDtypeStruct(a.shape, jnp.float32) for a in quad[:3]]
        out_specs += [rows_of(a) for a in quad[:3]]
    args += vectors
    in_specs += [whole(a) for a in vectors]
    out_shape += [jax.ShapeDtypeStruct(a.shape, jnp.float32) for a in vectors[:3]]
    out_specs += [whole(a) for a in vectors[:3]]
    return pl.pallas_call(
        adam_kernel,
        grid=(n_steps,),
        out_shape=out_shape,
        in_specs=in_specs,
        out_specs=out_specs,
        compiler_params=pltpu.CompilerParams(vmem_limit_bytes=VMEM_BYTES),
        name="adam",
    )(*args)


def fused_shards(
    tokens,
    cotangent,
    lengths,
    qkv_master,
    out_master,
    up_master,
    down_master,
    vector_master,
    qkv_first,
    qkv_second,
    out_first,
    out_second,
    up_first,
    up_second,
    down_first,
    down_second,
    vector_first,
    vector_second,
):
    masters = (qkv_master, out_master, up_master, down_master)
    output, input_grad, *grads, vector_grad = fused_layer(
        lengths, tokens, cotangent, masters, vector_master
    )
    firsts = (qkv_first, out_first, up_first, down_first)
    seconds = (qkv_second, out_second, up_second, down_second)
    vectors = [vector_master, vector_first, vector_second, vector_grad]
    return tuple(adam_all(output, input_grad, masters, firsts, seconds, grads, vectors))


def solution(mesh):
    return jax.shard_map(
        fused_shards if fits(mesh) else shards,
        mesh=mesh,
        in_specs=(
            P(("dp", "head"), None),
            P(("dp", "head"), None),
            P("dp"),
            P("dp", None),
            P("dp", None),
            P("dp", None),
            P("dp", None),
            P(),
            P("dp", None),
            P("dp", None),
            P("dp", None),
            P("dp", None),
            P("dp", None),
            P("dp", None),
            P("dp", None),
            P("dp", None),
            P(),
            P(),
        ),
        out_specs=(
            P(("dp", "head"), None),
            P(("dp", "head"), None),
            P("dp", None),
            P("dp", None),
            P("dp", None),
            P("dp", None),
            P("dp", None),
            P("dp", None),
            P("dp", None),
            P("dp", None),
            P("dp", None),
            P("dp", None),
            P("dp", None),
            P("dp", None),
            P(),
            P(),
            P(),
        ),
        check_vma=False,
    )
```

```python
import functools
import math

import jax
import jax.numpy as jnp
from jax import lax
from jax.experimental import pallas as pl
from jax.experimental.pallas import tpu as pltpu
from jax.sharding import PartitionSpec as P

D = 768
H = 12
HD = 64
FF = 3072
SPAN = 64
STEP = 10
OUT_FAN = 1


highest = lax.Precision.HIGHEST
norm_epsilon = 1e-05
first_decay = 0.9
second_decay = 0.999
adam_epsilon = 1e-08
weight_decay = 0.01
vector_rate = 0.2


def layer_norm(residual, gain_row, shift_row):
    center = residual - jnp.mean(residual, axis=-1, keepdims=True)
    spread = jnp.mean(center * center, axis=-1, keepdims=True)
    return center * lax.rsqrt(spread + norm_epsilon) * gain_row + shift_row


def exact_gelu(upper_pre):
    return jax.nn.gelu(upper_pre, approximate=False)


def group_layout(group_lengths, row_count):
    slot_sizes = (group_lengths + SPAN - 1) // SPAN * SPAN
    slot_ends = jnp.cumsum(slot_sizes)
    slot_starts = slot_ends - slot_sizes
    positions = jnp.arange(row_count, dtype=jnp.int32)
    member = (positions[:, None] >= slot_starts[None, :]) & (
        positions[:, None] < slot_ends[None, :]
    )
    seq_first = jnp.sum(jnp.where(member, slot_starts[None, :], 0), axis=1)
    length = jnp.sum(jnp.where(member, group_lengths[None, :], 0), axis=1)
    seq_numbers = jnp.arange(group_lengths.shape[0], dtype=jnp.int32)
    owners = jnp.sum(jnp.where(member, seq_numbers[None, :], 0), axis=1)
    offset = positions - seq_first
    live_rows = (offset < length).astype(jnp.float32)
    angles = 0.5 * math.pi * offset.astype(jnp.float32) / length.astype(jnp.float32)
    cosine = jnp.cos(angles)
    sine_part = jnp.sin(angles)
    span_owner = owners[::SPAN]
    span_order = jnp.arange(span_owner.shape[0], dtype=jnp.int32)
    same_seq = span_owner[None, :] == span_owner[:, None]
    earlier = (same_seq & (span_order[None, :] < span_order[:, None])).astype(jnp.float32)
    return (cosine, sine_part, live_rows, earlier)


def attend(query_rows, key_rows, value_rows, cosine, sine_part, live_rows, earlier):
    row_count = query_rows.shape[0]
    blocks = row_count // SPAN
    soft_query = jax.nn.softplus(query_rows)
    soft_key = jax.nn.softplus(key_rows)
    feat_query = (
        jnp.concatenate([soft_query * cosine[:, None], soft_query * sine_part[:, None]], axis=1)
        * live_rows[:, None]
    )
    feat_key = (
        jnp.concatenate([soft_key * cosine[:, None], soft_key * sine_part[:, None]], axis=1)
        * live_rows[:, None]
    )
    block_query = feat_query.reshape(blocks, SPAN, -1)
    block_key = feat_key.reshape(blocks, SPAN, -1)
    block_value = value_rows.reshape(blocks, SPAN, -1)
    lower_mask = (jnp.arange(SPAN)[:, None] >= jnp.arange(SPAN)[None, :]).astype(jnp.float32)
    scores = jnp.einsum("cik,cjk->cij", block_query, block_key, precision=highest) * lower_mask
    inner_sum = jnp.einsum("cij,cjd->cid", scores, block_value, precision=highest)
    inner_den = jnp.sum(scores, axis=2)
    states = jnp.einsum("cjk,cjd->ckd", block_key, block_value, precision=highest)
    key_sums = jnp.sum(block_key, axis=1)
    before = jnp.einsum("ce,ekd->ckd", earlier, states, precision=highest)
    before_sums = jnp.einsum("ce,ek->ck", earlier, key_sums, precision=highest)
    outer_sum = jnp.einsum("cik,ckd->cid", block_query, before, precision=highest)
    outer_den = jnp.einsum("cik,ck->ci", block_query, before_sums, precision=highest)
    numerator = (inner_sum + outer_sum).reshape(row_count, -1)
    denominator = (inner_den + outer_den).reshape(row_count) + (1.0 - live_rows)
    return numerator / denominator[:, None]


def contract_rows(left, right):
    return lax.dot_general(
        left, right, (((0,), (0,)), ((), ())), preferred_element_type=jnp.float32
    )


def contract_cols(left, right):
    return lax.dot_general(
        left, right, (((1,), (1,)), ((), ())), preferred_element_type=jnp.float32
    )


def adam_update(master, first, second, gradient, rate, decay):
    first_new = first_decay * first + (1.0 - first_decay) * gradient
    second_new = second_decay * second + (1.0 - second_decay) * gradient * gradient
    first_hat = first_new / (1.0 - first_decay**STEP)
    second_hat = second_new / (1.0 - second_decay**STEP)
    master_new = master - rate * (
        first_hat / (jnp.sqrt(second_hat) + adam_epsilon) + decay * master
    )
    return (first_new, second_new, master_new)


def shards(
    tokens,
    cotangent,
    lengths,
    qkv_master,
    out_master,
    up_master,
    down_master,
    vector_master,
    qkv_first,
    qkv_second,
    out_first,
    out_second,
    up_first,
    up_second,
    down_first,
    down_second,
    vector_first,
    vector_second,
):
    mix_weight, out_weight, up_weight, down_weight = (
        lax.all_gather(qkv_master.astype(jnp.bfloat16), "dp", axis=0, tiled=True),
        lax.all_gather(out_master.astype(jnp.bfloat16), "dp", axis=0, tiled=True),
        lax.all_gather(up_master.astype(jnp.bfloat16), "dp", axis=0, tiled=True),
        lax.all_gather(down_master.astype(jnp.bfloat16), "dp", axis=0, tiled=True),
    )
    tok_count = tokens.shape[0]
    width = tokens.shape[1]
    mixed_all = jnp.dot(tokens, mix_weight, preferred_element_type=jnp.float32) + vector_master[
        6:9
    ].reshape(-1)
    mixed_low = mixed_all.astype(jnp.bfloat16)
    query_part = mixed_low[:, :width].reshape(tok_count, H, 1, HD)
    key_part = mixed_low[:, width : 2 * width].reshape(tok_count, H, 1, HD)
    paired = jnp.concatenate([query_part, key_part], axis=2)
    paired = jnp.repeat(paired[:, :, None], 2, axis=2).reshape(tok_count, 4 * width)
    value_part = mixed_low[:, 2 * width :]
    paired_in, values_in = (
        lax.all_to_all(paired, "head", split_axis=1, concat_axis=0, tiled=True),
        lax.all_to_all(value_part, "head", split_axis=1, concat_axis=0, tiled=True),
    )
    group_rows = paired_in.shape[0]
    item_count = paired_in.shape[1] // (2 * HD)
    cosine, sine_part, live_rows, earlier = group_layout(lengths, group_rows)
    stacked = paired_in.reshape(group_rows, item_count, 2, HD).astype(jnp.float32)
    query_items = stacked[:, :, 0]
    key_items = stacked[:, :, 1]
    value_items = values_in.reshape(group_rows, item_count, HD // 2).astype(jnp.float32)

    def mix_items(query_set, key_set, value_set):

        def single(query_rows, key_rows, value_rows):
            return attend(query_rows, key_rows, value_rows, cosine, sine_part, live_rows, earlier)

        return jax.vmap(single, in_axes=1, out_axes=1)(query_set, key_set, value_set)

    attended, mix_back = jax.vjp(mix_items, query_items, key_items, value_items)
    heads_out = attended.reshape(group_rows, item_count * (HD // 2)).astype(jnp.bfloat16)
    heads = lax.all_to_all(heads_out, "head", split_axis=0, concat_axis=1, tiled=True)
    projected = jnp.dot(heads, out_weight, preferred_element_type=jnp.float32) + vector_master[4]
    resid_one = tokens.astype(jnp.float32) + projected
    hidden, norm_one_back = jax.vjp(layer_norm, resid_one, vector_master[0], vector_master[1])
    hidden_low = hidden.astype(jnp.bfloat16)
    upper_pre = jnp.dot(hidden_low, up_weight, preferred_element_type=jnp.float32) + vector_master[
        9:13
    ].reshape(-1)
    active, gelu_back = jax.vjp(exact_gelu, upper_pre)
    active_low = active.astype(jnp.bfloat16)
    lowered = (
        jnp.dot(active_low, down_weight, preferred_element_type=jnp.float32) + vector_master[5]
    )
    output, norm_two_back = jax.vjp(
        layer_norm, hidden + lowered, vector_master[2], vector_master[3]
    )
    grad_two, gain_two, shift_two = norm_two_back(cotangent)
    grad_two_low = grad_two.astype(jnp.bfloat16)
    down_grad = contract_rows(active_low, grad_two_low)
    (upper_grad,) = gelu_back(contract_cols(grad_two_low, down_weight))
    upper_low = upper_grad.astype(jnp.bfloat16)
    up_grad = contract_rows(hidden_low, upper_low)
    hidden_grad = grad_two + contract_cols(upper_low, up_weight)
    grad_one, gain_one, shift_one = norm_one_back(hidden_grad)
    grad_one_low = grad_one.astype(jnp.bfloat16)
    out_grad = contract_rows(heads, grad_one_low)
    heads_grad = contract_cols(grad_one_low, out_weight).astype(jnp.bfloat16)
    heads_back = lax.all_to_all(heads_grad, "head", split_axis=1, concat_axis=0, tiled=True)
    query_back, key_back, value_back = mix_back(
        heads_back.reshape(group_rows, item_count, HD // 2).astype(jnp.float32)
    )
    pair_back = (
        jnp.stack([query_back, key_back], axis=2)
        .astype(jnp.bfloat16)
        .reshape(group_rows, item_count * 2 * HD)
    )
    value_low = value_back.astype(jnp.bfloat16).reshape(group_rows, item_count * (HD // 2))
    pair_home, value_home = (
        lax.all_to_all(pair_back, "head", split_axis=0, concat_axis=1, tiled=True),
        lax.all_to_all(value_low, "head", split_axis=0, concat_axis=1, tiled=True),
    )
    summed = jnp.sum(pair_home.astype(jnp.float32).reshape(tok_count, H, 2, 2, HD), axis=2)
    mixed_grad = jnp.concatenate(
        [
            summed[:, :, 0].reshape(tok_count, width),
            summed[:, :, 1].reshape(tok_count, width),
            value_home.astype(jnp.float32),
        ],
        axis=1,
    )
    mixed_low_grad = mixed_grad.astype(jnp.bfloat16)
    mix_grad = contract_rows(tokens, mixed_low_grad)
    input_grad = grad_one + contract_cols(mixed_low_grad, mix_weight)
    vector_grad = jnp.concatenate(
        [
            jnp.stack(
                [
                    gain_one,
                    shift_one,
                    gain_two,
                    shift_two,
                    jnp.sum(grad_one, axis=0),
                    jnp.sum(grad_two, axis=0),
                ]
            ),
            jnp.sum(mixed_grad, axis=0).reshape(3, width),
            jnp.sum(upper_grad, axis=0).reshape(4, width),
        ],
        axis=0,
    )
    local_grads = (mix_grad, out_grad, up_grad, down_grad)
    row_parts = (
        lax.psum_scatter(
            local_grads[0].astype(jnp.bfloat16), "dp", scatter_dimension=0, tiled=True
        ).astype(jnp.float32),
        lax.psum_scatter(
            local_grads[1].astype(jnp.bfloat16), "dp", scatter_dimension=0, tiled=True
        ).astype(jnp.float32),
        lax.psum_scatter(
            local_grads[2].astype(jnp.bfloat16), "dp", scatter_dimension=0, tiled=True
        ).astype(jnp.float32),
        lax.psum_scatter(
            local_grads[3].astype(jnp.bfloat16), "dp", scatter_dimension=0, tiled=True
        ).astype(jnp.float32),
    )
    reduced = (
        lax.psum(row_parts[0].astype(jnp.bfloat16), "head").astype(jnp.float32),
        lax.psum(row_parts[1].astype(jnp.bfloat16), "head").astype(jnp.float32),
        lax.psum(row_parts[2].astype(jnp.bfloat16), "head").astype(jnp.float32),
        lax.psum(row_parts[3].astype(jnp.bfloat16), "head").astype(jnp.float32),
    )
    vector_total = lax.psum(vector_grad, ("dp", "head"))
    qkv_new = adam_update(
        qkv_master, qkv_first, qkv_second, reduced[0], 1.0 / math.sqrt(D), weight_decay
    )
    out_new = adam_update(
        out_master, out_first, out_second, reduced[1], 1.0 / math.sqrt(OUT_FAN), weight_decay
    )
    up_new = adam_update(
        up_master, up_first, up_second, reduced[2], 1.0 / math.sqrt(D), weight_decay
    )
    down_new = adam_update(
        down_master, down_first, down_second, reduced[3], 1.0 / math.sqrt(FF), weight_decay
    )
    vector_new = adam_update(
        vector_master, vector_first, vector_second, vector_total, vector_rate, 0.0
    )
    return (
        output.astype(jnp.bfloat16),
        input_grad,
        qkv_new[0],
        qkv_new[1],
        qkv_new[2],
        out_new[0],
        out_new[1],
        out_new[2],
        up_new[0],
        up_new[1],
        up_new[2],
        down_new[0],
        down_new[1],
        down_new[2],
        vector_new[0],
        vector_new[1],
        vector_new[2],
    )


PAIRS = H // 2
LANES = 2 * HD
GROUPS = 3
STATE_ROWS = (PAIRS // GROUPS) * LANES + 16
WIDE = D // GROUPS
TILES = FF // D
ROW_TILE = 256
MESH = pl.DeviceIdType.MESH
DOWN, UP, OUT, MIX = 0, TILES, 2 * TILES, 2 * TILES + 1
UNITS = 2 * TILES + 1 + GROUPS


def mm(left, right):
    return jnp.dot(left, right, preferred_element_type=jnp.float32)


def mm_cols(left, right):
    return lax.dot_general(
        left, right, (((1,), (1,)), ((), ())), preferred_element_type=jnp.float32
    )


def mm_rows(left, right):
    return lax.dot_general(
        left, right, (((0,), (0,)), ((), ())), preferred_element_type=jnp.float32
    )


def swap_halves(slab):
    return pltpu.roll(slab, HD, 1)


def low_cast(value):
    return value.astype(jnp.bfloat16)


def row_sum(value):
    return jnp.sum(value, axis=0, keepdims=True)


def gelu_parts(z):
    x = jnp.abs(z) * (1.0 / math.sqrt(2.0))
    t = 1.0 / (1.0 + 0.3275911 * x)
    bell = jnp.exp(-0.5 * z * z)
    poly = t * (
        0.254829592
        + t * (-0.284496736 + t * (1.421413741 + t * (-1.453152027 + t * 1.061405429)))
    )
    upper_tail = 0.5 * poly * bell
    phi = jnp.where(z >= 0, 1.0 - upper_tail, upper_tail)
    return z * phi, phi + z * (bell * (1.0 / math.sqrt(2.0 * math.pi)))


def over_rows(count, body, carry, start=0):
    for i in range(start, count):
        carry = body(i, carry)
    return carry


def norm_rows(residual):
    center = residual - jnp.mean(residual, axis=-1, keepdims=True)
    rstd = lax.rsqrt(jnp.mean(center * center, axis=-1, keepdims=True) + norm_epsilon)
    return center * rstd, rstd


def norm_rows_back(dy, normed, rstd, gain):
    e = dy * gain
    return rstd * (
        e
        - jnp.mean(e, axis=-1, keepdims=True)
        - normed * jnp.mean(e * normed, axis=-1, keepdims=True)
    )


def layer_kernel(
    n_head,
    n_seq,
    lens_ref,
    tok_hbm,
    cot_hbm,
    qkv_f,
    out_f,
    up_f,
    down_f,
    vec_ref,
    y_hbm,
    ig_hbm,
    g_qkv,
    g_out,
    g_up,
    g_down,
    vg_ref,
    w_qkv,
    w_out,
    w_up,
    w_down,
    tok,
    mixed,
    feat_q,
    feat_k,
    val_a,
    num_a,
    heads,
    norm_one,
    rstd_one,
    hid,
    hid_low,
    turned,
    act,
    gel,
    two_low,
    one_low,
    mask,
    mask_t,
    cs_ref,
    live_ref,
    keeps,
    state_own,
    state_in,
    back_own,
    back_in,
    state_sum,
    state_h,
    back_h,
    zcol,
    red_a,
    red_b,
    red_c,
    red_e,
    vec_land,
    load_sem,
    g_send,
    g_recv,
    s_send,
    s_recv,
    r_send,
    r_recv,
    v_send,
    v_recv,
    free_sem,
    ig_ref,
):
    T = tok.shape[0]
    rows = w_out.shape[3]
    half = rows // 2
    dp = lax.axis_index("dp")
    z = lax.axis_index("head")
    core = dp % 2
    xx = (dp // 2) % 2
    yy = dp // 4
    color = z % 2
    sib = (dp + 1 - 2 * core, z)
    xn = (dp + 2 - 4 * xx, z)
    yn = (dp + 4 - 8 * yy, z)
    z_one = (dp, z + 1 - 2 * color)
    z_two = (dp, (z + 3 + 2 * color) % n_head)

    def load(i, src, dst):
        return pltpu.make_async_copy(src, dst, load_sem.at[i])

    def spot(ref, i):
        return ref.at[pl.ds(i * rows, rows), :]

    loads = []
    for g in range(GROUPS):
        for part in range(3):
            loads.append(
                load(
                    len(loads),
                    qkv_f.at[:, pl.ds(part * D + g * WIDE, WIDE)],
                    hid.at[pl.ds(g * rows, rows), pl.ds(part * WIDE, WIDE)],
                )
            )
    loads.append(load(len(loads), out_f, spot(hid, GROUPS)))
    for j in range(TILES):
        loads.append(load(len(loads), up_f.at[:, pl.ds(j * D, D)], spot(norm_one, j)))
    loads.append(load(len(loads), down_f, ig_ref.at[pl.ds(0, TILES * rows), :]))
    load_tok = load(len(loads), tok_hbm, tok)
    load_cot = load(len(loads) + 1, cot_hbm, ig_ref)
    save_y = load(len(loads) + 2, one_low, y_hbm)
    save_ig = load(len(loads) + 3, ig_ref, ig_hbm)
    for copy in loads:
        copy.start()
    load_tok.start()

    barrier = pltpu.get_barrier_semaphore()
    peers = [sib, xn, yn]
    for k in range(1, n_head):
        peers.append((dp, (z + k) % n_head))
    for peer in peers:
        pl.semaphore_signal(barrier, inc=1, device_id=peer, device_id_type=MESH)

    def remote(src, dst, send, recv, target):
        return pltpu.make_async_remote_copy(
            src_ref=src,
            dst_ref=dst,
            send_sem=send,
            recv_sem=recv,
            device_id=target,
            device_id_type=MESH,
        )

    down_parts = ((0, 2), (2, 1), (3, 1))
    FIRST_DOWN = GROUPS + 1 + TILES // 2
    GATHERS = FIRST_DOWN + len(down_parts)

    def piece(g, y, x, c, which):
        if g < GROUPS:
            ref, size, base = w_qkv.at[g, y, x, c], rows, 0
        elif g == GROUPS:
            ref, size, base = w_out.at[y, x, c], rows, 0
        elif g < GROUPS + 1 + TILES // 2:
            i = g - GROUPS - 1
            if which is None:
                return w_up.at[pl.ds(2 * i, 2), y, x, c]
            return w_up.at[
                pl.ds(2 * i, 2), y, x, c, pl.ds(pl.multiple_of(which * half, half), half), :
            ]
        else:
            base, size = (rows * v for v in down_parts[g - FIRST_DOWN])
            ref = w_down.at[y, x, c]
        if which is None:
            return ref.at[pl.ds(base, size), :]
        return ref.at[pl.ds(base + which * (size // 2), size // 2), :]

    def own_masters(g):
        if g < GROUPS:
            for part in range(3):
                loads[3 * g + part].wait()
            w_qkv[g, yy, xx, core] = low_cast(hid[g * rows : (g + 1) * rows, :])
        elif g == GROUPS:
            loads[9].wait()
            w_out[yy, xx, core] = low_cast(hid[g * rows : (g + 1) * rows, :])
        elif g < GROUPS + 1 + TILES // 2:
            for j in range(2 * (g - GROUPS - 1), 2 * (g - GROUPS)):
                loads[10 + j].wait()
                w_up[j, yy, xx, core] = low_cast(norm_one[j * rows : (j + 1) * rows, :])
        else:
            if g == FIRST_DOWN:
                loads[10 + TILES].wait()
            base, size = (rows * v for v in down_parts[g - FIRST_DOWN])
            span = slice(base, base + size)
            w_down[yy, xx, core, span, :] = low_cast(ig_ref[span, :])

    here, mine_x, mine_y, mine_d = (yy, xx), (yy, 1 - xx), (1 - yy, xx), (1 - yy, 1 - xx)

    def gcopy(g, kind, chip, which, target, lands):
        ref = piece(g, chip[0], chip[1], core, which)
        return remote(ref, ref, g_send.at[g, kind], g_recv.at[g, lands], target)

    def landed(g, chip, which, lands):
        gcopy(g, 0, chip, which, sib, lands).wait_recv()

    blocks = ((mine_x, 0), (mine_x, 1), (mine_y, 0), (mine_y, 1), (mine_d, 0), (mine_d, 1))

    def hand_over(g, lands):
        chip, which = blocks[lands]
        gcopy(g, 10 + lands, chip, which, sib, 7 + lands).start()

    def arrived(g, lands):
        chip, which = blocks[lands]
        landed(g, chip, which, lands)

    def g_start(g):
        gcopy(g, 0, here, 0, xn, 0).start()
        gcopy(g, 1, here, 1, yn, 3).start()

        @pl.when(color == 0)
        def _():
            gcopy(g, 2, here, 1, xn, 1).start()
            gcopy(g, 3, here, 0, yn, 2).start()

        gcopy(g, 9, here, None, sib, 6).start()

    def g_own(g):
        own_masters(g)
        g_start(g)

    def g_first(g):
        arrived(g, 0)

        @pl.when(color == 1)
        def _():
            gcopy(g, 4, mine_x, 0, yn, 4).start()

        arrived(g, 3)

        @pl.when(color == 1)
        def _():
            gcopy(g, 5, mine_y, 1, xn, 5).start()

        hand_over(g, 0)
        hand_over(g, 3)

        @pl.when(color == 0)
        def _():
            arrived(g, 1)
            gcopy(g, 6, mine_x, 1, z_one, 1).start()
            arrived(g, 2)
            gcopy(g, 7, mine_y, 0, z_one, 2).start()
            hand_over(g, 1)
            hand_over(g, 2)

    def g_second(g):
        @pl.when(color == 1)
        def _():
            arrived(g, 4)
            gcopy(g, 8, mine_d, 0, z_one, 4).start()
            arrived(g, 5)
            gcopy(g, 16, mine_d, 1, z_one, 5).start()
            hand_over(g, 4)
            hand_over(g, 5)
            arrived(g, 1)
            hand_over(g, 1)
            arrived(g, 2)
            hand_over(g, 2)

    def g_third(g):
        @pl.when(color == 0)
        def _():
            arrived(g, 4)
            hand_over(g, 4)
            arrived(g, 5)
            hand_over(g, 5)

    def g_last(g):
        landed(g, here, None, 6)
        for lands in range(6):
            chip, which = blocks[lands]
            landed(g, chip, which, 7 + lands)

    def g_sent(g):
        def sent(kind, chip, which):
            gcopy(g, kind, chip, which, sib, 0).wait_send()

        sent(0, here, 0)
        sent(1, here, 1)
        sent(9, here, None)
        for lands in range(6):
            sent(10 + lands, *blocks[lands])

        @pl.when(color == 0)
        def _():
            sent(2, here, 1)
            sent(3, here, 0)
            sent(6, mine_x, 1)
            sent(7, mine_y, 0)

        @pl.when(color == 1)
        def _():
            sent(4, mine_x, 0)
            sent(5, mine_y, 1)
            sent(8, mine_d, 0)
            sent(16, mine_d, 1)

    plan = []
    for step in range(GATHERS + 2):
        acts = [(f, step - lag) for f, lag in ((g_third, 2), (g_second, 1), (g_first, 0))]
        acts = [(f, g) for f, g in acts if 0 <= g < GATHERS]
        if step + GATHER_AHEAD < GATHERS:
            acts.append((g_own, step + GATHER_AHEAD))
        plan.append(acts)

    def gather_step():
        if plan:
            for act_of, g in plan.pop(0):
                act_of(g)

    def gather_until(g):
        while any((g_third, g) in acts for acts in plan):
            gather_step()
        g_last(g)

    def unit_ref(k):
        if k < OUT:
            return w_up.at[k - UP]
        if k < MIX:
            return w_out
        return w_qkv.at[k - MIX]

    def own_half(k, y, x):
        return red_a[OUT + k, y, x] if k < UP else unit_ref(k)[y, x, core]

    middle = (z > 0) & (z < n_head - 1)
    top, low_part = pl.ds(0, half), pl.ds(half, half)

    def finals(k):
        if k < UP:
            return [(None, g_down.at[pl.ds(k * rows, rows), :])]
        if k < OUT:
            return [(None, g_up.at[:, pl.ds((k - UP) * D, D)])]
        if k < MIX:
            return [(None, g_out)]
        return [
            (part * WIDE, g_qkv.at[:, pl.ds(part * D + (k - MIX) * WIDE, WIDE)])
            for part in range(3)
        ]

    def r_final(k, i):
        mine = red_a.at[k, yy, xx]
        col, dst = finals(k)[i]
        return mine if col is None else mine.at[:, pl.ds(col, WIDE)], dst

    def r_copy(k, kind):
        mine = red_a.at[k, yy, xx]
        if kind == 0:
            src = red_a.at[UP + k] if k < UP else unit_ref(k).at[:, :, 1 - core]
            dst, target = red_a.at[k], sib
        elif kind == 1:
            src, dst, target = red_a.at[k, :, 1 - xx, top, :], red_b.at[k, 0], xn
        elif kind == 2:
            src, dst, target = red_a.at[k, 1 - yy, :, low_part, :], red_b.at[k, 1], yn
        elif kind == 3:
            src, dst, target = red_a.at[k, 1 - yy, xx, top, :], red_c.at[k, 0], yn
        elif kind == 4:
            src, dst, target = red_a.at[k, yy, 1 - xx, low_part, :], red_c.at[k, 1], xn
        elif kind == 5:
            src, dst, target = mine, red_e.at[k, 0], z_one
        elif kind == 6:
            src, dst, target = mine, red_e.at[k, 1], z_two
        else:
            src, dst = r_final(k, kind - 7)
            target = z_one
        return remote(src, dst, r_send.at[k, kind], r_recv.at[k, kind], target)

    def r_local(k, i):
        src, dst = r_final(k, i)
        return pltpu.make_async_copy(src, dst, r_recv.at[k, 10 + i])

    def added(one, two):
        return low_cast(one.astype(jnp.float32) + two.astype(jnp.float32))

    def r_start(k):
        r_copy(k, 0).start()

    def r_pair(k):
        r_copy(k, 0).wait_recv()
        for y in range(2):
            for x in range(2):
                red_a[k, y, x] = added(own_half(k, y, x), red_a[k, y, x])
        r_copy(k, 1).start()
        r_copy(k, 2).start()
        if k == UP - 1:
            for i in range(UP):
                r_copy(i, 0).wait_send()
            pl.semaphore_signal(free_sem, inc=1, device_id=sib, device_id_type=MESH)

    def r_plane(k):
        r_copy(k, 1).wait_recv()
        red_a[k, 1 - yy, xx, top, :] = added(red_a[k, 1 - yy, xx, top, :], red_b[k, 0, 1 - yy])
        r_copy(k, 3).start()
        r_copy(k, 2).wait_recv()
        red_a[k, yy, 1 - xx, low_part, :] = added(
            red_a[k, yy, 1 - xx, low_part, :], red_b[k, 1, 1 - xx]
        )
        r_copy(k, 4).start()
        red_a[k, yy, xx, top, :] = added(red_a[k, yy, xx, top, :], red_b[k, 0, yy])
        red_a[k, yy, xx, low_part, :] = added(red_a[k, yy, xx, low_part, :], red_b[k, 1, xx])

    def r_whole(k):
        r_copy(k, 3).wait_recv()
        r_copy(k, 4).wait_recv()
        red_a[k, yy, xx, top, :] = added(red_a[k, yy, xx, top, :], red_c[k, 0])
        red_a[k, yy, xx, low_part, :] = added(red_a[k, yy, xx, low_part, :], red_c[k, 1])

        @pl.when(~middle)
        def _():
            r_copy(k, 5).start()

    def r_z_first(k):
        @pl.when(middle)
        def _():
            r_copy(k, 5).wait_recv()
            red_a[k, yy, xx] = added(red_a[k, yy, xx], red_e[k, 0])
            r_copy(k, 6).start()

    def r_z_second(k):
        @pl.when(middle)
        def _():
            r_copy(k, 6).wait()
            red_a[k, yy, xx] = added(red_a[k, yy, xx], red_e[k, 1])
            for i in range(len(finals(k))):
                r_copy(k, 7 + i).start()
                r_local(k, i).start()

    def r_end(k):
        for kind in range(1 if k < UP else 0, 5):
            r_copy(k, kind).wait_send()

        @pl.when(middle)
        def _():
            for i in range(len(finals(k))):
                r_copy(k, 7 + i).wait_send()
                r_local(k, i).wait()

        @pl.when(~middle)
        def _():
            r_copy(k, 5).wait_send()
            for i in range(len(finals(k))):
                r_copy(k, 7 + i).wait_recv()

    stages = (r_pair, r_plane, r_whole, r_z_first, r_z_second)
    r_plan = []
    for tick in range(UNITS + len(stages)):
        acts = [(stages[s], tick - s) for s in reversed(range(1, len(stages)))]
        if tick == 0:
            r_plan.append([(r_pair, 0)])
        acts.append((r_pair, tick + 1))
        r_plan.append([(f, k) for f, k in acts if 0 <= k < UNITS])
    started = []

    def reduce_start(k):
        if k == UP:
            pl.semaphore_wait(free_sem, 1)
        r_start(k)
        started.append(k)

    def reduce_tick():
        if r_plan and all(k in started for _, k in r_plan[0]):
            for act_of, k in r_plan.pop(0):
                act_of(k)

    for g in range(min(GATHER_AHEAD, GATHERS)):
        own_masters(g)
    pl.semaphore_wait(barrier, len(peers))
    for g in range(min(GATHER_AHEAD, GATHERS)):
        g_start(g)

    lens = [lens_ref[s] for s in range(n_seq)]
    ends = []
    total = 0
    for s in range(n_seq):
        total = total + ((lens[s] + (SPAN - 1)) // SPAN) * SPAN
        ends.append(total)
    starts = [0] + ends[:-1]

    def owner_of(row):
        found = jnp.zeros_like(row)
        for s in range(n_seq):
            found = found + (row >= ends[s]).astype(jnp.int32)
        return found

    half_lane = lax.broadcasted_iota(jnp.int32, (T, LANES), 1)
    row = z * T + lax.broadcasted_iota(jnp.int32, (T, LANES), 0)
    first = jnp.zeros_like(row)
    length = jnp.ones_like(row)
    for s in range(n_seq):
        inside = (row >= starts[s]) & (row < ends[s])
        first = jnp.where(inside, starts[s], first)
        length = jnp.where(inside, lens[s], length)
    offset = row - first
    live = (offset < length).astype(jnp.float32)
    angle = 0.5 * math.pi * offset.astype(jnp.float32) / length.astype(jnp.float32)
    angle = jnp.where(half_lane < HD, angle, 0.5 * math.pi - angle)
    cs_ref[...] = jnp.cos(angle) * live
    live_ref[...] = live
    owners = owner_of(row)
    next_owner = owner_of(jnp.full((1, 1), (z + 1) * T, jnp.int32))
    last_owner = owner_of(jnp.full((1, 1), z * T - 1, jnp.int32))
    my_first = owner_of(jnp.full((1, 1), z * T, jnp.int32))
    my_last = owner_of(jnp.full((1, 1), (z + 1) * T - 1, jnp.int32))
    for i, edge in enumerate((next_owner, last_owner, my_first, my_last)):
        keeps[i] = low_cast((owners == edge).astype(jnp.float32))

    def fill_masks(i, carry):
        r0 = pl.multiple_of(i * ROW_TILE, ROW_TILE)
        t_i = r0 + lax.broadcasted_iota(jnp.int32, (ROW_TILE, T), 0)
        u_i = lax.broadcasted_iota(jnp.int32, (ROW_TILE, T), 1)
        same = owner_of(t_i + z * T) == owner_of(u_i + z * T)
        mask[pl.ds(r0, ROW_TILE), :] = low_cast((same & (u_i <= t_i)).astype(jnp.float32))
        mask_t[pl.ds(r0, ROW_TILE), :] = low_cast((same & (u_i >= t_i)).astype(jnp.float32))
        return carry

    lax.fori_loop(0, T // ROW_TILE, fill_masks, 0)

    sq_lane = lax.broadcasted_iota(jnp.int32, (LANES, LANES), 1)
    ones_lane = ((half_lane == HD) | (half_lane == HD + 1)).astype(jnp.float32)

    def softplus(v):
        return jnp.maximum(v, 0.0) + jnp.log1p(jnp.exp(-jnp.abs(v)))

    def slab(p, part):
        return p // 2, slice(None), pl.ds(part * WIDE + (p % 2) * LANES, LANES)

    def pair_cols(p):
        return pl.ds(p * LANES, LANES)

    def split(value):
        swapped = swap_halves(value)
        return jnp.where(half_lane < HD, value, swapped), jnp.where(half_lane < HD, swapped, value)

    def join(left, right):
        return jnp.where(half_lane < HD, left, swap_halves(right))

    def pack_states(p, left, right, own, n_ones):
        place = pl.ds((p % 2) * LANES, LANES)
        own[p // 2, place, :] = low_cast(jnp.where(sq_lane < HD, left, swap_halves(right)))
        for side, part in ((0, left), (1, right)):
            column = part[:, HD : HD + 1]
            if n_ones == 2:
                column = column + part[:, HD + 1 : HD + 2]
            zcol[...] = jnp.where(sq_lane == 2 * (p % 2) + side, column, zcol[...])

    def exchange(which, own, landed, g):
        target = z + 1 - 2 * which
        target = (target + n_head) % n_head
        return remote(
            own.at[g], landed.at[g], s_send.at[which, g], s_recv.at[which, g], (dp, target)
        )

    def place_of(which):
        return z if which == 0 else n_head - 1 - z

    def send_states(which, own, landed, g):
        own[g, 2 * LANES : STATE_ROWS, :] = low_cast(zcol[...].T[0:16, :])

        @pl.when(place_of(which) == 0)
        def _():
            exchange(which, own, landed, g).start()

    def pass_on(which, own, landed, out, n_ones, point):
        for place in range(1, n_head):
            g = point - place
            if 0 <= g < GROUPS:

                @pl.when(place_of(which) == place)
                def _(g=g, place=place):
                    exchange(which, own, landed, g).wait_recv()
                    state_sum[0:STATE_ROWS, :] = landed[g].astype(jnp.float32)
                    if place < n_head - 1:
                        through = (my_first == next_owner) if which == 0 else (my_last == last_owner)
                        own[g] = low_cast(
                            own[g].astype(jnp.float32)
                            + through.astype(jnp.float32) * state_sum[0:STATE_ROWS, :]
                        )
                        exchange(which, own, landed, g).start()
                    unpack(out, n_ones, g)

    def unpack(out, n_ones, g):
        columns = state_sum[2 * LANES : 3 * LANES, :].T
        wide = (sq_lane >= HD) & (sq_lane < HD + n_ones)
        for i in range(2):
            packed = state_sum[i * LANES : (i + 1) * LANES, :]
            for side in (0, 1):
                part = packed if side == 0 else swap_halves(packed)
                column = columns[:, 2 * i + side : 2 * i + side + 1]
                out[4 * g + 2 * i + side] = low_cast(
                    jnp.where(sq_lane < HD, part, jnp.where(wide, column, 0.0))
                )

    def exchange_sent(which, own, landed):
        @pl.when(place_of(which) < n_head - 1)
        def _():
            for g in range(GROUPS):
                exchange(which, own, landed, g).wait_send()

    state_sum[...] = jnp.zeros_like(state_sum)
    state_h[...] = jnp.zeros_like(state_h)
    back_h[...] = jnp.zeros_like(back_h)

    def pass_forward(point):
        pass_on(0, state_own, state_in, state_h, 2, point)

    def pass_backward(point):
        pass_on(1, back_own, back_in, back_h, 1, point)

    zcol[...] = jnp.zeros_like(zcol)

    def features_of(p, part, store):
        cs = cs_ref[...]
        left, right = split(softplus(mixed[slab(p, part)].astype(jnp.float32)))
        store[2 * p] = low_cast(left * cs)
        store[2 * p + 1] = low_cast(right * cs)

    def make_keys(p, carry):
        features_of(p, 1, feat_k)
        v_pair = mixed[slab(p, 2)].astype(jnp.float32)
        val_a[2 * p] = low_cast(jnp.where(half_lane < HD, v_pair, ones_lane))
        val_a[2 * p + 1] = low_cast(jnp.where(half_lane < HD, swap_halves(v_pair), ones_lane))
        left = mm_rows(feat_k[2 * p] * keeps[0], val_a[2 * p])
        right = mm_rows(feat_k[2 * p + 1] * keeps[0], val_a[2 * p + 1])
        pack_states(p, left, right, state_own, 1)
        return carry

    def make_queries(p, carry):
        features_of(p, 0, feat_q)
        return carry

    load_tok.wait()
    for g in range(GROUPS):
        gather_until(g)
        part = mm(tok[...], w_qkv[g].reshape(D, D))
        mixed[g, :, 0:WIDE] = low_cast(part[:, 0:WIDE] + vec_ref[6:7, g * WIDE : (g + 1) * WIDE])
        mixed[g, :, WIDE : 2 * WIDE] = low_cast(
            part[:, WIDE : 2 * WIDE] + vec_ref[7:8, g * WIDE : (g + 1) * WIDE]
        )
        mixed[g, :, 2 * WIDE :] = low_cast(part[:, 2 * WIDE :])
        over_rows(2 * g + 2, make_keys, 0, 2 * g)
        send_states(0, state_own, state_in, g)
        if g:
            pass_forward(g)

    def local_attend(h, carry):
        scores = low_cast(mm_cols(feat_q[h], feat_k[h])) * mask[...]
        num_a[h] = mm(scores, val_a[h])
        return carry

    for part in range(3):
        over_rows(2 * part + 2, make_queries, 0, 2 * part)
        over_rows(4 * part + 4, local_attend, 0, 4 * part)
        gather_step()
        pass_forward(3 + part)

    def finish_heads(p, carry):
        att = []
        for side in (0, 1):
            h = 2 * p + side
            whole = num_a[h] + mm(feat_q[h] * keeps[2], state_h[h])
            den = whole[:, HD : HD + 1] + (1.0 - live_ref[...])
            inverse = 1.0 / den
            got = whole * inverse
            num_a[h] = jnp.where(half_lane < HD, got, inverse)
            att.append(got)
        shift = vec_ref[8:9, pair_cols(p)]
        heads[:, pair_cols(p)] = low_cast(join(att[0], att[1]) + shift * live_ref[...])
        return carry

    for g in range(GROUPS):
        over_rows(2 * g + 2, finish_heads, 0, 2 * g)

    gather_step()

    gather_until(GROUPS)

    def tile_rows(i):
        return slice(i * ROW_TILE, (i + 1) * ROW_TILE)

    def first_norm(i, carry):
        r = tile_rows(i)
        w = w_out[...].reshape(D, D)
        residual = tok[r, :].astype(jnp.float32) + (mm(heads[r, :], w) + vec_ref[4:5, :])
        normed, rstd = norm_rows(residual)
        norm_one[r, :] = normed
        rstd_one[r, :] = jnp.broadcast_to(rstd, (ROW_TILE, LANES))
        hidden = normed * vec_ref[0:1, :] + vec_ref[1:2, :]
        hid[r, :] = hidden
        hid_low[r, :] = low_cast(hidden)
        return carry

    while any(act_of is g_own for acts in plan for act_of, _ in acts):
        gather_step()
    load_cot.start()
    over_rows(T // ROW_TILE, first_norm, 0)

    for j in range(TILES):
        if j % 2 == 0:
            gather_until(GROUPS + 1 + j // 2)

        def ff_up(i, carry, j=j):
            r = tile_rows(i)
            upper = mm(hid_low[r, :], w_up[j].reshape(D, D)) + vec_ref[9 + j : 10 + j, :]
            value, slope = gelu_parts(upper)
            act[r, j * D : (j + 1) * D] = low_cast(value)
            gel[r, j * D : (j + 1) * D] = low_cast(slope)
            return carry

        over_rows(T // ROW_TILE, ff_up, 0)
        gather_step()

    for g in range(FIRST_DOWN, GATHERS):
        gather_until(g)
    load_cot.wait()

    def second_norm(i, sums):
        r = tile_rows(i)
        lowered = mm(act[r, :], w_down[...].reshape(FF, D))
        normed, rstd = norm_rows(hid[r, :] + (lowered + vec_ref[5:6, :]))
        one_low[r, :] = low_cast(normed * vec_ref[2:3, :] + vec_ref[3:4, :])
        dy = ig_ref[r, :]
        d_two = norm_rows_back(dy, normed, rstd, vec_ref[2:3, :])
        hid[r, :] = d_two
        two_low[r, :] = low_cast(d_two)
        return sums[0] + row_sum(dy * normed), sums[1] + row_sum(dy), sums[2] + row_sum(d_two)

    zero_row = jnp.zeros((1, D), jnp.float32)
    gain_two, shift_two, bias_down = over_rows(
        T // ROW_TILE, second_norm, (zero_row, zero_row, zero_row)
    )
    save_y.start()
    vg_ref[2:3, :] = gain_two
    vg_ref[3:4, :] = shift_two
    vg_ref[5:6, :] = bias_down

    for j in range(TILES):
        got = low_cast(mm_rows(act[:, j * D : (j + 1) * D], two_low[...]))
        got = got.reshape(2, TILES, rows, D)
        for k in range(TILES):
            red_a[UP + k, j // 2, j % 2] = jnp.where(core == 0, got[1, k], got[0, k])
            red_a[OUT + k, j // 2, j % 2] = jnp.where(core == 0, got[0, k], got[1, k])
    for k in range(UP):
        reduce_start(k)

    for j in range(TILES):

        def ff_back(i, total, j=j):
            r = tile_rows(i)
            d_act = mm_cols(two_low[r, :], w_down[j // 2, j % 2].reshape(D, D))
            d_upper = d_act * gel[r, j * D : (j + 1) * D].astype(jnp.float32)
            gel[r, j * D : (j + 1) * D] = low_cast(d_upper)
            return total + row_sum(d_upper)

        vg_ref[9 + j : 10 + j, :] = over_rows(T // ROW_TILE, ff_back, zero_row)
        if j % 2 == 1:
            reduce_tick()

    save_y.wait()

    def first_norm_back(i, sums):
        r = tile_rows(i)
        dy = hid[r, :]
        for j in range(TILES):
            dy = dy + mm_cols(gel[r, j * D : (j + 1) * D], w_up[j].reshape(D, D))
        normed = norm_one[r, :]
        d_one = norm_rows_back(dy, normed, rstd_one[r, 0:1], vec_ref[0:1, :])
        ig_ref[r, :] = d_one
        one_low[r, :] = low_cast(d_one)
        return sums[0] + row_sum(dy * normed), sums[1] + row_sum(dy), sums[2] + row_sum(d_one)

    sums = (zero_row, zero_row, zero_row)
    steps = T // ROW_TILE
    sums = over_rows(steps, first_norm_back, sums)
    reduce_tick()
    vg_ref[0:1, :] = sums[0]
    vg_ref[1:2, :] = sums[1]
    vg_ref[4:5, :] = sums[2]

    for g in range(GROUPS + 1, FIRST_DOWN):
        g_sent(g)
    turned[...] = hid_low[...].T
    for j in range(TILES):
        got = low_cast(mm(turned[...], gel[:, j * D : (j + 1) * D]))
        w_up[j] = got.reshape(2, 2, 2, rows, D)

    d_heads = two_low
    d_heads[...] = low_cast(mm_cols(one_low[...], w_out[...].reshape(D, D)))
    g_sent(GROUPS)
    w_out[...] = low_cast(mm_rows(heads[...], one_low[...])).reshape(2, 2, 2, rows, D)
    reduce_tick()
    for k in range(UP, MIX):
        reduce_start(k)

    zcol[...] = jnp.zeros_like(zcol)

    def grad_slot(h):
        return slice(None), pl.ds(h * LANES, LANES)

    def back_states(p, carry):
        g_pair = d_heads[:, pair_cols(p)].astype(jnp.float32)
        parts = []
        for side in (0, 1):
            h = 2 * p + side
            saved = num_a[h]
            g = g_pair if side == 0 else swap_halves(g_pair)
            gn = jnp.where(half_lane < HD, g * swap_halves(saved), 0.0)
            gd = -jnp.sum(gn * saved, axis=1, keepdims=True)
            gd_high = low_cast(gd).astype(jnp.float32)
            gn = jnp.where(
                half_lane == HD, gd_high, jnp.where(half_lane == HD + 1, gd - gd_high, gn)
            )
            gn = low_cast(gn)
            act[grad_slot(h)] = gn
            parts.append(mm_rows(feat_q[h] * keeps[1], gn))
        pack_states(p, parts[0], parts[1], back_own, 2)
        return carry

    for g in range(GROUPS):
        over_rows(2 * g + 2, back_states, 0, 2 * g)
        send_states(1, back_own, back_in, g)
        if g == 1:
            reduce_tick()
    pass_backward(1)

    def sigmoid(v):
        e = jnp.exp(-jnp.abs(v))
        return jnp.where(v >= 0, 1.0, e) / (1.0 + e)

    def fold(value):
        value = value * cs_ref[...]
        return value + swap_halves(value)

    def through_features(p, part, left, right):
        value = mixed[slab(p, part)].astype(jnp.float32)
        d_part = sigmoid(value) * jnp.where(half_lane < HD, fold(left), fold(right))
        mixed[slab(p, part)] = low_cast(d_part)
        vg_ref[6 + part : 7 + part, pair_cols(p)] = row_sum(d_part)

    def query_back(p, carry):
        got = []
        for side in (0, 1):
            h = 2 * p + side
            ga = act[grad_slot(h)]
            d_scores = low_cast(mm_cols(ga, val_a[h])) * mask[...]
            got.append(mm(d_scores, feat_k[h]) + mm_cols(ga * keeps[2], state_h[h]))
        through_features(p, 0, got[0], got[1])
        return carry

    for part in range(3):
        over_rows(2 * part + 2, query_back, 0, 2 * part)
        if part == 0:
            reduce_tick()
            pass_backward(2)
    reduce_tick()

    def key_value_back(p, carry):
        keys, values = [], []
        for side in (0, 1):
            h = 2 * p + side
            fq, fk, va, ga = feat_q[h], feat_k[h], val_a[h], act[grad_slot(h)]
            d_scores_t = low_cast(mm_cols(va, ga)) * mask_t[...]
            keys.append(mm(d_scores_t, fq) + mm_cols(va * keeps[3], back_h[h]))
            scores_t = low_cast(mm_cols(fk, fq)) * mask_t[...]
            values.append(mm(scores_t, ga) + mm(fk * keeps[3], back_h[h]))
        through_features(p, 1, keys[0], keys[1])
        d_part = join(values[0], values[1])
        mixed[slab(p, 2)] = low_cast(d_part)
        vg_ref[8:9, pair_cols(p)] = row_sum(d_part)
        return carry

    turned[...] = tok[...].T
    for g in range(GROUPS):
        pass_backward(3 + g)
        over_rows(2 * g + 1, key_value_back, 0, 2 * g)
        reduce_tick()
        over_rows(2 * g + 2, key_value_back, 0, 2 * g + 1)
        ig_ref[...] += mm_cols(mixed[g], w_qkv[g].reshape(D, D))
        g_sent(g)
        w_qkv[g] = low_cast(mm(turned[...], mixed[g])).reshape(2, 2, 2, rows, D)
        reduce_start(MIX + g)
        reduce_tick()

    save_ig.start()

    def vcopy(level):
        target = (sib, xn, yn, z_one, z_two)[level]
        return remote(vg_ref, vec_land.at[level], v_send.at[level], v_recv.at[level], target)

    vg_ref[13:16, :] = jnp.zeros((3, D), jnp.float32)
    vcopy(0).start()
    for level in range(5):
        reduce_tick()
        vcopy(level).wait()
        vg_ref[...] += vec_land[level]
        if level < 4:
            vcopy(level + 1).start()
    while r_plan:
        reduce_tick()
    for k in range(UNITS):
        r_end(k)
    save_ig.wait()
    for g in range(FIRST_DOWN, GATHERS):
        g_sent(g)
    exchange_sent(0, state_own, state_in)
    exchange_sent(1, back_own, back_in)


GATHER_AHEAD = 3


def fits(mesh):
    return mesh.shape["dp"] == 8 and mesh.shape["head"] == 4


def fused_layer(lengths, tokens, cotangent, masters, vector_master):
    n_head = lax.axis_size("head")
    T = tokens.shape[0]
    rows = masters[1].shape[0]
    bf, f32 = jnp.bfloat16, jnp.float32
    V, S = pltpu.VMEM, jax.ShapeDtypeStruct
    vm, anywhere = pl.BlockSpec(memory_space=pltpu.VMEM), pl.BlockSpec(memory_space=pl.ANY)
    out_shape = (S((T, D), bf), S((T, D), f32)) + tuple(S(m.shape, bf) for m in masters)
    out_shape += (S((16, D), f32),)
    shard = (2, 2, 2, rows, D)
    scratch = [
        V((GROUPS, *shard), bf),
        V(shard, bf),
        V((TILES, *shard), bf),
        V((2, 2, 2, TILES * rows, D), bf),
        V((T, D), bf),
        V((GROUPS, T, D), bf),
        V((H, T, LANES), bf),
        V((H, T, LANES), bf),
        V((H, T, LANES), bf),
        V((H, T, LANES), f32),
        V((T, D), bf),
        V((T, D), f32),
        V((T, LANES), f32),
        V((T, D), f32),
        V((T, D), bf),
        V((D, T), bf),
        V((T, FF), bf),
        V((T, FF), bf),
        V((T, D), bf),
        V((T, D), bf),
        V((T, T), bf),
        V((T, T), bf),
        V((T, LANES), f32),
        V((T, LANES), f32),
        V((4, T, LANES), bf),
        V((GROUPS, STATE_ROWS, LANES), bf),
        V((GROUPS, STATE_ROWS, LANES), bf),
        V((GROUPS, STATE_ROWS, LANES), bf),
        V((GROUPS, STATE_ROWS, LANES), bf),
        V((3 * LANES, LANES), f32),
        V((H, LANES, LANES), bf),
        V((H, LANES, LANES), bf),
        V((LANES, LANES), f32),
        V((UNITS, 2, 2, rows, D), bf),
        V((UNITS, 2, 2, rows // 2, D), bf),
        V((UNITS, 2, rows // 2, D), bf),
        V((UNITS, 2, rows, D), bf),
        V((5, 16, D), f32),
        pltpu.SemaphoreType.DMA((19,)),
        pltpu.SemaphoreType.DMA((9, 17)),
        pltpu.SemaphoreType.DMA((9, 17)),
        pltpu.SemaphoreType.DMA((2, GROUPS)),
        pltpu.SemaphoreType.DMA((2, GROUPS)),
        pltpu.SemaphoreType.DMA((UNITS, 13)),
        pltpu.SemaphoreType.DMA((UNITS, 13)),
        pltpu.SemaphoreType.DMA((5,)),
        pltpu.SemaphoreType.DMA((5,)),
        pltpu.SemaphoreType.REGULAR,
        V((T, D), f32),
    ]
    return pl.pallas_call(
        functools.partial(layer_kernel, n_head, lengths.shape[0]),
        out_shape=out_shape,
        in_specs=[pl.BlockSpec(memory_space=pltpu.SMEM)] + [anywhere] * 6 + [vm],
        out_specs=[anywhere] * 6 + [vm],
        scratch_shapes=scratch,
        compiler_params=pltpu.CompilerParams(
            collective_id=0, has_side_effects=True, vmem_limit_bytes=VMEM_BYTES
        ),
        name="layer",
    )(lengths, tokens, cotangent, *masters, vector_master)


VMEM_BYTES = 63 * 1024 * 1024


RATES = (1.0 / math.sqrt(D), 1.0 / math.sqrt(OUT_FAN), 1.0 / math.sqrt(D), 1.0 / math.sqrt(FF))
ADAM_ROWS = 32


def adam_step(master, first, second, gradient, rate, decay):
    first_new = first_decay * first + (1.0 - first_decay) * gradient
    second_new = second_decay * second + (1.0 - second_decay) * gradient * gradient
    root = jnp.sqrt(second_new * (1.0 / (1.0 - second_decay**STEP)))
    ratio = (first_new * (rate / (1.0 - first_decay**STEP))) / (root + adam_epsilon)
    return first_new, second_new, master * (1.0 - rate * decay) - ratio


def adam_kernel(*refs):
    ins, outs = refs[:22], refs[22:]
    for i in range(2):
        outs[i][...] = ins[i][...]

    @pl.when(pl.program_id(0) == 0)
    def _():
        vector_new = adam_step(
            ins[18][...], ins[19][...], ins[20][...], ins[21][0:13, :], vector_rate, 0.0
        )
        for i in range(3):
            outs[14 + i][...] = vector_new[i]

    for m in range(4):
        master, first, second, grad = ins[2 + 4 * m : 6 + 4 * m]
        news = adam_step(
            master[...],
            first[...],
            second[...],
            grad[...].astype(jnp.float32),
            RATES[m],
            weight_decay,
        )
        for i in range(3):
            outs[2 + 3 * m + i][...] = news[i]


def adam_all(output, input_grad, masters, firsts, seconds, grads, vectors):
    n_steps = masters[1].shape[0] // ADAM_ROWS

    def rows_of(a):
        return pl.BlockSpec((a.shape[0] // n_steps, a.shape[1]), lambda i: (i, 0))

    def whole(a):
        return pl.BlockSpec(a.shape, lambda i: (0, 0))

    args = [output, input_grad]
    step_rows = pl.cdiv(output.shape[0], n_steps * ADAM_ROWS) * ADAM_ROWS
    in_specs = [pl.BlockSpec((step_rows, D), lambda i: (i, 0))] * 2
    out_shape = [jax.ShapeDtypeStruct(a.shape, a.dtype) for a in args]
    out_specs = list(in_specs)
    for quad in zip(masters, firsts, seconds, grads):
        args += quad
        in_specs += [rows_of(a) for a in quad]
        out_shape += [jax.ShapeDtypeStruct(a.shape, jnp.float32) for a in quad[:3]]
        out_specs += [rows_of(a) for a in quad[:3]]
    args += vectors
    in_specs += [whole(a) for a in vectors]
    out_shape += [jax.ShapeDtypeStruct(a.shape, jnp.float32) for a in vectors[:3]]
    out_specs += [whole(a) for a in vectors[:3]]
    return pl.pallas_call(
        adam_kernel,
        grid=(n_steps,),
        out_shape=out_shape,
        in_specs=in_specs,
        out_specs=out_specs,
        compiler_params=pltpu.CompilerParams(vmem_limit_bytes=VMEM_BYTES),
        name="adam",
    )(*args)


def fused_shards(
    tokens,
    cotangent,
    lengths,
    qkv_master,
    out_master,
    up_master,
    down_master,
    vector_master,
    qkv_first,
    qkv_second,
    out_first,
    out_second,
    up_first,
    up_second,
    down_first,
    down_second,
    vector_first,
    vector_second,
):
    masters = (qkv_master, out_master, up_master, down_master)
    output, input_grad, *grads, vector_grad = fused_layer(
        lengths, tokens, cotangent, masters, vector_master
    )
    firsts = (qkv_first, out_first, up_first, down_first)
    seconds = (qkv_second, out_second, up_second, down_second)
    vectors = [vector_master, vector_first, vector_second, vector_grad]
    return tuple(adam_all(output, input_grad, masters, firsts, seconds, grads, vectors))


def solution(mesh):
    return jax.shard_map(
        fused_shards if fits(mesh) else shards,
        mesh=mesh,
        in_specs=(
            P(("dp", "head"), None),
            P(("dp", "head"), None),
            P("dp"),
            P("dp", None),
            P("dp", None),
            P("dp", None),
            P("dp", None),
            P(),
            P("dp", None),
            P("dp", None),
            P("dp", None),
            P("dp", None),
            P("dp", None),
            P("dp", None),
            P("dp", None),
            P("dp", None),
            P(),
            P(),
        ),
        out_specs=(
            P(("dp", "head"), None),
            P(("dp", "head"), None),
            P("dp", None),
            P("dp", None),
            P("dp", None),
            P("dp", None),
            P("dp", None),
            P("dp", None),
            P("dp", None),
            P("dp", None),
            P("dp", None),
            P("dp", None),
            P("dp", None),
            P("dp", None),
            P(),
            P(),
            P(),
        ),
        check_vma=False,
    )
```
